128 devices in a mesh: page: 32 (over y, x, core), tp: 4 (over z).
Axes of the slice: x: 4, y: 4, z: 4, core: 2. Of those that a mesh axis runs over, the one named last changes fastest.
Arguments:
- x3: bfloat16 [800, 32, 4, 512], P('page', None, None, 'tp'), may hold values from -150 to 150
- res_group: int32 [32], P('page'), may hold values from 0 to 3, as said below
- merge_gain: float32 [4, 512], P(None, 'tp'), may hold values from 0.5 to 1.5
- merge_bias: float32 [4, 512], P(None, 'tp'), may hold values from -1.5 to 1.5
- merge_w: bfloat16 [4, 512, 1024], P(None, 'tp'), may hold values from -0.125 to 0.125
- ln1_gain: float32 [2, 1024], replicated, may hold values from 0.5 to 1.5
- ln1_bias: float32 [2, 1024], replicated, may hold values from -1.5 to 1.5
- qkv_w: bfloat16 [2, 1024, 3, 1024], P(None, None, None, 'tp'), may hold values from -0.1875 to 0.1875
- qv_bias: float32 [2, 2, 1024], P(None, None, 'tp'), may hold values from -2.5 to 2.5
- rel_table: float32 [2, 32, 361], P(None, 'tp'), may hold values from -4 to 4
- proj_w: bfloat16 [2, 1024, 1024], P(None, 'tp'), may hold values from -1 to 1
- proj_bias: float32 [2, 1024], replicated, may hold values from -1.5 to 1.5
- ln2_gain: float32 [2, 1024], replicated, may hold values from 0.5 to 1.5
- ln2_bias: float32 [2, 1024], replicated, may hold values from -1.5 to 1.5
- fc1_w: bfloat16 [2, 1024, 4096], P(None, None, 'tp'), may hold values from -0.1875 to 0.1875
- fc1_bias: float32 [2, 4096], P(None, 'tp'), may hold values from -1.5 to 1.5
- fc2_w: bfloat16 [2, 4096, 1024], P(None, 'tp'), may hold values from -0.125 to 0.125
- fc2_bias: float32 [2, 1024], replicated, may hold values from -1.5 to 1.5
- out_grad: bfloat16 [32, 20, 40, 1024], P('page'), may hold values from -6 to 6
Outputs:
- output: float32 [32, 20, 40, 1024], P('page')
- grad_x3: float32 [800, 32, 4, 512], P('page', None, None, 'tp')
- g_merge_gain: float32 [4, 512], P(None, 'tp')
- g_merge_bias: float32 [4, 512], P(None, 'tp')
- g_merge_w: float32 [4, 512, 1024], P(None, 'tp', 'page')
- g_ln1_gain: float32 [2, 1024], P(None, 'page')
- g_ln1_bias: float32 [2, 1024], P(None, 'page')
- g_qkv_w: float32 [2, 1024, 3, 1024], P(None, 'page', None, 'tp')
- g_qv_bias: float32 [2, 2, 1024], P(None, None, 'tp')
- g_rel_table: float32 [2, 32, 361], P(None, 'tp')
- g_proj_w: float32 [2, 1024, 1024], P(None, 'tp', 'page')
- g_proj_bias: float32 [2, 1024], P(None, 'page')
- g_ln2_gain: float32 [2, 1024], P(None, 'page')
- g_ln2_bias: float32 [2, 1024], P(None, 'page')
- g_fc1_w: float32 [2, 1024, 4096], P(None, 'page', 'tp')
- g_fc1_bias: float32 [2, 4096], P(None, 'tp')
- g_fc2_w: float32 [2, 4096, 1024], P(None, 'tp', 'page')
- g_fc2_bias: float32 [2, 1024], P(None, 'page')
The draws below stay inside these ranges and needn't reach their ends.
Inputs may be any that keep to these rules, and one draw needn't show every extreme that they name: Page p has 10 * (res_group[p] + 1) columns of real tokens, the rest of its 40 columns is padding; in every draw some page has all 4 window columns.
All inputs are finite; a program needn't handle non-finite values.
Results may differ from the reference program's by a relative error of at most 0.03.
Values may be sent and summed in bfloat16 or wider, within the bound.
No kernel may reach another device: no remote copies, remote signals or barrier semaphores. Data moves between devices by JAX's collectives and lax.ppermute only.
A program may use at most 256 MiB of HBM per device.

```python
import jax
import jax.numpy as jnp
from jax import lax

C3 = 512
D = 1024
HEADS = 32
HD = 32
FF = 4096
WIN = 10
WCOLS = 4
SHIFT = 5
GH = 20
GW = 40
POS = 800
RELS = 361
PAGES = 32


def draw_x3(key, part):
    key = jax.random.fold_in(key, 11)
    key_list = jax.random.split(key, 4)
    along_axis = jnp.arange(C3, dtype=jnp.float32)[None, :] / C3
    jitter = jax.random.uniform(key_list[1], (4, C3), jnp.float32)
    row_scale = 10.0 ** jax.random.uniform(key_list[2], (POS, PAGES, 1, 1), jnp.float32)
    common = jax.random.truncated_normal(key_list[3], -4.0, 4.0, (4, C3), jnp.float32)
    col_scale = 10.0 ** (4.0 * (0.5 * along_axis + 0.5 * jitter))
    base_draw = jax.random.truncated_normal(key_list[0], -4.0, 4.0, (POS, PAGES, 4, C3), jnp.float32)
    field = base_draw + 0.3 * common
    return (0.00025 * row_scale * col_scale * field).astype(jnp.bfloat16)


def draw_res_group(key, part):
    key = jax.random.fold_in(key, 12)
    key_one, key_two = jax.random.split(key)
    groups = jax.random.randint(key_one, (PAGES,), 0, WCOLS, dtype=jnp.int32)
    widest = jax.random.randint(key_two, (), 0, PAGES, dtype=jnp.int32)
    return groups.at[widest].set(WCOLS - 1)


def spiked(drawn, key, source, target, blocks, factor):
    owner, partner = [(jnp.arange(drawn.shape[axis_at]) // (drawn.shape[axis_at] // blocks)).reshape([-1 if axis == axis_at else 1 for axis in range(drawn.ndim)]) for axis_at in (source, target)]
    chosen = jax.random.permutation(key, blocks)[partner]
    strong = (owner == chosen) | (owner == (partner + blocks // 2) % blocks)
    return jnp.where(strong, factor * drawn, drawn)


def steps_of(stream_key, extent, cuts, low, high):
    factor_of, own = 1.0, jax.random.fold_in(stream_key, 6)
    for axis_at, blocks in cuts:
        draws = jnp.exp(jax.random.uniform(jax.random.fold_in(own, axis_at), (blocks,), jnp.float32, low / len(cuts), high / len(cuts)))
        factor_of = factor_of * jnp.repeat(draws, extent[axis_at] // blocks).reshape([-1 if axis == axis_at else 1 for axis in range(len(extent))])
    return factor_of


def bell_draw(own_key, extent, scale, reach, cuts=(), held_as=jnp.bfloat16):
    entries = scale * jax.random.normal(own_key, extent, jnp.float32)
    if cuts:
        entries = entries * steps_of(own_key, extent, cuts, -0.22, 0.18)
    return jnp.clip(entries, -reach, reach).astype(held_as)


def heavy_noise(key, dims, deviation, reach, shards, heavy, kind=jnp.bfloat16):
    drawn = deviation * jax.random.normal(key, dims, jnp.float32)
    if shards:
        drawn = drawn * steps_of(key, dims, shards, -0.22, 0.18)
    return jnp.clip(spiked(drawn, jax.random.fold_in(key, 3), *heavy), -reach, reach).astype(kind)


def setup_inputs(seed: int = 0) -> dict:
    splits = jax.random.split(jax.random.key(seed), 20)
    return {
        "x3": draw_x3(jax.random.fold_in(splits[19], 71), 0),
        "res_group": draw_res_group(jax.random.fold_in(splits[19], 71), 0),
        "merge_gain": jnp.clip(1.0 + 0.1 * jax.random.normal(splits[2], (4, C3), jnp.float32), 0.5, 1.5),
        "merge_bias": bell_draw(splits[3], (4, C3), 0.3, 1.5, ((1, 4),), jnp.float32),
        "merge_w": bell_draw(splits[4], (4, C3, D), (4 * C3) ** -0.5, 0.125, ((1, 4),)),
        "ln1_gain": jnp.clip(1.0 + 0.1 * jax.random.normal(splits[5], (2, D), jnp.float32), 0.5, 1.5),
        "ln1_bias": bell_draw(splits[6], (2, D), 0.3, 1.5, (), jnp.float32),
        "qkv_w": bell_draw(splits[7], (2, D, 3, D), D ** -0.5, 0.1875, ((3, 4),)),
        "qv_bias": bell_draw(splits[8], (2, 2, D), 0.5, 2.5, ((2, 4),), jnp.float32),
        "rel_table": bell_draw(splits[9], (2, HEADS, RELS), 1.0, 4.0, ((1, 4),), jnp.float32),
        "proj_w": bell_draw(splits[10], (2, D, D), (D // 32) ** -0.5, 1.0, ((1, 4),)),
        "proj_bias": bell_draw(splits[11], (2, D), 0.3, 1.5, (), jnp.float32),
        "ln2_gain": jnp.clip(1.0 + 0.1 * jax.random.normal(splits[12], (2, D), jnp.float32), 0.5, 1.5),
        "ln2_bias": bell_draw(splits[13], (2, D), 0.3, 1.5, (), jnp.float32),
        "fc1_w": bell_draw(splits[14], (2, D, FF), D ** -0.5, 0.1875, ((2, 4),)),
        "fc1_bias": bell_draw(splits[15], (2, FF), 0.3, 1.5, ((1, 4),), jnp.float32),
        "fc2_w": bell_draw(splits[16], (2, FF, D), (FF // 2) ** -0.5, 0.125, ((1, 4),)),
        "fc2_bias": bell_draw(splits[17], (2, D), 0.3, 1.5, (), jnp.float32),
        "out_grad": heavy_noise(splits[18], (PAGES, GH, GW, D), 1.0, 6.0, ((0, 32),), (0, 3, 32, 2.75)),
    }


EPS = 1e-05
HIGH = lax.Precision.HIGHEST

@jax.custom_vjp
def low(v):
    return lax.optimization_barrier(v.astype(jnp.bfloat16)).astype(jnp.float32)

@jax.custom_vjp
def low_back(v):
    return v

def low_keep(v):
    return (low(v), None)

def low_pass(kept, grad):
    return (grad,)

def back_keep(v):
    return (v, None)

def back_low(kept, grad):
    return (low(grad),)
low.defvjp(low_keep, low_pass)
low_back.defvjp(back_keep, back_low)

def rounded(value):
    return low_back(low(value))

def layer_norm(value, gain, shift_bias):
    center = value - lax.optimization_barrier(jnp.mean(value, axis=-1, keepdims=True))
    spread = lax.optimization_barrier(jnp.mean(center * center, axis=-1, keepdims=True))
    return center * lax.rsqrt(spread + EPS) * gain + shift_bias

def to_windows(grid):
    width = grid.shape[-1]
    blocks = grid.reshape(GH // WIN, WIN, GW // WIN, WIN, width).transpose(0, 2, 1, 3, 4)
    return blocks.reshape(-1, WIN * WIN, width)

def from_windows(tiles):
    width = tiles.shape[-1]
    blocks = tiles.reshape(GH // WIN, GW // WIN, WIN, WIN, width).transpose(0, 2, 1, 3, 4)
    return blocks.reshape(GH, GW, width)

def pair_index():
    places = jnp.arange(WIN * WIN, dtype=jnp.int32)
    row_of = places // WIN
    col_of = places % WIN
    return (row_of[:, None] - row_of[None, :] + WIN - 1) * (2 * WIN - 1) + (col_of[:, None] - col_of[None, :] + WIN - 1)

def window_mask(valid, offset):
    row_ids = jnp.arange(GH, dtype=jnp.int32)
    col_ids = jnp.arange(GW, dtype=jnp.int32)
    source_col = (col_ids + offset) % GW
    usable = jnp.broadcast_to((source_col < valid)[None, :], (GH, GW))
    if offset:
        row_region = (row_ids >= GH - WIN).astype(jnp.int32) + (row_ids >= GH - offset).astype(jnp.int32)
        col_region = (col_ids >= GW - WIN).astype(jnp.int32) + (col_ids >= GW - offset).astype(jnp.int32)
        region = row_region[:, None] * 3 + col_region[None, :]
    else:
        region = jnp.zeros((GH, GW), jnp.int32)
    region_tiles = to_windows(region[:, :, None])[:, :, 0]
    usable_tiles = to_windows(usable[:, :, None])[:, :, 0]
    allowed = (region_tiles[:, :, None] == region_tiles[:, None, :]) & usable_tiles[:, None, :]
    return jnp.where(allowed, jnp.float32(0.0), jnp.float32(-100.0))

def block(state, level, params, valid):
    merge_gain, merge_bias, merge_w, ln1_gain, ln1_bias, qkv_w, qv_bias, rel_table, proj_w, proj_bias, ln2_gain, ln2_bias, fc1_w, fc1_bias, fc2_w, fc2_bias = params
    offset = SHIFT if level == 1 else 0
    normed = low(layer_norm(state, ln1_gain[level], ln1_bias[level]))
    if offset:
        normed = jnp.roll(normed, (-offset, -offset), (0, 1))
    tiles = to_windows(normed)
    count = tiles.shape[0]
    mixed = jnp.einsum('wtd,dce->wtce', tiles, qkv_w[level], precision=HIGH)
    queries = rounded(mixed[:, :, 0] + qv_bias[level, 0]).reshape(count, WIN * WIN, HEADS, HD)
    key_rows = rounded(mixed[:, :, 1]).reshape(count, WIN * WIN, HEADS, HD)
    values = rounded(mixed[:, :, 2] + qv_bias[level, 1]).reshape(count, WIN * WIN, HEADS, HD)
    position_bias = rel_table[level][:, pair_index()]
    scores = jnp.einsum('wihd,wjhd->whij', queries, key_rows, precision=HIGH) * HD ** (-0.5)
    scores = low_back(scores + position_bias[None] + window_mask(valid, offset)[:, None])
    top = lax.optimization_barrier(jnp.max(scores, axis=-1, keepdims=True))
    exp_terms = jnp.exp(scores - top)
    prob_rows = exp_terms / lax.optimization_barrier(jnp.sum(exp_terms, axis=-1, keepdims=True))
    heads_out = jnp.einsum('whij,wjhd->wihd', low(prob_rows), values, precision=HIGH).reshape(count, WIN * WIN, D)
    heads_out = rounded(heads_out)
    branch = low_back(jnp.einsum('wte,ef->wtf', heads_out, proj_w[level], precision=HIGH) + proj_bias[level])
    branch = from_windows(branch)
    if offset:
        branch = jnp.roll(branch, (offset, offset), (0, 1))
    middle = state + branch
    second = low(layer_norm(middle, ln2_gain[level], ln2_bias[level]))
    hidden_pre = low_back(jnp.dot(second, fc1_w[level], precision=HIGH) + fc1_bias[level])
    activated = low(jax.nn.gelu(hidden_pre, approximate=False))
    mlp_branch = low_back(jnp.dot(activated, fc2_w[level], precision=HIGH) + fc2_bias[level])
    return middle + mlp_branch

def page_forward(page_in, group, params):
    merge_gain, merge_bias, merge_w = (params[0], params[1], params[2])
    valid = (group + 1) * WIN
    flat = page_in.reshape(POS, 4 * C3)
    merged_norm = low(layer_norm(flat, merge_gain.reshape(-1), merge_bias.reshape(-1)))
    state = low_back(jnp.dot(merged_norm, merge_w.reshape(4 * C3, D), precision=HIGH)).reshape(GH, GW, D)
    for level in range(2):
        state = block(state, level, params, valid)
    keep = (jnp.arange(GW, dtype=jnp.int32) < valid).astype(jnp.float32)
    return state * keep[None, :, None]

def reference(x3, res_group, merge_gain, merge_bias, merge_w, ln1_gain, ln1_bias, qkv_w, qv_bias, rel_table, proj_w, proj_bias, ln2_gain, ln2_bias, fc1_w, fc1_bias, fc2_w, fc2_bias, out_grad):
    params = tuple((item.astype(jnp.float32) for item in (merge_gain, merge_bias, merge_w, ln1_gain, ln1_bias, qkv_w, qv_bias, rel_table, proj_w, proj_bias, ln2_gain, ln2_bias, fc1_w, fc1_bias, fc2_w, fc2_bias)))
    pages_in = jnp.swapaxes(x3, 0, 1)

    def step(totals, item):
        page_in, group, cotangent = item
        result, pull = jax.vjp(lambda inputs, weights: page_forward(inputs, group, weights), page_in.astype(jnp.float32), params)
        grad_in, grad_params = pull(cotangent.astype(jnp.float32))
        return (jax.tree.map(jnp.add, totals, grad_params), (result, grad_in))
    zeros = jax.tree.map(jnp.zeros_like, params)
    totals, (results, grads_in) = lax.scan(step, zeros, (pages_in, res_group, out_grad))
    grad_x3 = jnp.swapaxes(grads_in, 0, 1)
    return (results, grad_x3, totals[0], totals[1], totals[2], totals[3], totals[4], totals[5], totals[6], totals[7], totals[8], totals[9], totals[10], totals[11], totals[12], totals[13], totals[14], totals[15])
```

```python
from functools import partial

import jax
import jax.numpy as jnp
import numpy as np
from jax import lax
from jax.experimental import pallas as pl
from jax.experimental.pallas import tpu as pltpu
from jax.sharding import Mesh
from jax.sharding import PartitionSpec as P

D = 1024
FF = 4096
MERGED = 2048
WIN = 10
SHIFT = 5
GH = 20
GW = 40
RELS = 361
TOK = 100
ROWS = 112
T = 2 * ROWS
SEND = 112
EPS = 1e-05
SCALE = 32 ** (-0.5)
YX = 16
TP = 4
UNITS = 26
HIGH = lax.Precision.HIGHEST
BF = jnp.bfloat16
F32 = jnp.float32
PAGE_AXES = ("y", "x", "core")
CHIP_AXES = ("y", "x")
GATHER_AXES = ("tp", "y", "x", "core")
VMEM = 58 << 20


def row_at(row, col):
    return (row // WIN) * ROWS + (row % WIN) * WIN + col


def place_matrices():
    own = np.zeros((T, T), np.float32)
    recv = np.zeros((T, SEND), np.float32)
    send = np.zeros((SEND, T), np.float32)
    pack = np.zeros((2 * TOK, T), np.float32)
    out = np.zeros((2 * TOK, T), np.float32)
    for row in range(GH):
        for col in range(WIN):
            source = (row + SHIFT) % GH
            if col < SHIFT:
                own[row_at(row, col), row_at(source, col + SHIFT)] = 1
                send[row * SHIFT + col, row_at(row, col)] = 1
            else:
                recv[row_at(row, col), source * SHIFT + col - SHIFT] = 1
            pack[row * WIN + col, row_at(row, col)] = 1
            out[source * WIN + col, row_at(row, col)] = 1
    return own, recv, send, pack, out


OWN, RECV, SENT, PACK, OUT = place_matrices()


def const(matrix):
    return jnp.asarray(matrix, BF)


def dot(left, right):
    return lax.dot_general(left, right, (((1,), (0,)), ((), ())), preferred_element_type=F32)


def dot_nt(left, right):
    return lax.dot_general(left, right, (((1,), (1,)), ((), ())), preferred_element_type=F32)


def dot_tn(left, right):
    return lax.dot_general(left, right, (((0,), (0,)), ((), ())), preferred_element_type=F32)


def select_rows(matrix, value):
    high = value.astype(BF)
    rest = value - high.astype(F32)
    mid = rest.astype(BF)
    low = (rest - mid.astype(F32)).astype(BF)
    return dot(matrix, high) + dot(matrix, mid) + dot(matrix, low)


def norm_stats(value):
    mean = jnp.mean(value, axis=-1, keepdims=True)
    center = value - mean
    return center, lax.rsqrt(jnp.mean(center * center, axis=-1, keepdims=True) + EPS)


def norm_back(upstream, normed, spread, gain):
    scaled = upstream * gain
    inner = (
        scaled
        - jnp.mean(scaled, axis=-1, keepdims=True)
        - normed * jnp.mean(scaled * normed, axis=-1, keepdims=True)
    )
    return spread * inner


def col_sum(value):
    return jnp.sum(value, axis=0, keepdims=True)


def whole(shape):
    return pl.BlockSpec(shape, lambda step, core: (0,) * len(shape))


def shape_of(shape, dtype):
    return jax.ShapeDtypeStruct(shape, dtype)


def run(kernel, steps, core, args, in_specs, outs, out_specs, scratch, flops, moved):
    return pl.pallas_call(
        kernel,
        grid_spec=pltpu.PrefetchScalarGridSpec(
            num_scalar_prefetch=1,
            grid=(steps,),
            in_specs=in_specs,
            out_specs=out_specs,
            scratch_shapes=scratch,
        ),
        out_shape=outs,
        compiler_params=pltpu.CompilerParams(
            vmem_limit_bytes=VMEM, dimension_semantics=("arbitrary",)
        ),
        cost_estimate=pl.CostEstimate(flops=flops, bytes_accessed=moved, transcendentals=0),
    )(core, *args)


def put_halves(core_ref, mine, other, low, high):
    @pl.when(core_ref[0] == 0)
    def _():
        mine(low)
        other(high)

    @pl.when(core_ref[0] != 0)
    def _():
        mine(high)
        other(low)


def merge_stats(x_ref, pack_ref, full):
    total = jnp.zeros((T, 1), F32)
    for part in range(TP):
        rows = dot_tn(pack_ref[...], x_ref[part])
        full[part] = rows
        total = total + jnp.sum(rows, axis=-1, keepdims=True)
    mean = total / MERGED
    square = jnp.zeros((T, 1), F32)
    for part in range(TP):
        center = full[part] - mean
        square = square + jnp.sum(center * center, axis=-1, keepdims=True)
    return mean, lax.rsqrt(square / MERGED + EPS)


def merge_kernel(
    core_ref, x_ref, pack_ref, gain_ref, bias_ref, w_ref, out_ref, mine_ref, other_ref, full, stats
):
    step = pl.program_id(0)

    @pl.when(step == 0)
    def _():
        mean, spread = merge_stats(x_ref, pack_ref, full)
        stats[0] = mean
        stats[1] = spread

    normed = (full[step] - stats[0]) * stats[1]
    value = (normed * gain_ref[0] + bias_ref[0]).astype(BF)

    def set_mine(part):
        mine_ref[...] = part

    def set_other(part):
        other_ref[...] = part

    put_halves(core_ref, set_mine, set_other, value[:, :256], value[:, 256:])
    term = dot(value, w_ref[...].reshape(512, D))

    @pl.when(step == 0)
    def _():
        out_ref[...] = term

    @pl.when(step != 0)
    def _():
        out_ref[...] += term


def merge_forward(core, parts, gain, bias, weights):
    return run(
        merge_kernel,
        TP,
        core,
        (parts, const(PACK), gain.reshape(TP, 1, 512), bias.reshape(TP, 1, 512), weights),
        [
            whole((TP, 2 * TOK, 512)),
            whole((2 * TOK, T)),
            pl.BlockSpec((1, 1, 512), lambda step, core: (step, 0, 0)),
            pl.BlockSpec((1, 1, 512), lambda step, core: (step, 0, 0)),
            pl.BlockSpec((YX, 2, 16, D), lambda step, core: (step, 12, 0, 0)),
        ],
        [shape_of((T, D), F32), shape_of((T, D), BF), shape_of((T, D), BF)],
        [
            whole((T, D)),
            pl.BlockSpec((T, 256), lambda step, core: (0, step)),
            pl.BlockSpec((T, 256), lambda step, core: (0, step)),
        ],
        [pltpu.VMEM((TP, T, 512), F32), pltpu.VMEM((2, T, 1), F32)],
        2 * T * MERGED * D,
        8 << 20,
    )


def merge_back_kernel(
    core_ref, x_ref, pack_ref, gain_ref, w_ref, dx_ref,
    start_ref, dm_ref, gains_ref, biases_ref,
    full, stats, upstream,
):
    step = pl.program_id(0)

    @pl.when(step == 0)
    def _():
        mean, spread = merge_stats(x_ref, pack_ref, full)
        stats[0] = mean
        stats[1] = spread
        stats[2] = jnp.zeros((T, 1), F32)
        stats[3] = jnp.zeros((T, 1), F32)
        start_ref[...] = dx_ref[...].astype(BF)

    grad = dot_nt(start_ref[...], w_ref[...].reshape(512, D))
    normed = (full[step] - stats[0]) * stats[1]
    full[step] = normed
    gains_ref[0] = col_sum(grad * normed)
    biases_ref[0] = col_sum(grad)
    scaled = grad * gain_ref[0]
    upstream[step] = scaled
    stats[2] += jnp.sum(scaled, axis=-1, keepdims=True)
    stats[3] += jnp.sum(scaled * normed, axis=-1, keepdims=True)

    @pl.when(step == TP - 1)
    def _():
        for part in range(TP):
            value = stats[1] * (
                upstream[part] - stats[2] / MERGED - full[part] * (stats[3] / MERGED)
            )
            dm_ref[part] = dot(pack_ref[...], value.astype(BF)).astype(BF)


def merge_backward(core, parts, gain, weights, grad):
    return run(
        merge_back_kernel,
        TP,
        core,
        (parts, const(PACK), gain.reshape(TP, 1, 512), weights, grad),
        [
            whole((TP, 2 * TOK, 512)),
            whole((2 * TOK, T)),
            pl.BlockSpec((1, 1, 512), lambda step, core: (step, 0, 0)),
            pl.BlockSpec((YX, 2, 16, D), lambda step, core: (step, 12, 0, 0)),
            whole((T, D)),
        ],
        [
            shape_of((T, D), BF),
            shape_of((TP, 2 * TOK, 512), BF),
            shape_of((TP, 1, 512), F32),
            shape_of((TP, 1, 512), F32),
        ],
        [
            whole((T, D)),
            whole((TP, 2 * TOK, 512)),
            pl.BlockSpec((1, 1, 512), lambda step, core: (step, 0, 0)),
            pl.BlockSpec((1, 1, 512), lambda step, core: (step, 0, 0)),
        ],
        [pltpu.VMEM((TP, T, 512), F32), pltpu.VMEM((4, T, 1), F32), pltpu.VMEM((TP, T, 512), F32)],
        2 * T * MERGED * D,
        8 << 20,
    )


def head_masks(rows):
    lane = lax.broadcasted_iota(jnp.int32, (rows, 128), 1)
    return [(lane >= 32 * place) & (lane < 32 * place + 32) for place in range(4)]


def spread_heads(value, masks):
    zero = jnp.zeros_like(value)
    return jnp.concatenate([jnp.where(mask, value, zero) for mask in masks], axis=0)


def fold_heads(value, masks):
    total = jnp.zeros((ROWS, 128), F32)
    for place, mask in enumerate(masks):
        total = jnp.where(mask, value[place * ROWS : (place + 1) * ROWS], total)
    return total


def attn_kernel(level, *refs):
    (core_ref, x_ref), refs = refs[:2], refs[2:]
    if level:
        (halo_ref, own_ref, recv_ref), refs = refs[:3], refs[3:]
    (
        gain_ref, bias_ref, wq_ref, wk_ref, wv_ref, wp_ref, qb_ref, vb_ref, table_ref, mask_ref,
        shift_ref,
    ), refs = refs[:11], refs[11:]
    (
        mid_ref, a_ref, q_ref, k_ref, v_ref, probs_ref, mine_ref, other_ref,
    ), refs = refs[:8], refs[8:]
    step = pl.program_id(0)

    @pl.when(step == 0)
    def _():
        value = x_ref[...]
        if level:
            value = select_rows(own_ref[...], value) + dot(recv_ref[...], halo_ref[...])
            refs[0][...] = value
        center, spread = norm_stats(value)
        a_ref[...] = (center * spread * gain_ref[...] + bias_ref[...]).astype(BF)
        mid_ref[...] = value + shift_ref[...]

    a = a_ref[...]
    q = (dot_nt(a, wq_ref[...].reshape(256, D)) + qb_ref[...]).astype(BF)
    k = dot_nt(a, wk_ref[...].reshape(256, D)).astype(BF)
    v = (dot_nt(a, wv_ref[...].reshape(256, D)) + vb_ref[...]).astype(BF)
    q_ref[...] = q
    k_ref[...] = k
    v_ref[...] = v
    masks = head_masks(ROWS)
    halves = []
    for half in range(2):
        lanes = slice(half * 128, half * 128 + 128)
        table = table_ref[4 * half : 4 * half + 4]
        parts = []
        for w in range(2):
            rows = slice(w * ROWS, (w + 1) * ROWS)
            raw = dot_nt(spread_heads(q[rows, lanes], masks), k[rows, lanes]) * SCALE
            scores = raw.reshape(4, ROWS, ROWS) + table + mask_ref[w][None]
            top = jnp.max(scores, axis=-1, keepdims=True)
            terms = jnp.exp(scores - top)
            probs = terms / jnp.sum(terms, axis=-1, keepdims=True)
            probs_ref[0, w, 4 * half : 4 * half + 4] = probs
            mixed = dot(probs.astype(BF).reshape(4 * ROWS, ROWS), v[rows, lanes])
            parts.append(fold_heads(mixed, masks))
        halves.append(jnp.concatenate(parts, axis=0).astype(BF))

    def set_mine(part):
        mine_ref[...] = part

    def set_other(part):
        other_ref[...] = part

    put_halves(core_ref, set_mine, set_other, *halves)
    heads = jnp.concatenate(halves, axis=1)
    mid_ref[...] += dot(heads, wp_ref[...].reshape(256, D))


def unit_spec(unit):
    return pl.BlockSpec((YX, 1, 16, D), lambda step, core: (step, unit, 0, 0))


def attn_forward(core, level, state, halo, weights, small, table, mask):
    gain, bias, qbias, vbias, shift = small
    unit = 16 + 4 * level
    args = [state]
    specs = [whole((T, D))]
    if level:
        args += [halo, const(OWN), const(RECV)]
        specs += [whole((SEND, D)), whole((T, T)), whole((T, SEND))]
    args += [gain, bias, weights, weights, weights, weights, qbias, vbias, table, mask, shift]
    cols = pl.BlockSpec((1, 256), lambda step, core: (0, step))
    specs += [whole((1, D)), whole((1, D))] + [unit_spec(unit + place) for place in range(4)]
    specs += [
        cols,
        cols,
        pl.BlockSpec((8, ROWS, ROWS), lambda step, core: (step, 0, 0)),
        whole((2, ROWS, ROWS)),
        whole((1, D)),
    ]
    block = pl.BlockSpec((T, 256), lambda step, core: (0, step))
    half = pl.BlockSpec((T, 128), lambda step, core: (0, step))
    outs = [
        shape_of((T, D), F32),
        shape_of((T, D), BF),
        shape_of((T, D), BF),
        shape_of((T, D), BF),
        shape_of((T, D), BF),
        shape_of((TP, 2, 8, ROWS, ROWS), F32),
        shape_of((T, D // 2), BF),
        shape_of((T, D // 2), BF),
    ]
    out_specs = [
        whole((T, D)),
        whole((T, D)),
        block,
        block,
        block,
        pl.BlockSpec((1, 2, 8, ROWS, ROWS), lambda step, core: (step, 0, 0, 0, 0)),
        half,
        half,
    ]
    if level:
        outs.append(shape_of((T, D), F32))
        out_specs.append(whole((T, D)))
    return run(
        partial(attn_kernel, level), TP, core, args, specs, outs, out_specs, [], 8 * T * D * D, 24 << 20
    )


def mlp_kernel(level, *refs):
    (
        core_ref, mid_ref, gain_ref, bias_ref, w1_ref, w2_ref, b1_ref, b2_ref, place_ref, keep_ref,
        c2_ref, slope_ref, mine_ref, other_ref, extra_ref,
    ), refs = refs[:15], refs[15:]
    total = refs[0]
    step = pl.program_id(0)

    @pl.when(step == 0)
    def _():
        value = mid_ref[...]
        center, spread = norm_stats(value)
        c2_ref[...] = (center * spread * gain_ref[...] + bias_ref[...]).astype(BF)
        total[...] = value + b2_ref[...]

    pre = dot_nt(c2_ref[...], w1_ref[...].reshape(512, D)) + b1_ref[...]
    phi = 0.5 + 0.5 * lax.erf(pre * (0.5**0.5))
    act = (pre * phi).astype(BF)
    slope_ref[...] = (phi + pre * ((2.0 * np.pi) ** -0.5 * jnp.exp(-0.5 * pre * pre))).astype(BF)

    low = lax.rem(step, 2) == core_ref[0]

    @pl.when(low)
    def _():
        mine_ref[...] = act

    @pl.when(jnp.logical_not(low))
    def _():
        other_ref[...] = act

    total[...] += dot(act, w2_ref[...].reshape(512, D))

    @pl.when(step == 2 * TP - 1)
    def _():
        value = total[...]
        if level:
            extra_ref[...] = dot(place_ref[...], (value * keep_ref[...]).astype(BF)).astype(BF)
        else:
            extra_ref[...] = dot(place_ref[...], value.astype(BF)).astype(BF)
            refs[1][...] = value


def mlp_forward(core, level, mid, weights, small, keep):
    gain, bias, b1, b2 = small
    place = const(OUT if level else SENT)
    quad = lambda unit: pl.BlockSpec((8, 4, 16, D), lambda step, core: (step, unit, 0, 0))
    half = pl.BlockSpec((T, 512), lambda step, core: (0, step // 2))
    outs = [
        shape_of((T, D), BF),
        shape_of((T, FF), BF),
        shape_of((T, FF // 2), BF),
        shape_of((T, FF // 2), BF),
        shape_of((place.shape[0], D), BF),
    ]
    out_specs = [
        whole((T, D)),
        pl.BlockSpec((T, 512), lambda step, core: (0, step)),
        half,
        half,
        whole((place.shape[0], D)),
    ]
    scratch = [pltpu.VMEM((T, D), F32)]
    if not level:
        outs.append(shape_of((T, D), F32))
        out_specs.append(whole((T, D)))

    def kernel(*refs):
        refs = list(refs)
        total = refs.pop()
        mlp_kernel(level, *refs[:15], total, *refs[15:])

    return run(
        kernel,
        2 * TP,
        core,
        (mid, gain, bias, weights, weights, b1, b2, place, keep),
        [
            whole((T, D)),
            whole((1, D)),
            whole((1, D)),
            quad(2 * level),
            quad(2 * level + 1),
            pl.BlockSpec((1, 512), lambda step, core: (0, step)),
            whole((1, D)),
            whole(place.shape),
            whole((T, 1)),
        ],
        outs,
        out_specs,
        scratch,
        4 * T * D * FF,
        24 << 20,
    )


def mlp_back_kernel(level, *refs):
    (core_ref, dx_ref), refs = refs[:2], refs[2:]
    if level:
        (keep_ref,), refs = refs[:1], refs[1:]
    else:
        (halo_ref, own_ref, sent_ref), refs = refs[:3], refs[3:]
    (mid_ref, gain_ref, w1_ref, w2_ref, slope_ref), refs = refs[:5], refs[5:]
    (
        dmid_ref, dmlp_ref, dattn_ref, mine_ref, other_ref, db1_ref, rows_ref, total, grad,
    ) = refs
    step = pl.program_id(0)

    @pl.when(step == 0)
    def _():
        if level:
            value = dx_ref[...].astype(F32) * keep_ref[...]
        else:
            value = select_rows_t(own_ref[...], dx_ref[...]) + dot_tn(sent_ref[...], halo_ref[...])
        grad[...] = value
        dmlp_ref[...] = value.astype(BF)
        total[...] = jnp.zeros((T, D), F32)

    dact = dot_nt(dmlp_ref[...], w2_ref[...].reshape(512, D))
    rounded = (dact * slope_ref[...].astype(F32)).astype(BF)
    db1_ref[...] = col_sum(rounded.astype(F32))

    low = lax.rem(step, 2) == core_ref[0]

    @pl.when(low)
    def _():
        mine_ref[...] = rounded

    @pl.when(jnp.logical_not(low))
    def _():
        other_ref[...] = rounded

    total[...] += dot(rounded, w1_ref[...].reshape(512, D))

    @pl.when(step == 2 * TP - 1)
    def _():
        center, spread = norm_stats(mid_ref[...])
        normed = center * spread
        upstream = total[...]
        dmid = grad[...] + norm_back(upstream, normed, spread, gain_ref[...])
        dmid_ref[...] = dmid
        dattn = dmid.astype(BF)
        dattn_ref[...] = dattn
        rows_ref[0:1] = col_sum(upstream * normed)
        rows_ref[1:2] = col_sum(upstream)
        rows_ref[2:3] = col_sum(dmlp_ref[...].astype(F32))
        rows_ref[3:4] = col_sum(dattn.astype(F32))


def select_rows_t(matrix, value):
    high = value.astype(BF)
    rest = value - high.astype(F32)
    mid = rest.astype(BF)
    low = (rest - mid.astype(F32)).astype(BF)
    return dot_tn(matrix, high) + dot_tn(matrix, mid) + dot_tn(matrix, low)


def mlp_backward(core, level, grad, halo, keep, mid, gain, weights, slope):
    quad = lambda unit: pl.BlockSpec((8, 4, 16, D), lambda step, core: (step, unit, 0, 0))
    half = pl.BlockSpec((T, 512), lambda step, core: (0, step // 2))
    if level:
        args, specs = [grad, keep], [whole((T, D)), whole((T, 1))]
    else:
        args = [grad, halo, const(OWN), const(SENT)]
        specs = [whole((T, D)), whole((SEND, D)), whole((T, T)), whole((SEND, T))]
    args += [mid, gain, weights, weights, slope]
    specs += [
        whole((T, D)),
        whole((1, D)),
        quad(2 * level),
        quad(2 * level + 1),
        pl.BlockSpec((T, 512), lambda step, core: (0, step)),
    ]
    return run(
        partial(mlp_back_kernel, level),
        2 * TP,
        core,
        args,
        specs,
        [
            shape_of((T, D), F32),
            shape_of((T, D), BF),
            shape_of((T, D), BF),
            shape_of((T, FF // 2), BF),
            shape_of((T, FF // 2), BF),
            shape_of((1, FF), F32),
            shape_of((4, D), F32),
        ],
        [
            whole((T, D)),
            whole((T, D)),
            whole((T, D)),
            half,
            half,
            pl.BlockSpec((1, 512), lambda step, core: (0, step)),
            whole((4, D)),
        ],
        [pltpu.VMEM((T, D), F32), pltpu.VMEM((T, D), F32)],
        4 * T * D * FF,
        24 << 20,
    )


def attn_back_kernel(level, *refs):
    (
        core_ref, dmid_ref, dattn_ref, x_ref, gain_ref, wq_ref, wk_ref, wv_ref, wp_ref,
        q_ref, k_ref, v_ref, probs_ref,
    ), refs = refs[:13], refs[13:]
    if level:
        (place_ref,), refs = refs[:1], refs[1:]
    (dx_ref, mine_ref, other_ref, pair_ref, sums_ref, rows_ref), refs = refs[:6], refs[6:]
    if level:
        (sent_ref,), refs = refs[:1], refs[1:]
    (total,) = refs
    step = pl.program_id(0)

    @pl.when(step == 0)
    def _():
        total[...] = jnp.zeros((T, D), F32)

    dheads = dot_nt(dattn_ref[...], wp_ref[...].reshape(256, D)).astype(BF)
    masks = head_masks(ROWS)
    dqs, dks, dvs = [], [], []
    for half in range(2):
        lanes = slice(half * 128, half * 128 + 128)
        dq_parts, dk_parts, dv_parts = [], [], []
        pairs = None
        for w in range(2):
            rows = slice(w * ROWS, (w + 1) * ROWS)
            probs = probs_ref[0, w, 4 * half : 4 * half + 4].reshape(4 * ROWS, ROWS)
            spread_out = spread_heads(dheads[rows, lanes], masks)
            dprobs = dot_nt(spread_out, v_ref[rows, lanes])
            dv_parts.append(dot_tn(probs.astype(BF), spread_out))
            inner = jnp.sum(probs * dprobs, axis=-1, keepdims=True)
            dscores = (probs * (dprobs - inner)).astype(BF)
            wide = dscores.astype(F32)
            pairs = wide if pairs is None else pairs + wide
            dq_parts.append(fold_heads(dot(dscores, k_ref[rows, lanes]), masks))
            dk_parts.append(dot_tn(dscores, spread_heads(q_ref[rows, lanes], masks)))
        pair_ref[4 * half : 4 * half + 4] = pairs.reshape(4, ROWS, ROWS)
        dqs.append((jnp.concatenate(dq_parts, axis=0) * SCALE).astype(BF))
        dks.append((jnp.concatenate(dk_parts, axis=0) * SCALE).astype(BF))
        dvs.append(jnp.concatenate(dv_parts, axis=0).astype(BF))

    def set_mine(part):
        mine_ref[...] = part

    def set_other(part):
        other_ref[...] = part

    put_halves(
        core_ref,
        set_mine,
        set_other,
        jnp.concatenate([dqs[0], dks[0], dvs[0]], axis=1),
        jnp.concatenate([dqs[1], dks[1], dvs[1]], axis=1),
    )
    dq = jnp.concatenate(dqs, axis=1)
    dk = jnp.concatenate(dks, axis=1)
    dv = jnp.concatenate(dvs, axis=1)
    sums_ref[0:1] = col_sum(dq.astype(F32))
    sums_ref[1:2] = col_sum(dv.astype(F32))
    total[...] += (
        dot(dq, wq_ref[...].reshape(256, D))
        + dot(dk, wk_ref[...].reshape(256, D))
        + dot(dv, wv_ref[...].reshape(256, D))
    )

    @pl.when(step == TP - 1)
    def _():
        center, spread = norm_stats(x_ref[...])
        normed = center * spread
        upstream = total[...]
        value = dmid_ref[...] + norm_back(upstream, normed, spread, gain_ref[...])
        dx_ref[...] = value
        rows_ref[0:1] = col_sum(upstream * normed)
        rows_ref[1:2] = col_sum(upstream)
        if level:
            sent_ref[...] = dot_tn(place_ref[...], value.astype(BF)).astype(BF)


def attn_backward(core, level, dmid, dattn, state, gain, weights, q, k, v, probs):
    unit = 16 + 4 * level
    block = pl.BlockSpec((T, 256), lambda step, core: (0, step))
    part = pl.BlockSpec((T, 384), lambda step, core: (0, step))
    args = [dmid, dattn, state, gain, weights, weights, weights, weights, q, k, v, probs]
    specs = [whole((T, D)), whole((T, D)), whole((T, D)), whole((1, D))]
    specs += [unit_spec(unit + place) for place in range(4)]
    specs += [
        block,
        block,
        block,
        pl.BlockSpec((1, 2, 8, ROWS, ROWS), lambda step, core: (step, 0, 0, 0, 0)),
    ]
    outs = [
        shape_of((T, D), F32),
        shape_of((T, 1536), BF),
        shape_of((T, 1536), BF),
        shape_of((32, ROWS, ROWS), F32),
        shape_of((2, D), F32),
        shape_of((2, D), F32),
    ]
    out_specs = [
        whole((T, D)),
        part,
        part,
        pl.BlockSpec((8, ROWS, ROWS), lambda step, core: (step, 0, 0)),
        pl.BlockSpec((2, 256), lambda step, core: (0, step)),
        whole((2, D)),
    ]
    if level:
        args.append(const(RECV))
        specs.append(whole((T, SEND)))
        outs.append(shape_of((SEND, D), BF))
        out_specs.append(whole((SEND, D)))
    return run(
        partial(attn_back_kernel, level),
        TP,
        core,
        args,
        specs,
        outs,
        out_specs,
        [pltpu.VMEM((T, D), F32)],
        8 * T * D * D,
        24 << 20,
    )


def weight_kernel(plan, width, *refs):
    core_ref, refs = refs[0], refs[1:]
    out_ref = refs[-1]
    place = 0
    column = 0
    for lefts, size in plan:
        left = jnp.concatenate([refs[place][...], refs[place + 1][...]], axis=0)
        right = jnp.concatenate([refs[place + 2][...], refs[place + 3][...]], axis=0)
        value = dot_tn(left, right).astype(BF)
        out_ref[:, 0, :, column : column + size] = value.reshape(YX, 64, size)
        column += size
        place += 4


def weight_grads(core, items):
    plan = [(None, right[0].shape[1] // TP) for left, right in items]
    width = sum(size for unused, size in plan)
    args, specs = [], []
    for (left, right), (unused, size) in zip(items, plan):
        args += [left[0], left[1], right[0], right[1]]
        block = pl.BlockSpec((T, size), lambda step, core: (0, step))
        specs += [whole((T, D)), whole((T, D)), block, block]
    return run(
        partial(weight_kernel, plan, width),
        TP,
        core,
        args,
        specs,
        shape_of((YX, TP, 64, width), BF),
        pl.BlockSpec((YX, 1, 64, width), lambda step, core: (0, step, 0, 0)),
        [],
        4 * T * D * width * TP,
        (2 * D * width * TP) + (8 << 20),
    )


def table_index():
    place = np.zeros((RELS, WIN * 190), np.float32)
    for row in range(WIN):
        for step in range(19):
            for col in range(WIN):
                place[(18 - step) * 19 + row - col + 9, row * 190 + step * WIN + col] = 1
    return place


PAIRS = table_index()


def spread_tables(tables):
    compact = jnp.dot(tables.reshape(64, RELS), jnp.asarray(PAIRS), precision=HIGH)
    compact = compact.reshape(2, 32, WIN, 190)
    rows = [compact[..., (9 - row) * WIN : (9 - row) * WIN + TOK] for row in range(WIN)]
    full = jnp.stack(rows, axis=2).reshape(2, 32, TOK, TOK)
    return jnp.pad(full, ((0, 0), (0, 0), (0, ROWS - TOK), (0, ROWS - TOK)))


def fold_tables(pairs):
    total = jnp.zeros((32, WIN, 190), F32)
    for row in range(WIN):
        low = (9 - row) * WIN
        total = total + jnp.pad(
            pairs[:, row * WIN : (row + 1) * WIN, :TOK], ((0, 0), (0, 0), (low, 90 - low))
        )
    return jnp.dot(total.reshape(32, -1), jnp.asarray(PAIRS.T), precision=HIGH)


def window_masks(level, valid, column):
    place = np.arange(ROWS)
    row = np.minimum(place // WIN, WIN - 1)
    col = jnp.asarray(place % WIN, jnp.int32)
    real = jnp.asarray(place < TOK)
    offset = SHIFT if level else 0
    rolled = column * WIN + col
    usable = (rolled + offset) % GW < valid
    masks = []
    for w in range(2):
        rolled_row = w * WIN + row
        row_region = (rolled_row >= GH - WIN).astype(np.int32) + (rolled_row >= GH - SHIFT)
        col_region = (rolled >= GW - WIN).astype(jnp.int32) + (rolled >= GW - SHIFT)
        region = jnp.asarray(row_region * 3, jnp.int32) + col_region
        allowed = usable[None, :]
        if level:
            allowed = allowed & (region[:, None] == region[None, :])
        mask = jnp.where(allowed, F32(0.0), F32(-100.0))
        mask = jnp.where(real[None, :], mask, F32(-1e30))
        masks.append(jnp.broadcast_to(mask, (ROWS, ROWS)))
    return jnp.stack(masks)


def gather_tp(value, place):
    parts = [value]
    for step in range(1, TP):
        parts.append(lax.ppermute(value, "tp", [(i, (i + step) % TP) for i in range(TP)]))
    stacked = jnp.stack(parts)
    order = (place - jnp.arange(TP)) % TP
    return [lax.dynamic_index_in_dim(stacked, order[i], 0, keepdims=False) for i in range(TP)]


def swap_core(value):
    return lax.ppermute(value, "core", [(0, 1), (1, 0)])


def sum_all(value):
    for axis, gap in (("core", 1), ("x", 1), ("x", 2), ("y", 1), ("y", 2), ("tp", 1), ("tp", 2)):
        size = 2 if axis == "core" else 4
        sent = value.astype(BF)
        got = lax.ppermute(sent, axis, [(i, i ^ gap) for i in range(size)])
        value = sent.astype(F32) + got.astype(F32)
    return value


def body(
    x3,
    res_group,
    merge_gain,
    merge_bias,
    merge_w,
    ln1_gain,
    ln1_bias,
    qkv_w,
    qv_bias,
    rel_table,
    proj_w,
    proj_bias,
    ln2_gain,
    ln2_bias,
    fc1_w,
    fc1_bias,
    fc2_w,
    fc2_bias,
    out_grad,
):
    core_at = lax.axis_index("core")
    chip_at = lax.axis_index("y") * 4 + lax.axis_index("x")
    column = lax.axis_index("tp")
    core = core_at.astype(jnp.int32).reshape(1)

    def cut(value, axis, size):
        return lax.dynamic_slice_in_dim(value, chip_at * size, size, axis)

    up = jnp.swapaxes(cut(fc1_w, 2, 64), 1, 2)
    down = cut(fc2_w, 1, 64)
    mix = cut(qkv_w, 3, 16).transpose(0, 2, 3, 1).reshape(2, 48, D)
    proj = cut(proj_w, 1, 16)
    piece = jnp.concatenate(
        [
            up[0], down[0], up[1], down[1], mix[0], proj[0], mix[1], proj[1],
            cut(merge_w.reshape(512, D), 0, 32),
        ]
    )
    piece = lax.dynamic_slice_in_dim(piece, core_at * 208, 208, 0)
    weights = lax.all_gather(piece, GATHER_AXES, axis=0, tiled=True).reshape(64, UNITS, 16, D)

    pages = lax.all_to_all(x3, PAGE_AXES, split_axis=1, concat_axis=0, tiled=True)
    tiles = pages.reshape(GH, TP, WIN, 512).transpose(1, 0, 2, 3).reshape(TP * 2 * TOK, 512)
    parts = lax.all_to_all(tiles, "tp", split_axis=0, concat_axis=0, tiled=True)
    parts = parts.reshape(TP, 2 * TOK, 512)

    packed = jnp.concatenate(
        [
            merge_gain.reshape(-1),
            merge_bias.reshape(-1),
            qv_bias.reshape(-1),
            fc1_bias.reshape(-1),
            rel_table.reshape(-1),
            jnp.zeros((10240 - 9872,), F32),
        ]
    ).reshape(80, 128)
    quarters = [part.reshape(-1) for part in gather_tp(packed, column)]

    def joined(low, shape, axis):
        size = int(np.prod(shape))
        return jnp.concatenate([part[low : low + size].reshape(shape) for part in quarters], axis)

    merge_gain_all = joined(0, (1, 512), 0)
    merge_bias_all = joined(512, (1, 512), 0)
    qv_bias_all = joined(1024, (2, 2, 256), 2)
    fc1_bias_all = joined(2048, (2, 1024), 1)
    tables = spread_tables(joined(4096, (2, 8, RELS), 1))

    valid = (res_group[0] + 1) * WIN
    masks = [window_masks(level, valid, column) for level in range(2)]
    spot = np.arange(T) % ROWS
    keep = ((column * WIN + SHIFT + jnp.asarray(spot % WIN, jnp.int32)) % GW < valid) & jnp.asarray(
        spot < TOK
    )
    keep = keep.astype(F32)[:, None]
    cotangent = jnp.roll(out_grad[0], (-SHIFT, -SHIFT), (0, 1))
    cotangent = lax.dynamic_slice_in_dim(cotangent, column * WIN, WIN, 1).reshape(2, TOK, D)
    cotangent = jnp.pad(cotangent, ((0, 0), (0, ROWS - TOK), (0, 0))).reshape(T, D)

    state, merged_mine, merged_other = merge_forward(
        core, parts, merge_gain_all, merge_bias_all, weights
    )
    kept = []
    halo = None
    for level in range(2):
        small = (
            ln1_gain[level : level + 1],
            ln1_bias[level : level + 1],
            qv_bias_all[level, 0:1],
            qv_bias_all[level, 1:2],
            proj_bias[level : level + 1],
        )
        got = attn_forward(
            core, level, state, halo, weights, small, tables[level], masks[level]
        )
        mid, a, q, k, v, probs, heads_mine, heads_other = got[:8]
        start = got[8] if level else state
        small = (
            ln2_gain[level : level + 1],
            ln2_bias[level : level + 1],
            fc1_bias_all[level : level + 1],
            fc2_bias[level : level + 1],
        )
        more = mlp_forward(core, level, mid, weights, small, keep)
        c2, slope, act_mine, act_other, extra = more[:5]
        kept.append((start, mid, a, q, k, v, probs, slope, c2))
        kept[-1] += ((heads_mine, swap_core(heads_other)), (act_mine, swap_core(act_other)))
        if not level:
            state = more[5]
            halo = lax.ppermute(extra, "tp", [((i + 1) % TP, i) for i in range(TP)])
    tiles_out = lax.all_gather(extra, "tp", axis=0, tiled=False).reshape(TP, GH, WIN, D)
    output = jnp.roll(tiles_out.transpose(1, 0, 2, 3).reshape(GH, GW, D), SHIFT, 1)
    output = output.astype(F32)[None]

    grads = [None, None]
    sums = [None, None]
    grad, halo = cotangent, None
    for level in (1, 0):
        start, mid, a, q, k, v, probs, slope, c2, heads, act = kept[level]
        dmid, dmlp, dattn, dpre_mine, dpre_other, db1, rows_two = mlp_backward(
            core, level, grad, halo, keep, mid, ln2_gain[level : level + 1], weights, slope
        )
        got = attn_backward(
            core, level, dmid, dattn, start, ln1_gain[level : level + 1], weights, q, k, v, probs
        )
        grad, mixed_mine, mixed_other, pairs, dqv, rows_one = got[:6]
        if level:
            halo = lax.ppermute(got[6], "tp", [(i, (i + 1) % TP) for i in range(TP)])
        sums[level] = (db1, rows_two, dqv, rows_one, fold_tables(pairs))
        items = [
            ((c2, swap_core(c2)), (dpre_mine, swap_core(dpre_other))),
            ((dmlp, swap_core(dmlp)), act),
            ((a, swap_core(a)), (mixed_mine, swap_core(mixed_other))),
            ((dattn, swap_core(dattn)), heads),
        ]
        if level:
            grads[level] = weight_grads(core, items)
    first, dm, dgain, dbias = merge_backward(core, parts, merge_gain_all, weights, grad)
    items.append(((first, swap_core(first)), (merged_mine, swap_core(merged_other))))
    grads[0] = weight_grads(core, items)

    back = lax.all_to_all(
        dm.reshape(TP * 2 * TOK, 512), "tp", split_axis=0, concat_axis=0, tiled=True
    )
    back = back.reshape(TP, GH, WIN, 512).transpose(1, 0, 2, 3).reshape(800, 1, 4, 128)
    grad_x3 = lax.all_to_all(back, PAGE_AXES, split_axis=0, concat_axis=1, tiled=True).astype(F32)

    scattered = [
        lax.psum_scatter(grads[level], CHIP_AXES, scatter_dimension=0, tiled=True)[0]
        for level in (1, 0)
    ]
    shares = lax.psum_scatter(
        jnp.concatenate(scattered, axis=-1), "tp", scatter_dimension=0, tiled=True
    )[0]
    shares = shares.reshape(2, 32, -1)
    kept_share = lax.dynamic_index_in_dim(shares, core_at, 0, keepdims=False)
    got_share = swap_core(lax.dynamic_index_in_dim(shares, 1 - core_at, 0, keepdims=False))
    first_half = jnp.where(core_at == 0, kept_share, got_share).astype(F32)
    second_half = jnp.where(core_at == 0, got_share, kept_share).astype(F32)

    def wide(low, size):
        return jnp.concatenate(
            [first_half[:, low : low + size], second_half[:, low : low + size]], axis=1
        )

    base = (1536, 0)
    g_fc1 = jnp.stack([wide(low, 512) for low in base])
    g_fc2 = jnp.stack([wide(low + 512, 512).T for low in base])
    g_qkv = jnp.stack(
        [jnp.stack([wide(low + 1024 + 128 * s, 128) for s in range(3)], axis=1) for low in base]
    )
    g_proj = jnp.stack([wide(low + 1408, 128).T for low in base])
    g_merge_w = wide(3072, 256).T.reshape(4, 128, 32)

    flat = []
    for level in range(2):
        db1, rows_two, dqv, rows_one, table = sums[level]
        flat += [rows_one, rows_two, dqv, db1, table]
    flat += [dgain, dbias]
    flat = jnp.concatenate([item.reshape(-1) for item in flat])
    count = flat.shape[0]
    flat = jnp.pad(flat, (0, -count % 16384)).reshape(-1, 1024)
    flat = sum_all(flat).reshape(-1)
    page_at = chip_at * 2 + core_at

    def take(low, shape):
        return flat[low : low + int(np.prod(shape))].reshape(shape)

    def page_part(value):
        return lax.dynamic_slice_in_dim(value, page_at * 32, 32, value.ndim - 1)

    def tp_part(value, axis):
        size = value.shape[axis] // TP
        return lax.dynamic_slice_in_dim(value, column * size, size, axis)

    span = 2 * D + 4 * D + 2 * D + FF + 32 * RELS
    rows = [take(level * span, (6, D)) for level in range(2)]
    rows = page_part(jnp.stack(rows))
    dqv = tp_part(jnp.stack([take(level * span + 6 * D, (2, D)) for level in range(2)]), 2)
    db1 = tp_part(jnp.stack([take(level * span + 8 * D, (FF,)) for level in range(2)]), 1)
    table = tp_part(
        jnp.stack([take(level * span + 8 * D + FF, (32, RELS)) for level in range(2)]), 1
    )
    dgain = tp_part(take(2 * span, (TP, 512)), 0).reshape(4, 128)
    dbias = tp_part(take(2 * span + MERGED, (TP, 512)), 0).reshape(4, 128)
    return (
        output,
        grad_x3,
        dgain,
        dbias,
        g_merge_w,
        rows[:, 0],
        rows[:, 1],
        g_qkv,
        dqv,
        table,
        g_proj,
        rows[:, 5],
        rows[:, 2],
        rows[:, 3],
        g_fc1,
        db1,
        g_fc2,
        rows[:, 4],
    )


def solution(mesh):
    grid = Mesh(mesh.devices.reshape(4, 4, 2, TP), ("y", "x", "core", "tp"))
    page = PAGE_AXES
    return jax.shard_map(
        body,
        mesh=grid,
        in_specs=(
            P(page, None, None, "tp"),
            P(page),
            P(None, "tp"),
            P(None, "tp"),
            P(None, "tp", None),
            P(),
            P(),
            P(None, None, None, "tp"),
            P(None, None, "tp"),
            P(None, "tp", None),
            P(None, "tp", None),
            P(),
            P(),
            P(),
            P(None, None, "tp"),
            P(None, "tp"),
            P(None, "tp", None),
            P(),
            P(page, None, None, None),
        ),
        out_specs=(
            P(page, None, None, None),
            P(page, None, None, "tp"),
            P(None, "tp"),
            P(None, "tp"),
            P(None, "tp", page),
            P(None, page),
            P(None, page),
            P(None, page, None, "tp"),
            P(None, None, "tp"),
            P(None, "tp", None),
            P(None, "tp", page),
            P(None, page),
            P(None, page),
            P(None, page),
            P(None, page, "tp"),
            P(None, "tp"),
            P(None, "tp", page),
            P(None, page),
        ),
        check_vma=False,
    )
```

```python
from functools import partial

import jax
import jax.numpy as jnp
import numpy as np
from jax import lax
from jax.experimental import pallas as pl
from jax.experimental.pallas import tpu as pltpu
from jax.sharding import Mesh
from jax.sharding import PartitionSpec as P

D = 1024
FF = 4096
MERGED = 2048
WIN = 10
SHIFT = 5
GH = 20
GW = 40
RELS = 361
TOK = 100
ROWS = 112
T = 2 * ROWS
SEND = 112
EPS = 1e-05
SCALE = 32 ** (-0.5)
YX = 16
TP = 4
UNITS = 26
HIGH = lax.Precision.HIGHEST
BF = jnp.bfloat16
F32 = jnp.float32
PAGE_AXES = ("y", "x", "core")
CHIP_AXES = ("y", "x")
GATHER_AXES = ("tp", "y", "x", "core")
VMEM = 58 << 20


def row_at(row, col):
    return (row // WIN) * ROWS + (row % WIN) * WIN + col


def place_matrices():
    own = np.zeros((T, T), np.float32)
    recv = np.zeros((T, SEND), np.float32)
    send = np.zeros((SEND, T), np.float32)
    pack = np.zeros((2 * TOK, T), np.float32)
    out = np.zeros((2 * TOK, T), np.float32)
    for row in range(GH):
        for col in range(WIN):
            source = (row + SHIFT) % GH
            if col < SHIFT:
                own[row_at(row, col), row_at(source, col + SHIFT)] = 1
                send[row * SHIFT + col, row_at(row, col)] = 1
            else:
                recv[row_at(row, col), source * SHIFT + col - SHIFT] = 1
            pack[row * WIN + col, row_at(row, col)] = 1
            out[source * WIN + col, row_at(row, col)] = 1
    return own, recv, send, pack, out


OWN, RECV, SENT, PACK, OUT = place_matrices()


def const(matrix):
    return jnp.asarray(matrix, BF)


def dot(left, right):
    return lax.dot_general(left, right, (((1,), (0,)), ((), ())), preferred_element_type=F32)


def dot_nt(left, right):
    return lax.dot_general(left, right, (((1,), (1,)), ((), ())), preferred_element_type=F32)


def dot_tn(left, right):
    return lax.dot_general(left, right, (((0,), (0,)), ((), ())), preferred_element_type=F32)


def select_rows(matrix, value):
    high = value.astype(BF)
    rest = value - high.astype(F32)
    mid = rest.astype(BF)
    low = (rest - mid.astype(F32)).astype(BF)
    return dot(matrix, high) + dot(matrix, mid) + dot(matrix, low)


def norm_stats(value):
    mean = jnp.mean(value, axis=-1, keepdims=True)
    center = value - mean
    return center, lax.rsqrt(jnp.mean(center * center, axis=-1, keepdims=True) + EPS)


def norm_back(upstream, normed, spread, gain):
    scaled = upstream * gain
    inner = (
        scaled
        - jnp.mean(scaled, axis=-1, keepdims=True)
        - normed * jnp.mean(scaled * normed, axis=-1, keepdims=True)
    )
    return spread * inner


def col_sum(value):
    return jnp.sum(value, axis=0, keepdims=True)


def whole(shape):
    return pl.BlockSpec(shape, lambda step, core: (0,) * len(shape))


def shape_of(shape, dtype):
    return jax.ShapeDtypeStruct(shape, dtype)


def run(kernel, steps, core, args, in_specs, outs, out_specs, scratch, flops, moved):
    return pl.pallas_call(
        kernel,
        grid_spec=pltpu.PrefetchScalarGridSpec(
            num_scalar_prefetch=1,
            grid=(steps,),
            in_specs=in_specs,
            out_specs=out_specs,
            scratch_shapes=scratch,
        ),
        out_shape=outs,
        compiler_params=pltpu.CompilerParams(
            vmem_limit_bytes=VMEM, dimension_semantics=("arbitrary",)
        ),
        cost_estimate=pl.CostEstimate(flops=flops, bytes_accessed=moved, transcendentals=0),
    )(core, *args)


def put_halves(core_ref, mine, other, low, high):
    @pl.when(core_ref[0] == 0)
    def _():
        mine(low)
        other(high)

    @pl.when(core_ref[0] != 0)
    def _():
        mine(high)
        other(low)


def pack_kernel(place_ref, up_ref, down_ref, mix_ref, proj_ref, merge_ref, out_ref, all_ref):
    for level in range(2):
        all_ref[8 * level : 8 * level + 4] = up_ref[level].reshape(4, 16, D)
        all_ref[8 * level + 4 : 8 * level + 8] = down_ref[level].reshape(4, 16, D)
        for part in range(3):
            for group in range(4):
                all_ref[16 + 4 * level + part, :, 256 * group : 256 * group + 256] = mix_ref[
                    level, part, 16 * group : 16 * group + 16
                ]
        all_ref[19 + 4 * level] = proj_ref[level]
    all_ref[24:26] = merge_ref[...].reshape(2, 16, D)
    out_ref[...] = all_ref[pl.ds(place_ref[1] * 13, 13)]


def pack_weights(place, up, down, mix, proj, merge):
    piece = pl.pallas_call(
        pack_kernel,
        grid_spec=pltpu.PrefetchScalarGridSpec(
            num_scalar_prefetch=1,
            grid=(1,),
            in_specs=[
                pl.BlockSpec((2, 64, D), lambda step, place: (0, place[0], 0)),
                pl.BlockSpec((2, 64, D), lambda step, place: (0, place[0], 0)),
                pl.BlockSpec((2, 3, 64, 256), lambda step, place: (0, 0, place[0], 0)),
                pl.BlockSpec((2, 16, D), lambda step, place: (0, place[0], 0)),
                pl.BlockSpec((32, D), lambda step, place: (place[0], 0)),
            ],
            out_specs=whole((13, 16, D)),
            scratch_shapes=[pltpu.VMEM((UNITS, 16, D), BF)],
        ),
        out_shape=shape_of((13, 16, D), BF),
        compiler_params=pltpu.CompilerParams(vmem_limit_bytes=VMEM),
        cost_estimate=pl.CostEstimate(flops=0, bytes_accessed=1 << 20, transcendentals=0),
    )(place, up, down, mix, proj, merge)
    return piece.reshape(208, D)


def merge_stats(x_ref, pack_ref, full):
    total = jnp.zeros((T, 1), F32)
    for part in range(TP):
        rows = dot_tn(pack_ref[...], x_ref[part])
        full[part] = rows
        total = total + jnp.sum(rows, axis=-1, keepdims=True)
    mean = total / MERGED
    square = jnp.zeros((T, 1), F32)
    for part in range(TP):
        center = full[part] - mean
        square = square + jnp.sum(center * center, axis=-1, keepdims=True)
    return mean, lax.rsqrt(square / MERGED + EPS)


def merge_kernel(
    core_ref, x_ref, pack_ref, gain_ref, bias_ref, w_ref, out_ref, mine_ref, other_ref, full, stats
):
    step = pl.program_id(0)

    @pl.when(step == 0)
    def _():
        mean, spread = merge_stats(x_ref, pack_ref, full)
        stats[0] = mean
        stats[1] = spread

    normed = (full[step] - stats[0]) * stats[1]
    value = (normed * gain_ref[0] + bias_ref[0]).astype(BF)

    def set_mine(part):
        mine_ref[...] = part

    def set_other(part):
        other_ref[...] = part

    put_halves(core_ref, set_mine, set_other, value[:, :256], value[:, 256:])
    term = dot(value, w_ref[...].reshape(512, D))

    @pl.when(step == 0)
    def _():
        out_ref[...] = term

    @pl.when(step != 0)
    def _():
        out_ref[...] += term


def merge_forward(core, parts, gain, bias, weights):
    return run(
        merge_kernel,
        TP,
        core,
        (parts, const(PACK), gain.reshape(TP, 1, 512), bias.reshape(TP, 1, 512), weights),
        [
            whole((TP, 2 * TOK, 512)),
            whole((2 * TOK, T)),
            pl.BlockSpec((1, 1, 512), lambda step, core: (step, 0, 0)),
            pl.BlockSpec((1, 1, 512), lambda step, core: (step, 0, 0)),
            pl.BlockSpec((YX, 2, 16, D), lambda step, core: (step, 12, 0, 0)),
        ],
        [shape_of((T, D), F32), shape_of((T, D), BF), shape_of((T, D), BF)],
        [
            whole((T, D)),
            pl.BlockSpec((T, 256), lambda step, core: (0, step)),
            pl.BlockSpec((T, 256), lambda step, core: (0, step)),
        ],
        [pltpu.VMEM((TP, T, 512), F32), pltpu.VMEM((2, T, 1), F32)],
        2 * T * MERGED * D,
        8 << 20,
    )


def merge_back_kernel(
    core_ref, x_ref, pack_ref, gain_ref, w_ref, dx_ref,
    start_ref, dm_ref, gains_ref, biases_ref,
    full, stats, upstream,
):
    step = pl.program_id(0)

    @pl.when(step == 0)
    def _():
        mean, spread = merge_stats(x_ref, pack_ref, full)
        stats[0] = mean
        stats[1] = spread
        stats[2] = jnp.zeros((T, 1), F32)
        stats[3] = jnp.zeros((T, 1), F32)
        start_ref[...] = dx_ref[...].astype(BF)

    grad = dot_nt(start_ref[...], w_ref[...].reshape(512, D))
    normed = (full[step] - stats[0]) * stats[1]
    full[step] = normed
    gains_ref[0] = col_sum(grad * normed)
    biases_ref[0] = col_sum(grad)
    scaled = grad * gain_ref[0]
    upstream[step] = scaled
    stats[2] += jnp.sum(scaled, axis=-1, keepdims=True)
    stats[3] += jnp.sum(scaled * normed, axis=-1, keepdims=True)

    @pl.when(step == TP - 1)
    def _():
        for part in range(TP):
            value = stats[1] * (
                upstream[part] - stats[2] / MERGED - full[part] * (stats[3] / MERGED)
            )
            dm_ref[part] = dot(pack_ref[...], value.astype(BF)).astype(BF)


def merge_backward(core, parts, gain, weights, grad):
    return run(
        merge_back_kernel,
        TP,
        core,
        (parts, const(PACK), gain.reshape(TP, 1, 512), weights, grad),
        [
            whole((TP, 2 * TOK, 512)),
            whole((2 * TOK, T)),
            pl.BlockSpec((1, 1, 512), lambda step, core: (step, 0, 0)),
            pl.BlockSpec((YX, 2, 16, D), lambda step, core: (step, 12, 0, 0)),
            whole((T, D)),
        ],
        [
            shape_of((T, D), BF),
            shape_of((TP, 2 * TOK, 512), BF),
            shape_of((TP, 1, 512), F32),
            shape_of((TP, 1, 512), F32),
        ],
        [
            whole((T, D)),
            whole((TP, 2 * TOK, 512)),
            pl.BlockSpec((1, 1, 512), lambda step, core: (step, 0, 0)),
            pl.BlockSpec((1, 1, 512), lambda step, core: (step, 0, 0)),
        ],
        [pltpu.VMEM((TP, T, 512), F32), pltpu.VMEM((4, T, 1), F32), pltpu.VMEM((TP, T, 512), F32)],
        2 * T * MERGED * D,
        8 << 20,
    )


def head_masks(rows):
    lane = lax.broadcasted_iota(jnp.int32, (rows, 128), 1)
    return [(lane >= 32 * place) & (lane < 32 * place + 32) for place in range(4)]


def spread_heads(value, masks):
    zero = jnp.zeros_like(value)
    return jnp.concatenate([jnp.where(mask, value, zero) for mask in masks], axis=0)


def fold_heads(value, masks):
    total = jnp.zeros((ROWS, 128), F32)
    for place, mask in enumerate(masks):
        total = jnp.where(mask, value[place * ROWS : (place + 1) * ROWS], total)
    return total


def unfold(ref):
    value = ref[...].reshape(YX, 16, D)
    parts = [value[:, :, 256 * group : 256 * group + 256] for group in range(4)]
    return jnp.stack(parts, axis=1).reshape(D, 256)


def attn_kernel(level, *refs):
    (core_ref, x_ref), refs = refs[:2], refs[2:]
    if level:
        (halo_ref, own_ref, recv_ref), refs = refs[:3], refs[3:]
    (
        gain_ref, bias_ref, wq_ref, wk_ref, wv_ref, wp_ref, qb_ref, vb_ref, table_ref, mask_ref,
        shift_ref,
    ), refs = refs[:11], refs[11:]
    (
        mid_ref, a_ref, q_ref, k_ref, v_ref, probs_ref, mine_ref, other_ref,
    ), refs = refs[:8], refs[8:]
    step = pl.program_id(0)

    @pl.when(step == 0)
    def _():
        value = x_ref[...]
        if level:
            value = select_rows(own_ref[...], value) + dot(recv_ref[...], halo_ref[...])
            refs[0][...] = value
        center, spread = norm_stats(value)
        a_ref[...] = (center * spread * gain_ref[...] + bias_ref[...]).astype(BF)
        mid_ref[...] = value + shift_ref[...]

    a = a_ref[...]
    q = (dot(a, unfold(wq_ref)) + qb_ref[...]).astype(BF)
    k = dot(a, unfold(wk_ref)).astype(BF)
    v = (dot(a, unfold(wv_ref)) + vb_ref[...]).astype(BF)
    q_ref[...] = q
    k_ref[...] = k
    v_ref[...] = v
    masks = head_masks(ROWS)
    halves = []
    for half in range(2):
        lanes = slice(half * 128, half * 128 + 128)
        table = table_ref[4 * half : 4 * half + 4]
        parts = []
        for w in range(2):
            rows = slice(w * ROWS, (w + 1) * ROWS)
            raw = dot_nt(spread_heads(q[rows, lanes], masks), k[rows, lanes]) * SCALE
            scores = raw.reshape(4, ROWS, ROWS) + table + mask_ref[w][None]
            top = jnp.max(scores, axis=-1, keepdims=True)
            terms = jnp.exp(scores - top)
            probs = terms / jnp.sum(terms, axis=-1, keepdims=True)
            probs_ref[0, w, 4 * half : 4 * half + 4] = probs
            mixed = dot(probs.astype(BF).reshape(4 * ROWS, ROWS), v[rows, lanes])
            parts.append(fold_heads(mixed, masks))
        halves.append(jnp.concatenate(parts, axis=0).astype(BF))

    def set_mine(part):
        mine_ref[...] = part

    def set_other(part):
        other_ref[...] = part

    put_halves(core_ref, set_mine, set_other, *halves)
    heads = jnp.concatenate(halves, axis=1)
    mid_ref[...] += dot(heads, wp_ref[...].reshape(256, D))


def unit_spec(unit):
    return pl.BlockSpec((YX, 1, 16, D), lambda step, core: (step, unit, 0, 0))


def attn_forward(core, level, state, halo, weights, small, table, mask):
    gain, bias, qbias, vbias, shift = small
    unit = 16 + 4 * level
    args = [state]
    specs = [whole((T, D))]
    if level:
        args += [halo, const(OWN), const(RECV)]
        specs += [whole((SEND, D)), whole((T, T)), whole((T, SEND))]
    args += [gain, bias, weights, weights, weights, weights, qbias, vbias, table, mask, shift]
    cols = pl.BlockSpec((1, 256), lambda step, core: (0, step))
    specs += [whole((1, D)), whole((1, D))] + [unit_spec(unit + place) for place in range(4)]
    specs += [
        cols,
        cols,
        pl.BlockSpec((8, ROWS, ROWS), lambda step, core: (step, 0, 0)),
        whole((2, ROWS, ROWS)),
        whole((1, D)),
    ]
    block = pl.BlockSpec((T, 256), lambda step, core: (0, step))
    half = pl.BlockSpec((T, 128), lambda step, core: (0, step))
    outs = [
        shape_of((T, D), F32),
        shape_of((T, D), BF),
        shape_of((T, D), BF),
        shape_of((T, D), BF),
        shape_of((T, D), BF),
        shape_of((TP, 2, 8, ROWS, ROWS), F32),
        shape_of((T, D // 2), BF),
        shape_of((T, D // 2), BF),
    ]
    out_specs = [
        whole((T, D)),
        whole((T, D)),
        block,
        block,
        block,
        pl.BlockSpec((1, 2, 8, ROWS, ROWS), lambda step, core: (step, 0, 0, 0, 0)),
        half,
        half,
    ]
    if level:
        outs.append(shape_of((T, D), F32))
        out_specs.append(whole((T, D)))
    return run(
        partial(attn_kernel, level), TP, core, args, specs, outs, out_specs, [], 8 * T * D * D, 24 << 20
    )


def quad_spec(unit):
    return pl.BlockSpec((YX, 4, 16, D), lambda step, core: (step, unit, 0, 0))


def mlp_kernel(level, *refs):
    (
        core_ref, mid_ref, gain_ref, bias_ref, w1_ref, w2_ref, b1_ref, b2_ref, place_ref, keep_ref,
        c2_ref, slope_ref, mine_ref, other_ref, extra_ref,
    ), refs = refs[:15], refs[15:]
    total = refs[0]
    step = pl.program_id(0)

    @pl.when(step == 0)
    def _():
        value = mid_ref[...]
        center, spread = norm_stats(value)
        c2_ref[...] = (center * spread * gain_ref[...] + bias_ref[...]).astype(BF)
        total[...] = value + b2_ref[...]

    pre = dot(c2_ref[...], w1_ref[...].reshape(D, D)) + b1_ref[...]
    phi = 0.5 + 0.5 * lax.erf(pre * (0.5**0.5))
    act = (pre * phi).astype(BF)
    slope_ref[...] = (phi + pre * ((2.0 * np.pi) ** -0.5 * jnp.exp(-0.5 * pre * pre))).astype(BF)

    def set_mine(part):
        mine_ref[...] = part

    def set_other(part):
        other_ref[...] = part

    put_halves(core_ref, set_mine, set_other, act[:, :512], act[:, 512:])
    total[...] += dot(act, w2_ref[...].reshape(D, D))

    @pl.when(step == TP - 1)
    def _():
        value = total[...]
        if level:
            extra_ref[...] = dot(place_ref[...], (value * keep_ref[...]).astype(BF)).astype(BF)
        else:
            extra_ref[...] = dot(place_ref[...], value.astype(BF)).astype(BF)
            refs[1][...] = value


def mlp_forward(core, level, mid, weights, small, keep):
    gain, bias, b1, b2 = small
    place = const(OUT if level else SENT)
    half = pl.BlockSpec((T, 512), lambda step, core: (0, step))
    outs = [
        shape_of((T, D), BF),
        shape_of((T, FF), BF),
        shape_of((T, FF // 2), BF),
        shape_of((T, FF // 2), BF),
        shape_of((place.shape[0], D), BF),
    ]
    out_specs = [
        whole((T, D)),
        pl.BlockSpec((T, D), lambda step, core: (0, step)),
        half,
        half,
        whole((place.shape[0], D)),
    ]
    scratch = [pltpu.VMEM((T, D), F32)]
    if not level:
        outs.append(shape_of((T, D), F32))
        out_specs.append(whole((T, D)))

    def kernel(*refs):
        refs = list(refs)
        total = refs.pop()
        mlp_kernel(level, *refs[:15], total, *refs[15:])

    return run(
        kernel,
        TP,
        core,
        (mid, gain, bias, weights, weights, b1, b2, place, keep),
        [
            whole((T, D)),
            whole((1, D)),
            whole((1, D)),
            quad_spec(2 * level),
            quad_spec(2 * level + 1),
            pl.BlockSpec((1, D), lambda step, core: (0, step)),
            whole((1, D)),
            whole(place.shape),
            whole((T, 1)),
        ],
        outs,
        out_specs,
        scratch,
        4 * T * D * FF,
        24 << 20,
    )


def mlp_back_kernel(level, *refs):
    (core_ref, dx_ref), refs = refs[:2], refs[2:]
    if level:
        (keep_ref,), refs = refs[:1], refs[1:]
    else:
        (halo_ref, own_ref, sent_ref), refs = refs[:3], refs[3:]
    (mid_ref, gain_ref, w1_ref, w2_ref, slope_ref), refs = refs[:5], refs[5:]
    (
        dmid_ref, dmlp_ref, dattn_ref, mine_ref, other_ref, db1_ref, rows_ref, total, grad,
    ) = refs
    step = pl.program_id(0)

    @pl.when(step == 0)
    def _():
        if level:
            value = dx_ref[...].astype(F32) * keep_ref[...]
        else:
            value = select_rows_t(own_ref[...], dx_ref[...]) + dot_tn(sent_ref[...], halo_ref[...])
        grad[...] = value
        dmlp_ref[...] = value.astype(BF)
        total[...] = jnp.zeros((T, D), F32)

    dact = dot_nt(dmlp_ref[...], w2_ref[...].reshape(D, D))
    rounded = (dact * slope_ref[...].astype(F32)).astype(BF)
    db1_ref[...] = col_sum(rounded.astype(F32))

    def set_mine(part):
        mine_ref[...] = part

    def set_other(part):
        other_ref[...] = part

    put_halves(core_ref, set_mine, set_other, rounded[:, :512], rounded[:, 512:])
    total[...] += dot_nt(rounded, w1_ref[...].reshape(D, D))

    @pl.when(step == TP - 1)
    def _():
        center, spread = norm_stats(mid_ref[...])
        normed = center * spread
        upstream = total[...]
        dmid = grad[...] + norm_back(upstream, normed, spread, gain_ref[...])
        dmid_ref[...] = dmid
        dattn = dmid.astype(BF)
        dattn_ref[...] = dattn
        rows_ref[0:1] = col_sum(upstream * normed)
        rows_ref[1:2] = col_sum(upstream)
        rows_ref[2:3] = col_sum(dmlp_ref[...].astype(F32))
        rows_ref[3:4] = col_sum(dattn.astype(F32))


def select_rows_t(matrix, value):
    high = value.astype(BF)
    rest = value - high.astype(F32)
    mid = rest.astype(BF)
    low = (rest - mid.astype(F32)).astype(BF)
    return dot_tn(matrix, high) + dot_tn(matrix, mid) + dot_tn(matrix, low)


def mlp_backward(core, level, grad, halo, keep, mid, gain, weights, slope):
    half = pl.BlockSpec((T, 512), lambda step, core: (0, step))
    if level:
        args, specs = [grad, keep], [whole((T, D)), whole((T, 1))]
    else:
        args = [grad, halo, const(OWN), const(SENT)]
        specs = [whole((T, D)), whole((SEND, D)), whole((T, T)), whole((SEND, T))]
    args += [mid, gain, weights, weights, slope]
    specs += [
        whole((T, D)),
        whole((1, D)),
        quad_spec(2 * level),
        quad_spec(2 * level + 1),
        pl.BlockSpec((T, D), lambda step, core: (0, step)),
    ]
    return run(
        partial(mlp_back_kernel, level),
        TP,
        core,
        args,
        specs,
        [
            shape_of((T, D), F32),
            shape_of((T, D), BF),
            shape_of((T, D), BF),
            shape_of((T, FF // 2), BF),
            shape_of((T, FF // 2), BF),
            shape_of((1, FF), F32),
            shape_of((4, D), F32),
        ],
        [
            whole((T, D)),
            whole((T, D)),
            whole((T, D)),
            half,
            half,
            pl.BlockSpec((1, D), lambda step, core: (0, step)),
            whole((4, D)),
        ],
        [pltpu.VMEM((T, D), F32), pltpu.VMEM((T, D), F32)],
        4 * T * D * FF,
        24 << 20,
    )


def attn_back_kernel(level, *refs):
    (
        core_ref, dmid_ref, dattn_ref, x_ref, gain_ref, wq_ref, wk_ref, wv_ref, wp_ref,
        q_ref, k_ref, v_ref, probs_ref,
    ), refs = refs[:13], refs[13:]
    if level:
        (place_ref,), refs = refs[:1], refs[1:]
    (dx_ref, mine_ref, other_ref, pair_ref, sums_ref, rows_ref), refs = refs[:6], refs[6:]
    if level:
        (sent_ref,), refs = refs[:1], refs[1:]
    (total,) = refs
    step = pl.program_id(0)

    @pl.when(step == 0)
    def _():
        total[...] = jnp.zeros((T, D), F32)

    dheads = dot_nt(dattn_ref[...], wp_ref[...].reshape(256, D)).astype(BF)
    masks = head_masks(ROWS)
    dqs, dks, dvs = [], [], []
    for half in range(2):
        lanes = slice(half * 128, half * 128 + 128)
        dq_parts, dk_parts, dv_parts = [], [], []
        pairs = None
        for w in range(2):
            rows = slice(w * ROWS, (w + 1) * ROWS)
            probs = probs_ref[0, w, 4 * half : 4 * half + 4].reshape(4 * ROWS, ROWS)
            spread_out = spread_heads(dheads[rows, lanes], masks)
            dprobs = dot_nt(spread_out, v_ref[rows, lanes])
            dv_parts.append(dot_tn(probs.astype(BF), spread_out))
            inner = jnp.sum(probs * dprobs, axis=-1, keepdims=True)
            dscores = (probs * (dprobs - inner)).astype(BF)
            wide = dscores.astype(F32)
            pairs = wide if pairs is None else pairs + wide
            dq_parts.append(fold_heads(dot(dscores, k_ref[rows, lanes]), masks))
            dk_parts.append(dot_tn(dscores, spread_heads(q_ref[rows, lanes], masks)))
        pair_ref[4 * half : 4 * half + 4] = pairs.reshape(4, ROWS, ROWS)
        dqs.append((jnp.concatenate(dq_parts, axis=0) * SCALE).astype(BF))
        dks.append((jnp.concatenate(dk_parts, axis=0) * SCALE).astype(BF))
        dvs.append(jnp.concatenate(dv_parts, axis=0).astype(BF))

    def set_mine(part):
        mine_ref[...] = part

    def set_other(part):
        other_ref[...] = part

    put_halves(
        core_ref,
        set_mine,
        set_other,
        jnp.concatenate([dqs[0], dks[0], dvs[0]], axis=1),
        jnp.concatenate([dqs[1], dks[1], dvs[1]], axis=1),
    )
    dq = jnp.concatenate(dqs, axis=1)
    dk = jnp.concatenate(dks, axis=1)
    dv = jnp.concatenate(dvs, axis=1)
    sums_ref[0:1] = col_sum(dq.astype(F32))
    sums_ref[1:2] = col_sum(dv.astype(F32))
    total[...] += (
        dot_nt(dq, unfold(wq_ref))
        + dot_nt(dk, unfold(wk_ref))
        + dot_nt(dv, unfold(wv_ref))
    )

    @pl.when(step == TP - 1)
    def _():
        center, spread = norm_stats(x_ref[...])
        normed = center * spread
        upstream = total[...]
        value = dmid_ref[...] + norm_back(upstream, normed, spread, gain_ref[...])
        dx_ref[...] = value
        rows_ref[0:1] = col_sum(upstream * normed)
        rows_ref[1:2] = col_sum(upstream)
        if level:
            sent_ref[...] = dot_tn(place_ref[...], value.astype(BF)).astype(BF)


def attn_backward(core, level, dmid, dattn, state, gain, weights, q, k, v, probs):
    unit = 16 + 4 * level
    block = pl.BlockSpec((T, 256), lambda step, core: (0, step))
    part = pl.BlockSpec((T, 384), lambda step, core: (0, step))
    args = [dmid, dattn, state, gain, weights, weights, weights, weights, q, k, v, probs]
    specs = [whole((T, D)), whole((T, D)), whole((T, D)), whole((1, D))]
    specs += [unit_spec(unit + place) for place in range(4)]
    specs += [
        block,
        block,
        block,
        pl.BlockSpec((1, 2, 8, ROWS, ROWS), lambda step, core: (step, 0, 0, 0, 0)),
    ]
    outs = [
        shape_of((T, D), F32),
        shape_of((T, 1536), BF),
        shape_of((T, 1536), BF),
        shape_of((32, ROWS, ROWS), F32),
        shape_of((2, D), F32),
        shape_of((2, D), F32),
    ]
    out_specs = [
        whole((T, D)),
        part,
        part,
        pl.BlockSpec((8, ROWS, ROWS), lambda step, core: (step, 0, 0)),
        pl.BlockSpec((2, 256), lambda step, core: (0, step)),
        whole((2, D)),
    ]
    if level:
        args.append(const(RECV))
        specs.append(whole((T, SEND)))
        outs.append(shape_of((SEND, D), BF))
        out_specs.append(whole((SEND, D)))
    return run(
        partial(attn_back_kernel, level),
        TP,
        core,
        args,
        specs,
        outs,
        out_specs,
        [pltpu.VMEM((T, D), F32)],
        8 * T * D * D,
        24 << 20,
    )


def weight_kernel(plan, *refs):
    refs, out_ref = refs[1:-1], refs[-1]
    place = 0
    column = 0
    for kind, size in plan:
        one, two, three, four = refs[place : place + 4]
        if kind == "matrix":
            left = jnp.concatenate([one[...], two[...]], axis=0)
            right = jnp.concatenate([three[...], four[...]], axis=0)
            value = dot_tn(left, right)
        else:
            value = (one[...].astype(F32) + two[...].astype(F32)) + (
                three[...].astype(F32) + four[...].astype(F32)
            )
        out_ref[:, 0, :, column : column + size] = value.astype(BF).reshape(YX, 64, size)
        column += size
        place += 4


def weight_grads(core, items, sums):
    plan, args, specs = [], [], []
    for left, right in items:
        size = right[0].shape[1] // TP
        plan.append(("matrix", size))
        args += [left[0], left[1], right[0], right[1]]
        block = pl.BlockSpec((T, size), lambda step, core: (0, step))
        specs += [whole((T, D)), whole((T, D)), block, block]
    for pieces in sums:
        plan.append(("sum", 128))
        args += pieces
        specs += [pl.BlockSpec((D, 128), lambda step, core: (0, step))] * 4
    width = sum(size for unused, size in plan)
    return run(
        partial(weight_kernel, plan),
        TP,
        core,
        args,
        specs,
        shape_of((YX, TP, 64, width), BF),
        pl.BlockSpec((YX, 1, 64, width), lambda step, core: (0, step, 0, 0)),
        [],
        4 * T * D * width * TP,
        (2 * D * width * TP) + (8 << 20),
    )


def quarter_kernel(core_ref, one, two, three, four, *outs):
    left = jnp.concatenate([one[...], two[...]], axis=0)
    right = jnp.concatenate([three[...], four[...]], axis=0)
    value = dot_tn(left, right).astype(BF)
    for ahead, out in enumerate(outs):

        @pl.when(pl.program_id(0) == ahead)
        def _(out=out):
            out[...] = value


def quarter_grads(core, left, right):
    block = pl.BlockSpec((T, 512), lambda step, core: (0, lax.rem(core[1] + step, TP)))
    return run(
        quarter_kernel,
        TP,
        core,
        (left[0], left[1], right[0], right[1]),
        [whole((T, D)), whole((T, D)), block, block],
        [shape_of((D, 512), BF)] * TP,
        [whole((D, 512))] * TP,
        [],
        4 * T * D * 2048,
        8 << 20,
    )


def send_ahead(pieces):
    return [pieces[0]] + [
        lax.ppermute(pieces[step], "tp", [(i, (i + step) % TP) for i in range(TP)])
        for step in range(1, TP)
    ]


def sum_quarters(value, column):
    pieces = [
        lax.dynamic_index_in_dim(value, (column + step) % TP, 0, keepdims=False)
        for step in range(TP)
    ]
    got = [piece.astype(F32) for piece in send_ahead(pieces)]
    return (got[0] + got[1]) + (got[2] + got[3])


def table_index():
    place = np.zeros((RELS, WIN * 190), np.float32)
    for row in range(WIN):
        for step in range(19):
            for col in range(WIN):
                place[(18 - step) * 19 + row - col + 9, row * 190 + step * WIN + col] = 1
    return place


PAIRS = table_index()


def spread_tables(tables):
    compact = jnp.dot(tables.reshape(64, RELS), jnp.asarray(PAIRS), precision=HIGH)
    compact = compact.reshape(2, 32, WIN, 190)
    rows = [compact[..., (9 - row) * WIN : (9 - row) * WIN + TOK] for row in range(WIN)]
    full = jnp.stack(rows, axis=2).reshape(2, 32, TOK, TOK)
    return jnp.pad(full, ((0, 0), (0, 0), (0, ROWS - TOK), (0, ROWS - TOK)))


def fold_tables(pairs):
    total = jnp.zeros((32, WIN, 190), F32)
    for row in range(WIN):
        low = (9 - row) * WIN
        total = total + jnp.pad(
            pairs[:, row * WIN : (row + 1) * WIN, :TOK], ((0, 0), (0, 0), (low, 90 - low))
        )
    return jnp.dot(total.reshape(32, -1), jnp.asarray(PAIRS.T), precision=HIGH)


def window_masks(level, valid, column):
    place = np.arange(ROWS)
    row = np.minimum(place // WIN, WIN - 1)
    col = jnp.asarray(place % WIN, jnp.int32)
    real = jnp.asarray(place < TOK)
    offset = SHIFT if level else 0
    rolled = column * WIN + col
    usable = (rolled + offset) % GW < valid
    masks = []
    for w in range(2):
        rolled_row = w * WIN + row
        row_region = (rolled_row >= GH - WIN).astype(np.int32) + (rolled_row >= GH - SHIFT)
        col_region = (rolled >= GW - WIN).astype(jnp.int32) + (rolled >= GW - SHIFT)
        region = jnp.asarray(row_region * 3, jnp.int32) + col_region
        allowed = usable[None, :]
        if level:
            allowed = allowed & (region[:, None] == region[None, :])
        mask = jnp.where(allowed, F32(0.0), F32(-100.0))
        mask = jnp.where(real[None, :], mask, F32(-1e30))
        masks.append(jnp.broadcast_to(mask, (ROWS, ROWS)))
    return jnp.stack(masks)


def gather_tp(value, place):
    parts = [value]
    for step in range(1, TP):
        parts.append(lax.ppermute(value, "tp", [(i, (i + step) % TP) for i in range(TP)]))
    stacked = jnp.stack(parts)
    order = (place - jnp.arange(TP)) % TP
    return [lax.dynamic_index_in_dim(stacked, order[i], 0, keepdims=False) for i in range(TP)]


def swap_core(value):
    return lax.ppermute(value, "core", [(0, 1), (1, 0)])


def sum_all(value):
    for axis, gap in (("core", 1), ("x", 1), ("x", 2), ("y", 1), ("y", 2), ("tp", 1), ("tp", 2)):
        size = 2 if axis == "core" else 4
        sent = value.astype(BF)
        got = lax.ppermute(sent, axis, [(i, i ^ gap) for i in range(size)])
        value = sent.astype(F32) + got.astype(F32)
    return value


def body(
    x3,
    res_group,
    merge_gain,
    merge_bias,
    merge_w,
    ln1_gain,
    ln1_bias,
    qkv_w,
    qv_bias,
    rel_table,
    proj_w,
    proj_bias,
    ln2_gain,
    ln2_bias,
    fc1_w,
    fc1_bias,
    fc2_w,
    fc2_bias,
    out_grad,
):
    core_at = lax.axis_index("core")
    chip_at = lax.axis_index("y") * 4 + lax.axis_index("x")
    column = lax.axis_index("tp")
    core = jnp.stack([core_at, column]).astype(jnp.int32)

    piece = pack_weights(
        jnp.stack([chip_at, core_at]).astype(jnp.int32),
        fc1_w,
        fc2_w,
        jnp.swapaxes(qkv_w, 1, 2),
        proj_w,
        merge_w.reshape(512, D),
    )
    weights = lax.all_gather(piece, GATHER_AXES, axis=0, tiled=True).reshape(64, UNITS, 16, D)

    pages = lax.all_to_all(x3, PAGE_AXES, split_axis=1, concat_axis=0, tiled=True)
    tiles = pages.reshape(GH, TP, WIN, 512).transpose(1, 0, 2, 3).reshape(TP * 2 * TOK, 512)
    parts = lax.all_to_all(tiles, "tp", split_axis=0, concat_axis=0, tiled=True)
    parts = parts.reshape(TP, 2 * TOK, 512)

    packed = jnp.concatenate(
        [
            merge_gain.reshape(-1),
            merge_bias.reshape(-1),
            qv_bias.reshape(-1),
            fc1_bias.reshape(-1),
            rel_table.reshape(-1),
            jnp.zeros((10240 - 9872,), F32),
        ]
    ).reshape(80, 128)
    quarters = [part.reshape(-1) for part in gather_tp(packed, column)]

    def joined(low, shape, axis):
        size = int(np.prod(shape))
        return jnp.concatenate([part[low : low + size].reshape(shape) for part in quarters], axis)

    merge_gain_all = joined(0, (1, 512), 0)
    merge_bias_all = joined(512, (1, 512), 0)
    qv_bias_all = joined(1024, (2, 2, 256), 2)
    fc1_bias_all = joined(2048, (2, 1024), 1)
    tables = spread_tables(joined(4096, (2, 8, RELS), 1))

    valid = (res_group[0] + 1) * WIN
    masks = [window_masks(level, valid, column) for level in range(2)]
    spot = np.arange(T) % ROWS
    keep = ((column * WIN + SHIFT + jnp.asarray(spot % WIN, jnp.int32)) % GW < valid) & jnp.asarray(
        spot < TOK
    )
    keep = keep.astype(F32)[:, None]
    cotangent = jnp.roll(out_grad[0], (-SHIFT, -SHIFT), (0, 1))
    cotangent = lax.dynamic_slice_in_dim(cotangent, column * WIN, WIN, 1).reshape(2, TOK, D)
    cotangent = jnp.pad(cotangent, ((0, 0), (0, ROWS - TOK), (0, 0))).reshape(T, D)

    state, merged_mine, merged_other = merge_forward(
        core, parts, merge_gain_all, merge_bias_all, weights
    )
    kept = []
    halo = None
    for level in range(2):
        small = (
            ln1_gain[level : level + 1],
            ln1_bias[level : level + 1],
            qv_bias_all[level, 0:1],
            qv_bias_all[level, 1:2],
            proj_bias[level : level + 1],
        )
        got = attn_forward(
            core, level, state, halo, weights, small, tables[level], masks[level]
        )
        mid, a, q, k, v, probs, heads_mine, heads_other = got[:8]
        start = got[8] if level else state
        small = (
            ln2_gain[level : level + 1],
            ln2_bias[level : level + 1],
            fc1_bias_all[level : level + 1],
            fc2_bias[level : level + 1],
        )
        more = mlp_forward(core, level, mid, weights, small, keep)
        c2, slope, act_mine, act_other, extra = more[:5]
        kept.append((start, mid, a, q, k, v, probs, slope, c2))
        kept[-1] += ((heads_mine, swap_core(heads_other)), (act_mine, swap_core(act_other)))
        if not level:
            state = more[5]
            halo = lax.ppermute(extra, "tp", [((i + 1) % TP, i) for i in range(TP)])
    tiles_out = lax.all_gather(extra, "tp", axis=0, tiled=False).reshape(TP, GH, WIN, D)
    pieces = [None, None]
    sums = [None, None]
    grad, halo = cotangent, None
    for level in (1, 0):
        start, mid, a, q, k, v, probs, slope, c2, heads, act = kept[level]
        dmid, dmlp, dattn, dpre_mine, dpre_other, db1, rows_two = mlp_backward(
            core, level, grad, halo, keep, mid, ln2_gain[level : level + 1], weights, slope
        )
        got = attn_backward(
            core, level, dmid, dattn, start, ln1_gain[level : level + 1], weights, q, k, v, probs
        )
        grad, mixed_mine, mixed_other, pairs, dqv, rows_one = got[:6]
        if level:
            halo = lax.ppermute(got[6], "tp", [(i, (i + 1) % TP) for i in range(TP)])
        sums[level] = (db1, rows_two, dqv, rows_one, fold_tables(pairs))
        pieces[level] = send_ahead(
            quarter_grads(core, (c2, swap_core(c2)), (dpre_mine, swap_core(dpre_other)))
        )
        items = [
            ((dmlp, swap_core(dmlp)), act),
            ((a, swap_core(a)), (mixed_mine, swap_core(mixed_other))),
            ((dattn, swap_core(dattn)), heads),
        ]
        if level:
            late = weight_grads(core, items, [])
            late, tiles_out = lax.optimization_barrier((late, tiles_out))
            late = lax.psum_scatter(late, CHIP_AXES, scatter_dimension=0, tiled=True)
            late = lax.optimization_barrier(late)[0]
    first, dm, dgain, dbias = merge_backward(core, parts, merge_gain_all, weights, grad)
    items.append(((first, swap_core(first)), (merged_mine, swap_core(merged_other))))
    early = weight_grads(core, items, [pieces[1], pieces[0]])
    early = lax.psum_scatter(early, CHIP_AXES, scatter_dimension=0, tiled=True)
    early = lax.optimization_barrier(early)[0]

    output = jnp.roll(tiles_out.transpose(1, 0, 2, 3).reshape(GH, GW, D), SHIFT, 1)
    output = output.astype(F32)[None]
    back = lax.all_to_all(
        dm.reshape(TP * 2 * TOK, 512), "tp", split_axis=0, concat_axis=0, tiled=True
    )
    back = back.reshape(TP, GH, WIN, 512).transpose(1, 0, 2, 3).reshape(800, 1, 4, 128)
    grad_x3 = lax.all_to_all(back, PAGE_AXES, split_axis=0, concat_axis=1, tiled=True).astype(F32)

    def both_cores(value):
        rows = value.reshape(2, 32, -1)
        kept_rows = lax.dynamic_index_in_dim(rows, core_at, 0, keepdims=False).astype(F32)
        sent_rows = lax.dynamic_index_in_dim(rows, 1 - core_at, 0, keepdims=False)
        got_rows = swap_core(sent_rows.astype(BF)).astype(F32)
        return (
            jnp.where(core_at == 0, kept_rows, got_rows),
            jnp.where(core_at == 0, got_rows, kept_rows),
        )

    def wide(halves, low, size):
        return jnp.concatenate([half[:, low : low + size] for half in halves], axis=1)

    late = both_cores(sum_quarters(late, column))
    complete = early[..., 1280:].reshape(TP, 64, 2, 128).transpose(1, 2, 0, 3).reshape(64, D)
    early = both_cores(
        jnp.concatenate([sum_quarters(early[..., :1280], column), complete.astype(F32)], axis=1)
    )
    pair = (early, late)
    g_fc1 = jnp.stack([wide(early, 1280 + 512, 512), wide(early, 1280, 512)])
    g_fc2 = jnp.stack([wide(half, 0, 512).T for half in pair])
    g_qkv = jnp.stack(
        [jnp.stack([wide(half, 512 + 128 * s, 128) for s in range(3)], axis=1) for half in pair]
    )
    g_proj = jnp.stack([wide(half, 896, 128).T for half in pair])
    g_merge_w = wide(early, 1024, 256).T.reshape(4, 128, 32)

    flat = []
    for level in range(2):
        db1, rows_two, dqv, rows_one, table = sums[level]
        flat += [rows_one, rows_two, dqv, db1, table]
    flat += [dgain, dbias]
    flat = jnp.concatenate([item.reshape(-1) for item in flat])
    count = flat.shape[0]
    flat = jnp.pad(flat, (0, -count % 16384)).reshape(-1, 1024)
    flat = sum_all(flat).reshape(-1)
    page_at = chip_at * 2 + core_at

    def take(low, shape):
        return flat[low : low + int(np.prod(shape))].reshape(shape)

    def page_part(value):
        return lax.dynamic_slice_in_dim(value, page_at * 32, 32, value.ndim - 1)

    def tp_part(value, axis):
        size = value.shape[axis] // TP
        return lax.dynamic_slice_in_dim(value, column * size, size, axis)

    span = 2 * D + 4 * D + 2 * D + FF + 32 * RELS
    rows = [take(level * span, (6, D)) for level in range(2)]
    rows = page_part(jnp.stack(rows))
    dqv = tp_part(jnp.stack([take(level * span + 6 * D, (2, D)) for level in range(2)]), 2)
    db1 = tp_part(jnp.stack([take(level * span + 8 * D, (FF,)) for level in range(2)]), 1)
    table = tp_part(
        jnp.stack([take(level * span + 8 * D + FF, (32, RELS)) for level in range(2)]), 1
    )
    dgain = tp_part(take(2 * span, (TP, 512)), 0).reshape(4, 128)
    dbias = tp_part(take(2 * span + MERGED, (TP, 512)), 0).reshape(4, 128)
    return (
        output,
        grad_x3,
        dgain,
        dbias,
        g_merge_w,
        rows[:, 0],
        rows[:, 1],
        g_qkv,
        dqv,
        table,
        g_proj,
        rows[:, 5],
        rows[:, 2],
        rows[:, 3],
        g_fc1,
        db1,
        g_fc2,
        rows[:, 4],
    )


def solution(mesh):
    grid = Mesh(mesh.devices.reshape(4, 4, 2, TP), ("y", "x", "core", "tp"))
    page = PAGE_AXES
    return jax.shard_map(
        body,
        mesh=grid,
        in_specs=(
            P(page, None, None, "tp"),
            P(page),
            P(None, "tp"),
            P(None, "tp"),
            P(None, "tp", None),
            P(),
            P(),
            P(None, None, None, "tp"),
            P(None, None, "tp"),
            P(None, "tp", None),
            P(None, "tp", None),
            P(),
            P(),
            P(),
            P(None, None, "tp"),
            P(None, "tp"),
            P(None, "tp", None),
            P(),
            P(page, None, None, None),
        ),
        out_specs=(
            P(page, None, None, None),
            P(page, None, None, "tp"),
            P(None, "tp"),
            P(None, "tp"),
            P(None, "tp", page),
            P(None, page),
            P(None, page),
            P(None, page, None, "tp"),
            P(None, None, "tp"),
            P(None, "tp", None),
            P(None, "tp", page),
            P(None, page),
            P(None, page),
            P(None, page),
            P(None, page, "tp"),
            P(None, "tp"),
            P(None, "tp", page),
            P(None, page),
        ),
        check_vma=False,
    )
```

```python
from functools import partial

import jax
import jax.numpy as jnp
import numpy as np
from jax import lax
from jax.experimental import pallas as pl
from jax.experimental.pallas import tpu as pltpu
from jax.sharding import Mesh
from jax.sharding import PartitionSpec as P

D = 1024
FF = 4096
MERGED = 2048
WIN = 10
SHIFT = 5
GH = 20
GW = 40
RELS = 361
TOK = 100
ROWS = 112
T = 2 * ROWS
SEND = 112
EPS = 1e-05
SCALE = 32 ** (-0.5)
YX = 16
TP = 4
UNITS = 26
HIGH = lax.Precision.HIGHEST
BF = jnp.bfloat16
F32 = jnp.float32
PAGE_AXES = ("y", "x", "core")
CHIP_AXES = ("y", "x")
GATHER_AXES = ("tp", "y", "x", "core")
VMEM = 58 << 20


def row_at(row, col):
    return (row // WIN) * ROWS + (row % WIN) * WIN + col


def place_matrices():
    own = np.zeros((T, T), np.float32)
    recv = np.zeros((T, SEND), np.float32)
    send = np.zeros((SEND, T), np.float32)
    pack = np.zeros((2 * TOK, T), np.float32)
    out = np.zeros((2 * TOK, T), np.float32)
    for row in range(GH):
        for col in range(WIN):
            source = (row + SHIFT) % GH
            if col < SHIFT:
                own[row_at(row, col), row_at(source, col + SHIFT)] = 1
                send[row * SHIFT + col, row_at(row, col)] = 1
            else:
                recv[row_at(row, col), source * SHIFT + col - SHIFT] = 1
            pack[row * WIN + col, row_at(row, col)] = 1
            out[source * WIN + col, row_at(row, col)] = 1
    return own, recv, send, pack, out


OWN, RECV, SENT, PACK, OUT = place_matrices()


def const(matrix):
    return jnp.asarray(matrix, BF)


def dot(left, right):
    return lax.dot_general(left, right, (((1,), (0,)), ((), ())), preferred_element_type=F32)


def dot_nt(left, right):
    return lax.dot_general(left, right, (((1,), (1,)), ((), ())), preferred_element_type=F32)


def dot_tn(left, right):
    return lax.dot_general(left, right, (((0,), (0,)), ((), ())), preferred_element_type=F32)


def select_rows(matrix, value):
    high = value.astype(BF)
    rest = value - high.astype(F32)
    mid = rest.astype(BF)
    low = (rest - mid.astype(F32)).astype(BF)
    return dot(matrix, high) + dot(matrix, mid) + dot(matrix, low)


def norm_stats(value):
    mean = jnp.mean(value, axis=-1, keepdims=True)
    center = value - mean
    return center, lax.rsqrt(jnp.mean(center * center, axis=-1, keepdims=True) + EPS)


def norm_back(upstream, normed, spread, gain):
    scaled = upstream * gain
    inner = (
        scaled
        - jnp.mean(scaled, axis=-1, keepdims=True)
        - normed * jnp.mean(scaled * normed, axis=-1, keepdims=True)
    )
    return spread * inner


def col_sum(value):
    return jnp.sum(value, axis=0, keepdims=True)


def whole(shape):
    return pl.BlockSpec(shape, lambda step, core: (0,) * len(shape))


def shape_of(shape, dtype):
    return jax.ShapeDtypeStruct(shape, dtype)


def run(kernel, steps, core, args, in_specs, outs, out_specs, scratch, flops, moved):
    return pl.pallas_call(
        kernel,
        grid_spec=pltpu.PrefetchScalarGridSpec(
            num_scalar_prefetch=1,
            grid=(steps,),
            in_specs=in_specs,
            out_specs=out_specs,
            scratch_shapes=scratch,
        ),
        out_shape=outs,
        compiler_params=pltpu.CompilerParams(
            vmem_limit_bytes=VMEM, dimension_semantics=("arbitrary",)
        ),
        cost_estimate=pl.CostEstimate(flops=0, bytes_accessed=1024, transcendentals=0),
    )(core, *args)


def put_halves(core_ref, mine, other, low, high):
    @pl.when(core_ref[0] == 0)
    def _():
        mine(low)
        other(high)

    @pl.when(core_ref[0] != 0)
    def _():
        mine(high)
        other(low)


def pack_kernel(place_ref, up_ref, down_ref, mix_ref, proj_ref, merge_ref, out_ref, all_ref):
    for level in range(2):
        all_ref[8 * level : 8 * level + 4] = up_ref[level].reshape(4, 16, D)
        all_ref[8 * level + 4 : 8 * level + 8] = down_ref[level].reshape(4, 16, D)
        for part in range(3):
            for group in range(4):
                all_ref[16 + 4 * level + part, :, 256 * group : 256 * group + 256] = mix_ref[
                    level, part, 16 * group : 16 * group + 16
                ]
        all_ref[19 + 4 * level] = proj_ref[level]
    all_ref[24:26] = merge_ref[...].reshape(2, 16, D)
    out_ref[...] = all_ref[pl.ds(place_ref[1] * 13, 13)]


def pack_weights(place, up, down, mix, proj, merge):
    piece = pl.pallas_call(
        pack_kernel,
        grid_spec=pltpu.PrefetchScalarGridSpec(
            num_scalar_prefetch=1,
            grid=(1,),
            in_specs=[
                pl.BlockSpec((2, 64, D), lambda step, place: (0, place[0], 0)),
                pl.BlockSpec((2, 64, D), lambda step, place: (0, place[0], 0)),
                pl.BlockSpec((2, 3, 64, 256), lambda step, place: (0, 0, place[0], 0)),
                pl.BlockSpec((2, 16, D), lambda step, place: (0, place[0], 0)),
                pl.BlockSpec((32, D), lambda step, place: (place[0], 0)),
            ],
            out_specs=whole((13, 16, D)),
            scratch_shapes=[pltpu.VMEM((UNITS, 16, D), BF)],
        ),
        out_shape=shape_of((13, 16, D), BF),
        compiler_params=pltpu.CompilerParams(vmem_limit_bytes=VMEM),
        cost_estimate=pl.CostEstimate(flops=0, bytes_accessed=1 << 20, transcendentals=0),
    )(place, up, down, mix, proj, merge)
    return piece.reshape(208, D)


def merge_stats(x_ref, pack_ref, full):
    total = jnp.zeros((T, 1), F32)
    for part in range(TP):
        rows = dot_tn(pack_ref[...], x_ref[part])
        full[part] = rows
        total = total + jnp.sum(rows, axis=-1, keepdims=True)
    mean = total / MERGED
    square = jnp.zeros((T, 1), F32)
    for part in range(TP):
        center = full[part] - mean
        square = square + jnp.sum(center * center, axis=-1, keepdims=True)
    return mean, lax.rsqrt(square / MERGED + EPS)


def merge_kernel(
    core_ref, x_ref, pack_ref, gain_ref, bias_ref, w_ref, out_ref, mine_ref, other_ref, full, stats
):
    step = pl.program_id(0)

    @pl.when(step == 0)
    def _():
        mean, spread = merge_stats(x_ref, pack_ref, full)
        stats[0] = mean
        stats[1] = spread

    normed = (full[step] - stats[0]) * stats[1]
    value = (normed * gain_ref[0] + bias_ref[0]).astype(BF)

    def set_mine(part):
        mine_ref[...] = part

    def set_other(part):
        other_ref[...] = part

    put_halves(core_ref, set_mine, set_other, value[:, :256], value[:, 256:])
    term = dot(value, w_ref[...].reshape(512, D))

    @pl.when(step == 0)
    def _():
        out_ref[...] = term

    @pl.when(step != 0)
    def _():
        out_ref[...] += term


def merge_forward(core, parts, gain, bias, weights):
    return run(
        merge_kernel,
        TP,
        core,
        (parts, const(PACK), gain.reshape(TP, 1, 512), bias.reshape(TP, 1, 512), weights),
        [
            whole((TP, 2 * TOK, 512)),
            whole((2 * TOK, T)),
            pl.BlockSpec((1, 1, 512), lambda step, core: (step, 0, 0)),
            pl.BlockSpec((1, 1, 512), lambda step, core: (step, 0, 0)),
            pl.BlockSpec((YX, 2, 16, D), lambda step, core: (step, 12, 0, 0)),
        ],
        [shape_of((T, D), F32), shape_of((T, D), BF), shape_of((T, D), BF)],
        [
            whole((T, D)),
            pl.BlockSpec((T, 256), lambda step, core: (0, step)),
            pl.BlockSpec((T, 256), lambda step, core: (0, step)),
        ],
        [pltpu.VMEM((TP, T, 512), F32), pltpu.VMEM((2, T, 1), F32)],
        2 * T * MERGED * D,
        8 << 20,
    )


def merge_back_kernel(
    core_ref, x_ref, pack_ref, gain_ref, w_ref, dx_ref,
    start_ref, dm_ref, gains_ref, biases_ref,
    full, stats, upstream,
):
    step = pl.program_id(0)

    @pl.when(step == 0)
    def _():
        mean, spread = merge_stats(x_ref, pack_ref, full)
        stats[0] = mean
        stats[1] = spread
        stats[2] = jnp.zeros((T, 1), F32)
        stats[3] = jnp.zeros((T, 1), F32)
        start_ref[...] = dx_ref[...].astype(BF)

    grad = dot_nt(start_ref[...], w_ref[...].reshape(512, D))
    normed = (full[step] - stats[0]) * stats[1]
    full[step] = normed
    gains_ref[0] = col_sum(grad * normed)
    biases_ref[0] = col_sum(grad)
    scaled = grad * gain_ref[0]
    upstream[step] = scaled
    stats[2] += jnp.sum(scaled, axis=-1, keepdims=True)
    stats[3] += jnp.sum(scaled * normed, axis=-1, keepdims=True)

    @pl.when(step == TP - 1)
    def _():
        for part in range(TP):
            value = stats[1] * (
                upstream[part] - stats[2] / MERGED - full[part] * (stats[3] / MERGED)
            )
            dm_ref[part] = dot(pack_ref[...], value.astype(BF)).astype(BF)


def merge_backward(core, parts, gain, weights, grad):
    return run(
        merge_back_kernel,
        TP,
        core,
        (parts, const(PACK), gain.reshape(TP, 1, 512), weights, grad),
        [
            whole((TP, 2 * TOK, 512)),
            whole((2 * TOK, T)),
            pl.BlockSpec((1, 1, 512), lambda step, core: (step, 0, 0)),
            pl.BlockSpec((YX, 2, 16, D), lambda step, core: (step, 12, 0, 0)),
            whole((T, D)),
        ],
        [
            shape_of((T, D), BF),
            shape_of((TP, 2 * TOK, 512), BF),
            shape_of((TP, 1, 512), F32),
            shape_of((TP, 1, 512), F32),
        ],
        [
            whole((T, D)),
            whole((TP, 2 * TOK, 512)),
            pl.BlockSpec((1, 1, 512), lambda step, core: (step, 0, 0)),
            pl.BlockSpec((1, 1, 512), lambda step, core: (step, 0, 0)),
        ],
        [pltpu.VMEM((TP, T, 512), F32), pltpu.VMEM((4, T, 1), F32), pltpu.VMEM((TP, T, 512), F32)],
        2 * T * MERGED * D,
        8 << 20,
    )


def head_masks(rows):
    lane = lax.broadcasted_iota(jnp.int32, (rows, 128), 1)
    return [(lane >= 32 * place) & (lane < 32 * place + 32) for place in range(4)]


def spread_heads(value, masks):
    zero = jnp.zeros_like(value)
    return jnp.concatenate([jnp.where(mask, value, zero) for mask in masks], axis=0)


def fold_heads(value, masks):
    total = jnp.zeros((ROWS, 128), F32)
    for place, mask in enumerate(masks):
        total = jnp.where(mask, value[place * ROWS : (place + 1) * ROWS], total)
    return total


def unfold(ref):
    value = ref[...].reshape(YX, 16, D)
    parts = [value[:, :, 256 * group : 256 * group + 256] for group in range(4)]
    return jnp.stack(parts, axis=1).reshape(D, 256)


def attn_kernel(level, *refs):
    (core_ref, x_ref), refs = refs[:2], refs[2:]
    if level:
        (halo_ref, own_ref, recv_ref), refs = refs[:3], refs[3:]
    (
        gain_ref, bias_ref, wq_ref, wk_ref, wv_ref, wp_ref, qb_ref, vb_ref, table_ref, mask_ref,
        shift_ref,
    ), refs = refs[:11], refs[11:]
    (
        mid_ref, a_ref, q_ref, k_ref, v_ref, probs_ref, mine_ref, other_ref,
    ), refs = refs[:8], refs[8:]
    step = pl.program_id(0)

    @pl.when(step == 0)
    def _():
        value = x_ref[...]
        if level:
            value = select_rows(own_ref[...], value) + dot(recv_ref[...], halo_ref[...])
            refs[0][...] = value
        center, spread = norm_stats(value)
        a_ref[...] = (center * spread * gain_ref[...] + bias_ref[...]).astype(BF)
        mid_ref[...] = value + shift_ref[...]

    a = a_ref[...]
    q = (dot(a, unfold(wq_ref)) + qb_ref[...]).astype(BF)
    k = dot(a, unfold(wk_ref)).astype(BF)
    v = (dot(a, unfold(wv_ref)) + vb_ref[...]).astype(BF)
    q_ref[...] = q
    k_ref[...] = k
    v_ref[...] = v
    masks = head_masks(ROWS)
    halves = []
    for half in range(2):
        lanes = slice(half * 128, half * 128 + 128)
        table = table_ref[4 * half : 4 * half + 4]
        parts = []
        for w in range(2):
            rows = slice(w * ROWS, (w + 1) * ROWS)
            raw = dot_nt(spread_heads(q[rows, lanes], masks), k[rows, lanes]) * SCALE
            scores = raw.reshape(4, ROWS, ROWS) + table + mask_ref[w][None]
            top = jnp.max(scores, axis=-1, keepdims=True)
            terms = jnp.exp(scores - top)
            probs = (terms / jnp.sum(terms, axis=-1, keepdims=True)).astype(BF)
            probs_ref[0, w, 4 * half : 4 * half + 4] = probs
            mixed = dot(probs.reshape(4 * ROWS, ROWS), v[rows, lanes])
            parts.append(fold_heads(mixed, masks))
        halves.append(jnp.concatenate(parts, axis=0).astype(BF))

    def set_mine(part):
        mine_ref[...] = part

    def set_other(part):
        other_ref[...] = part

    put_halves(core_ref, set_mine, set_other, *halves)
    heads = jnp.concatenate(halves, axis=1)
    mid_ref[...] += dot(heads, wp_ref[...].reshape(256, D))


def unit_spec(unit):
    return pl.BlockSpec((YX, 1, 16, D), lambda step, core: (step, unit, 0, 0))


def attn_forward(core, level, state, halo, weights, small, table, mask):
    gain, bias, qbias, vbias, shift = small
    unit = 16 + 4 * level
    args = [state]
    specs = [whole((T, D))]
    if level:
        args += [halo, const(OWN), const(RECV)]
        specs += [whole((SEND, D)), whole((T, T)), whole((T, SEND))]
    args += [gain, bias, weights, weights, weights, weights, qbias, vbias, table, mask, shift]
    cols = pl.BlockSpec((1, 256), lambda step, core: (0, step))
    specs += [whole((1, D)), whole((1, D))] + [unit_spec(unit + place) for place in range(4)]
    specs += [
        cols,
        cols,
        pl.BlockSpec((8, ROWS, ROWS), lambda step, core: (step, 0, 0)),
        whole((2, ROWS, ROWS)),
        whole((1, D)),
    ]
    block = pl.BlockSpec((T, 256), lambda step, core: (0, step))
    half = pl.BlockSpec((T, 128), lambda step, core: (0, step))
    outs = [
        shape_of((T, D), F32),
        shape_of((T, D), BF),
        shape_of((T, D), BF),
        shape_of((T, D), BF),
        shape_of((T, D), BF),
        shape_of((TP, 2, 8, ROWS, ROWS), BF),
        shape_of((T, D // 2), BF),
        shape_of((T, D // 2), BF),
    ]
    out_specs = [
        whole((T, D)),
        whole((T, D)),
        block,
        block,
        block,
        pl.BlockSpec((1, 2, 8, ROWS, ROWS), lambda step, core: (step, 0, 0, 0, 0)),
        half,
        half,
    ]
    if level:
        outs.append(shape_of((T, D), F32))
        out_specs.append(whole((T, D)))
    return run(
        partial(attn_kernel, level), TP, core, args, specs, outs, out_specs, [], 8 * T * D * D, 24 << 20
    )


def quad_spec(unit):
    return pl.BlockSpec((YX, 4, 16, D), lambda step, core: (step, unit, 0, 0))


def mlp_kernel(level, *refs):
    (
        core_ref, mid_ref, gain_ref, bias_ref, w1_ref, w2_ref, b1_ref, b2_ref, place_ref, keep_ref,
        c2_ref, slope_ref, mine_ref, other_ref, extra_ref,
    ), refs = refs[:15], refs[15:]
    total = refs[0]
    step = pl.program_id(0)

    @pl.when(step == 0)
    def _():
        value = mid_ref[...]
        center, spread = norm_stats(value)
        c2_ref[...] = (center * spread * gain_ref[...] + bias_ref[...]).astype(BF)
        total[...] = value + b2_ref[...]

    pre = dot(c2_ref[...], w1_ref[...].reshape(D, D)) + b1_ref[...]
    phi = 0.5 + 0.5 * lax.erf(pre * (0.5**0.5))
    act = (pre * phi).astype(BF)
    slope_ref[...] = (phi + pre * ((2.0 * np.pi) ** -0.5 * jnp.exp(-0.5 * pre * pre))).astype(BF)

    def set_mine(part):
        mine_ref[...] = part

    def set_other(part):
        other_ref[...] = part

    put_halves(core_ref, set_mine, set_other, act[:, :512], act[:, 512:])
    total[...] += dot(act, w2_ref[...].reshape(D, D))

    @pl.when(step == TP - 1)
    def _():
        value = total[...]
        if level:
            extra_ref[...] = dot(place_ref[...], (value * keep_ref[...]).astype(BF)).astype(BF)
        else:
            extra_ref[...] = dot(place_ref[...], value.astype(BF)).astype(BF)
            refs[1][...] = value


def mlp_forward(core, level, mid, weights, small, keep):
    gain, bias, b1, b2 = small
    place = const(OUT if level else SENT)
    half = pl.BlockSpec((T, 512), lambda step, core: (0, step))
    outs = [
        shape_of((T, D), BF),
        shape_of((T, FF), BF),
        shape_of((T, FF // 2), BF),
        shape_of((T, FF // 2), BF),
        shape_of((place.shape[0], D), BF),
    ]
    out_specs = [
        whole((T, D)),
        pl.BlockSpec((T, D), lambda step, core: (0, step)),
        half,
        half,
        whole((place.shape[0], D)),
    ]
    scratch = [pltpu.VMEM((T, D), F32)]
    if not level:
        outs.append(shape_of((T, D), F32))
        out_specs.append(whole((T, D)))

    def kernel(*refs):
        refs = list(refs)
        total = refs.pop()
        mlp_kernel(level, *refs[:15], total, *refs[15:])

    return run(
        kernel,
        TP,
        core,
        (mid, gain, bias, weights, weights, b1, b2, place, keep),
        [
            whole((T, D)),
            whole((1, D)),
            whole((1, D)),
            quad_spec(2 * level),
            quad_spec(2 * level + 1),
            pl.BlockSpec((1, D), lambda step, core: (0, step)),
            whole((1, D)),
            whole(place.shape),
            whole((T, 1)),
        ],
        outs,
        out_specs,
        scratch,
        4 * T * D * FF,
        24 << 20,
    )


def mlp_back_kernel(level, *refs):
    (core_ref, dx_ref), refs = refs[:2], refs[2:]
    if level:
        (keep_ref,), refs = refs[:1], refs[1:]
    else:
        (halo_ref, own_ref, sent_ref), refs = refs[:3], refs[3:]
    (mid_ref, gain_ref, w1_ref, w2_ref, slope_ref), refs = refs[:5], refs[5:]
    (
        dmid_ref, dmlp_ref, dattn_ref, mine_ref, other_ref, db1_ref, rows_ref, total, grad,
    ) = refs
    step = pl.program_id(0)

    @pl.when(step == 0)
    def _():
        if level:
            value = dx_ref[...].astype(F32) * keep_ref[...]
        else:
            value = select_rows_t(own_ref[...], dx_ref[...]) + dot_tn(sent_ref[...], halo_ref[...])
        grad[...] = value
        dmlp_ref[...] = value.astype(BF)
        total[...] = jnp.zeros((T, D), F32)

    dact = dot_nt(dmlp_ref[...], w2_ref[...].reshape(D, D))
    rounded = (dact * slope_ref[...].astype(F32)).astype(BF)
    db1_ref[...] = col_sum(rounded.astype(F32))

    def set_mine(part):
        mine_ref[...] = part

    def set_other(part):
        other_ref[...] = part

    put_halves(core_ref, set_mine, set_other, rounded[:, :512], rounded[:, 512:])
    total[...] += dot_nt(rounded, w1_ref[...].reshape(D, D))

    @pl.when(step == TP - 1)
    def _():
        center, spread = norm_stats(mid_ref[...])
        normed = center * spread
        upstream = total[...]
        dmid = grad[...] + norm_back(upstream, normed, spread, gain_ref[...])
        dmid_ref[...] = dmid
        dattn = dmid.astype(BF)
        dattn_ref[...] = dattn
        rows_ref[0:1] = col_sum(upstream * normed)
        rows_ref[1:2] = col_sum(upstream)
        rows_ref[2:3] = col_sum(dmlp_ref[...].astype(F32))
        rows_ref[3:4] = col_sum(dattn.astype(F32))


def select_rows_t(matrix, value):
    high = value.astype(BF)
    rest = value - high.astype(F32)
    mid = rest.astype(BF)
    low = (rest - mid.astype(F32)).astype(BF)
    return dot_tn(matrix, high) + dot_tn(matrix, mid) + dot_tn(matrix, low)


def mlp_backward(core, level, grad, halo, keep, mid, gain, weights, slope):
    half = pl.BlockSpec((T, 512), lambda step, core: (0, step))
    if level:
        args, specs = [grad, keep], [whole((T, D)), whole((T, 1))]
    else:
        args = [grad, halo, const(OWN), const(SENT)]
        specs = [whole((T, D)), whole((SEND, D)), whole((T, T)), whole((SEND, T))]
    args += [mid, gain, weights, weights, slope]
    specs += [
        whole((T, D)),
        whole((1, D)),
        quad_spec(2 * level),
        quad_spec(2 * level + 1),
        pl.BlockSpec((T, D), lambda step, core: (0, step)),
    ]
    return run(
        partial(mlp_back_kernel, level),
        TP,
        core,
        args,
        specs,
        [
            shape_of((T, D), F32),
            shape_of((T, D), BF),
            shape_of((T, D), BF),
            shape_of((T, FF // 2), BF),
            shape_of((T, FF // 2), BF),
            shape_of((1, FF), F32),
            shape_of((4, D), F32),
        ],
        [
            whole((T, D)),
            whole((T, D)),
            whole((T, D)),
            half,
            half,
            pl.BlockSpec((1, D), lambda step, core: (0, step)),
            whole((4, D)),
        ],
        [pltpu.VMEM((T, D), F32), pltpu.VMEM((T, D), F32)],
        4 * T * D * FF,
        24 << 20,
    )


def attn_back_kernel(level, *refs):
    (
        core_ref, dmid_ref, dattn_ref, x_ref, gain_ref, wq_ref, wk_ref, wv_ref, wp_ref,
        q_ref, k_ref, v_ref, probs_ref,
    ), refs = refs[:13], refs[13:]
    if level:
        (place_ref,), refs = refs[:1], refs[1:]
    (dx_ref, mine_ref, other_ref, pair_ref, sums_ref, rows_ref), refs = refs[:6], refs[6:]
    if level:
        (sent_ref,), refs = refs[:1], refs[1:]
    (total,) = refs
    step = pl.program_id(0)

    @pl.when(step == 0)
    def _():
        total[...] = jnp.zeros((T, D), F32)

    dheads = dot_nt(dattn_ref[...], wp_ref[...].reshape(256, D)).astype(BF)
    masks = head_masks(ROWS)
    dqs, dks, dvs = [], [], []
    for half in range(2):
        lanes = slice(half * 128, half * 128 + 128)
        dq_parts, dk_parts, dv_parts = [], [], []
        pairs = None
        for w in range(2):
            rows = slice(w * ROWS, (w + 1) * ROWS)
            rounded = probs_ref[0, w, 4 * half : 4 * half + 4].reshape(4 * ROWS, ROWS)
            probs = rounded.astype(F32)
            spread_out = spread_heads(dheads[rows, lanes], masks)
            dprobs = dot_nt(spread_out, v_ref[rows, lanes])
            dv_parts.append(dot_tn(rounded, spread_out))
            inner = jnp.sum(probs * dprobs, axis=-1, keepdims=True)
            dscores = (probs * (dprobs - inner)).astype(BF)
            wide = dscores.astype(F32)
            pairs = wide if pairs is None else pairs + wide
            dq_parts.append(fold_heads(dot(dscores, k_ref[rows, lanes]), masks))
            dk_parts.append(dot_tn(dscores, spread_heads(q_ref[rows, lanes], masks)))
        pair_ref[4 * half : 4 * half + 4] = pairs.reshape(4, ROWS, ROWS)
        dqs.append((jnp.concatenate(dq_parts, axis=0) * SCALE).astype(BF))
        dks.append((jnp.concatenate(dk_parts, axis=0) * SCALE).astype(BF))
        dvs.append(jnp.concatenate(dv_parts, axis=0).astype(BF))

    def set_mine(part):
        mine_ref[...] = part

    def set_other(part):
        other_ref[...] = part

    put_halves(
        core_ref,
        set_mine,
        set_other,
        jnp.concatenate([dqs[0], dks[0], dvs[0]], axis=1),
        jnp.concatenate([dqs[1], dks[1], dvs[1]], axis=1),
    )
    dq = jnp.concatenate(dqs, axis=1)
    dk = jnp.concatenate(dks, axis=1)
    dv = jnp.concatenate(dvs, axis=1)
    sums_ref[0:1] = col_sum(dq.astype(F32))
    sums_ref[1:2] = col_sum(dv.astype(F32))
    total[...] += (
        dot_nt(dq, unfold(wq_ref))
        + dot_nt(dk, unfold(wk_ref))
        + dot_nt(dv, unfold(wv_ref))
    )

    @pl.when(step == TP - 1)
    def _():
        center, spread = norm_stats(x_ref[...])
        normed = center * spread
        upstream = total[...]
        value = dmid_ref[...] + norm_back(upstream, normed, spread, gain_ref[...])
        dx_ref[...] = value
        rows_ref[0:1] = col_sum(upstream * normed)
        rows_ref[1:2] = col_sum(upstream)
        if level:
            sent_ref[...] = dot_tn(place_ref[...], value.astype(BF)).astype(BF)


def attn_backward(core, level, dmid, dattn, state, gain, weights, q, k, v, probs):
    unit = 16 + 4 * level
    block = pl.BlockSpec((T, 256), lambda step, core: (0, step))
    part = pl.BlockSpec((T, 384), lambda step, core: (0, step))
    args = [dmid, dattn, state, gain, weights, weights, weights, weights, q, k, v, probs]
    specs = [whole((T, D)), whole((T, D)), whole((T, D)), whole((1, D))]
    specs += [unit_spec(unit + place) for place in range(4)]
    specs += [
        block,
        block,
        block,
        pl.BlockSpec((1, 2, 8, ROWS, ROWS), lambda step, core: (step, 0, 0, 0, 0)),
    ]
    outs = [
        shape_of((T, D), F32),
        shape_of((T, 1536), BF),
        shape_of((T, 1536), BF),
        shape_of((32, ROWS, ROWS), F32),
        shape_of((2, D), F32),
        shape_of((2, D), F32),
    ]
    out_specs = [
        whole((T, D)),
        part,
        part,
        pl.BlockSpec((8, ROWS, ROWS), lambda step, core: (step, 0, 0)),
        pl.BlockSpec((2, 256), lambda step, core: (0, step)),
        whole((2, D)),
    ]
    if level:
        args.append(const(RECV))
        specs.append(whole((T, SEND)))
        outs.append(shape_of((SEND, D), BF))
        out_specs.append(whole((SEND, D)))
    return run(
        partial(attn_back_kernel, level),
        TP,
        core,
        args,
        specs,
        outs,
        out_specs,
        [pltpu.VMEM((T, D), F32)],
        8 * T * D * D,
        24 << 20,
    )


def weight_kernel(plan, *refs):
    refs, out_ref = refs[1:-1], refs[-1]
    place = 0
    column = 0
    for kind, size in plan:
        one, two, three, four = refs[place : place + 4]
        if kind == "matrix":
            left = jnp.concatenate([one[...], two[...]], axis=0)
            right = jnp.concatenate([three[...], four[...]], axis=0)
            value = dot_tn(left, right)
        else:
            value = (one[...].astype(F32) + two[...].astype(F32)) + (
                three[...].astype(F32) + four[...].astype(F32)
            )
        out_ref[:, 0, :, column : column + size] = value.astype(BF).reshape(YX, 64, size)
        column += size
        place += 4


def weight_grads(core, items, sums):
    plan, args, specs = [], [], []
    for left, right in items:
        size = right[0].shape[1] // TP
        plan.append(("matrix", size))
        args += [left[0], left[1], right[0], right[1]]
        block = pl.BlockSpec((T, size), lambda step, core: (0, step))
        specs += [whole((T, D)), whole((T, D)), block, block]
    for pieces in sums:
        plan.append(("sum", 128))
        args += pieces
        specs += [pl.BlockSpec((D, 128), lambda step, core: (0, step))] * 4
    width = sum(size for unused, size in plan)
    return run(
        partial(weight_kernel, plan),
        TP,
        core,
        args,
        specs,
        shape_of((YX, TP, 64, width), BF),
        pl.BlockSpec((YX, 1, 64, width), lambda step, core: (0, step, 0, 0)),
        [],
        4 * T * D * width * TP,
        (2 * D * width * TP) + (8 << 20),
    )


def quarter_kernel(core_ref, one, two, three, four, *outs):
    left = jnp.concatenate([one[...], two[...]], axis=0)
    right = jnp.concatenate([three[...], four[...]], axis=0)
    value = dot_tn(left, right).astype(BF)
    for ahead, out in enumerate(outs):

        @pl.when(pl.program_id(0) == ahead)
        def _(out=out):
            out[...] = value


def quarter_grads(core, left, right):
    block = pl.BlockSpec((T, 512), lambda step, core: (0, lax.rem(core[1] + step, TP)))
    return run(
        quarter_kernel,
        TP,
        core,
        (left[0], left[1], right[0], right[1]),
        [whole((T, D)), whole((T, D)), block, block],
        [shape_of((D, 512), BF)] * TP,
        [whole((D, 512))] * TP,
        [],
        4 * T * D * 2048,
        8 << 20,
    )


def send_ahead(pieces):
    return [pieces[0]] + [
        lax.ppermute(pieces[step], "tp", [(i, (i + step) % TP) for i in range(TP)])
        for step in range(1, TP)
    ]


def sum_quarters(value, column):
    pieces = [
        lax.dynamic_index_in_dim(value, (column + step) % TP, 0, keepdims=False)
        for step in range(TP)
    ]
    got = [piece.astype(F32) for piece in send_ahead(pieces)]
    return (got[0] + got[1]) + (got[2] + got[3])


def table_index():
    place = np.zeros((RELS, WIN * 190), np.float32)
    for row in range(WIN):
        for step in range(19):
            for col in range(WIN):
                place[(18 - step) * 19 + row - col + 9, row * 190 + step * WIN + col] = 1
    return place


PAIRS = table_index()


def spread_tables(tables):
    compact = jnp.dot(tables.reshape(64, RELS), jnp.asarray(PAIRS), precision=HIGH)
    compact = compact.reshape(2, 32, WIN, 190)
    rows = [compact[..., (9 - row) * WIN : (9 - row) * WIN + TOK] for row in range(WIN)]
    full = jnp.stack(rows, axis=2).reshape(2, 32, TOK, TOK)
    return jnp.pad(full, ((0, 0), (0, 0), (0, ROWS - TOK), (0, ROWS - TOK)))


def fold_tables(pairs):
    total = jnp.zeros((32, WIN, 190), F32)
    for row in range(WIN):
        low = (9 - row) * WIN
        total = total + jnp.pad(
            pairs[:, row * WIN : (row + 1) * WIN, :TOK], ((0, 0), (0, 0), (low, 90 - low))
        )
    return jnp.dot(total.reshape(32, -1), jnp.asarray(PAIRS.T), precision=HIGH)


def window_masks(level, valid, column):
    place = np.arange(ROWS)
    row = np.minimum(place // WIN, WIN - 1)
    col = jnp.asarray(place % WIN, jnp.int32)
    real = jnp.asarray(place < TOK)
    offset = SHIFT if level else 0
    rolled = column * WIN + col
    usable = (rolled + offset) % GW < valid
    masks = []
    for w in range(2):
        rolled_row = w * WIN + row
        row_region = (rolled_row >= GH - WIN).astype(np.int32) + (rolled_row >= GH - SHIFT)
        col_region = (rolled >= GW - WIN).astype(jnp.int32) + (rolled >= GW - SHIFT)
        region = jnp.asarray(row_region * 3, jnp.int32) + col_region
        allowed = usable[None, :]
        if level:
            allowed = allowed & (region[:, None] == region[None, :])
        mask = jnp.where(allowed, F32(0.0), F32(-100.0))
        mask = jnp.where(real[None, :], mask, F32(-1e30))
        masks.append(jnp.broadcast_to(mask, (ROWS, ROWS)))
    return jnp.stack(masks)


def gather_tp(value, place):
    parts = [value]
    for step in range(1, TP):
        parts.append(lax.ppermute(value, "tp", [(i, (i + step) % TP) for i in range(TP)]))
    stacked = jnp.stack(parts)
    order = (place - jnp.arange(TP)) % TP
    return [lax.dynamic_index_in_dim(stacked, order[i], 0, keepdims=False) for i in range(TP)]


def after(value, others):
    return lax.optimization_barrier((value, others))


def swap_core(value):
    return lax.ppermute(value, "core", [(0, 1), (1, 0)])


def sum_all(value):
    for axis, gap in (("core", 1), ("x", 1), ("x", 2), ("y", 1), ("y", 2), ("tp", 1), ("tp", 2)):
        size = 2 if axis == "core" else 4
        sent = value.astype(BF)
        got = lax.ppermute(sent, axis, [(i, i ^ gap) for i in range(size)])
        value = sent.astype(F32) + got.astype(F32)
    return value


def body(
    x3,
    res_group,
    merge_gain,
    merge_bias,
    merge_w,
    ln1_gain,
    ln1_bias,
    qkv_w,
    qv_bias,
    rel_table,
    proj_w,
    proj_bias,
    ln2_gain,
    ln2_bias,
    fc1_w,
    fc1_bias,
    fc2_w,
    fc2_bias,
    out_grad,
):
    core_at = lax.axis_index("core")
    chip_at = lax.axis_index("y") * 4 + lax.axis_index("x")
    column = lax.axis_index("tp")
    core = jnp.stack([core_at, column]).astype(jnp.int32)

    piece = pack_weights(
        jnp.stack([chip_at, core_at]).astype(jnp.int32),
        fc1_w,
        fc2_w,
        jnp.swapaxes(qkv_w, 1, 2),
        proj_w,
        merge_w.reshape(512, D),
    )
    weights = lax.all_gather(piece, GATHER_AXES, axis=0, tiled=True).reshape(64, UNITS, 16, D)

    pages = lax.all_to_all(x3, PAGE_AXES, split_axis=1, concat_axis=0, tiled=True)
    tiles = pages.reshape(GH, TP, WIN, 512).transpose(1, 0, 2, 3).reshape(TP * 2 * TOK, 512)
    parts = lax.all_to_all(tiles, "tp", split_axis=0, concat_axis=0, tiled=True)
    parts = parts.reshape(TP, 2 * TOK, 512)

    packed = jnp.concatenate(
        [
            merge_gain.reshape(-1),
            merge_bias.reshape(-1),
            qv_bias.reshape(-1),
            fc1_bias.reshape(-1),
            rel_table.reshape(-1),
            jnp.zeros((10240 - 9872,), F32),
        ]
    ).reshape(80, 128)
    quarters = [part.reshape(-1) for part in gather_tp(packed, column)]

    def joined(low, shape, axis):
        size = int(np.prod(shape))
        return jnp.concatenate([part[low : low + size].reshape(shape) for part in quarters], axis)

    merge_gain_all = joined(0, (1, 512), 0)
    merge_bias_all = joined(512, (1, 512), 0)
    qv_bias_all = joined(1024, (2, 2, 256), 2)
    fc1_bias_all = joined(2048, (2, 1024), 1)
    tables = spread_tables(joined(4096, (2, 8, RELS), 1))

    valid = (res_group[0] + 1) * WIN
    masks = [window_masks(level, valid, column) for level in range(2)]
    spot = np.arange(T) % ROWS
    keep = ((column * WIN + SHIFT + jnp.asarray(spot % WIN, jnp.int32)) % GW < valid) & jnp.asarray(
        spot < TOK
    )
    keep = keep.astype(F32)[:, None]
    cotangent = jnp.roll(out_grad[0], (-SHIFT, -SHIFT), (0, 1))
    cotangent = lax.dynamic_slice_in_dim(cotangent, column * WIN, WIN, 1).reshape(2, TOK, D)
    cotangent = jnp.pad(cotangent, ((0, 0), (0, ROWS - TOK), (0, 0))).reshape(T, D)

    state, merged_mine, merged_other = merge_forward(
        core, parts, merge_gain_all, merge_bias_all, weights
    )
    kept = []
    halo = None
    pending = [swap_core(merged_other)]
    for level in range(2):
        small = (
            ln1_gain[level : level + 1],
            ln1_bias[level : level + 1],
            qv_bias_all[level, 0:1],
            qv_bias_all[level, 1:2],
            proj_bias[level : level + 1],
        )
        got = attn_forward(
            core, level, state, halo, weights, small, tables[level], masks[level]
        )
        mid, a, q, k, v, probs, heads_mine, heads_other = got[:8]
        start = got[8] if level else state
        mid, pending = after(mid, pending)
        small = (
            ln2_gain[level : level + 1],
            ln2_bias[level : level + 1],
            fc1_bias_all[level : level + 1],
            fc2_bias[level : level + 1],
        )
        swapped = pending + [swap_core(a), swap_core(heads_other)]
        more = mlp_forward(core, level, mid, weights, small, keep)
        c2, slope, act_mine, act_other, extra = more[:5]
        extra, swapped = after(extra, swapped)
        pending = [swap_core(c2), swap_core(act_other)]
        kept.append([start, mid, a, q, k, v, probs, slope, c2, act_mine, heads_mine, swapped])
        if not level:
            state = more[5]
            halo = lax.ppermute(extra, "tp", [((i + 1) % TP, i) for i in range(TP)])
    tiles_out = lax.all_gather(extra, "tp", axis=0, tiled=False).reshape(TP, GH, WIN, D)

    sums = [None, None]
    start, mid, a, q, k, v, probs, slope, c2, act_mine, heads_mine, swapped = kept[1]
    c2_zero, act_zero, a_got, heads_got = swapped
    dmid, dmlp, dattn, dpre_mine, dpre_other, db1, rows_two = mlp_backward(
        core, 1, cotangent, None, keep, mid, ln2_gain[1:2], weights, slope
    )
    dattn, pending = after(dattn, pending)
    c2_got, act_got = pending
    moved = [swap_core(dmlp), swap_core(dpre_other), swap_core(dattn)]
    got = attn_backward(core, 1, dmid, dattn, start, ln1_gain[1:2], weights, q, k, v, probs)
    grad, mixed_mine, mixed_other, pairs, dqv, rows_one, sent = got
    sent, moved = after(sent, moved)
    halo = lax.ppermute(sent, "tp", [(i, (i + 1) % TP) for i in range(TP)])
    mixed_got = swap_core(mixed_other)
    sums[1] = (db1, rows_two, dqv, rows_one, fold_tables(pairs))
    items = [
        ((dmlp, moved[0]), (act_mine, act_got)),
        ((a, a_got), (mixed_mine, mixed_got)),
        ((dattn, moved[2]), (heads_mine, heads_got)),
    ]
    late = weight_grads(core, items, [])
    late, tiles_out = lax.optimization_barrier((late, tiles_out))
    late, dpre_got = lax.optimization_barrier((late, moved[1]))
    exchange = send_ahead(quarter_grads(core, (c2, c2_got), (dpre_mine, dpre_got)))
    late = lax.psum_scatter(late, CHIP_AXES, scatter_dimension=0, tiled=True)
    late = lax.optimization_barrier(late)[0]

    start, mid, a, q, k, v, probs, slope, c2, act_mine, heads_mine, swapped = kept[0]
    merged_got, a_got, heads_got = swapped
    dmid, dmlp, dattn, dpre_mine, dpre_other, db1, rows_two = mlp_backward(
        core, 0, grad, halo, keep, mid, ln2_gain[0:1], weights, slope
    )
    got = attn_backward(core, 0, dmid, dattn, start, ln1_gain[0:1], weights, q, k, v, probs)
    grad, mixed_mine, mixed_other, pairs, dqv, rows_one = got
    grad, (moved, exchange) = after(grad, ([dmlp, dpre_other, dattn], exchange))
    moved = [swap_core(value) for value in moved]
    sums[0] = (db1, rows_two, dqv, rows_one, fold_tables(pairs))
    first, dm, dgain, dbias = merge_backward(core, parts, merge_gain_all, weights, grad)
    mixed_got = swap_core(mixed_other)
    first_got = swap_core(first)
    items = [
        ((c2, c2_zero), (dpre_mine, moved[1])),
        ((dmlp, moved[0]), (act_mine, act_zero)),
        ((a, a_got), (mixed_mine, mixed_got)),
        ((dattn, moved[2]), (heads_mine, heads_got)),
        ((first, first_got), (merged_mine, merged_got)),
    ]
    early = weight_grads(core, items, [exchange])
    early = lax.psum_scatter(early, CHIP_AXES, scatter_dimension=0, tiled=True)
    early = lax.optimization_barrier(early)[0]

    output = jnp.roll(tiles_out.transpose(1, 0, 2, 3).reshape(GH, GW, D), SHIFT, 1)
    output = output.astype(F32)[None]
    back = lax.all_to_all(
        dm.reshape(TP * 2 * TOK, 512), "tp", split_axis=0, concat_axis=0, tiled=True
    )
    back = back.reshape(TP, GH, WIN, 512).transpose(1, 0, 2, 3).reshape(800, 1, 4, 128)
    grad_x3 = lax.all_to_all(back, PAGE_AXES, split_axis=0, concat_axis=1, tiled=True).astype(F32)

    def both_cores(value):
        rows = value.reshape(2, 32, -1)
        kept_rows = lax.dynamic_index_in_dim(rows, core_at, 0, keepdims=False).astype(F32)
        sent_rows = lax.dynamic_index_in_dim(rows, 1 - core_at, 0, keepdims=False)
        got_rows = swap_core(sent_rows.astype(BF)).astype(F32)
        return (
            jnp.where(core_at == 0, kept_rows, got_rows),
            jnp.where(core_at == 0, got_rows, kept_rows),
        )

    def wide(halves, low, size):
        return jnp.concatenate([half[:, low : low + size] for half in halves], axis=1)

    late = both_cores(sum_quarters(late, column))
    complete = early[..., 1792:].transpose(1, 0, 2).reshape(64, 512)
    early = both_cores(
        jnp.concatenate([sum_quarters(early[..., :1792], column), complete.astype(F32)], axis=1)
    )
    g_fc1 = jnp.stack([wide(early, 0, 512), wide(early, 1792, 512)])
    g_fc2 = jnp.stack([wide(early, 512, 512).T, wide(late, 0, 512).T])
    pair = ((early, 1024), (late, 512))
    g_qkv = jnp.stack(
        [jnp.stack([wide(half, low + 128 * s, 128) for s in range(3)], axis=1) for half, low in pair]
    )
    g_proj = jnp.stack([wide(half, low + 384, 128).T for half, low in pair])
    g_merge_w = wide(early, 1536, 256).T.reshape(4, 128, 32)

    flat = []
    for level in range(2):
        db1, rows_two, dqv, rows_one, table = sums[level]
        flat += [rows_one, rows_two, dqv, db1, table]
    flat += [dgain, dbias]
    flat = jnp.concatenate([item.reshape(-1) for item in flat])
    count = flat.shape[0]
    flat = jnp.pad(flat, (0, -count % 16384)).reshape(-1, 1024)
    flat = sum_all(flat).reshape(-1)
    page_at = chip_at * 2 + core_at

    def take(low, shape):
        return flat[low : low + int(np.prod(shape))].reshape(shape)

    def page_part(value):
        return lax.dynamic_slice_in_dim(value, page_at * 32, 32, value.ndim - 1)

    def tp_part(value, axis):
        size = value.shape[axis] // TP
        return lax.dynamic_slice_in_dim(value, column * size, size, axis)

    span = 2 * D + 4 * D + 2 * D + FF + 32 * RELS
    rows = [take(level * span, (6, D)) for level in range(2)]
    rows = page_part(jnp.stack(rows))
    dqv = tp_part(jnp.stack([take(level * span + 6 * D, (2, D)) for level in range(2)]), 2)
    db1 = tp_part(jnp.stack([take(level * span + 8 * D, (FF,)) for level in range(2)]), 1)
    table = tp_part(
        jnp.stack([take(level * span + 8 * D + FF, (32, RELS)) for level in range(2)]), 1
    )
    dgain = tp_part(take(2 * span, (TP, 512)), 0).reshape(4, 128)
    dbias = tp_part(take(2 * span + MERGED, (TP, 512)), 0).reshape(4, 128)
    return (
        output,
        grad_x3,
        dgain,
        dbias,
        g_merge_w,
        rows[:, 0],
        rows[:, 1],
        g_qkv,
        dqv,
        table,
        g_proj,
        rows[:, 5],
        rows[:, 2],
        rows[:, 3],
        g_fc1,
        db1,
        g_fc2,
        rows[:, 4],
    )


def solution(mesh):
    grid = Mesh(mesh.devices.reshape(4, 4, 2, TP), ("y", "x", "core", "tp"))
    page = PAGE_AXES
    return jax.shard_map(
        body,
        mesh=grid,
        in_specs=(
            P(page, None, None, "tp"),
            P(page),
            P(None, "tp"),
            P(None, "tp"),
            P(None, "tp", None),
            P(),
            P(),
            P(None, None, None, "tp"),
            P(None, None, "tp"),
            P(None, "tp", None),
            P(None, "tp", None),
            P(),
            P(),
            P(),
            P(None, None, "tp"),
            P(None, "tp"),
            P(None, "tp", None),
            P(),
            P(page, None, None, None),
        ),
        out_specs=(
            P(page, None, None, None),
            P(page, None, None, "tp"),
            P(None, "tp"),
            P(None, "tp"),
            P(None, "tp", page),
            P(None, page),
            P(None, page),
            P(None, page, None, "tp"),
            P(None, None, "tp"),
            P(None, "tp", None),
            P(None, "tp", page),
            P(None, page),
            P(None, page),
            P(None, page),
            P(None, page, "tp"),
            P(None, "tp"),
            P(None, "tp", page),
            P(None, page),
        ),
        check_vma=False,
    )
```

```python
from functools import partial

import jax
import jax.numpy as jnp
import numpy as np
from jax import lax
from jax.experimental import pallas as pl
from jax.experimental.pallas import tpu as pltpu
from jax.sharding import Mesh
from jax.sharding import PartitionSpec as P

D = 1024
FF = 4096
MERGED = 2048
WIN = 10
SHIFT = 5
GH = 20
GW = 40
RELS = 361
TOK = 100
ROWS = 112
T = 2 * ROWS
SEND = 112
EPS = 1e-05
SCALE = 32 ** (-0.5)
YX = 16
TP = 4
UNITS = 26
HIGH = lax.Precision.HIGHEST
BF = jnp.bfloat16
F32 = jnp.float32
PAGE_AXES = ("y", "x", "core")
CHIP_AXES = ("y", "x")
GATHER_AXES = ("tp", "y", "x", "core")
VMEM = 58 << 20


def row_at(row, col):
    return (row // WIN) * ROWS + (row % WIN) * WIN + col


def place_matrices():
    own = np.zeros((T, T), np.float32)
    recv = np.zeros((T, SEND), np.float32)
    send = np.zeros((SEND, T), np.float32)
    pack = np.zeros((2 * TOK, T), np.float32)
    out = np.zeros((2 * TOK, T), np.float32)
    for row in range(GH):
        for col in range(WIN):
            source = (row + SHIFT) % GH
            if col < SHIFT:
                own[row_at(row, col), row_at(source, col + SHIFT)] = 1
                send[row * SHIFT + col, row_at(row, col)] = 1
            else:
                recv[row_at(row, col), source * SHIFT + col - SHIFT] = 1
            pack[row * WIN + col, row_at(row, col)] = 1
            out[source * WIN + col, row_at(row, col)] = 1
    return own, recv, send, pack, out


OWN, RECV, SENT, PACK, OUT = place_matrices()


def const(matrix):
    return jnp.asarray(matrix, BF)


def dot(left, right):
    return lax.dot_general(left, right, (((1,), (0,)), ((), ())), preferred_element_type=F32)


def dot_nt(left, right):
    return lax.dot_general(left, right, (((1,), (1,)), ((), ())), preferred_element_type=F32)


def dot_tn(left, right):
    return lax.dot_general(left, right, (((0,), (0,)), ((), ())), preferred_element_type=F32)


def select_rows(matrix, value):
    high = value.astype(BF)
    rest = value - high.astype(F32)
    mid = rest.astype(BF)
    low = (rest - mid.astype(F32)).astype(BF)
    return dot(matrix, high) + dot(matrix, mid) + dot(matrix, low)


def norm_stats(value):
    mean = jnp.mean(value, axis=-1, keepdims=True)
    center = value - mean
    return center, lax.rsqrt(jnp.mean(center * center, axis=-1, keepdims=True) + EPS)


def norm_back(upstream, normed, spread, gain):
    scaled = upstream * gain
    inner = (
        scaled
        - jnp.mean(scaled, axis=-1, keepdims=True)
        - normed * jnp.mean(scaled * normed, axis=-1, keepdims=True)
    )
    return spread * inner


def col_sum(value):
    return jnp.sum(value, axis=0, keepdims=True)


def whole(shape):
    return pl.BlockSpec(shape, lambda step, core: (0,) * len(shape))


def shape_of(shape, dtype):
    return jax.ShapeDtypeStruct(shape, dtype)


def run(kernel, steps, core, args, in_specs, outs, out_specs, scratch, flops, moved):
    return pl.pallas_call(
        kernel,
        grid_spec=pltpu.PrefetchScalarGridSpec(
            num_scalar_prefetch=1,
            grid=(steps,),
            in_specs=in_specs,
            out_specs=out_specs,
            scratch_shapes=scratch,
        ),
        out_shape=outs,
        compiler_params=pltpu.CompilerParams(
            vmem_limit_bytes=VMEM, dimension_semantics=("arbitrary",)
        ),
        cost_estimate=pl.CostEstimate(flops=0, bytes_accessed=1024, transcendentals=0),
    )(core, *args)


def put_halves(core_ref, mine, other, low, high):
    @pl.when(core_ref[0] == 0)
    def _():
        mine(low)
        other(high)

    @pl.when(core_ref[0] != 0)
    def _():
        mine(high)
        other(low)


def pack_kernel(place_ref, up_ref, down_ref, mix_ref, proj_ref, merge_ref, out_ref, all_ref):
    for level in range(2):
        all_ref[8 * level : 8 * level + 4] = up_ref[level].reshape(4, 16, D)
        all_ref[8 * level + 4 : 8 * level + 8] = down_ref[level].reshape(4, 16, D)
        for part in range(3):
            for group in range(4):
                all_ref[16 + 4 * level + part, :, 256 * group : 256 * group + 256] = mix_ref[
                    level, part, 16 * group : 16 * group + 16
                ]
        all_ref[19 + 4 * level] = proj_ref[level]
    all_ref[24:26] = merge_ref[...].reshape(2, 16, D)
    out_ref[...] = all_ref[pl.ds(place_ref[1] * 13, 13)]


def pack_weights(place, up, down, mix, proj, merge):
    piece = pl.pallas_call(
        pack_kernel,
        grid_spec=pltpu.PrefetchScalarGridSpec(
            num_scalar_prefetch=1,
            grid=(1,),
            in_specs=[
                pl.BlockSpec((2, 64, D), lambda step, place: (0, place[0], 0)),
                pl.BlockSpec((2, 64, D), lambda step, place: (0, place[0], 0)),
                pl.BlockSpec((2, 3, 64, 256), lambda step, place: (0, 0, place[0], 0)),
                pl.BlockSpec((2, 16, D), lambda step, place: (0, place[0], 0)),
                pl.BlockSpec((32, D), lambda step, place: (place[0], 0)),
            ],
            out_specs=whole((13, 16, D)),
            scratch_shapes=[pltpu.VMEM((UNITS, 16, D), BF)],
        ),
        out_shape=shape_of((13, 16, D), BF),
        compiler_params=pltpu.CompilerParams(vmem_limit_bytes=VMEM),
        cost_estimate=pl.CostEstimate(flops=0, bytes_accessed=1 << 20, transcendentals=0),
    )(place, up, down, mix, proj, merge)
    return piece.reshape(208, D)


def merge_stats(x_ref, pack_ref, full):
    total = jnp.zeros((T, 1), F32)
    for part in range(TP):
        rows = dot_tn(pack_ref[...], x_ref[part])
        full[part] = rows
        total = total + jnp.sum(rows, axis=-1, keepdims=True)
    mean = total / MERGED
    square = jnp.zeros((T, 1), F32)
    for part in range(TP):
        center = full[part] - mean
        square = square + jnp.sum(center * center, axis=-1, keepdims=True)
    return mean, lax.rsqrt(square / MERGED + EPS)


def merge_kernel(
    core_ref, x_ref, pack_ref, gain_ref, bias_ref, w_ref, out_ref, mine_ref, other_ref, full, stats
):
    step = pl.program_id(0)

    @pl.when(step == 0)
    def _():
        mean, spread = merge_stats(x_ref, pack_ref, full)
        stats[0] = mean
        stats[1] = spread

    normed = (full[step] - stats[0]) * stats[1]
    value = (normed * gain_ref[0] + bias_ref[0]).astype(BF)

    def set_mine(part):
        mine_ref[...] = part

    def set_other(part):
        other_ref[...] = part

    put_halves(core_ref, set_mine, set_other, value[:, :256], value[:, 256:])
    term = dot(value, w_ref[...].reshape(512, D))

    @pl.when(step == 0)
    def _():
        out_ref[...] = term

    @pl.when(step != 0)
    def _():
        out_ref[...] += term


def merge_forward(core, parts, gain, bias, weights):
    return run(
        merge_kernel,
        TP,
        core,
        (parts, const(PACK), gain.reshape(TP, 1, 512), bias.reshape(TP, 1, 512), weights),
        [
            whole((TP, 2 * TOK, 512)),
            whole((2 * TOK, T)),
            pl.BlockSpec((1, 1, 512), lambda step, core: (step, 0, 0)),
            pl.BlockSpec((1, 1, 512), lambda step, core: (step, 0, 0)),
            pl.BlockSpec((YX, 2, 16, D), lambda step, core: (step, 12, 0, 0)),
        ],
        [shape_of((T, D), F32), shape_of((T, D), BF), shape_of((T, D), BF)],
        [
            whole((T, D)),
            pl.BlockSpec((T, 256), lambda step, core: (0, step)),
            pl.BlockSpec((T, 256), lambda step, core: (0, step)),
        ],
        [pltpu.VMEM((TP, T, 512), F32), pltpu.VMEM((2, T, 1), F32)],
        2 * T * MERGED * D,
        8 << 20,
    )


def merge_back_kernel(
    core_ref, x_ref, pack_ref, gain_ref, w_ref, dx_ref,
    start_ref, dm_ref, gains_ref, biases_ref,
    full, stats, upstream,
):
    step = pl.program_id(0)

    @pl.when(step == 0)
    def _():
        mean, spread = merge_stats(x_ref, pack_ref, full)
        stats[0] = mean
        stats[1] = spread
        stats[2] = jnp.zeros((T, 1), F32)
        stats[3] = jnp.zeros((T, 1), F32)
        start_ref[...] = dx_ref[...].astype(BF)

    grad = dot_nt(start_ref[...], w_ref[...].reshape(512, D))
    normed = (full[step] - stats[0]) * stats[1]
    full[step] = normed
    gains_ref[0] = col_sum(grad * normed)
    biases_ref[0] = col_sum(grad)
    scaled = grad * gain_ref[0]
    upstream[step] = scaled
    stats[2] += jnp.sum(scaled, axis=-1, keepdims=True)
    stats[3] += jnp.sum(scaled * normed, axis=-1, keepdims=True)

    @pl.when(step == TP - 1)
    def _():
        for part in range(TP):
            value = stats[1] * (
                upstream[part] - stats[2] / MERGED - full[part] * (stats[3] / MERGED)
            )
            dm_ref[part] = dot(pack_ref[...], value.astype(BF)).astype(BF)


def merge_backward(core, parts, gain, weights, grad):
    return run(
        merge_back_kernel,
        TP,
        core,
        (parts, const(PACK), gain.reshape(TP, 1, 512), weights, grad),
        [
            whole((TP, 2 * TOK, 512)),
            whole((2 * TOK, T)),
            pl.BlockSpec((1, 1, 512), lambda step, core: (step, 0, 0)),
            pl.BlockSpec((YX, 2, 16, D), lambda step, core: (step, 12, 0, 0)),
            whole((T, D)),
        ],
        [
            shape_of((T, D), BF),
            shape_of((TP, 2 * TOK, 512), BF),
            shape_of((TP, 1, 512), F32),
            shape_of((TP, 1, 512), F32),
        ],
        [
            whole((T, D)),
            whole((TP, 2 * TOK, 512)),
            pl.BlockSpec((1, 1, 512), lambda step, core: (step, 0, 0)),
            pl.BlockSpec((1, 1, 512), lambda step, core: (step, 0, 0)),
        ],
        [pltpu.VMEM((TP, T, 512), F32), pltpu.VMEM((4, T, 1), F32), pltpu.VMEM((TP, T, 512), F32)],
        2 * T * MERGED * D,
        8 << 20,
    )


def head_masks(rows):
    lane = lax.broadcasted_iota(jnp.int32, (rows, 128), 1)
    return [(lane >= 32 * place) & (lane < 32 * place + 32) for place in range(4)]


def spread_heads(value, masks):
    zero = jnp.zeros_like(value)
    return jnp.concatenate([jnp.where(mask, value, zero) for mask in masks], axis=0)


def fold_heads(value, masks):
    total = jnp.zeros((ROWS, 128), F32)
    for place, mask in enumerate(masks):
        total = jnp.where(mask, value[place * ROWS : (place + 1) * ROWS], total)
    return total


def unfold(ref):
    value = ref[...].reshape(YX, 16, D)
    parts = [value[:, :, 256 * group : 256 * group + 256] for group in range(4)]
    return jnp.stack(parts, axis=1).reshape(D, 256)


def attn_kernel(level, *refs):
    (core_ref, x_ref), refs = refs[:2], refs[2:]
    if level:
        (halo_ref, own_ref, recv_ref), refs = refs[:3], refs[3:]
    (
        gain_ref, bias_ref, wq_ref, wk_ref, wv_ref, wp_ref, qb_ref, vb_ref, table_ref, mask_ref,
        shift_ref,
    ), refs = refs[:11], refs[11:]
    (
        mid_ref, a_ref, q_ref, k_ref, v_ref, probs_ref, mine_ref, other_ref,
    ), refs = refs[:8], refs[8:]
    step = pl.program_id(0)

    @pl.when(step == 0)
    def _():
        value = x_ref[...]
        if level:
            value = select_rows(own_ref[...], value) + dot(recv_ref[...], halo_ref[...])
            refs[0][...] = value
        center, spread = norm_stats(value)
        a_ref[...] = (center * spread * gain_ref[...] + bias_ref[...]).astype(BF)
        mid_ref[...] = value + shift_ref[...]

    a = a_ref[...]
    q = (dot(a, unfold(wq_ref)) + qb_ref[...]).astype(BF)
    k = dot(a, unfold(wk_ref)).astype(BF)
    v = (dot(a, unfold(wv_ref)) + vb_ref[...]).astype(BF)
    q_ref[...] = q
    k_ref[...] = k
    v_ref[...] = v
    masks = head_masks(ROWS)
    halves = []
    for half in range(2):
        lanes = slice(half * 128, half * 128 + 128)
        table = table_ref[4 * half : 4 * half + 4]
        parts = []
        for w in range(2):
            rows = slice(w * ROWS, (w + 1) * ROWS)
            raw = dot_nt(spread_heads(q[rows, lanes], masks), k[rows, lanes]) * SCALE
            scores = raw.reshape(4, ROWS, ROWS) + table + mask_ref[w][None]
            top = jnp.max(scores, axis=-1, keepdims=True)
            terms = jnp.exp(scores - top)
            probs = (terms / jnp.sum(terms, axis=-1, keepdims=True)).astype(BF)
            probs_ref[0, w, 4 * half : 4 * half + 4] = probs
            mixed = dot(probs.reshape(4 * ROWS, ROWS), v[rows, lanes])
            parts.append(fold_heads(mixed, masks))
        halves.append(jnp.concatenate(parts, axis=0).astype(BF))

    def set_mine(part):
        mine_ref[...] = part

    def set_other(part):
        other_ref[...] = part

    put_halves(core_ref, set_mine, set_other, *halves)
    heads = jnp.concatenate(halves, axis=1)
    mid_ref[...] += dot(heads, wp_ref[...].reshape(256, D))


def unit_spec(unit):
    return pl.BlockSpec((YX, 1, 16, D), lambda step, core: (step, unit, 0, 0))


def attn_forward(core, level, state, halo, weights, small, table, mask):
    gain, bias, qbias, vbias, shift = small
    unit = 16 + 4 * level
    args = [state]
    specs = [whole((T, D))]
    if level:
        args += [halo, const(OWN), const(RECV)]
        specs += [whole((SEND, D)), whole((T, T)), whole((T, SEND))]
    args += [gain, bias, weights, weights, weights, weights, qbias, vbias, table, mask, shift]
    cols = pl.BlockSpec((1, 256), lambda step, core: (0, step))
    specs += [whole((1, D)), whole((1, D))] + [unit_spec(unit + place) for place in range(4)]
    specs += [
        cols,
        cols,
        pl.BlockSpec((8, ROWS, ROWS), lambda step, core: (step, 0, 0)),
        whole((2, ROWS, ROWS)),
        whole((1, D)),
    ]
    block = pl.BlockSpec((T, 256), lambda step, core: (0, step))
    half = pl.BlockSpec((T, 128), lambda step, core: (0, step))
    outs = [
        shape_of((T, D), F32),
        shape_of((T, D), BF),
        shape_of((T, D), BF),
        shape_of((T, D), BF),
        shape_of((T, D), BF),
        shape_of((TP, 2, 8, ROWS, ROWS), BF),
        shape_of((T, D // 2), BF),
        shape_of((T, D // 2), BF),
    ]
    out_specs = [
        whole((T, D)),
        whole((T, D)),
        block,
        block,
        block,
        pl.BlockSpec((1, 2, 8, ROWS, ROWS), lambda step, core: (step, 0, 0, 0, 0)),
        half,
        half,
    ]
    if level:
        outs.append(shape_of((T, D), F32))
        out_specs.append(whole((T, D)))
    return run(
        partial(attn_kernel, level), TP, core, args, specs, outs, out_specs, [], 8 * T * D * D, 24 << 20
    )


def quad_spec(unit, ahead=False):
    if ahead:
        return pl.BlockSpec(
            (YX, 4, 16, D), lambda step, core: (lax.rem(core[1] + step, TP), unit, 0, 0)
        )
    return pl.BlockSpec((YX, 4, 16, D), lambda step, core: (step, unit, 0, 0))


def wide_spec(rows, ahead=False):
    if ahead:
        return pl.BlockSpec((rows, D), lambda step, core: (0, lax.rem(core[1] + step, TP)))
    return pl.BlockSpec((rows, D), lambda step, core: (0, step))


def mlp_kernel(level, *refs):
    (
        core_ref, mid_ref, gain_ref, bias_ref, w1_ref, w2_ref, b1_ref, b2_ref, place_ref, keep_ref,
        c2_ref, slope_ref, extra_ref,
    ), refs = refs[:13], refs[13:]
    act_refs, total = refs[:-1], refs[-1]
    step = pl.program_id(0)

    @pl.when(step == 0)
    def _():
        value = mid_ref[...]
        center, spread = norm_stats(value)
        c2_ref[...] = (center * spread * gain_ref[...] + bias_ref[...]).astype(BF)
        total[...] = value + b2_ref[...]

    pre = dot(c2_ref[...], w1_ref[...].reshape(D, D)) + b1_ref[...]
    phi = 0.5 + 0.5 * lax.erf(pre * (0.5**0.5))
    act = (pre * phi).astype(BF)
    slope_ref[...] = (phi + pre * ((2.0 * np.pi) ** -0.5 * jnp.exp(-0.5 * pre * pre))).astype(BF)

    if level:
        for ahead in range(TP):

            @pl.when(step == ahead)
            def _(ahead=ahead):
                act_refs[ahead][...] = act

    else:

        def set_mine(part):
            act_refs[0][...] = part

        def set_other(part):
            act_refs[1][...] = part

        put_halves(core_ref, set_mine, set_other, act[:, :512], act[:, 512:])

    total[...] += dot(act, w2_ref[...].reshape(D, D))

    @pl.when(step == TP - 1)
    def _():
        value = total[...]
        if level:
            extra_ref[...] = dot(place_ref[...], (value * keep_ref[...]).astype(BF)).astype(BF)
        else:
            extra_ref[...] = dot(place_ref[...], value.astype(BF)).astype(BF)
            act_refs[2][...] = value


def mlp_forward(core, level, mid, weights, small, keep):
    gain, bias, b1, b2 = small
    place = const(OUT if level else SENT)
    outs = [
        shape_of((T, D), BF),
        shape_of((T, FF), BF),
        shape_of((place.shape[0], D), BF),
    ]
    out_specs = [whole((T, D)), wide_spec(T, level), whole((place.shape[0], D))]
    if level:
        outs += [shape_of((T, D), BF)] * TP
        out_specs += [whole((T, D))] * TP
    else:
        half = pl.BlockSpec((T, 512), lambda step, core: (0, step))
        outs += [shape_of((T, FF // 2), BF)] * 2 + [shape_of((T, D), F32)]
        out_specs += [half, half, whole((T, D))]
    return run(
        partial(mlp_kernel, level),
        TP,
        core,
        (mid, gain, bias, weights, weights, b1, b2, place, keep),
        [
            whole((T, D)),
            whole((1, D)),
            whole((1, D)),
            quad_spec(2 * level, level),
            quad_spec(2 * level + 1, level),
            wide_spec(1, level),
            whole((1, D)),
            whole(place.shape),
            whole((T, 1)),
        ],
        outs,
        out_specs,
        [pltpu.VMEM((T, D), F32)],
        4 * T * D * FF,
        24 << 20,
    )


def mlp_back_kernel(level, *refs):
    (core_ref, dx_ref), refs = refs[:2], refs[2:]
    if level:
        (keep_ref,), refs = refs[:1], refs[1:]
    else:
        (halo_ref, own_ref, sent_ref), refs = refs[:3], refs[3:]
    (mid_ref, gain_ref, w1_ref, w2_ref, slope_ref), refs = refs[:5], refs[5:]
    (
        dmid_ref, dmlp_ref, dattn_ref, mine_ref, other_ref, db1_ref, rows_ref, total, grad,
    ) = refs
    step = pl.program_id(0)

    @pl.when(step == 0)
    def _():
        if level:
            value = dx_ref[...].astype(F32) * keep_ref[...]
        else:
            value = select_rows_t(own_ref[...], dx_ref[...]) + dot_tn(sent_ref[...], halo_ref[...])
        grad[...] = value
        dmlp_ref[...] = value.astype(BF)
        total[...] = jnp.zeros((T, D), F32)

    dact = dot_nt(dmlp_ref[...], w2_ref[...].reshape(D, D))
    rounded = (dact * slope_ref[...].astype(F32)).astype(BF)
    db1_ref[...] = col_sum(rounded.astype(F32))

    def set_mine(part):
        mine_ref[...] = part

    def set_other(part):
        other_ref[...] = part

    put_halves(core_ref, set_mine, set_other, rounded[:, :512], rounded[:, 512:])
    total[...] += dot_nt(rounded, w1_ref[...].reshape(D, D))

    @pl.when(step == TP - 1)
    def _():
        center, spread = norm_stats(mid_ref[...])
        normed = center * spread
        upstream = total[...]
        dmid = grad[...] + norm_back(upstream, normed, spread, gain_ref[...])
        dmid_ref[...] = dmid
        dattn = dmid.astype(BF)
        dattn_ref[...] = dattn
        rows_ref[0:1] = col_sum(upstream * normed)
        rows_ref[1:2] = col_sum(upstream)
        rows_ref[2:3] = col_sum(dmlp_ref[...].astype(F32))
        rows_ref[3:4] = col_sum(dattn.astype(F32))


def select_rows_t(matrix, value):
    high = value.astype(BF)
    rest = value - high.astype(F32)
    mid = rest.astype(BF)
    low = (rest - mid.astype(F32)).astype(BF)
    return dot_tn(matrix, high) + dot_tn(matrix, mid) + dot_tn(matrix, low)


def mlp_backward(core, level, grad, halo, keep, mid, gain, weights, slope):
    half = pl.BlockSpec((T, 512), lambda step, core: (0, step))
    if level:
        args, specs = [grad, keep], [whole((T, D)), whole((T, 1))]
    else:
        args = [grad, halo, const(OWN), const(SENT)]
        specs = [whole((T, D)), whole((SEND, D)), whole((T, T)), whole((SEND, T))]
    args += [mid, gain, weights, weights, slope]
    specs += [
        whole((T, D)),
        whole((1, D)),
        quad_spec(2 * level),
        quad_spec(2 * level + 1),
        pl.BlockSpec((T, D), lambda step, core: (0, step)),
    ]
    return run(
        partial(mlp_back_kernel, level),
        TP,
        core,
        args,
        specs,
        [
            shape_of((T, D), F32),
            shape_of((T, D), BF),
            shape_of((T, D), BF),
            shape_of((T, FF // 2), BF),
            shape_of((T, FF // 2), BF),
            shape_of((1, FF), F32),
            shape_of((4, D), F32),
        ],
        [
            whole((T, D)),
            whole((T, D)),
            whole((T, D)),
            half,
            half,
            pl.BlockSpec((1, D), lambda step, core: (0, step)),
            whole((4, D)),
        ],
        [pltpu.VMEM((T, D), F32), pltpu.VMEM((T, D), F32)],
        4 * T * D * FF,
        24 << 20,
    )


def attn_back_kernel(level, *refs):
    (
        core_ref, dmid_ref, dattn_ref, x_ref, gain_ref, wq_ref, wk_ref, wv_ref, wp_ref,
        q_ref, k_ref, v_ref, probs_ref,
    ), refs = refs[:13], refs[13:]
    if level:
        (place_ref,), refs = refs[:1], refs[1:]
    (dx_ref, mine_ref, other_ref, pair_ref, sums_ref, rows_ref), refs = refs[:6], refs[6:]
    if level:
        (sent_ref,), refs = refs[:1], refs[1:]
    (total,) = refs
    step = pl.program_id(0)

    @pl.when(step == 0)
    def _():
        total[...] = jnp.zeros((T, D), F32)

    dheads = dot_nt(dattn_ref[...], wp_ref[...].reshape(256, D)).astype(BF)
    masks = head_masks(ROWS)
    dqs, dks, dvs = [], [], []
    for half in range(2):
        lanes = slice(half * 128, half * 128 + 128)
        dq_parts, dk_parts, dv_parts = [], [], []
        pairs = None
        for w in range(2):
            rows = slice(w * ROWS, (w + 1) * ROWS)
            rounded = probs_ref[0, w, 4 * half : 4 * half + 4].reshape(4 * ROWS, ROWS)
            probs = rounded.astype(F32)
            spread_out = spread_heads(dheads[rows, lanes], masks)
            dprobs = dot_nt(spread_out, v_ref[rows, lanes])
            dv_parts.append(dot_tn(rounded, spread_out))
            inner = jnp.sum(probs * dprobs, axis=-1, keepdims=True)
            dscores = (probs * (dprobs - inner)).astype(BF)
            wide = dscores.astype(F32)
            pairs = wide if pairs is None else pairs + wide
            dq_parts.append(fold_heads(dot(dscores, k_ref[rows, lanes]), masks))
            dk_parts.append(dot_tn(dscores, spread_heads(q_ref[rows, lanes], masks)))
        pair_ref[4 * half : 4 * half + 4] = pairs.reshape(4, ROWS, ROWS)
        dqs.append((jnp.concatenate(dq_parts, axis=0) * SCALE).astype(BF))
        dks.append((jnp.concatenate(dk_parts, axis=0) * SCALE).astype(BF))
        dvs.append(jnp.concatenate(dv_parts, axis=0).astype(BF))

    def set_mine(part):
        mine_ref[...] = part

    def set_other(part):
        other_ref[...] = part

    put_halves(
        core_ref,
        set_mine,
        set_other,
        jnp.concatenate([dqs[0], dks[0], dvs[0]], axis=1),
        jnp.concatenate([dqs[1], dks[1], dvs[1]], axis=1),
    )
    dq = jnp.concatenate(dqs, axis=1)
    dk = jnp.concatenate(dks, axis=1)
    dv = jnp.concatenate(dvs, axis=1)
    sums_ref[0:1] = col_sum(dq.astype(F32))
    sums_ref[1:2] = col_sum(dv.astype(F32))
    total[...] += (
        dot_nt(dq, unfold(wq_ref))
        + dot_nt(dk, unfold(wk_ref))
        + dot_nt(dv, unfold(wv_ref))
    )

    @pl.when(step == TP - 1)
    def _():
        center, spread = norm_stats(x_ref[...])
        normed = center * spread
        upstream = total[...]
        value = dmid_ref[...] + norm_back(upstream, normed, spread, gain_ref[...])
        dx_ref[...] = value
        rows_ref[0:1] = col_sum(upstream * normed)
        rows_ref[1:2] = col_sum(upstream)
        if level:
            sent_ref[...] = dot_tn(place_ref[...], value.astype(BF)).astype(BF)


def attn_backward(core, level, dmid, dattn, state, gain, weights, q, k, v, probs):
    unit = 16 + 4 * level
    block = pl.BlockSpec((T, 256), lambda step, core: (0, step))
    part = pl.BlockSpec((T, 384), lambda step, core: (0, step))
    args = [dmid, dattn, state, gain, weights, weights, weights, weights, q, k, v, probs]
    specs = [whole((T, D)), whole((T, D)), whole((T, D)), whole((1, D))]
    specs += [unit_spec(unit + place) for place in range(4)]
    specs += [
        block,
        block,
        block,
        pl.BlockSpec((1, 2, 8, ROWS, ROWS), lambda step, core: (step, 0, 0, 0, 0)),
    ]
    outs = [
        shape_of((T, D), F32),
        shape_of((T, 1536), BF),
        shape_of((T, 1536), BF),
        shape_of((32, ROWS, ROWS), F32),
        shape_of((2, D), F32),
        shape_of((2, D), F32),
    ]
    out_specs = [
        whole((T, D)),
        part,
        part,
        pl.BlockSpec((8, ROWS, ROWS), lambda step, core: (step, 0, 0)),
        pl.BlockSpec((2, 256), lambda step, core: (0, step)),
        whole((2, D)),
    ]
    if level:
        args.append(const(RECV))
        specs.append(whole((T, SEND)))
        outs.append(shape_of((SEND, D), BF))
        out_specs.append(whole((SEND, D)))
    return run(
        partial(attn_back_kernel, level),
        TP,
        core,
        args,
        specs,
        outs,
        out_specs,
        [pltpu.VMEM((T, D), F32)],
        8 * T * D * D,
        24 << 20,
    )


def weight_kernel(plan, *refs):
    refs, out_ref = refs[1:-1], refs[-1]
    place = 0
    column = 0
    for kind, size, count in plan:
        parts = [ref[...] for ref in refs[place : place + count]]
        if kind == "matrix":
            value = dot_tn(
                jnp.concatenate(parts[:2], axis=0), jnp.concatenate(parts[2:], axis=0)
            )
        else:
            value = sum(part.astype(F32) for part in parts)
        out_ref[:, 0, :, column : column + size] = value.astype(BF).reshape(YX, 64, size)
        column += size
        place += count


def weight_grads(core, items, sums):
    plan, args, specs = [], [], []
    for left, right in items:
        size = right[0].shape[1] // TP
        plan.append(("matrix", size, 4))
        args += [left[0], left[1], right[0], right[1]]
        block = pl.BlockSpec((T, size), lambda step, core: (0, step))
        specs += [whole((T, D)), whole((T, D)), block, block]
    for pieces in sums:
        plan.append(("sum", 128, len(pieces)))
        args += pieces
        specs += [pl.BlockSpec((D, 128), lambda step, core: (0, step))] * len(pieces)
    width = sum(size for unused, size, count in plan)
    return run(
        partial(weight_kernel, plan),
        TP,
        core,
        args,
        specs,
        shape_of((YX, TP, 64, width), BF),
        pl.BlockSpec((YX, 1, 64, width), lambda step, core: (0, step, 0, 0)),
        [],
        4 * T * D * width * TP,
        (2 * D * width * TP) + (8 << 20),
    )


def column_kernel(core_ref, left_ref, left_other_ref, *refs):
    rights, (out_ref, total) = refs[:-2], refs[-2:]
    step = pl.program_id(0)
    left = jnp.concatenate([left_ref[0], left_other_ref[0]], axis=0)
    for back in range(TP):

        @pl.when(step == back)
        def _(back=back):
            right = jnp.concatenate([rights[back][...], rights[TP + back][...]], axis=0)
            value = dot_tn(left, right)
            total[...] = value if back == 0 else total[...] + value

    @pl.when(step == TP - 1)
    def _():
        out_ref[...] = total[...].astype(BF)


def column_grads(core, left, left_other, right, right_other):
    tile = pl.BlockSpec((1, T, D), lambda step, core: (lax.rem(core[1] + TP - step, TP), 0, 0))
    half = pl.BlockSpec((T, 512), lambda step, core: (0, core[0]))
    return run(
        column_kernel,
        TP,
        core,
        [left, left_other] + right + right_other,
        [tile, tile] + [half] * (2 * TP),
        shape_of((D, 512), BF),
        whole((D, 512)),
        [pltpu.VMEM((D, 512), F32)],
        4 * T * D * 2048,
        8 << 20,
    )


def quarter_kernel(core_ref, one, two, three, four, *outs):
    left = jnp.concatenate([one[...], two[...]], axis=0)
    right = jnp.concatenate([three[...], four[...]], axis=0)
    value = dot_tn(left, right).astype(BF)
    for ahead, out in enumerate(outs):

        @pl.when(pl.program_id(0) == ahead)
        def _(out=out):
            out[...] = value


def quarter_grads(core, left, right):
    block = pl.BlockSpec((T, 512), lambda step, core: (0, lax.rem(core[1] + step, TP)))
    return run(
        quarter_kernel,
        TP,
        core,
        (left[0], left[1], right[0], right[1]),
        [whole((T, D)), whole((T, D)), block, block],
        [shape_of((D, 512), BF)] * TP,
        [whole((D, 512))] * TP,
        [],
        4 * T * D * 2048,
        8 << 20,
    )


def send_ahead(pieces):
    return [pieces[0]] + [
        lax.ppermute(pieces[step], "tp", [(i, (i + step) % TP) for i in range(TP)])
        for step in range(1, TP)
    ]


def sum_quarters(value, column):
    pieces = [
        lax.dynamic_index_in_dim(value, (column + step) % TP, 0, keepdims=False)
        for step in range(TP)
    ]
    got = [piece.astype(F32) for piece in send_ahead(pieces)]
    return (got[0] + got[1]) + (got[2] + got[3])


def table_index():
    place = np.zeros((RELS, WIN * 190), np.float32)
    for row in range(WIN):
        for step in range(19):
            for col in range(WIN):
                place[(18 - step) * 19 + row - col + 9, row * 190 + step * WIN + col] = 1
    return place


PAIRS = table_index()


def spread_tables(tables):
    compact = jnp.dot(tables.reshape(64, RELS), jnp.asarray(PAIRS), precision=HIGH)
    compact = compact.reshape(2, 32, WIN, 190)
    rows = [compact[..., (9 - row) * WIN : (9 - row) * WIN + TOK] for row in range(WIN)]
    full = jnp.stack(rows, axis=2).reshape(2, 32, TOK, TOK)
    return jnp.pad(full, ((0, 0), (0, 0), (0, ROWS - TOK), (0, ROWS - TOK)))


def fold_tables(pairs):
    total = jnp.zeros((32, WIN, 190), F32)
    for row in range(WIN):
        low = (9 - row) * WIN
        total = total + jnp.pad(
            pairs[:, row * WIN : (row + 1) * WIN, :TOK], ((0, 0), (0, 0), (low, 90 - low))
        )
    return jnp.dot(total.reshape(32, -1), jnp.asarray(PAIRS.T), precision=HIGH)


def window_masks(level, valid, column):
    place = np.arange(ROWS)
    row = np.minimum(place // WIN, WIN - 1)
    col = jnp.asarray(place % WIN, jnp.int32)
    real = jnp.asarray(place < TOK)
    offset = SHIFT if level else 0
    rolled = column * WIN + col
    usable = (rolled + offset) % GW < valid
    masks = []
    for w in range(2):
        rolled_row = w * WIN + row
        row_region = (rolled_row >= GH - WIN).astype(np.int32) + (rolled_row >= GH - SHIFT)
        col_region = (rolled >= GW - WIN).astype(jnp.int32) + (rolled >= GW - SHIFT)
        region = jnp.asarray(row_region * 3, jnp.int32) + col_region
        allowed = usable[None, :]
        if level:
            allowed = allowed & (region[:, None] == region[None, :])
        mask = jnp.where(allowed, F32(0.0), F32(-100.0))
        mask = jnp.where(real[None, :], mask, F32(-1e30))
        masks.append(jnp.broadcast_to(mask, (ROWS, ROWS)))
    return jnp.stack(masks)


def gather_tp(value, place):
    parts = [value]
    for step in range(1, TP):
        parts.append(lax.ppermute(value, "tp", [(i, (i + step) % TP) for i in range(TP)]))
    stacked = jnp.stack(parts)
    order = (place - jnp.arange(TP)) % TP
    return [lax.dynamic_index_in_dim(stacked, order[i], 0, keepdims=False) for i in range(TP)]


def after(value, others):
    return lax.optimization_barrier((value, others))


def swap_core(value):
    return lax.ppermute(value, "core", [(0, 1), (1, 0)])


def sum_all(value):
    for axis, gap in (("core", 1), ("x", 1), ("x", 2), ("y", 1), ("y", 2), ("tp", 1), ("tp", 2)):
        size = 2 if axis == "core" else 4
        sent = value.astype(BF)
        got = lax.ppermute(sent, axis, [(i, i ^ gap) for i in range(size)])
        value = sent.astype(F32) + got.astype(F32)
    return value


def body(
    x3,
    res_group,
    merge_gain,
    merge_bias,
    merge_w,
    ln1_gain,
    ln1_bias,
    qkv_w,
    qv_bias,
    rel_table,
    proj_w,
    proj_bias,
    ln2_gain,
    ln2_bias,
    fc1_w,
    fc1_bias,
    fc2_w,
    fc2_bias,
    out_grad,
):
    core_at = lax.axis_index("core")
    chip_at = lax.axis_index("y") * 4 + lax.axis_index("x")
    column = lax.axis_index("tp")
    core = jnp.stack([core_at, column]).astype(jnp.int32)

    piece = pack_weights(
        jnp.stack([chip_at, core_at]).astype(jnp.int32),
        fc1_w,
        fc2_w,
        jnp.swapaxes(qkv_w, 1, 2),
        proj_w,
        merge_w.reshape(512, D),
    )
    weights = lax.all_gather(piece, GATHER_AXES, axis=0, tiled=True).reshape(64, UNITS, 16, D)

    pages = lax.all_to_all(x3, PAGE_AXES, split_axis=1, concat_axis=0, tiled=True)
    tiles = pages.reshape(GH, TP, WIN, 512).transpose(1, 0, 2, 3).reshape(TP * 2 * TOK, 512)
    parts = lax.all_to_all(tiles, "tp", split_axis=0, concat_axis=0, tiled=True)
    parts = parts.reshape(TP, 2 * TOK, 512)

    packed = jnp.concatenate(
        [
            merge_gain.reshape(-1),
            merge_bias.reshape(-1),
            qv_bias.reshape(-1),
            fc1_bias.reshape(-1),
            rel_table.reshape(-1),
            jnp.zeros((10240 - 9872,), F32),
        ]
    ).reshape(80, 128)
    quarters = [part.reshape(-1) for part in gather_tp(packed, column)]

    def joined(low, shape, axis):
        size = int(np.prod(shape))
        return jnp.concatenate([part[low : low + size].reshape(shape) for part in quarters], axis)

    merge_gain_all = joined(0, (1, 512), 0)
    merge_bias_all = joined(512, (1, 512), 0)
    qv_bias_all = joined(1024, (2, 2, 256), 2)
    fc1_bias_all = joined(2048, (2, 1024), 1)
    tables = spread_tables(joined(4096, (2, 8, RELS), 1))

    valid = (res_group[0] + 1) * WIN
    masks = [window_masks(level, valid, column) for level in range(2)]
    spot = np.arange(T) % ROWS
    keep = ((column * WIN + SHIFT + jnp.asarray(spot % WIN, jnp.int32)) % GW < valid) & jnp.asarray(
        spot < TOK
    )
    keep = keep.astype(F32)[:, None]
    page_keep = (jnp.asarray(np.arange(GW), jnp.int32) < valid).astype(BF)[None, :, None]
    tiles = jnp.roll(out_grad[0] * page_keep, (-SHIFT, -SHIFT), (0, 1))
    tiles = tiles.reshape(2, WIN, TP, WIN, D).transpose(2, 0, 1, 3, 4).reshape(TP, 2, TOK, D)
    tiles = jnp.pad(tiles, ((0, 0), (0, 0), (0, ROWS - TOK), (0, 0))).reshape(TP, T, D)
    cotangent = lax.dynamic_index_in_dim(tiles, column, 0, keepdims=False)
    tiles_got = swap_core(tiles)

    state, merged_mine, merged_other = merge_forward(
        core, parts, merge_gain_all, merge_bias_all, weights
    )
    kept = []
    halo = None
    pending = [swap_core(merged_other)]
    for level in range(2):
        small = (
            ln1_gain[level : level + 1],
            ln1_bias[level : level + 1],
            qv_bias_all[level, 0:1],
            qv_bias_all[level, 1:2],
            proj_bias[level : level + 1],
        )
        got = attn_forward(
            core, level, state, halo, weights, small, tables[level], masks[level]
        )
        mid, a, q, k, v, probs, heads_mine, heads_other = got[:8]
        start = got[8] if level else state
        mid, pending = after(mid, pending)
        small = (
            ln2_gain[level : level + 1],
            ln2_bias[level : level + 1],
            fc1_bias_all[level : level + 1],
            fc2_bias[level : level + 1],
        )
        swapped = pending + [swap_core(a), swap_core(heads_other)]
        more = mlp_forward(core, level, mid, weights, small, keep)
        c2, slope, extra = more[:3]
        extra, swapped = after(extra, swapped)
        pending = [swap_core(c2)]
        kept.append([start, mid, a, q, k, v, probs, slope, c2, heads_mine, swapped])
        if not level:
            act_mine, state = more[3], more[5]
            pending.append(swap_core(more[4]))
            halo = lax.ppermute(extra, "tp", [((i + 1) % TP, i) for i in range(TP)])
    acts = send_ahead(more[3:])

    sums = [None, None]
    start, mid, a, q, k, v, probs, slope, c2, heads_mine, swapped = kept[1]
    c2_zero, act_zero, a_got, heads_got = swapped
    dmid, dmlp, dattn, dpre_mine, dpre_other, db1, rows_two = mlp_backward(
        core, 1, cotangent, None, keep, mid, ln2_gain[1:2], weights, slope
    )
    dattn, pending = after(dattn, pending)
    moved = [swap_core(dpre_other), swap_core(dattn)]
    got = attn_backward(core, 1, dmid, dattn, start, ln1_gain[1:2], weights, q, k, v, probs)
    grad, mixed_mine, mixed_other, pairs, dqv, rows_one, sent = got
    sent, (moved, acts) = after(sent, (moved, acts))
    halo = lax.ppermute(sent, "tp", [(i, (i + 1) % TP) for i in range(TP)])
    acts_got = [swap_core(value) for value in acts]
    mixed_got = swap_core(mixed_other)
    sums[1] = (db1, rows_two, dqv, rows_one, fold_tables(pairs))
    down = column_grads(core, tiles, tiles_got, acts, acts_got)
    items = [
        ((a, a_got), (mixed_mine, mixed_got)),
        ((dattn, moved[1]), (heads_mine, heads_got)),
    ]
    late = weight_grads(core, items, [[down]])
    late, dpre_got, halo = lax.optimization_barrier((late, moved[0], halo))
    exchange = send_ahead(quarter_grads(core, (c2, pending[0]), (dpre_mine, dpre_got)))
    late = lax.psum_scatter(late, CHIP_AXES, scatter_dimension=0, tiled=True)
    late = lax.optimization_barrier(late)[0]

    start, mid, a, q, k, v, probs, slope, c2, heads_mine, swapped = kept[0]
    merged_got, a_got, heads_got = swapped
    dmid, dmlp, dattn, dpre_mine, dpre_other, db1, rows_two = mlp_backward(
        core, 0, grad, halo, keep, mid, ln2_gain[0:1], weights, slope
    )
    got = attn_backward(core, 0, dmid, dattn, start, ln1_gain[0:1], weights, q, k, v, probs)
    grad, mixed_mine, mixed_other, pairs, dqv, rows_one = got
    grad, (moved, exchange) = after(grad, ([dmlp, dpre_other, dattn], exchange))
    moved = [swap_core(value) for value in moved]
    sums[0] = (db1, rows_two, dqv, rows_one, fold_tables(pairs))
    first, dm, dgain, dbias = merge_backward(core, parts, merge_gain_all, weights, grad)
    mixed_got = swap_core(mixed_other)
    first_got = swap_core(first)
    items = [
        ((c2, c2_zero), (dpre_mine, moved[1])),
        ((dmlp, moved[0]), (act_mine, act_zero)),
        ((a, a_got), (mixed_mine, mixed_got)),
        ((dattn, moved[2]), (heads_mine, heads_got)),
        ((first, first_got), (merged_mine, merged_got)),
    ]
    early = weight_grads(core, items, [exchange])
    early, extra = lax.optimization_barrier((early, extra))
    early = lax.psum_scatter(early, CHIP_AXES, scatter_dimension=0, tiled=True)
    early = lax.optimization_barrier(early)[0]

    tiles_out = jnp.stack(gather_tp(extra, column)).reshape(TP, GH, WIN, D)
    output = jnp.roll(tiles_out.transpose(1, 0, 2, 3).reshape(GH, GW, D), SHIFT, 1)
    output = output.astype(F32)[None]
    back = lax.all_to_all(
        dm.reshape(TP * 2 * TOK, 512), "tp", split_axis=0, concat_axis=0, tiled=True
    )
    back = back.reshape(TP, GH, WIN, 512).transpose(1, 0, 2, 3).reshape(800, 1, 4, 128)
    grad_x3 = lax.all_to_all(back, PAGE_AXES, split_axis=0, concat_axis=1, tiled=True).astype(F32)

    def both_cores(value):
        rows = value.reshape(2, 32, -1)
        kept_rows = lax.dynamic_index_in_dim(rows, core_at, 0, keepdims=False).astype(F32)
        sent_rows = lax.dynamic_index_in_dim(rows, 1 - core_at, 0, keepdims=False)
        got_rows = swap_core(sent_rows.astype(BF)).astype(F32)
        return (
            jnp.where(core_at == 0, kept_rows, got_rows),
            jnp.where(core_at == 0, got_rows, kept_rows),
        )

    def wide(halves, low, size):
        return jnp.concatenate([half[:, low : low + size] for half in halves], axis=1)

    complete = late[..., 512:].transpose(1, 0, 2).reshape(64, 512)
    late = both_cores(
        jnp.concatenate([sum_quarters(late[..., :512], column), complete.astype(F32)], axis=1)
    )
    complete = early[..., 1792:].transpose(1, 0, 2).reshape(64, 512)
    early = both_cores(
        jnp.concatenate([sum_quarters(early[..., :1792], column), complete.astype(F32)], axis=1)
    )
    g_fc1 = jnp.stack([wide(early, 0, 512), wide(early, 1792, 512)])
    g_fc2 = jnp.stack([wide(early, 512, 512).T, wide(late, 512, 512).T])
    pair = ((early, 1024), (late, 0))
    g_qkv = jnp.stack(
        [jnp.stack([wide(half, low + 128 * s, 128) for s in range(3)], axis=1) for half, low in pair]
    )
    g_proj = jnp.stack([wide(half, low + 384, 128).T for half, low in pair])
    g_merge_w = wide(early, 1536, 256).T.reshape(4, 128, 32)

    flat = []
    for level in range(2):
        db1, rows_two, dqv, rows_one, table = sums[level]
        flat += [rows_one, rows_two, dqv, db1, table]
    flat += [dgain, dbias]
    flat = jnp.concatenate([item.reshape(-1) for item in flat])
    count = flat.shape[0]
    flat = jnp.pad(flat, (0, -count % 16384)).reshape(-1, 1024)
    flat = sum_all(flat).reshape(-1)
    page_at = chip_at * 2 + core_at

    def take(low, shape):
        return flat[low : low + int(np.prod(shape))].reshape(shape)

    def page_part(value):
        return lax.dynamic_slice_in_dim(value, page_at * 32, 32, value.ndim - 1)

    def tp_part(value, axis):
        size = value.shape[axis] // TP
        return lax.dynamic_slice_in_dim(value, column * size, size, axis)

    span = 2 * D + 4 * D + 2 * D + FF + 32 * RELS
    rows = [take(level * span, (6, D)) for level in range(2)]
    rows = page_part(jnp.stack(rows))
    dqv = tp_part(jnp.stack([take(level * span + 6 * D, (2, D)) for level in range(2)]), 2)
    db1 = tp_part(jnp.stack([take(level * span + 8 * D, (FF,)) for level in range(2)]), 1)
    table = tp_part(
        jnp.stack([take(level * span + 8 * D + FF, (32, RELS)) for level in range(2)]), 1
    )
    dgain = tp_part(take(2 * span, (TP, 512)), 0).reshape(4, 128)
    dbias = tp_part(take(2 * span + MERGED, (TP, 512)), 0).reshape(4, 128)
    return (
        output,
        grad_x3,
        dgain,
        dbias,
        g_merge_w,
        rows[:, 0],
        rows[:, 1],
        g_qkv,
        dqv,
        table,
        g_proj,
        rows[:, 5],
        rows[:, 2],
        rows[:, 3],
        g_fc1,
        db1,
        g_fc2,
        rows[:, 4],
    )


def solution(mesh):
    grid = Mesh(mesh.devices.reshape(4, 4, 2, TP), ("y", "x", "core", "tp"))
    page = PAGE_AXES
    return jax.shard_map(
        body,
        mesh=grid,
        in_specs=(
            P(page, None, None, "tp"),
            P(page),
            P(None, "tp"),
            P(None, "tp"),
            P(None, "tp", None),
            P(),
            P(),
            P(None, None, None, "tp"),
            P(None, None, "tp"),
            P(None, "tp", None),
            P(None, "tp", None),
            P(),
            P(),
            P(),
            P(None, None, "tp"),
            P(None, "tp"),
            P(None, "tp", None),
            P(),
            P(page, None, None, None),
        ),
        out_specs=(
            P(page, None, None, None),
            P(page, None, None, "tp"),
            P(None, "tp"),
            P(None, "tp"),
            P(None, "tp", page),
            P(None, page),
            P(None, page),
            P(None, page, None, "tp"),
            P(None, None, "tp"),
            P(None, "tp", None),
            P(None, "tp", page),
            P(None, page),
            P(None, page),
            P(None, page),
            P(None, page, "tp"),
            P(None, "tp"),
            P(None, "tp", page),
            P(None, page),
        ),
        check_vma=False,
    )
```

```python
from functools import partial

import jax
import jax.numpy as jnp
import numpy as np
from jax import lax
from jax.experimental import pallas as pl
from jax.experimental.pallas import tpu as pltpu
from jax.sharding import Mesh
from jax.sharding import PartitionSpec as P

D = 1024
FF = 4096
MERGED = 2048
WIN = 10
SHIFT = 5
GH = 20
GW = 40
RELS = 361
TOK = 100
ROWS = 112
T = 2 * ROWS
SEND = 112
EPS = 1e-05
SCALE = 32 ** (-0.5)
YX = 16
TP = 4
UNITS = 26
HIGH = lax.Precision.HIGHEST
BF = jnp.bfloat16
F32 = jnp.float32
PAGE_AXES = ("y", "x", "core")
CHIP_AXES = ("y", "x")
GATHER_AXES = ("tp", "y", "x", "core")
VMEM = 58 << 20


def row_at(row, col):
    return (row // WIN) * ROWS + (row % WIN) * WIN + col


def place_matrices():
    own = np.zeros((T, T), np.float32)
    recv = np.zeros((T, SEND), np.float32)
    send = np.zeros((SEND, T), np.float32)
    pack = np.zeros((2 * TOK, T), np.float32)
    out = np.zeros((2 * TOK, T), np.float32)
    for row in range(GH):
        for col in range(WIN):
            source = (row + SHIFT) % GH
            if col < SHIFT:
                own[row_at(row, col), row_at(source, col + SHIFT)] = 1
                send[row * SHIFT + col, row_at(row, col)] = 1
            else:
                recv[row_at(row, col), source * SHIFT + col - SHIFT] = 1
            pack[row * WIN + col, row_at(row, col)] = 1
            out[source * WIN + col, row_at(row, col)] = 1
    return own, recv, send, pack, out


OWN, RECV, SENT, PACK, OUT = place_matrices()


def const(matrix):
    return jnp.asarray(matrix, BF)


def dot(left, right):
    return lax.dot_general(left, right, (((1,), (0,)), ((), ())), preferred_element_type=F32)


def dot_nt(left, right):
    return lax.dot_general(left, right, (((1,), (1,)), ((), ())), preferred_element_type=F32)


def dot_tn(left, right):
    return lax.dot_general(left, right, (((0,), (0,)), ((), ())), preferred_element_type=F32)


def select_rows(matrix, value):
    high = value.astype(BF)
    rest = value - high.astype(F32)
    mid = rest.astype(BF)
    low = (rest - mid.astype(F32)).astype(BF)
    return dot(matrix, high) + dot(matrix, mid) + dot(matrix, low)


def norm_stats(value):
    mean = jnp.mean(value, axis=-1, keepdims=True)
    center = value - mean
    return center, lax.rsqrt(jnp.mean(center * center, axis=-1, keepdims=True) + EPS)


def norm_back(upstream, normed, spread, gain):
    scaled = upstream * gain
    inner = (
        scaled
        - jnp.mean(scaled, axis=-1, keepdims=True)
        - normed * jnp.mean(scaled * normed, axis=-1, keepdims=True)
    )
    return spread * inner


def col_sum(value):
    return jnp.sum(value, axis=0, keepdims=True)


def whole(shape):
    return pl.BlockSpec(shape, lambda step, core: (0,) * len(shape))


def shape_of(shape, dtype):
    return jax.ShapeDtypeStruct(shape, dtype)


def run(kernel, steps, core, args, in_specs, outs, out_specs, scratch, flops, moved):
    return pl.pallas_call(
        kernel,
        grid_spec=pltpu.PrefetchScalarGridSpec(
            num_scalar_prefetch=1,
            grid=(steps,),
            in_specs=in_specs,
            out_specs=out_specs,
            scratch_shapes=scratch,
        ),
        out_shape=outs,
        compiler_params=pltpu.CompilerParams(
            vmem_limit_bytes=VMEM, dimension_semantics=("arbitrary",)
        ),
        cost_estimate=pl.CostEstimate(flops=0, bytes_accessed=1024, transcendentals=0),
    )(core, *args)


def put_halves(core_ref, mine, other, low, high):
    @pl.when(core_ref[0] == 0)
    def _():
        mine(low)
        other(high)

    @pl.when(core_ref[0] != 0)
    def _():
        mine(high)
        other(low)


def pack_kernel(place_ref, up_ref, down_ref, mix_ref, proj_ref, merge_ref, out_ref, all_ref):
    for level in range(2):
        all_ref[8 * level : 8 * level + 4] = up_ref[level].reshape(4, 16, D)
        all_ref[8 * level + 4 : 8 * level + 8] = down_ref[level].reshape(4, 16, D)
        for part in range(3):
            for group in range(4):
                all_ref[16 + 4 * level + part, :, 256 * group : 256 * group + 256] = mix_ref[
                    level, part, 16 * group : 16 * group + 16
                ]
        all_ref[19 + 4 * level] = proj_ref[level]
    all_ref[24:26] = merge_ref[...].reshape(2, 16, D)
    out_ref[...] = all_ref[pl.ds(place_ref[1] * 13, 13)]


def pack_weights(place, up, down, mix, proj, merge):
    piece = pl.pallas_call(
        pack_kernel,
        grid_spec=pltpu.PrefetchScalarGridSpec(
            num_scalar_prefetch=1,
            grid=(1,),
            in_specs=[
                pl.BlockSpec((2, 64, D), lambda step, place: (0, place[0], 0)),
                pl.BlockSpec((2, 64, D), lambda step, place: (0, place[0], 0)),
                pl.BlockSpec((2, 3, 64, 256), lambda step, place: (0, 0, place[0], 0)),
                pl.BlockSpec((2, 16, D), lambda step, place: (0, place[0], 0)),
                pl.BlockSpec((32, D), lambda step, place: (place[0], 0)),
            ],
            out_specs=whole((13, 16, D)),
            scratch_shapes=[pltpu.VMEM((UNITS, 16, D), BF)],
        ),
        out_shape=shape_of((13, 16, D), BF),
        compiler_params=pltpu.CompilerParams(vmem_limit_bytes=VMEM),
        cost_estimate=pl.CostEstimate(flops=0, bytes_accessed=1 << 20, transcendentals=0),
    )(place, up, down, mix, proj, merge)
    return piece.reshape(208, D)


def merge_stats(x_ref, pack_ref, full):
    total = jnp.zeros((T, 1), F32)
    for part in range(TP):
        rows = dot_tn(pack_ref[...], x_ref[part])
        full[part] = rows
        total = total + jnp.sum(rows, axis=-1, keepdims=True)
    mean = total / MERGED
    square = jnp.zeros((T, 1), F32)
    for part in range(TP):
        center = full[part] - mean
        square = square + jnp.sum(center * center, axis=-1, keepdims=True)
    return mean, lax.rsqrt(square / MERGED + EPS)


def merge_kernel(
    core_ref, x_ref, pack_ref, gain_ref, bias_ref, w_ref, out_ref, mine_ref, other_ref, full, stats
):
    step = pl.program_id(0)

    @pl.when(step == 0)
    def _():
        mean, spread = merge_stats(x_ref, pack_ref, full)
        stats[0] = mean
        stats[1] = spread

    normed = (full[step] - stats[0]) * stats[1]
    value = (normed * gain_ref[0] + bias_ref[0]).astype(BF)

    def set_mine(part):
        mine_ref[...] = part

    def set_other(part):
        other_ref[...] = part

    put_halves(core_ref, set_mine, set_other, value[:, :256], value[:, 256:])
    term = dot(value, w_ref[...].reshape(512, D))

    @pl.when(step == 0)
    def _():
        out_ref[...] = term

    @pl.when(step != 0)
    def _():
        out_ref[...] += term


def merge_forward(core, parts, gain, bias, weights):
    return run(
        merge_kernel,
        TP,
        core,
        (parts, const(PACK), gain.reshape(TP, 1, 512), bias.reshape(TP, 1, 512), weights),
        [
            whole((TP, 2 * TOK, 512)),
            whole((2 * TOK, T)),
            pl.BlockSpec((1, 1, 512), lambda step, core: (step, 0, 0)),
            pl.BlockSpec((1, 1, 512), lambda step, core: (step, 0, 0)),
            pl.BlockSpec((YX, 2, 16, D), lambda step, core: (step, 12, 0, 0)),
        ],
        [shape_of((T, D), F32), shape_of((T, D), BF), shape_of((T, D), BF)],
        [
            whole((T, D)),
            pl.BlockSpec((T, 256), lambda step, core: (0, step)),
            pl.BlockSpec((T, 256), lambda step, core: (0, step)),
        ],
        [pltpu.VMEM((TP, T, 512), F32), pltpu.VMEM((2, T, 1), F32)],
        2 * T * MERGED * D,
        8 << 20,
    )


def merge_back_kernel(
    core_ref, x_ref, pack_ref, gain_ref, w_ref, dx_ref,
    start_ref, dm_ref, gains_ref, biases_ref,
    full, stats, upstream,
):
    step = pl.program_id(0)

    @pl.when(step == 0)
    def _():
        mean, spread = merge_stats(x_ref, pack_ref, full)
        stats[0] = mean
        stats[1] = spread
        stats[2] = jnp.zeros((T, 1), F32)
        stats[3] = jnp.zeros((T, 1), F32)
        start_ref[...] = dx_ref[...].astype(BF)

    grad = dot_nt(start_ref[...], w_ref[...].reshape(512, D))
    normed = (full[step] - stats[0]) * stats[1]
    full[step] = normed
    gains_ref[0] = col_sum(grad * normed)
    biases_ref[0] = col_sum(grad)
    scaled = grad * gain_ref[0]
    upstream[step] = scaled
    stats[2] += jnp.sum(scaled, axis=-1, keepdims=True)
    stats[3] += jnp.sum(scaled * normed, axis=-1, keepdims=True)

    @pl.when(step == TP - 1)
    def _():
        for part in range(TP):
            value = stats[1] * (
                upstream[part] - stats[2] / MERGED - full[part] * (stats[3] / MERGED)
            )
            dm_ref[part] = dot(pack_ref[...], value.astype(BF)).astype(BF)


def merge_backward(core, parts, gain, weights, grad):
    return run(
        merge_back_kernel,
        TP,
        core,
        (parts, const(PACK), gain.reshape(TP, 1, 512), weights, grad),
        [
            whole((TP, 2 * TOK, 512)),
            whole((2 * TOK, T)),
            pl.BlockSpec((1, 1, 512), lambda step, core: (step, 0, 0)),
            pl.BlockSpec((YX, 2, 16, D), lambda step, core: (step, 12, 0, 0)),
            whole((T, D)),
        ],
        [
            shape_of((T, D), BF),
            shape_of((TP, 2 * TOK, 512), BF),
            shape_of((TP, 1, 512), F32),
            shape_of((TP, 1, 512), F32),
        ],
        [
            whole((T, D)),
            whole((TP, 2 * TOK, 512)),
            pl.BlockSpec((1, 1, 512), lambda step, core: (step, 0, 0)),
            pl.BlockSpec((1, 1, 512), lambda step, core: (step, 0, 0)),
        ],
        [pltpu.VMEM((TP, T, 512), F32), pltpu.VMEM((4, T, 1), F32), pltpu.VMEM((TP, T, 512), F32)],
        2 * T * MERGED * D,
        8 << 20,
    )


def head_masks(rows):
    lane = lax.broadcasted_iota(jnp.int32, (rows, 128), 1)
    return [(lane >= 32 * place) & (lane < 32 * place + 32) for place in range(4)]


def spread_heads(value, masks):
    zero = jnp.zeros_like(value)
    return jnp.concatenate([jnp.where(mask, value, zero) for mask in masks], axis=0)


def fold_heads(value, masks):
    total = jnp.zeros((ROWS, 128), F32)
    for place, mask in enumerate(masks):
        total = jnp.where(mask, value[place * ROWS : (place + 1) * ROWS], total)
    return total


def unfold(ref):
    value = ref[...].reshape(YX, 16, D)
    parts = [value[:, :, 256 * group : 256 * group + 256] for group in range(4)]
    return jnp.stack(parts, axis=1).reshape(D, 256)


def attn_kernel(level, *refs):
    (core_ref, x_ref), refs = refs[:2], refs[2:]
    if level:
        (halo_ref, own_ref, recv_ref), refs = refs[:3], refs[3:]
    (
        gain_ref, bias_ref, wq_ref, wk_ref, wv_ref, wp_ref, qb_ref, vb_ref, table_ref, mask_ref,
        shift_ref,
    ), refs = refs[:11], refs[11:]
    (
        mid_ref, a_ref, q_ref, k_ref, v_ref, probs_ref, mine_ref, other_ref,
    ), refs = refs[:8], refs[8:]
    step = pl.program_id(0)

    @pl.when(step == 0)
    def _():
        value = x_ref[...]
        if level:
            value = select_rows(own_ref[...], value) + dot(recv_ref[...], halo_ref[...])
            refs[0][...] = value
        center, spread = norm_stats(value)
        a_ref[...] = (center * spread * gain_ref[...] + bias_ref[...]).astype(BF)
        mid_ref[...] = value + shift_ref[...]

    a = a_ref[...]
    q = (dot(a, unfold(wq_ref)) + qb_ref[...]).astype(BF)
    k = dot(a, unfold(wk_ref)).astype(BF)
    v = (dot(a, unfold(wv_ref)) + vb_ref[...]).astype(BF)
    q_ref[...] = q
    k_ref[...] = k
    v_ref[...] = v
    masks = head_masks(ROWS)
    halves = []
    for half in range(2):
        lanes = slice(half * 128, half * 128 + 128)
        table = table_ref[4 * half : 4 * half + 4]
        parts = []
        for w in range(2):
            rows = slice(w * ROWS, (w + 1) * ROWS)
            raw = dot_nt(spread_heads(q[rows, lanes], masks), k[rows, lanes]) * SCALE
            scores = raw.reshape(4, ROWS, ROWS) + table + mask_ref[w][None]
            top = jnp.max(scores, axis=-1, keepdims=True)
            terms = jnp.exp(scores - top)
            probs = (terms / jnp.sum(terms, axis=-1, keepdims=True)).astype(BF)
            probs_ref[0, w, 4 * half : 4 * half + 4] = probs
            mixed = dot(probs.reshape(4 * ROWS, ROWS), v[rows, lanes])
            parts.append(fold_heads(mixed, masks))
        halves.append(jnp.concatenate(parts, axis=0).astype(BF))

    def set_mine(part):
        mine_ref[...] = part

    def set_other(part):
        other_ref[...] = part

    put_halves(core_ref, set_mine, set_other, *halves)
    heads = jnp.concatenate(halves, axis=1)
    mid_ref[...] += dot(heads, wp_ref[...].reshape(256, D))


def unit_spec(unit):
    return pl.BlockSpec((YX, 1, 16, D), lambda step, core: (step, unit, 0, 0))


def attn_forward(core, level, state, halo, weights, small, table, mask):
    gain, bias, qbias, vbias, shift = small
    unit = 16 + 4 * level
    args = [state]
    specs = [whole((T, D))]
    if level:
        args += [halo, const(OWN), const(RECV)]
        specs += [whole((SEND, D)), whole((T, T)), whole((T, SEND))]
    args += [gain, bias, weights, weights, weights, weights, qbias, vbias, table, mask, shift]
    cols = pl.BlockSpec((1, 256), lambda step, core: (0, step))
    specs += [whole((1, D)), whole((1, D))] + [unit_spec(unit + place) for place in range(4)]
    specs += [
        cols,
        cols,
        pl.BlockSpec((8, ROWS, ROWS), lambda step, core: (step, 0, 0)),
        whole((2, ROWS, ROWS)),
        whole((1, D)),
    ]
    block = pl.BlockSpec((T, 256), lambda step, core: (0, step))
    half = pl.BlockSpec((T, 128), lambda step, core: (0, step))
    outs = [
        shape_of((T, D), F32),
        shape_of((T, D), BF),
        shape_of((T, D), BF),
        shape_of((T, D), BF),
        shape_of((T, D), BF),
        shape_of((TP, 2, 8, ROWS, ROWS), BF),
        shape_of((T, D // 2), BF),
        shape_of((T, D // 2), BF),
    ]
    out_specs = [
        whole((T, D)),
        whole((T, D)),
        block,
        block,
        block,
        pl.BlockSpec((1, 2, 8, ROWS, ROWS), lambda step, core: (step, 0, 0, 0, 0)),
        half,
        half,
    ]
    if level:
        outs.append(shape_of((T, D), F32))
        out_specs.append(whole((T, D)))
    return run(
        partial(attn_kernel, level), TP, core, args, specs, outs, out_specs, [], 8 * T * D * D, 24 << 20
    )


def quad_spec(unit, ahead=False):
    if ahead:
        return pl.BlockSpec(
            (YX, 4, 16, D), lambda step, core: (lax.rem(core[1] + step, TP), unit, 0, 0)
        )
    return pl.BlockSpec((YX, 4, 16, D), lambda step, core: (step, unit, 0, 0))


def wide_spec(rows, ahead=False):
    if ahead:
        return pl.BlockSpec((rows, D), lambda step, core: (0, lax.rem(core[1] + step, TP)))
    return pl.BlockSpec((rows, D), lambda step, core: (0, step))


def mlp_kernel(level, *refs):
    (
        core_ref, mid_ref, gain_ref, bias_ref, w1_ref, w2_ref, b1_ref, b2_ref, place_ref, keep_ref,
        c2_ref, slope_ref, extra_ref,
    ), refs = refs[:13], refs[13:]
    act_refs, total = refs[:-1], refs[-1]
    step = pl.program_id(0)

    @pl.when(step == 0)
    def _():
        value = mid_ref[...]
        center, spread = norm_stats(value)
        c2_ref[...] = (center * spread * gain_ref[...] + bias_ref[...]).astype(BF)
        total[...] = value + b2_ref[...]

    pre = dot(c2_ref[...], w1_ref[...].reshape(D, D)) + b1_ref[...]
    phi = 0.5 + 0.5 * lax.erf(pre * (0.5**0.5))
    act = (pre * phi).astype(BF)
    slope_ref[...] = (phi + pre * ((2.0 * np.pi) ** -0.5 * jnp.exp(-0.5 * pre * pre))).astype(BF)

    if level:
        for ahead in range(TP):

            @pl.when(step == ahead)
            def _(ahead=ahead):
                act_refs[ahead][...] = act

    else:

        def set_mine(part):
            act_refs[0][...] = part

        def set_other(part):
            act_refs[1][...] = part

        put_halves(core_ref, set_mine, set_other, act[:, :512], act[:, 512:])

    total[...] += dot(act, w2_ref[...].reshape(D, D))

    @pl.when(step == TP - 1)
    def _():
        value = total[...]
        if level:
            extra_ref[...] = dot(place_ref[...], (value * keep_ref[...]).astype(BF)).astype(BF)
        else:
            extra_ref[...] = dot(place_ref[...], value.astype(BF)).astype(BF)
            act_refs[2][...] = value


def mlp_forward(core, level, mid, weights, small, keep):
    gain, bias, b1, b2 = small
    place = const(OUT if level else SENT)
    outs = [
        shape_of((T, D), BF),
        shape_of((T, FF), BF),
        shape_of((place.shape[0], D), BF),
    ]
    out_specs = [whole((T, D)), wide_spec(T, level), whole((place.shape[0], D))]
    if level:
        outs += [shape_of((T, D), BF)] * TP
        out_specs += [whole((T, D))] * TP
    else:
        half = pl.BlockSpec((T, 512), lambda step, core: (0, step))
        outs += [shape_of((T, FF // 2), BF)] * 2 + [shape_of((T, D), F32)]
        out_specs += [half, half, whole((T, D))]
    return run(
        partial(mlp_kernel, level),
        TP,
        core,
        (mid, gain, bias, weights, weights, b1, b2, place, keep),
        [
            whole((T, D)),
            whole((1, D)),
            whole((1, D)),
            quad_spec(2 * level, level),
            quad_spec(2 * level + 1, level),
            wide_spec(1, level),
            whole((1, D)),
            whole(place.shape),
            whole((T, 1)),
        ],
        outs,
        out_specs,
        [pltpu.VMEM((T, D), F32)],
        4 * T * D * FF,
        24 << 20,
    )


def mlp_back_kernel(level, *refs):
    (core_ref, dx_ref), refs = refs[:2], refs[2:]
    if level:
        (keep_ref,), refs = refs[:1], refs[1:]
    else:
        (halo_ref, own_ref, sent_ref), refs = refs[:3], refs[3:]
    (mid_ref, gain_ref, w1_ref, w2_ref, slope_ref), refs = refs[:5], refs[5:]
    (
        dmid_ref, dmlp_ref, dattn_ref, mine_ref, other_ref, db1_ref, rows_ref, total, grad,
    ) = refs
    step = pl.program_id(0)

    @pl.when(step == 0)
    def _():
        if level:
            value = dx_ref[...].astype(F32) * keep_ref[...]
        else:
            value = select_rows_t(own_ref[...], dx_ref[...]) + dot_tn(sent_ref[...], halo_ref[...])
        grad[...] = value
        dmlp_ref[...] = value.astype(BF)
        total[...] = jnp.zeros((T, D), F32)

    dact = dot_nt(dmlp_ref[...], w2_ref[...].reshape(D, D))
    rounded = (dact * slope_ref[...].astype(F32)).astype(BF)
    db1_ref[...] = col_sum(rounded.astype(F32))

    def set_mine(part):
        mine_ref[...] = part

    def set_other(part):
        other_ref[...] = part

    put_halves(core_ref, set_mine, set_other, rounded[:, :512], rounded[:, 512:])
    total[...] += dot_nt(rounded, w1_ref[...].reshape(D, D))

    @pl.when(step == TP - 1)
    def _():
        center, spread = norm_stats(mid_ref[...])
        normed = center * spread
        upstream = total[...]
        dmid = grad[...] + norm_back(upstream, normed, spread, gain_ref[...])
        dmid_ref[...] = dmid
        dattn = dmid.astype(BF)
        dattn_ref[...] = dattn
        rows_ref[0:1] = col_sum(upstream * normed)
        rows_ref[1:2] = col_sum(upstream)
        rows_ref[2:3] = col_sum(dmlp_ref[...].astype(F32))
        rows_ref[3:4] = col_sum(dattn.astype(F32))


def select_rows_t(matrix, value):
    high = value.astype(BF)
    rest = value - high.astype(F32)
    mid = rest.astype(BF)
    low = (rest - mid.astype(F32)).astype(BF)
    return dot_tn(matrix, high) + dot_tn(matrix, mid) + dot_tn(matrix, low)


def mlp_backward(core, level, grad, halo, keep, mid, gain, weights, slope):
    half = pl.BlockSpec((T, 512), lambda step, core: (0, step))
    if level:
        args, specs = [grad, keep], [whole((T, D)), whole((T, 1))]
    else:
        args = [grad, halo, const(OWN), const(SENT)]
        specs = [whole((T, D)), whole((SEND, D)), whole((T, T)), whole((SEND, T))]
    args += [mid, gain, weights, weights, slope]
    specs += [
        whole((T, D)),
        whole((1, D)),
        quad_spec(2 * level),
        quad_spec(2 * level + 1),
        pl.BlockSpec((T, D), lambda step, core: (0, step)),
    ]
    return run(
        partial(mlp_back_kernel, level),
        TP,
        core,
        args,
        specs,
        [
            shape_of((T, D), F32),
            shape_of((T, D), BF),
            shape_of((T, D), BF),
            shape_of((T, FF // 2), BF),
            shape_of((T, FF // 2), BF),
            shape_of((1, FF), F32),
            shape_of((4, D), F32),
        ],
        [
            whole((T, D)),
            whole((T, D)),
            whole((T, D)),
            half,
            half,
            pl.BlockSpec((1, D), lambda step, core: (0, step)),
            whole((4, D)),
        ],
        [pltpu.VMEM((T, D), F32), pltpu.VMEM((T, D), F32)],
        4 * T * D * FF,
        24 << 20,
    )


def attn_back_kernel(level, *refs):
    (
        core_ref, dmid_ref, dattn_ref, x_ref, gain_ref, wq_ref, wk_ref, wv_ref, wp_ref,
        q_ref, k_ref, v_ref, probs_ref,
    ), refs = refs[:13], refs[13:]
    if level:
        (place_ref,), refs = refs[:1], refs[1:]
    (dx_ref, mine_ref, other_ref, pair_ref, sums_ref, rows_ref), refs = refs[:6], refs[6:]
    if level:
        (sent_ref,), refs = refs[:1], refs[1:]
    (total,) = refs
    step = pl.program_id(0)

    @pl.when(step == 0)
    def _():
        total[...] = jnp.zeros((T, D), F32)

    dheads = dot_nt(dattn_ref[...], wp_ref[...].reshape(256, D)).astype(BF)
    masks = head_masks(ROWS)
    dqs, dks, dvs = [], [], []
    for half in range(2):
        lanes = slice(half * 128, half * 128 + 128)
        dq_parts, dk_parts, dv_parts = [], [], []
        pairs = None
        for w in range(2):
            rows = slice(w * ROWS, (w + 1) * ROWS)
            rounded = probs_ref[0, w, 4 * half : 4 * half + 4].reshape(4 * ROWS, ROWS)
            probs = rounded.astype(F32)
            spread_out = spread_heads(dheads[rows, lanes], masks)
            dprobs = dot_nt(spread_out, v_ref[rows, lanes])
            dv_parts.append(dot_tn(rounded, spread_out))
            inner = jnp.sum(probs * dprobs, axis=-1, keepdims=True)
            dscores = (probs * (dprobs - inner)).astype(BF)
            wide = dscores.astype(F32)
            pairs = wide if pairs is None else pairs + wide
            dq_parts.append(fold_heads(dot(dscores, k_ref[rows, lanes]), masks))
            dk_parts.append(dot_tn(dscores, spread_heads(q_ref[rows, lanes], masks)))
        pair_ref[4 * half : 4 * half + 4] = pairs.reshape(4, ROWS, ROWS)
        dqs.append((jnp.concatenate(dq_parts, axis=0) * SCALE).astype(BF))
        dks.append((jnp.concatenate(dk_parts, axis=0) * SCALE).astype(BF))
        dvs.append(jnp.concatenate(dv_parts, axis=0).astype(BF))

    def set_mine(part):
        mine_ref[...] = part

    def set_other(part):
        other_ref[...] = part

    put_halves(
        core_ref,
        set_mine,
        set_other,
        jnp.concatenate([dqs[0], dks[0], dvs[0]], axis=1),
        jnp.concatenate([dqs[1], dks[1], dvs[1]], axis=1),
    )
    dq = jnp.concatenate(dqs, axis=1)
    dk = jnp.concatenate(dks, axis=1)
    dv = jnp.concatenate(dvs, axis=1)
    sums_ref[0:1] = col_sum(dq.astype(F32))
    sums_ref[1:2] = col_sum(dv.astype(F32))
    total[...] += (
        dot_nt(dq, unfold(wq_ref))
        + dot_nt(dk, unfold(wk_ref))
        + dot_nt(dv, unfold(wv_ref))
    )

    @pl.when(step == TP - 1)
    def _():
        center, spread = norm_stats(x_ref[...])
        normed = center * spread
        upstream = total[...]
        value = dmid_ref[...] + norm_back(upstream, normed, spread, gain_ref[...])
        dx_ref[...] = value
        rows_ref[0:1] = col_sum(upstream * normed)
        rows_ref[1:2] = col_sum(upstream)
        if level:
            sent_ref[...] = dot_tn(place_ref[...], value.astype(BF)).astype(BF)


def attn_backward(core, level, dmid, dattn, state, gain, weights, q, k, v, probs):
    unit = 16 + 4 * level
    block = pl.BlockSpec((T, 256), lambda step, core: (0, step))
    part = pl.BlockSpec((T, 384), lambda step, core: (0, step))
    args = [dmid, dattn, state, gain, weights, weights, weights, weights, q, k, v, probs]
    specs = [whole((T, D)), whole((T, D)), whole((T, D)), whole((1, D))]
    specs += [unit_spec(unit + place) for place in range(4)]
    specs += [
        block,
        block,
        block,
        pl.BlockSpec((1, 2, 8, ROWS, ROWS), lambda step, core: (step, 0, 0, 0, 0)),
    ]
    outs = [
        shape_of((T, D), F32),
        shape_of((T, 1536), BF),
        shape_of((T, 1536), BF),
        shape_of((32, ROWS, ROWS), F32),
        shape_of((2, D), F32),
        shape_of((2, D), F32),
    ]
    out_specs = [
        whole((T, D)),
        part,
        part,
        pl.BlockSpec((8, ROWS, ROWS), lambda step, core: (step, 0, 0)),
        pl.BlockSpec((2, 256), lambda step, core: (0, step)),
        whole((2, D)),
    ]
    if level:
        args.append(const(RECV))
        specs.append(whole((T, SEND)))
        outs.append(shape_of((SEND, D), BF))
        out_specs.append(whole((SEND, D)))
    return run(
        partial(attn_back_kernel, level),
        TP,
        core,
        args,
        specs,
        outs,
        out_specs,
        [pltpu.VMEM((T, D), F32)],
        8 * T * D * D,
        24 << 20,
    )


def weight_kernel(plan, *refs):
    refs, out_ref = refs[1:-1], refs[-1]
    place = 0
    column = 0
    for kind, size, count in plan:
        parts = [ref[...] for ref in refs[place : place + count]]
        if kind == "matrix":
            value = dot_tn(
                jnp.concatenate(parts[:2], axis=0), jnp.concatenate(parts[2:], axis=0)
            )
        else:
            value = sum(part.astype(F32) for part in parts)
        out_ref[:, 0, :, column : column + size] = value.astype(BF).reshape(YX, 64, size)
        column += size
        place += count


def weight_grads(core, items, sums):
    plan, args, specs = [], [], []
    for left, right in items:
        size = right[0].shape[1] // TP
        plan.append(("matrix", size, 4))
        args += [left[0], left[1], right[0], right[1]]
        block = pl.BlockSpec((T, size), lambda step, core: (0, step))
        specs += [whole((T, D)), whole((T, D)), block, block]
    for pieces in sums:
        plan.append(("sum", 128, len(pieces)))
        args += pieces
        specs += [pl.BlockSpec((D, 128), lambda step, core: (0, step))] * len(pieces)
    width = sum(size for unused, size, count in plan)
    return run(
        partial(weight_kernel, plan),
        TP,
        core,
        args,
        specs,
        shape_of((YX, TP, 64, width), BF),
        pl.BlockSpec((YX, 1, 64, width), lambda step, core: (0, step, 0, 0)),
        [],
        4 * T * D * width * TP,
        (2 * D * width * TP) + (8 << 20),
    )


def column_kernel(core_ref, left_ref, left_other_ref, *refs):
    rights, (out_ref, total) = refs[:-2], refs[-2:]
    step = pl.program_id(0)
    left = jnp.concatenate([left_ref[0], left_other_ref[0]], axis=0)
    for back in range(TP):

        @pl.when(step == back)
        def _(back=back):
            right = jnp.concatenate([rights[back][...], rights[TP + back][...]], axis=0)
            value = dot_tn(left, right)
            total[...] = value if back == 0 else total[...] + value

    @pl.when(step == TP - 1)
    def _():
        out_ref[...] = total[...].astype(BF)


def column_grads(core, left, left_other, right, right_other):
    tile = pl.BlockSpec((1, T, D), lambda step, core: (lax.rem(core[1] + TP - step, TP), 0, 0))
    half = pl.BlockSpec((T, 512), lambda step, core: (0, core[0]))
    return run(
        column_kernel,
        TP,
        core,
        [left, left_other] + right + right_other,
        [tile, tile] + [half] * (2 * TP),
        shape_of((D, 512), BF),
        whole((D, 512)),
        [pltpu.VMEM((D, 512), F32)],
        4 * T * D * 2048,
        8 << 20,
    )


def send_ahead(pieces):
    return [pieces[0]] + [
        lax.ppermute(pieces[step], "tp", [(i, (i + step) % TP) for i in range(TP)])
        for step in range(1, TP)
    ]


def sum_quarters(value, column):
    pieces = [
        lax.dynamic_index_in_dim(value, (column + step) % TP, 0, keepdims=False)
        for step in range(TP)
    ]
    got = [piece.astype(F32) for piece in send_ahead(pieces)]
    return (got[0] + got[1]) + (got[2] + got[3])


def table_index():
    place = np.zeros((RELS, WIN * 190), np.float32)
    for row in range(WIN):
        for step in range(19):
            for col in range(WIN):
                place[(18 - step) * 19 + row - col + 9, row * 190 + step * WIN + col] = 1
    return place


PAIRS = table_index()


def spread_tables(tables):
    compact = jnp.dot(tables.reshape(64, RELS), jnp.asarray(PAIRS), precision=HIGH)
    compact = compact.reshape(2, 32, WIN, 190)
    rows = [compact[..., (9 - row) * WIN : (9 - row) * WIN + TOK] for row in range(WIN)]
    full = jnp.stack(rows, axis=2).reshape(2, 32, TOK, TOK)
    return jnp.pad(full, ((0, 0), (0, 0), (0, ROWS - TOK), (0, ROWS - TOK)))


def fold_tables(pairs):
    total = jnp.zeros((32, WIN, 190), F32)
    for row in range(WIN):
        low = (9 - row) * WIN
        total = total + jnp.pad(
            pairs[:, row * WIN : (row + 1) * WIN, :TOK], ((0, 0), (0, 0), (low, 90 - low))
        )
    return jnp.dot(total.reshape(32, -1), jnp.asarray(PAIRS.T), precision=HIGH)


def window_masks(level, valid, column):
    place = np.arange(ROWS)
    row = np.minimum(place // WIN, WIN - 1)
    col = jnp.asarray(place % WIN, jnp.int32)
    real = jnp.asarray(place < TOK)
    offset = SHIFT if level else 0
    rolled = column * WIN + col
    usable = (rolled + offset) % GW < valid
    masks = []
    for w in range(2):
        rolled_row = w * WIN + row
        row_region = (rolled_row >= GH - WIN).astype(np.int32) + (rolled_row >= GH - SHIFT)
        col_region = (rolled >= GW - WIN).astype(jnp.int32) + (rolled >= GW - SHIFT)
        region = jnp.asarray(row_region * 3, jnp.int32) + col_region
        allowed = usable[None, :]
        if level:
            allowed = allowed & (region[:, None] == region[None, :])
        mask = jnp.where(allowed, F32(0.0), F32(-100.0))
        mask = jnp.where(real[None, :], mask, F32(-1e30))
        masks.append(jnp.broadcast_to(mask, (ROWS, ROWS)))
    return jnp.stack(masks)


def gather_tp(value, place):
    parts = [value]
    for step in range(1, TP):
        parts.append(lax.ppermute(value, "tp", [(i, (i + step) % TP) for i in range(TP)]))
    stacked = jnp.stack(parts)
    order = (place - jnp.arange(TP)) % TP
    return [lax.dynamic_index_in_dim(stacked, order[i], 0, keepdims=False) for i in range(TP)]


def after(value, others):
    return lax.optimization_barrier((value, others))


def swap_core(value):
    return lax.ppermute(value, "core", [(0, 1), (1, 0)])


def sum_all(value):
    for axis, gap in (("core", 1), ("x", 1), ("x", 2), ("y", 1), ("y", 2), ("tp", 1), ("tp", 2)):
        size = 2 if axis == "core" else 4
        sent = value.astype(BF)
        got = lax.ppermute(sent, axis, [(i, i ^ gap) for i in range(size)])
        value = sent.astype(F32) + got.astype(F32)
    return value


def body(
    x3,
    res_group,
    merge_gain,
    merge_bias,
    merge_w,
    ln1_gain,
    ln1_bias,
    qkv_w,
    qv_bias,
    rel_table,
    proj_w,
    proj_bias,
    ln2_gain,
    ln2_bias,
    fc1_w,
    fc1_bias,
    fc2_w,
    fc2_bias,
    out_grad,
):
    core_at = lax.axis_index("core")
    chip_at = lax.axis_index("y") * 4 + lax.axis_index("x")
    column = lax.axis_index("tp")
    core = jnp.stack([core_at, column]).astype(jnp.int32)

    piece = pack_weights(
        jnp.stack([chip_at, core_at]).astype(jnp.int32),
        fc1_w,
        fc2_w,
        jnp.swapaxes(qkv_w, 1, 2),
        proj_w,
        merge_w.reshape(512, D),
    )
    weights = lax.all_gather(piece, GATHER_AXES, axis=0, tiled=True).reshape(64, UNITS, 16, D)

    pages = lax.all_to_all(x3, PAGE_AXES, split_axis=1, concat_axis=0, tiled=True)
    tiles = pages.reshape(GH, TP, WIN, 512).transpose(1, 0, 2, 3).reshape(TP * 2 * TOK, 512)
    parts = lax.all_to_all(tiles, "tp", split_axis=0, concat_axis=0, tiled=True)
    parts = parts.reshape(TP, 2 * TOK, 512)

    packed = jnp.concatenate(
        [
            merge_gain.reshape(-1),
            merge_bias.reshape(-1),
            qv_bias.reshape(-1),
            fc1_bias.reshape(-1),
            rel_table.reshape(-1),
            jnp.zeros((10240 - 9872,), F32),
        ]
    ).reshape(80, 128)
    quarters = [part.reshape(-1) for part in gather_tp(packed, column)]

    def joined(low, shape, axis):
        size = int(np.prod(shape))
        return jnp.concatenate([part[low : low + size].reshape(shape) for part in quarters], axis)

    merge_gain_all = joined(0, (1, 512), 0)
    merge_bias_all = joined(512, (1, 512), 0)
    qv_bias_all = joined(1024, (2, 2, 256), 2)
    fc1_bias_all = joined(2048, (2, 1024), 1)
    tables = spread_tables(joined(4096, (2, 8, RELS), 1))

    valid = (res_group[0] + 1) * WIN
    masks = [window_masks(level, valid, column) for level in range(2)]
    spot = np.arange(T) % ROWS
    keep = ((column * WIN + SHIFT + jnp.asarray(spot % WIN, jnp.int32)) % GW < valid) & jnp.asarray(
        spot < TOK
    )
    keep = keep.astype(F32)[:, None]
    page_keep = (jnp.asarray(np.arange(GW), jnp.int32) < valid).astype(BF)[None, :, None]
    tiles = jnp.roll(out_grad[0] * page_keep, (-SHIFT, -SHIFT), (0, 1))
    tiles = tiles.reshape(2, WIN, TP, WIN, D).transpose(2, 0, 1, 3, 4).reshape(TP, 2, TOK, D)
    tiles = jnp.pad(tiles, ((0, 0), (0, 0), (0, ROWS - TOK), (0, 0))).reshape(TP, T, D)
    cotangent = lax.dynamic_index_in_dim(tiles, column, 0, keepdims=False)
    tiles_got = swap_core(tiles)

    weights, (tables, masks, tiles, tiles_got, cotangent, keep, parts) = after(
        weights, (tables, masks, tiles, tiles_got, cotangent, keep, parts)
    )
    state, merged_mine, merged_other = merge_forward(
        core, parts, merge_gain_all, merge_bias_all, weights
    )
    kept = []
    halo = None
    pending = [swap_core(merged_other)]
    for level in range(2):
        small = (
            ln1_gain[level : level + 1],
            ln1_bias[level : level + 1],
            qv_bias_all[level, 0:1],
            qv_bias_all[level, 1:2],
            proj_bias[level : level + 1],
        )
        got = attn_forward(
            core, level, state, halo, weights, small, tables[level], masks[level]
        )
        mid, a, q, k, v, probs, heads_mine, heads_other = got[:8]
        start = got[8] if level else state
        mid, pending = after(mid, pending)
        small = (
            ln2_gain[level : level + 1],
            ln2_bias[level : level + 1],
            fc1_bias_all[level : level + 1],
            fc2_bias[level : level + 1],
        )
        swapped = pending + [swap_core(a), swap_core(heads_other)]
        more = mlp_forward(core, level, mid, weights, small, keep)
        c2, slope, extra = more[:3]
        extra, swapped = after(extra, swapped)
        pending = [swap_core(c2)]
        kept.append([start, mid, a, q, k, v, probs, slope, c2, heads_mine, swapped])
        if not level:
            act_mine, state = more[3], more[5]
            pending.append(swap_core(more[4]))
            halo = lax.ppermute(extra, "tp", [((i + 1) % TP, i) for i in range(TP)])
    acts = send_ahead(more[3:])

    sums = [None, None]
    start, mid, a, q, k, v, probs, slope, c2, heads_mine, swapped = kept[1]
    c2_zero, act_zero, a_got, heads_got = swapped
    dmid, dmlp, dattn, dpre_mine, dpre_other, db1, rows_two = mlp_backward(
        core, 1, cotangent, None, keep, mid, ln2_gain[1:2], weights, slope
    )
    dattn, pending = after(dattn, pending)
    got = attn_backward(core, 1, dmid, dattn, start, ln1_gain[1:2], weights, q, k, v, probs)
    grad, mixed_mine, mixed_other, pairs, dqv, rows_one, sent = got
    sent, (moved, acts) = after(sent, ([dpre_other, dattn], acts))
    halo = lax.ppermute(sent, "tp", [(i, (i + 1) % TP) for i in range(TP)])
    acts_got = [swap_core(value) for value in acts]
    moved = [swap_core(value) for value in moved]
    mixed_got = swap_core(mixed_other)
    sums[1] = (db1, rows_two, dqv, rows_one, fold_tables(pairs))
    down = column_grads(core, tiles, tiles_got, acts, acts_got)
    items = [
        ((c2, pending[0]), (dpre_mine, moved[0])),
        ((a, a_got), (mixed_mine, mixed_got)),
        ((dattn, moved[1]), (heads_mine, heads_got)),
    ]
    late = weight_grads(core, items, [[down]])
    late, halo = lax.optimization_barrier((late, halo))
    late = lax.psum_scatter(late, CHIP_AXES, scatter_dimension=0, tiled=True)
    late = lax.optimization_barrier(late)[0]

    start, mid, a, q, k, v, probs, slope, c2, heads_mine, swapped = kept[0]
    merged_got, a_got, heads_got = swapped
    dmid, dmlp, dattn, dpre_mine, dpre_other, db1, rows_two = mlp_backward(
        core, 0, grad, halo, keep, mid, ln2_gain[0:1], weights, slope
    )
    got = attn_backward(core, 0, dmid, dattn, start, ln1_gain[0:1], weights, q, k, v, probs)
    grad, mixed_mine, mixed_other, pairs, dqv, rows_one = got
    grad, moved = after(grad, [dmlp, dpre_other, dattn])
    moved = [swap_core(value) for value in moved]
    sums[0] = (db1, rows_two, dqv, rows_one, fold_tables(pairs))
    first, dm, dgain, dbias = merge_backward(core, parts, merge_gain_all, weights, grad)
    mixed_got = swap_core(mixed_other)
    first_got = swap_core(first)
    items = [
        ((c2, c2_zero), (dpre_mine, moved[1])),
        ((dmlp, moved[0]), (act_mine, act_zero)),
        ((a, a_got), (mixed_mine, mixed_got)),
        ((dattn, moved[2]), (heads_mine, heads_got)),
        ((first, first_got), (merged_mine, merged_got)),
    ]
    early = weight_grads(core, items, [])
    early, extra = lax.optimization_barrier((early, extra))
    early = lax.psum_scatter(early, CHIP_AXES, scatter_dimension=0, tiled=True)
    early = lax.optimization_barrier(early)[0]

    tiles_out = jnp.stack(gather_tp(extra, column)).reshape(TP, GH, WIN, D)
    output = jnp.roll(tiles_out.transpose(1, 0, 2, 3).reshape(GH, GW, D), SHIFT, 1)
    output = output.astype(F32)[None]
    back = lax.all_to_all(
        dm.reshape(TP * 2 * TOK, 512), "tp", split_axis=0, concat_axis=0, tiled=True
    )
    back = back.reshape(TP, GH, WIN, 512).transpose(1, 0, 2, 3).reshape(800, 1, 4, 128)
    grad_x3 = lax.all_to_all(back, PAGE_AXES, split_axis=0, concat_axis=1, tiled=True).astype(F32)

    def both_cores(value):
        rows = value.reshape(2, 32, -1)
        kept_rows = lax.dynamic_index_in_dim(rows, core_at, 0, keepdims=False).astype(F32)
        sent_rows = lax.dynamic_index_in_dim(rows, 1 - core_at, 0, keepdims=False)
        got_rows = swap_core(sent_rows.astype(BF)).astype(F32)
        return (
            jnp.where(core_at == 0, kept_rows, got_rows),
            jnp.where(core_at == 0, got_rows, kept_rows),
        )

    def wide(halves, low, size):
        return jnp.concatenate([half[:, low : low + size] for half in halves], axis=1)

    complete = late[..., 1024:].transpose(1, 0, 2).reshape(64, 512)
    late = both_cores(
        jnp.concatenate([sum_quarters(late[..., :1024], column), complete.astype(F32)], axis=1)
    )
    early = both_cores(sum_quarters(early, column))
    g_fc1 = jnp.stack([wide(early, 0, 512), wide(late, 0, 512)])
    g_fc2 = jnp.stack([wide(early, 512, 512).T, wide(late, 1024, 512).T])
    pair = ((early, 1024), (late, 512))
    g_qkv = jnp.stack(
        [jnp.stack([wide(half, low + 128 * s, 128) for s in range(3)], axis=1) for half, low in pair]
    )
    g_proj = jnp.stack([wide(half, low + 384, 128).T for half, low in pair])
    g_merge_w = wide(early, 1536, 256).T.reshape(4, 128, 32)

    flat = []
    for level in range(2):
        db1, rows_two, dqv, rows_one, table = sums[level]
        flat += [rows_one, rows_two, dqv, db1, table]
    flat += [dgain, dbias]
    flat = jnp.concatenate([item.reshape(-1) for item in flat])
    count = flat.shape[0]
    flat = jnp.pad(flat, (0, -count % 16384)).reshape(-1, 1024)
    flat = sum_all(flat).reshape(-1)
    page_at = chip_at * 2 + core_at

    def take(low, shape):
        return flat[low : low + int(np.prod(shape))].reshape(shape)

    def page_part(value):
        return lax.dynamic_slice_in_dim(value, page_at * 32, 32, value.ndim - 1)

    def tp_part(value, axis):
        size = value.shape[axis] // TP
        return lax.dynamic_slice_in_dim(value, column * size, size, axis)

    span = 2 * D + 4 * D + 2 * D + FF + 32 * RELS
    rows = [take(level * span, (6, D)) for level in range(2)]
    rows = page_part(jnp.stack(rows))
    dqv = tp_part(jnp.stack([take(level * span + 6 * D, (2, D)) for level in range(2)]), 2)
    db1 = tp_part(jnp.stack([take(level * span + 8 * D, (FF,)) for level in range(2)]), 1)
    table = tp_part(
        jnp.stack([take(level * span + 8 * D + FF, (32, RELS)) for level in range(2)]), 1
    )
    dgain = tp_part(take(2 * span, (TP, 512)), 0).reshape(4, 128)
    dbias = tp_part(take(2 * span + MERGED, (TP, 512)), 0).reshape(4, 128)
    return (
        output,
        grad_x3,
        dgain,
        dbias,
        g_merge_w,
        rows[:, 0],
        rows[:, 1],
        g_qkv,
        dqv,
        table,
        g_proj,
        rows[:, 5],
        rows[:, 2],
        rows[:, 3],
        g_fc1,
        db1,
        g_fc2,
        rows[:, 4],
    )


def solution(mesh):
    grid = Mesh(mesh.devices.reshape(4, 4, 2, TP), ("y", "x", "core", "tp"))
    page = PAGE_AXES
    return jax.shard_map(
        body,
        mesh=grid,
        in_specs=(
            P(page, None, None, "tp"),
            P(page),
            P(None, "tp"),
            P(None, "tp"),
            P(None, "tp", None),
            P(),
            P(),
            P(None, None, None, "tp"),
            P(None, None, "tp"),
            P(None, "tp", None),
            P(None, "tp", None),
            P(),
            P(),
            P(),
            P(None, None, "tp"),
            P(None, "tp"),
            P(None, "tp", None),
            P(),
            P(page, None, None, None),
        ),
        out_specs=(
            P(page, None, None, None),
            P(page, None, None, "tp"),
            P(None, "tp"),
            P(None, "tp"),
            P(None, "tp", page),
            P(None, page),
            P(None, page),
            P(None, page, None, "tp"),
            P(None, None, "tp"),
            P(None, "tp", None),
            P(None, "tp", page),
            P(None, page),
            P(None, page),
            P(None, page),
            P(None, page, "tp"),
            P(None, "tp"),
            P(None, "tp", page),
            P(None, page),
        ),
        check_vma=False,
    )
```

```python
from functools import partial

import jax
import jax.numpy as jnp
import numpy as np
from jax import lax
from jax.experimental import pallas as pl
from jax.experimental.pallas import tpu as pltpu
from jax.sharding import Mesh
from jax.sharding import PartitionSpec as P

D = 1024
FF = 4096
MERGED = 2048
WIN = 10
SHIFT = 5
GH = 20
GW = 40
RELS = 361
TOK = 100
ROWS = 112
T = 2 * ROWS
SEND = 112
EPS = 1e-05
SCALE = 32 ** (-0.5)
YX = 16
TP = 4
UNITS = 26
HIGH = lax.Precision.HIGHEST
BF = jnp.bfloat16
F32 = jnp.float32
PAGE_AXES = ("y", "x", "core")
CHIP_AXES = ("y", "x")
GATHER_AXES = ("tp", "y", "x", "core")
VMEM = 58 << 20


def row_at(row, col):
    return (row // WIN) * ROWS + (row % WIN) * WIN + col


def place_matrices():
    own = np.zeros((T, T), np.float32)
    recv = np.zeros((T, SEND), np.float32)
    send = np.zeros((SEND, T), np.float32)
    pack = np.zeros((2 * TOK, T), np.float32)
    out = np.zeros((2 * TOK, T), np.float32)
    for row in range(GH):
        for col in range(WIN):
            source = (row + SHIFT) % GH
            if col < SHIFT:
                own[row_at(row, col), row_at(source, col + SHIFT)] = 1
                send[row * SHIFT + col, row_at(row, col)] = 1
            else:
                recv[row_at(row, col), source * SHIFT + col - SHIFT] = 1
            pack[row * WIN + col, row_at(row, col)] = 1
            out[source * WIN + col, row_at(row, col)] = 1
    return own, recv, send, pack, out


OWN, RECV, SENT, PACK, OUT = place_matrices()


def const(matrix):
    return jnp.asarray(matrix, BF)


def dot(left, right):
    return lax.dot_general(left, right, (((1,), (0,)), ((), ())), preferred_element_type=F32)


def dot_nt(left, right):
    return lax.dot_general(left, right, (((1,), (1,)), ((), ())), preferred_element_type=F32)


def dot_tn(left, right):
    return lax.dot_general(left, right, (((0,), (0,)), ((), ())), preferred_element_type=F32)


def select_rows(matrix, value):
    high = value.astype(BF)
    rest = value - high.astype(F32)
    mid = rest.astype(BF)
    low = (rest - mid.astype(F32)).astype(BF)
    return dot(matrix, high) + dot(matrix, mid) + dot(matrix, low)


def norm_stats(value):
    mean = jnp.mean(value, axis=-1, keepdims=True)
    center = value - mean
    return center, lax.rsqrt(jnp.mean(center * center, axis=-1, keepdims=True) + EPS)


def norm_back(upstream, normed, spread, gain):
    scaled = upstream * gain
    inner = (
        scaled
        - jnp.mean(scaled, axis=-1, keepdims=True)
        - normed * jnp.mean(scaled * normed, axis=-1, keepdims=True)
    )
    return spread * inner


def col_sum(value):
    return jnp.sum(value, axis=0, keepdims=True)


def whole(shape):
    return pl.BlockSpec(shape, lambda step, core: (0,) * len(shape))


def shape_of(shape, dtype):
    return jax.ShapeDtypeStruct(shape, dtype)


def run(kernel, steps, core, args, in_specs, outs, out_specs, scratch, flops, moved):
    return pl.pallas_call(
        kernel,
        grid_spec=pltpu.PrefetchScalarGridSpec(
            num_scalar_prefetch=1,
            grid=(steps,),
            in_specs=in_specs,
            out_specs=out_specs,
            scratch_shapes=scratch,
        ),
        out_shape=outs,
        compiler_params=pltpu.CompilerParams(
            vmem_limit_bytes=VMEM, dimension_semantics=("arbitrary",)
        ),
        cost_estimate=pl.CostEstimate(flops=0, bytes_accessed=1024, transcendentals=0),
    )(core, *args)


def put_halves(core_ref, mine, other, low, high):
    @pl.when(core_ref[0] == 0)
    def _():
        mine(low)
        other(high)

    @pl.when(core_ref[0] != 0)
    def _():
        mine(high)
        other(low)


def pack_kernel(place_ref, up_ref, down_ref, mix_ref, proj_ref, merge_ref, out_ref, all_ref):
    for level in range(2):
        all_ref[8 * level : 8 * level + 4] = up_ref[level].reshape(4, 16, D)
        all_ref[8 * level + 4 : 8 * level + 8] = down_ref[level].reshape(4, 16, D)
        for part in range(3):
            for group in range(4):
                all_ref[16 + 4 * level + part, :, 256 * group : 256 * group + 256] = mix_ref[
                    level, part, 16 * group : 16 * group + 16
                ]
        all_ref[19 + 4 * level] = proj_ref[level]
    all_ref[24:26] = merge_ref[...].reshape(2, 16, D)
    out_ref[...] = all_ref[pl.ds(place_ref[1] * 13, 13)]


def pack_weights(place, up, down, mix, proj, merge):
    piece = pl.pallas_call(
        pack_kernel,
        grid_spec=pltpu.PrefetchScalarGridSpec(
            num_scalar_prefetch=1,
            grid=(1,),
            in_specs=[
                pl.BlockSpec((2, 64, D), lambda step, place: (0, place[0], 0)),
                pl.BlockSpec((2, 64, D), lambda step, place: (0, place[0], 0)),
                pl.BlockSpec((2, 3, 64, 256), lambda step, place: (0, 0, place[0], 0)),
                pl.BlockSpec((2, 16, D), lambda step, place: (0, place[0], 0)),
                pl.BlockSpec((32, D), lambda step, place: (place[0], 0)),
            ],
            out_specs=whole((13, 16, D)),
            scratch_shapes=[pltpu.VMEM((UNITS, 16, D), BF)],
        ),
        out_shape=shape_of((13, 16, D), BF),
        compiler_params=pltpu.CompilerParams(vmem_limit_bytes=VMEM),
        cost_estimate=pl.CostEstimate(flops=0, bytes_accessed=1 << 20, transcendentals=0),
    )(place, up, down, mix, proj, merge)
    return piece.reshape(208, D)


def merge_stats(x_ref, pack_ref, full):
    total = jnp.zeros((T, 1), F32)
    for part in range(TP):
        rows = dot_tn(pack_ref[...], x_ref[part])
        full[part] = rows
        total = total + jnp.sum(rows, axis=-1, keepdims=True)
    mean = total / MERGED
    square = jnp.zeros((T, 1), F32)
    for part in range(TP):
        center = full[part] - mean
        square = square + jnp.sum(center * center, axis=-1, keepdims=True)
    return mean, lax.rsqrt(square / MERGED + EPS)


def merge_kernel(
    core_ref, x_ref, pack_ref, gain_ref, bias_ref, w_ref, out_ref, mine_ref, other_ref, full, stats
):
    step = pl.program_id(0)

    @pl.when(step == 0)
    def _():
        mean, spread = merge_stats(x_ref, pack_ref, full)
        stats[0] = mean
        stats[1] = spread

    normed = (full[step] - stats[0]) * stats[1]
    value = (normed * gain_ref[0] + bias_ref[0]).astype(BF)

    def set_mine(part):
        mine_ref[...] = part

    def set_other(part):
        other_ref[...] = part

    put_halves(core_ref, set_mine, set_other, value[:, :256], value[:, 256:])
    term = dot(value, w_ref[...].reshape(512, D))

    @pl.when(step == 0)
    def _():
        out_ref[...] = term

    @pl.when(step != 0)
    def _():
        out_ref[...] += term


def merge_forward(core, parts, gain, bias, weights):
    return run(
        merge_kernel,
        TP,
        core,
        (parts, const(PACK), gain.reshape(TP, 1, 512), bias.reshape(TP, 1, 512), weights),
        [
            whole((TP, 2 * TOK, 512)),
            whole((2 * TOK, T)),
            pl.BlockSpec((1, 1, 512), lambda step, core: (step, 0, 0)),
            pl.BlockSpec((1, 1, 512), lambda step, core: (step, 0, 0)),
            pl.BlockSpec((YX, 2, 16, D), lambda step, core: (step, 12, 0, 0)),
        ],
        [shape_of((T, D), F32), shape_of((T, D), BF), shape_of((T, D), BF)],
        [
            whole((T, D)),
            pl.BlockSpec((T, 256), lambda step, core: (0, step)),
            pl.BlockSpec((T, 256), lambda step, core: (0, step)),
        ],
        [pltpu.VMEM((TP, T, 512), F32), pltpu.VMEM((2, T, 1), F32)],
        2 * T * MERGED * D,
        8 << 20,
    )


def merge_back_kernel(
    core_ref, x_ref, pack_ref, gain_ref, w_ref, dx_ref,
    start_ref, dm_ref, gains_ref, biases_ref,
    full, stats, upstream,
):
    step = pl.program_id(0)

    @pl.when(step == 0)
    def _():
        mean, spread = merge_stats(x_ref, pack_ref, full)
        stats[0] = mean
        stats[1] = spread
        stats[2] = jnp.zeros((T, 1), F32)
        stats[3] = jnp.zeros((T, 1), F32)
        start_ref[...] = dx_ref[...].astype(BF)

    grad = dot_nt(start_ref[...], w_ref[...].reshape(512, D))
    normed = (full[step] - stats[0]) * stats[1]
    full[step] = normed
    gains_ref[0] = col_sum(grad * normed)
    biases_ref[0] = col_sum(grad)
    scaled = grad * gain_ref[0]
    upstream[step] = scaled
    stats[2] += jnp.sum(scaled, axis=-1, keepdims=True)
    stats[3] += jnp.sum(scaled * normed, axis=-1, keepdims=True)

    @pl.when(step == TP - 1)
    def _():
        for part in range(TP):
            value = stats[1] * (
                upstream[part] - stats[2] / MERGED - full[part] * (stats[3] / MERGED)
            )
            dm_ref[part] = dot(pack_ref[...], value.astype(BF)).astype(BF)


def merge_backward(core, parts, gain, weights, grad):
    return run(
        merge_back_kernel,
        TP,
        core,
        (parts, const(PACK), gain.reshape(TP, 1, 512), weights, grad),
        [
            whole((TP, 2 * TOK, 512)),
            whole((2 * TOK, T)),
            pl.BlockSpec((1, 1, 512), lambda step, core: (step, 0, 0)),
            pl.BlockSpec((YX, 2, 16, D), lambda step, core: (step, 12, 0, 0)),
            whole((T, D)),
        ],
        [
            shape_of((T, D), BF),
            shape_of((TP, 2 * TOK, 512), BF),
            shape_of((TP, 1, 512), F32),
            shape_of((TP, 1, 512), F32),
        ],
        [
            whole((T, D)),
            whole((TP, 2 * TOK, 512)),
            pl.BlockSpec((1, 1, 512), lambda step, core: (step, 0, 0)),
            pl.BlockSpec((1, 1, 512), lambda step, core: (step, 0, 0)),
        ],
        [pltpu.VMEM((TP, T, 512), F32), pltpu.VMEM((4, T, 1), F32), pltpu.VMEM((TP, T, 512), F32)],
        2 * T * MERGED * D,
        8 << 20,
    )


def head_masks(rows):
    lane = lax.broadcasted_iota(jnp.int32, (rows, 128), 1)
    return [(lane >= 32 * place) & (lane < 32 * place + 32) for place in range(4)]


def spread_heads(value, masks):
    zero = jnp.zeros_like(value)
    return jnp.concatenate([jnp.where(mask, value, zero) for mask in masks], axis=0)


def fold_heads(value, masks):
    total = jnp.zeros((ROWS, 128), F32)
    for place, mask in enumerate(masks):
        total = jnp.where(mask, value[place * ROWS : (place + 1) * ROWS], total)
    return total


def unfold(ref):
    value = ref[...].reshape(YX, 16, D)
    parts = [value[:, :, 256 * group : 256 * group + 256] for group in range(4)]
    return jnp.stack(parts, axis=1).reshape(D, 256)


def attn_kernel(level, *refs):
    (core_ref, x_ref), refs = refs[:2], refs[2:]
    if level:
        (halo_ref, own_ref, recv_ref), refs = refs[:3], refs[3:]
    (
        gain_ref, bias_ref, wq_ref, wk_ref, wv_ref, wp_ref, qb_ref, vb_ref, table_ref, mask_ref,
        shift_ref,
    ), refs = refs[:11], refs[11:]
    (
        mid_ref, a_ref, q_ref, k_ref, v_ref, probs_ref, mine_ref, other_ref,
    ), refs = refs[:8], refs[8:]
    step = pl.program_id(0)

    @pl.when(step == 0)
    def _():
        value = x_ref[...]
        if level:
            value = select_rows(own_ref[...], value) + dot(recv_ref[...], halo_ref[...])
            refs[0][...] = value
        center, spread = norm_stats(value)
        a_ref[...] = (center * spread * gain_ref[...] + bias_ref[...]).astype(BF)
        mid_ref[...] = value + shift_ref[...]

    a = a_ref[...]
    q = (dot(a, unfold(wq_ref)) + qb_ref[...]).astype(BF)
    k = dot(a, unfold(wk_ref)).astype(BF)
    v = (dot(a, unfold(wv_ref)) + vb_ref[...]).astype(BF)
    q_ref[...] = q
    k_ref[...] = k
    v_ref[...] = v
    masks = head_masks(ROWS)
    halves = []
    for half in range(2):
        lanes = slice(half * 128, half * 128 + 128)
        table = table_ref[4 * half : 4 * half + 4]
        parts = []
        for w in range(2):
            rows = slice(w * ROWS, (w + 1) * ROWS)
            raw = dot_nt(spread_heads(q[rows, lanes], masks), k[rows, lanes]) * SCALE
            scores = raw.reshape(4, ROWS, ROWS) + table + mask_ref[w][None]
            top = jnp.max(scores, axis=-1, keepdims=True)
            terms = jnp.exp(scores - top)
            probs = (terms / jnp.sum(terms, axis=-1, keepdims=True)).astype(BF)
            probs_ref[0, w, 4 * half : 4 * half + 4] = probs
            mixed = dot(probs.reshape(4 * ROWS, ROWS), v[rows, lanes])
            parts.append(fold_heads(mixed, masks))
        halves.append(jnp.concatenate(parts, axis=0).astype(BF))

    def set_mine(part):
        mine_ref[...] = part

    def set_other(part):
        other_ref[...] = part

    put_halves(core_ref, set_mine, set_other, *halves)
    heads = jnp.concatenate(halves, axis=1)
    mid_ref[...] += dot(heads, wp_ref[...].reshape(256, D))


def unit_spec(unit):
    return pl.BlockSpec((YX, 1, 16, D), lambda step, core: (step, unit, 0, 0))


def attn_forward(core, level, state, halo, weights, small, table, mask):
    gain, bias, qbias, vbias, shift = small
    unit = 16 + 4 * level
    args = [state]
    specs = [whole((T, D))]
    if level:
        args += [halo, const(OWN), const(RECV)]
        specs += [whole((SEND, D)), whole((T, T)), whole((T, SEND))]
    args += [gain, bias, weights, weights, weights, weights, qbias, vbias, table, mask, shift]
    cols = pl.BlockSpec((1, 256), lambda step, core: (0, step))
    specs += [whole((1, D)), whole((1, D))] + [unit_spec(unit + place) for place in range(4)]
    specs += [
        cols,
        cols,
        pl.BlockSpec((8, ROWS, ROWS), lambda step, core: (step, 0, 0)),
        whole((2, ROWS, ROWS)),
        whole((1, D)),
    ]
    block = pl.BlockSpec((T, 256), lambda step, core: (0, step))
    half = pl.BlockSpec((T, 128), lambda step, core: (0, step))
    outs = [
        shape_of((T, D), F32),
        shape_of((T, D), BF),
        shape_of((T, D), BF),
        shape_of((T, D), BF),
        shape_of((T, D), BF),
        shape_of((TP, 2, 8, ROWS, ROWS), BF),
        shape_of((T, D // 2), BF),
        shape_of((T, D // 2), BF),
    ]
    out_specs = [
        whole((T, D)),
        whole((T, D)),
        block,
        block,
        block,
        pl.BlockSpec((1, 2, 8, ROWS, ROWS), lambda step, core: (step, 0, 0, 0, 0)),
        half,
        half,
    ]
    if level:
        outs.append(shape_of((T, D), F32))
        out_specs.append(whole((T, D)))
    return run(
        partial(attn_kernel, level), TP, core, args, specs, outs, out_specs, [], 8 * T * D * D, 24 << 20
    )


def quad_spec(unit):
    return pl.BlockSpec(
        (YX, 4, 16, D), lambda step, core: (lax.rem(core[1] + step, TP), unit, 0, 0)
    )


def wide_spec(rows):
    return pl.BlockSpec((rows, D), lambda step, core: (0, lax.rem(core[1] + step, TP)))


def mlp_kernel(level, *refs):
    (
        core_ref, mid_ref, gain_ref, bias_ref, w1_ref, w2_ref, b1_ref, b2_ref, place_ref, keep_ref,
        c2_ref, slope_ref, extra_ref,
    ), refs = refs[:13], refs[13:]
    act_refs, total = refs[:-1], refs[-1]
    step = pl.program_id(0)

    @pl.when(step == 0)
    def _():
        value = mid_ref[...]
        center, spread = norm_stats(value)
        c2_ref[...] = (center * spread * gain_ref[...] + bias_ref[...]).astype(BF)
        total[...] = value + b2_ref[...]

    pre = dot(c2_ref[...], w1_ref[...].reshape(D, D)) + b1_ref[...]
    phi = 0.5 + 0.5 * lax.erf(pre * (0.5**0.5))
    act = (pre * phi).astype(BF)
    slope_ref[...] = (phi + pre * ((2.0 * np.pi) ** -0.5 * jnp.exp(-0.5 * pre * pre))).astype(BF)

    for ahead in range(TP):

        @pl.when(step == ahead)
        def _(ahead=ahead):
            act_refs[ahead][...] = act

    total[...] += dot(act, w2_ref[...].reshape(D, D))

    @pl.when(step == TP - 1)
    def _():
        value = total[...]
        if level:
            extra_ref[...] = dot(place_ref[...], (value * keep_ref[...]).astype(BF)).astype(BF)
        else:
            extra_ref[...] = dot(place_ref[...], value.astype(BF)).astype(BF)
            act_refs[TP][...] = value


def mlp_forward(core, level, mid, weights, small, keep):
    gain, bias, b1, b2 = small
    place = const(OUT if level else SENT)
    outs = [
        shape_of((T, D), BF),
        shape_of((T, FF), BF),
        shape_of((place.shape[0], D), BF),
    ]
    out_specs = [whole((T, D)), wide_spec(T), whole((place.shape[0], D))]
    outs += [shape_of((T, D), BF)] * TP
    out_specs += [whole((T, D))] * TP
    if not level:
        outs.append(shape_of((T, D), F32))
        out_specs.append(whole((T, D)))
    return run(
        partial(mlp_kernel, level),
        TP,
        core,
        (mid, gain, bias, weights, weights, b1, b2, place, keep),
        [
            whole((T, D)),
            whole((1, D)),
            whole((1, D)),
            quad_spec(2 * level),
            quad_spec(2 * level + 1),
            wide_spec(1),
            whole((1, D)),
            whole(place.shape),
            whole((T, 1)),
        ],
        outs,
        out_specs,
        [pltpu.VMEM((T, D), F32)],
        4 * T * D * FF,
        24 << 20,
    )


def mlp_back_kernel(level, *refs):
    (core_ref, dx_ref), refs = refs[:2], refs[2:]
    if level:
        (keep_ref,), refs = refs[:1], refs[1:]
    else:
        (halo_ref, own_ref, sent_ref), refs = refs[:3], refs[3:]
    (mid_ref, gain_ref, w1_ref, w2_ref, slope_ref), refs = refs[:5], refs[5:]
    (dmid_ref, dmlp_ref, dattn_ref, db1_ref, rows_ref), refs = refs[:5], refs[5:]
    dpre_refs, (total, grad) = refs[:-2], refs[-2:]
    step = pl.program_id(0)

    @pl.when(step == 0)
    def _():
        if level:
            value = dx_ref[...].astype(F32) * keep_ref[...]
        else:
            value = select_rows_t(own_ref[...], dx_ref[...]) + dot_tn(sent_ref[...], halo_ref[...])
        grad[...] = value
        dmlp_ref[...] = value.astype(BF)
        total[...] = jnp.zeros((T, D), F32)

    dact = dot_nt(dmlp_ref[...], w2_ref[...].reshape(D, D))
    rounded = (dact * slope_ref[...].astype(F32)).astype(BF)
    db1_ref[...] = col_sum(rounded.astype(F32))
    if level:

        def set_mine(part):
            dpre_refs[0][...] = part

        def set_other(part):
            dpre_refs[1][...] = part

        put_halves(core_ref, set_mine, set_other, rounded[:, :512], rounded[:, 512:])
    else:
        for ahead in range(TP):

            @pl.when(step == ahead)
            def _(ahead=ahead):
                dpre_refs[ahead][...] = rounded

    total[...] += dot_nt(rounded, w1_ref[...].reshape(D, D))

    @pl.when(step == TP - 1)
    def _():
        center, spread = norm_stats(mid_ref[...])
        normed = center * spread
        upstream = total[...]
        dmid = grad[...] + norm_back(upstream, normed, spread, gain_ref[...])
        dmid_ref[...] = dmid
        dattn = dmid.astype(BF)
        dattn_ref[...] = dattn
        rows_ref[0:1] = col_sum(upstream * normed)
        rows_ref[1:2] = col_sum(upstream)
        rows_ref[2:3] = col_sum(dmlp_ref[...].astype(F32))
        rows_ref[3:4] = col_sum(dattn.astype(F32))


def select_rows_t(matrix, value):
    high = value.astype(BF)
    rest = value - high.astype(F32)
    mid = rest.astype(BF)
    low = (rest - mid.astype(F32)).astype(BF)
    return dot_tn(matrix, high) + dot_tn(matrix, mid) + dot_tn(matrix, low)


def mlp_backward(core, level, grad, halo, keep, mid, gain, weights, slope):
    if level:
        args, specs = [grad, keep], [whole((T, D)), whole((T, 1))]
        half = pl.BlockSpec((T, 512), lambda step, core: (0, lax.rem(core[1] + step, TP)))
        pre_shapes, pre_specs = [shape_of((T, FF // 2), BF)] * 2, [half] * 2
    else:
        args = [grad, halo, const(OWN), const(SENT)]
        specs = [whole((T, D)), whole((SEND, D)), whole((T, T)), whole((SEND, T))]
        pre_shapes, pre_specs = [shape_of((T, D), BF)] * TP, [whole((T, D))] * TP
    args += [mid, gain, weights, weights, slope]
    specs += [
        whole((T, D)),
        whole((1, D)),
        quad_spec(2 * level),
        quad_spec(2 * level + 1),
        wide_spec(T),
    ]
    return run(
        partial(mlp_back_kernel, level),
        TP,
        core,
        args,
        specs,
        [
            shape_of((T, D), F32),
            shape_of((T, D), BF),
            shape_of((T, D), BF),
            shape_of((1, FF), F32),
            shape_of((4, D), F32),
        ]
        + pre_shapes,
        [
            whole((T, D)),
            whole((T, D)),
            whole((T, D)),
            wide_spec(1),
            whole((4, D)),
        ]
        + pre_specs,
        [pltpu.VMEM((T, D), F32), pltpu.VMEM((T, D), F32)],
        4 * T * D * FF,
        24 << 20,
    )


def attn_back_kernel(level, *refs):
    (
        core_ref, dmid_ref, dattn_ref, x_ref, gain_ref, wq_ref, wk_ref, wv_ref, wp_ref,
        q_ref, k_ref, v_ref, probs_ref,
    ), refs = refs[:13], refs[13:]
    if level:
        (place_ref,), refs = refs[:1], refs[1:]
    (dx_ref, mine_ref, other_ref, pair_ref, sums_ref, rows_ref), refs = refs[:6], refs[6:]
    if level:
        (sent_ref,), refs = refs[:1], refs[1:]
    (total,) = refs
    step = pl.program_id(0)

    @pl.when(step == 0)
    def _():
        total[...] = jnp.zeros((T, D), F32)

    dheads = dot_nt(dattn_ref[...], wp_ref[...].reshape(256, D)).astype(BF)
    masks = head_masks(ROWS)
    dqs, dks, dvs = [], [], []
    for half in range(2):
        lanes = slice(half * 128, half * 128 + 128)
        dq_parts, dk_parts, dv_parts = [], [], []
        pairs = None
        for w in range(2):
            rows = slice(w * ROWS, (w + 1) * ROWS)
            rounded = probs_ref[0, w, 4 * half : 4 * half + 4].reshape(4 * ROWS, ROWS)
            probs = rounded.astype(F32)
            spread_out = spread_heads(dheads[rows, lanes], masks)
            dprobs = dot_nt(spread_out, v_ref[rows, lanes])
            dv_parts.append(dot_tn(rounded, spread_out))
            inner = jnp.sum(probs * dprobs, axis=-1, keepdims=True)
            dscores = (probs * (dprobs - inner)).astype(BF)
            wide = dscores.astype(F32)
            pairs = wide if pairs is None else pairs + wide
            dq_parts.append(fold_heads(dot(dscores, k_ref[rows, lanes]), masks))
            dk_parts.append(dot_tn(dscores, spread_heads(q_ref[rows, lanes], masks)))
        pair_ref[4 * half : 4 * half + 4] = pairs.reshape(4, ROWS, ROWS)
        dqs.append((jnp.concatenate(dq_parts, axis=0) * SCALE).astype(BF))
        dks.append((jnp.concatenate(dk_parts, axis=0) * SCALE).astype(BF))
        dvs.append(jnp.concatenate(dv_parts, axis=0).astype(BF))

    def set_mine(part):
        mine_ref[...] = part

    def set_other(part):
        other_ref[...] = part

    put_halves(
        core_ref,
        set_mine,
        set_other,
        jnp.concatenate([dqs[0], dks[0], dvs[0]], axis=1),
        jnp.concatenate([dqs[1], dks[1], dvs[1]], axis=1),
    )
    dq = jnp.concatenate(dqs, axis=1)
    dk = jnp.concatenate(dks, axis=1)
    dv = jnp.concatenate(dvs, axis=1)
    sums_ref[0:1] = col_sum(dq.astype(F32))
    sums_ref[1:2] = col_sum(dv.astype(F32))
    total[...] += (
        dot_nt(dq, unfold(wq_ref))
        + dot_nt(dk, unfold(wk_ref))
        + dot_nt(dv, unfold(wv_ref))
    )

    @pl.when(step == TP - 1)
    def _():
        center, spread = norm_stats(x_ref[...])
        normed = center * spread
        upstream = total[...]
        value = dmid_ref[...] + norm_back(upstream, normed, spread, gain_ref[...])
        dx_ref[...] = value
        rows_ref[0:1] = col_sum(upstream * normed)
        rows_ref[1:2] = col_sum(upstream)
        if level:
            sent_ref[...] = dot_tn(place_ref[...], value.astype(BF)).astype(BF)


def attn_backward(core, level, dmid, dattn, state, gain, weights, q, k, v, probs):
    unit = 16 + 4 * level
    block = pl.BlockSpec((T, 256), lambda step, core: (0, step))
    part = pl.BlockSpec((T, 384), lambda step, core: (0, step))
    args = [dmid, dattn, state, gain, weights, weights, weights, weights, q, k, v, probs]
    specs = [whole((T, D)), whole((T, D)), whole((T, D)), whole((1, D))]
    specs += [unit_spec(unit + place) for place in range(4)]
    specs += [
        block,
        block,
        block,
        pl.BlockSpec((1, 2, 8, ROWS, ROWS), lambda step, core: (step, 0, 0, 0, 0)),
    ]
    outs = [
        shape_of((T, D), F32),
        shape_of((T, 1536), BF),
        shape_of((T, 1536), BF),
        shape_of((32, ROWS, ROWS), F32),
        shape_of((2, D), F32),
        shape_of((2, D), F32),
    ]
    out_specs = [
        whole((T, D)),
        part,
        part,
        pl.BlockSpec((8, ROWS, ROWS), lambda step, core: (step, 0, 0)),
        pl.BlockSpec((2, 256), lambda step, core: (0, step)),
        whole((2, D)),
    ]
    if level:
        args.append(const(RECV))
        specs.append(whole((T, SEND)))
        outs.append(shape_of((SEND, D), BF))
        out_specs.append(whole((SEND, D)))
    return run(
        partial(attn_back_kernel, level),
        TP,
        core,
        args,
        specs,
        outs,
        out_specs,
        [pltpu.VMEM((T, D), F32)],
        8 * T * D * D,
        24 << 20,
    )


def weight_kernel(plan, *refs):
    refs, out_ref = refs[1:-1], refs[-1]
    place = 0
    column = 0
    for kind, size, count in plan:
        parts = [ref[...] for ref in refs[place : place + count]]
        if kind == "matrix":
            value = dot_tn(
                jnp.concatenate(parts[:2], axis=0), jnp.concatenate(parts[2:], axis=0)
            )
        else:
            value = sum(part.astype(F32) for part in parts)
        out_ref[:, 0, :, column : column + size] = value.astype(BF).reshape(YX, 64, size)
        column += size
        place += count


def weight_grads(core, items, sums):
    plan, args, specs = [], [], []
    for left, right in items:
        size = right[0].shape[1] // TP
        plan.append(("matrix", size, 4))
        args += [left[0], left[1], right[0], right[1]]
        block = pl.BlockSpec((T, size), lambda step, core: (0, step))
        specs += [whole((T, D)), whole((T, D)), block, block]
    for pieces in sums:
        plan.append(("sum", 128, len(pieces)))
        args += pieces
        specs += [pl.BlockSpec((D, 128), lambda step, core: (0, step))] * len(pieces)
    width = sum(size for unused, size, count in plan)
    return run(
        partial(weight_kernel, plan),
        TP,
        core,
        args,
        specs,
        shape_of((YX, TP, 64, width), BF),
        pl.BlockSpec((YX, 1, 64, width), lambda step, core: (0, step, 0, 0)),
        [],
        4 * T * D * width * TP,
        (2 * D * width * TP) + (8 << 20),
    )


def column_kernel(core_ref, *refs):
    lefts, rights, (other_ref, mine_ref) = refs[:TP], refs[TP : 2 * TP], refs[2 * TP :]
    left = jnp.concatenate([ref[...] for ref in lefts], axis=0)
    right = jnp.concatenate([ref[...] for ref in rights], axis=0)
    value = dot_tn(left, right).astype(BF)

    @pl.when(pl.program_id(0) == 0)
    def _():
        other_ref[...] = value

    @pl.when(pl.program_id(0) == 1)
    def _():
        mine_ref[...] = value


def column_grads(core, lefts, rights):
    half = pl.BlockSpec((T, 512), lambda step, core: (0, (core[0] + 1 + step) % 2))
    return run(
        column_kernel,
        2,
        core,
        list(lefts) + list(rights),
        [whole((T, D))] * TP + [half] * TP,
        [shape_of((D, 512), BF)] * 2,
        [whole((D, 512))] * 2,
        [],
        4 * T * D * 2048,
        8 << 20,
    )


def send_ahead(pieces):
    return [pieces[0]] + [
        lax.ppermute(pieces[step], "tp", [(i, (i + step) % TP) for i in range(TP)])
        for step in range(1, TP)
    ]


def send_all(value):
    return send_ahead([value] * TP)


def sum_quarters(value, column):
    pieces = [
        lax.dynamic_index_in_dim(value, (column + step) % TP, 0, keepdims=False)
        for step in range(TP)
    ]
    got = [piece.astype(F32) for piece in send_ahead(pieces)]
    return (got[0] + got[1]) + (got[2] + got[3])


def table_index():
    place = np.zeros((RELS, WIN * 190), np.float32)
    for row in range(WIN):
        for step in range(19):
            for col in range(WIN):
                place[(18 - step) * 19 + row - col + 9, row * 190 + step * WIN + col] = 1
    return place


PAIRS = table_index()


def spread_tables(tables):
    compact = jnp.dot(tables.reshape(64, RELS), jnp.asarray(PAIRS), precision=HIGH)
    compact = compact.reshape(2, 32, WIN, 190)
    rows = [compact[..., (9 - row) * WIN : (9 - row) * WIN + TOK] for row in range(WIN)]
    full = jnp.stack(rows, axis=2).reshape(2, 32, TOK, TOK)
    return jnp.pad(full, ((0, 0), (0, 0), (0, ROWS - TOK), (0, ROWS - TOK)))


def fold_tables(pairs):
    total = jnp.zeros((32, WIN, 190), F32)
    for row in range(WIN):
        low = (9 - row) * WIN
        total = total + jnp.pad(
            pairs[:, row * WIN : (row + 1) * WIN, :TOK], ((0, 0), (0, 0), (low, 90 - low))
        )
    return jnp.dot(total.reshape(32, -1), jnp.asarray(PAIRS.T), precision=HIGH)


def window_masks(level, valid, column):
    place = np.arange(ROWS)
    row = np.minimum(place // WIN, WIN - 1)
    col = jnp.asarray(place % WIN, jnp.int32)
    real = jnp.asarray(place < TOK)
    offset = SHIFT if level else 0
    rolled = column * WIN + col
    usable = (rolled + offset) % GW < valid
    masks = []
    for w in range(2):
        rolled_row = w * WIN + row
        row_region = (rolled_row >= GH - WIN).astype(np.int32) + (rolled_row >= GH - SHIFT)
        col_region = (rolled >= GW - WIN).astype(jnp.int32) + (rolled >= GW - SHIFT)
        region = jnp.asarray(row_region * 3, jnp.int32) + col_region
        allowed = usable[None, :]
        if level:
            allowed = allowed & (region[:, None] == region[None, :])
        mask = jnp.where(allowed, F32(0.0), F32(-100.0))
        mask = jnp.where(real[None, :], mask, F32(-1e30))
        masks.append(jnp.broadcast_to(mask, (ROWS, ROWS)))
    return jnp.stack(masks)


def gather_tp(value, place):
    parts = [value]
    for step in range(1, TP):
        parts.append(lax.ppermute(value, "tp", [(i, (i + step) % TP) for i in range(TP)]))
    stacked = jnp.stack(parts)
    order = (place - jnp.arange(TP)) % TP
    return [lax.dynamic_index_in_dim(stacked, order[i], 0, keepdims=False) for i in range(TP)]


def after(value, others):
    return lax.optimization_barrier((value, others))


def swap_core(value):
    return lax.ppermute(value, "core", [(0, 1), (1, 0)])


def sum_all(value):
    sent = value.astype(BF)
    value = sent.astype(F32) + swap_core(sent).astype(F32)
    for axis in ("x", "y", "tp"):
        sent = value.astype(BF)
        got = [
            lax.ppermute(sent, axis, [(i, (i + gap) % 4) for i in range(4)]).astype(F32)
            for gap in (1, 2, 3)
        ]
        value = (sent.astype(F32) + got[1]) + (got[0] + got[2])
    return value


def body(
    x3,
    res_group,
    merge_gain,
    merge_bias,
    merge_w,
    ln1_gain,
    ln1_bias,
    qkv_w,
    qv_bias,
    rel_table,
    proj_w,
    proj_bias,
    ln2_gain,
    ln2_bias,
    fc1_w,
    fc1_bias,
    fc2_w,
    fc2_bias,
    out_grad,
):
    core_at = lax.axis_index("core")
    chip_at = lax.axis_index("y") * 4 + lax.axis_index("x")
    column = lax.axis_index("tp")
    core = jnp.stack([core_at, column]).astype(jnp.int32)

    piece = pack_weights(
        jnp.stack([chip_at, core_at]).astype(jnp.int32),
        fc1_w,
        fc2_w,
        jnp.swapaxes(qkv_w, 1, 2),
        proj_w,
        merge_w.reshape(512, D),
    )
    weights = lax.all_gather(piece, GATHER_AXES, axis=0, tiled=True).reshape(64, UNITS, 16, D)

    pages = lax.all_to_all(x3, PAGE_AXES, split_axis=1, concat_axis=0, tiled=True)
    tiles = pages.reshape(GH, TP, WIN, 512).transpose(1, 0, 2, 3).reshape(TP * 2 * TOK, 512)
    parts = lax.all_to_all(tiles, "tp", split_axis=0, concat_axis=0, tiled=True)
    parts = parts.reshape(TP, 2 * TOK, 512)

    packed = jnp.concatenate(
        [
            merge_gain.reshape(-1),
            merge_bias.reshape(-1),
            qv_bias.reshape(-1),
            fc1_bias.reshape(-1),
            rel_table.reshape(-1),
            jnp.zeros((10240 - 9872,), F32),
        ]
    ).reshape(80, 128)
    quarters = [part.reshape(-1) for part in gather_tp(packed, column)]

    def joined(low, shape, axis):
        size = int(np.prod(shape))
        return jnp.concatenate([part[low : low + size].reshape(shape) for part in quarters], axis)

    merge_gain_all = joined(0, (1, 512), 0)
    merge_bias_all = joined(512, (1, 512), 0)
    qv_bias_all = joined(1024, (2, 2, 256), 2)
    fc1_bias_all = joined(2048, (2, 1024), 1)
    tables = spread_tables(joined(4096, (2, 8, RELS), 1))
    tables = [tables[0], tables[1]]

    valid = (res_group[0] + 1) * WIN
    masks = [window_masks(level, valid, column) for level in range(2)]
    spot = np.arange(T) % ROWS
    keep = ((column * WIN + SHIFT + jnp.asarray(spot % WIN, jnp.int32)) % GW < valid) & jnp.asarray(
        spot < TOK
    )
    keep = keep.astype(F32)[:, None]
    page_keep = (jnp.asarray(np.arange(GW), jnp.int32) < valid).astype(BF)[None, :, None]
    tiles = jnp.roll(out_grad[0] * page_keep, (-SHIFT, -SHIFT), (0, 1))
    tiles = tiles.reshape(2, WIN, TP, WIN, D).transpose(2, 0, 1, 3, 4).reshape(TP, 2, TOK, D)
    tiles = jnp.pad(tiles, ((0, 0), (0, 0), (0, ROWS - TOK), (0, 0))).reshape(TP, T, D)
    tiles = [
        lax.dynamic_index_in_dim(tiles, (column + TP - back) % TP, 0, keepdims=False)
        for back in range(TP)
    ]

    weights, (tables, masks, tiles, keep, parts) = after(
        weights, (tables, masks, tiles, keep, parts)
    )
    state, merged_mine, merged_other = merge_forward(
        core, parts, merge_gain_all, merge_bias_all, weights
    )
    kept = []
    halo = None
    pending = [swap_core(merged_other)]
    for level in range(2):
        small = (
            ln1_gain[level : level + 1],
            ln1_bias[level : level + 1],
            qv_bias_all[level, 0:1],
            qv_bias_all[level, 1:2],
            proj_bias[level : level + 1],
        )
        got = attn_forward(
            core, level, state, halo, weights, small, tables[level], masks[level]
        )
        mid, a, q, k, v, probs, heads_mine, heads_other = got[:8]
        start = got[8] if level else state
        mid, pending = after(mid, pending)
        small = (
            ln2_gain[level : level + 1],
            ln2_bias[level : level + 1],
            fc1_bias_all[level : level + 1],
            fc2_bias[level : level + 1],
        )
        swapped = [a, heads_other] if level else [swap_core(a), swap_core(heads_other)]
        more = mlp_forward(core, level, mid, weights, small, keep)
        c2, slope, extra = more[:3]
        acts = list(more[3 : 3 + TP])
        if level:
            slope, (swapped, c2_all) = after(slope, (swapped, c2_all))
            swapped = [swap_core(value) for value in swapped]
        else:
            (merged_got,) = pending
            pending = swapped
            state = more[3 + TP]
            halo = lax.ppermute(extra, "tp", [((i + 1) % TP, i) for i in range(TP)])
            halo, c2 = lax.optimization_barrier((halo, c2))
            c2_all = send_all(c2)
        kept.append([start, mid, a, q, k, v, probs, slope, c2, acts, heads_mine])
    a_zero, heads_zero = pending
    a_got, heads_got = swapped
    acts = send_ahead(acts)

    sums = [None, None]
    start, mid, a, q, k, v, probs, slope, c2, unused, heads_mine = kept[1]
    dmid, dmlp, dattn, db1, rows_two, dpre_mine, dpre_other = mlp_backward(
        core, 1, tiles[0], None, keep, mid, ln2_gain[1:2], weights, slope
    )
    got = attn_backward(core, 1, dmid, dattn, start, ln1_gain[1:2], weights, q, k, v, probs)
    grad, mixed_mine, mixed_other, pairs, dqv, rows_one, sent = got
    sent, (dpre_other, dattn_sent, acts, c2_sent, a_got, heads_got) = after(
        sent, (dpre_other, dattn, acts, c2, a_got, heads_got)
    )
    halo = lax.ppermute(sent, "tp", [(i, (i + 1) % TP) for i in range(TP)])
    dpre_got, dattn_got, mixed_got, c2_got = [
        swap_core(value) for value in (dpre_other, dattn_sent, mixed_other, c2_sent)
    ]
    sums[1] = (db1, rows_two, dqv, rows_one, pairs)
    down_other, down_mine = column_grads(core, tiles, acts)
    items = [
        ((c2, c2_got), (dpre_mine, dpre_got)),
        ((a, a_got), (mixed_mine, mixed_got)),
        ((dattn, dattn_got), (heads_mine, heads_got)),
    ]
    late = weight_grads(core, items, [[down_mine, swap_core(down_other)]])
    start, mid, a, q, k, v, probs, slope, c2, acts, heads_mine = kept[0]
    late, halo, acts = lax.optimization_barrier((late, halo, acts))
    acts = send_ahead(acts)
    late = lax.psum_scatter(late, CHIP_AXES, scatter_dimension=0, tiled=True)
    late = lax.optimization_barrier(late)[0]

    got = mlp_backward(core, 0, grad, halo, keep, mid, ln2_gain[0:1], weights, slope)
    dmid, dmlp, dattn, db1, rows_two = got[:5]
    dattn, (dpre, acts) = after(dattn, (list(got[5:]), acts))
    dpre = send_ahead(dpre)
    got = attn_backward(core, 0, dmid, dattn, start, ln1_gain[0:1], weights, q, k, v, probs)
    grad, mixed_mine, mixed_other, pairs, dqv, rows_one = got
    sums[0] = (db1, rows_two, dqv, rows_one, pairs)
    first, dm, dgain, dbias = merge_backward(core, parts, merge_gain_all, weights, grad)
    first, (dpre, dmlp) = after(first, (dpre, dmlp))
    dmlp_all = send_all(dmlp)
    up_other, up_mine = column_grads(core, c2_all, dpre)
    first, dattn_sent, mixed_other = lax.optimization_barrier((first, dattn, mixed_other))
    first_got, dattn_got, mixed_got = [
        swap_core(value) for value in (first, dattn_sent, mixed_other)
    ]
    down_other, down_mine = column_grads(core, dmlp_all, acts)
    items = [
        ((a, a_zero), (mixed_mine, mixed_got)),
        ((dattn, dattn_got), (heads_mine, heads_zero)),
        ((first, first_got), (merged_mine, merged_got)),
    ]
    early = weight_grads(
        core, items, [[up_mine, swap_core(up_other)], [down_mine, swap_core(down_other)]]
    )
    early, (extra, sums, dgain, dbias) = after(early, (extra, sums, dgain, dbias))
    early = lax.psum_scatter(early, CHIP_AXES, scatter_dimension=0, tiled=True)
    early = lax.optimization_barrier(early)[0]

    tiles_out = jnp.stack(gather_tp(extra, column)).reshape(TP, GH, WIN, D)
    output = jnp.roll(tiles_out.transpose(1, 0, 2, 3).reshape(GH, GW, D), SHIFT, 1)
    output = output.astype(F32)[None]
    back = lax.all_to_all(
        dm.reshape(TP * 2 * TOK, 512), "tp", split_axis=0, concat_axis=0, tiled=True
    )
    back = back.reshape(TP, GH, WIN, 512).transpose(1, 0, 2, 3).reshape(800, 1, 4, 128)
    grad_x3 = lax.all_to_all(back, PAGE_AXES, split_axis=0, concat_axis=1, tiled=True).astype(F32)

    def both_cores(value):
        rows = value.reshape(2, 32, -1)
        kept_rows = lax.dynamic_index_in_dim(rows, core_at, 0, keepdims=False).astype(F32)
        sent_rows = lax.dynamic_index_in_dim(rows, 1 - core_at, 0, keepdims=False)
        got_rows = swap_core(sent_rows.astype(BF)).astype(F32)
        return (
            jnp.where(core_at == 0, kept_rows, got_rows),
            jnp.where(core_at == 0, got_rows, kept_rows),
        )

    def wide(halves, low, size):
        return jnp.concatenate([half[:, low : low + size] for half in halves], axis=1)

    def finish(value, split):
        complete = value[..., split:].reshape(TP, 64, -1, 128).transpose(1, 2, 0, 3)
        partial_sums = sum_quarters(value[..., :split], column)
        return both_cores(
            jnp.concatenate([partial_sums, complete.reshape(64, -1).astype(F32)], axis=1)
        )

    late = finish(late, 1024)
    early = finish(early, 768)
    g_fc1 = jnp.stack([wide(early, 768, 512), wide(late, 0, 512)])
    g_fc2 = jnp.stack([wide(early, 1280, 512).T, wide(late, 1024, 512).T])
    pair = ((early, 0), (late, 512))
    g_qkv = jnp.stack(
        [jnp.stack([wide(half, low + 128 * s, 128) for s in range(3)], axis=1) for half, low in pair]
    )
    g_proj = jnp.stack([wide(half, low + 384, 128).T for half, low in pair])
    g_merge_w = wide(early, 512, 256).T.reshape(4, 128, 32)

    flat = []
    for level in range(2):
        db1, rows_two, dqv, rows_one, pairs = sums[level]
        flat += [rows_one, rows_two, dqv, db1, fold_tables(pairs)]
    flat += [dgain, dbias]
    flat = jnp.concatenate([item.reshape(-1) for item in flat])
    count = flat.shape[0]
    flat = jnp.pad(flat, (0, -count % 16384)).reshape(-1, 1024)
    flat = sum_all(flat).reshape(-1)
    page_at = chip_at * 2 + core_at

    def take(low, shape):
        return flat[low : low + int(np.prod(shape))].reshape(shape)

    def page_part(value):
        return lax.dynamic_slice_in_dim(value, page_at * 32, 32, value.ndim - 1)

    def tp_part(value, axis):
        size = value.shape[axis] // TP
        return lax.dynamic_slice_in_dim(value, column * size, size, axis)

    span = 2 * D + 4 * D + 2 * D + FF + 32 * RELS
    rows = [take(level * span, (6, D)) for level in range(2)]
    rows = page_part(jnp.stack(rows))
    dqv = tp_part(jnp.stack([take(level * span + 6 * D, (2, D)) for level in range(2)]), 2)
    db1 = tp_part(jnp.stack([take(level * span + 8 * D, (FF,)) for level in range(2)]), 1)
    table = tp_part(
        jnp.stack([take(level * span + 8 * D + FF, (32, RELS)) for level in range(2)]), 1
    )
    dgain = tp_part(take(2 * span, (TP, 512)), 0).reshape(4, 128)
    dbias = tp_part(take(2 * span + MERGED, (TP, 512)), 0).reshape(4, 128)
    return (
        output,
        grad_x3,
        dgain,
        dbias,
        g_merge_w,
        rows[:, 0],
        rows[:, 1],
        g_qkv,
        dqv,
        table,
        g_proj,
        rows[:, 5],
        rows[:, 2],
        rows[:, 3],
        g_fc1,
        db1,
        g_fc2,
        rows[:, 4],
    )


def solution(mesh):
    grid = Mesh(mesh.devices.reshape(4, 4, 2, TP), ("y", "x", "core", "tp"))
    page = PAGE_AXES
    return jax.shard_map(
        body,
        mesh=grid,
        in_specs=(
            P(page, None, None, "tp"),
            P(page),
            P(None, "tp"),
            P(None, "tp"),
            P(None, "tp", None),
            P(),
            P(),
            P(None, None, None, "tp"),
            P(None, None, "tp"),
            P(None, "tp", None),
            P(None, "tp", None),
            P(),
            P(),
            P(),
            P(None, None, "tp"),
            P(None, "tp"),
            P(None, "tp", None),
            P(),
            P(page, None, None, None),
        ),
        out_specs=(
            P(page, None, None, None),
            P(page, None, None, "tp"),
            P(None, "tp"),
            P(None, "tp"),
            P(None, "tp", page),
            P(None, page),
            P(None, page),
            P(None, page, None, "tp"),
            P(None, None, "tp"),
            P(None, "tp", None),
            P(None, "tp", page),
            P(None, page),
            P(None, page),
            P(None, page),
            P(None, page, "tp"),
            P(None, "tp"),
            P(None, "tp", page),
            P(None, page),
        ),
        check_vma=False,
    )
```

```python
from functools import partial

import jax
import jax.numpy as jnp
import numpy as np
from jax import lax
from jax.experimental import pallas as pl
from jax.experimental.pallas import tpu as pltpu
from jax.sharding import Mesh
from jax.sharding import PartitionSpec as P

D = 1024
FF = 4096
MERGED = 2048
WIN = 10
SHIFT = 5
GH = 20
GW = 40
RELS = 361
TOK = 100
ROWS = 112
T = 2 * ROWS
SEND = 112
EPS = 1e-05
SCALE = 32 ** (-0.5)
YX = 16
TP = 4
UNITS = 26
HIGH = lax.Precision.HIGHEST
BF = jnp.bfloat16
F32 = jnp.float32
PAGE_AXES = ("y", "x", "core")
CHIP_AXES = ("y", "x")
GATHER_AXES = ("tp", "y", "x", "core")
VMEM = 58 << 20


def row_at(row, col):
    return (row // WIN) * ROWS + (row % WIN) * WIN + col


def place_matrices():
    own = np.zeros((T, T), np.float32)
    recv = np.zeros((T, SEND), np.float32)
    send = np.zeros((SEND, T), np.float32)
    pack = np.zeros((2 * TOK, T), np.float32)
    out = np.zeros((2 * TOK, T), np.float32)
    for row in range(GH):
        for col in range(WIN):
            source = (row + SHIFT) % GH
            if col < SHIFT:
                own[row_at(row, col), row_at(source, col + SHIFT)] = 1
                send[row * SHIFT + col, row_at(row, col)] = 1
            else:
                recv[row_at(row, col), source * SHIFT + col - SHIFT] = 1
            pack[row * WIN + col, row_at(row, col)] = 1
            out[source * WIN + col, row_at(row, col)] = 1
    return own, recv, send, pack, out


OWN, RECV, SENT, PACK, OUT = place_matrices()


def const(matrix):
    return jnp.asarray(matrix, BF)


def dot(left, right):
    return lax.dot_general(left, right, (((1,), (0,)), ((), ())), preferred_element_type=F32)


def dot_nt(left, right):
    return lax.dot_general(left, right, (((1,), (1,)), ((), ())), preferred_element_type=F32)


def dot_tn(left, right):
    return lax.dot_general(left, right, (((0,), (0,)), ((), ())), preferred_element_type=F32)


def select_rows(matrix, value):
    high = value.astype(BF)
    rest = value - high.astype(F32)
    mid = rest.astype(BF)
    low = (rest - mid.astype(F32)).astype(BF)
    return dot(matrix, high) + dot(matrix, mid) + dot(matrix, low)


def norm_stats(value):
    mean = jnp.mean(value, axis=-1, keepdims=True)
    center = value - mean
    return center, lax.rsqrt(jnp.mean(center * center, axis=-1, keepdims=True) + EPS)


def norm_back(upstream, normed, spread, gain):
    scaled = upstream * gain
    inner = (
        scaled
        - jnp.mean(scaled, axis=-1, keepdims=True)
        - normed * jnp.mean(scaled * normed, axis=-1, keepdims=True)
    )
    return spread * inner


def col_sum(value):
    return jnp.sum(value, axis=0, keepdims=True)


def whole(shape):
    return pl.BlockSpec(shape, lambda step, core: (0,) * len(shape))


def shape_of(shape, dtype):
    return jax.ShapeDtypeStruct(shape, dtype)


def run(kernel, steps, core, args, in_specs, outs, out_specs, scratch, flops, moved):
    return pl.pallas_call(
        kernel,
        grid_spec=pltpu.PrefetchScalarGridSpec(
            num_scalar_prefetch=1,
            grid=(steps,),
            in_specs=in_specs,
            out_specs=out_specs,
            scratch_shapes=scratch,
        ),
        out_shape=outs,
        compiler_params=pltpu.CompilerParams(
            vmem_limit_bytes=VMEM, dimension_semantics=("arbitrary",)
        ),
        cost_estimate=pl.CostEstimate(flops=0, bytes_accessed=1024, transcendentals=0),
    )(core, *args)


def put_halves(core_ref, mine, other, low, high):
    @pl.when(core_ref[0] == 0)
    def _():
        mine(low)
        other(high)

    @pl.when(core_ref[0] != 0)
    def _():
        mine(high)
        other(low)


def pack_kernel(place_ref, up_ref, down_ref, mix_ref, proj_ref, merge_ref, out_ref, all_ref):
    for level in range(2):
        all_ref[8 * level : 8 * level + 4] = up_ref[level].reshape(4, 16, D)
        all_ref[8 * level + 4 : 8 * level + 8] = down_ref[level].reshape(4, 16, D)
        for part in range(3):
            for group in range(4):
                all_ref[16 + 4 * level + part, :, 256 * group : 256 * group + 256] = mix_ref[
                    level, part, 16 * group : 16 * group + 16
                ]
        all_ref[19 + 4 * level] = proj_ref[level]
    all_ref[24:26] = merge_ref[...].reshape(2, 16, D)
    out_ref[...] = all_ref[pl.ds(place_ref[1] * 13, 13)]


def pack_weights(place, up, down, mix, proj, merge):
    piece = pl.pallas_call(
        pack_kernel,
        grid_spec=pltpu.PrefetchScalarGridSpec(
            num_scalar_prefetch=1,
            grid=(1,),
            in_specs=[
                pl.BlockSpec((2, 64, D), lambda step, place: (0, place[0], 0)),
                pl.BlockSpec((2, 64, D), lambda step, place: (0, place[0], 0)),
                pl.BlockSpec((2, 3, 64, 256), lambda step, place: (0, 0, place[0], 0)),
                pl.BlockSpec((2, 16, D), lambda step, place: (0, place[0], 0)),
                pl.BlockSpec((32, D), lambda step, place: (place[0], 0)),
            ],
            out_specs=whole((13, 16, D)),
            scratch_shapes=[pltpu.VMEM((UNITS, 16, D), BF)],
        ),
        out_shape=shape_of((13, 16, D), BF),
        compiler_params=pltpu.CompilerParams(vmem_limit_bytes=VMEM),
        cost_estimate=pl.CostEstimate(flops=0, bytes_accessed=1 << 20, transcendentals=0),
    )(place, up, down, mix, proj, merge)
    return piece.reshape(208, D)


def merge_stats(x_ref, pack_ref, full):
    total = jnp.zeros((T, 1), F32)
    for part in range(TP):
        rows = dot_tn(pack_ref[...], x_ref[part])
        full[part] = rows
        total = total + jnp.sum(rows, axis=-1, keepdims=True)
    mean = total / MERGED
    square = jnp.zeros((T, 1), F32)
    for part in range(TP):
        center = full[part] - mean
        square = square + jnp.sum(center * center, axis=-1, keepdims=True)
    return mean, lax.rsqrt(square / MERGED + EPS)


def merge_kernel(
    core_ref, x_ref, pack_ref, gain_ref, bias_ref, w_ref, out_ref, mine_ref, other_ref, full, stats
):
    step = pl.program_id(0)

    @pl.when(step == 0)
    def _():
        mean, spread = merge_stats(x_ref, pack_ref, full)
        stats[0] = mean
        stats[1] = spread

    normed = (full[step] - stats[0]) * stats[1]
    value = (normed * gain_ref[0] + bias_ref[0]).astype(BF)

    def set_mine(part):
        mine_ref[...] = part

    def set_other(part):
        other_ref[...] = part

    put_halves(core_ref, set_mine, set_other, value[:, :256], value[:, 256:])
    term = dot(value, w_ref[...].reshape(512, D))

    @pl.when(step == 0)
    def _():
        out_ref[...] = term

    @pl.when(step != 0)
    def _():
        out_ref[...] += term


def merge_forward(core, parts, gain, bias, weights):
    return run(
        merge_kernel,
        TP,
        core,
        (parts, const(PACK), gain.reshape(TP, 1, 512), bias.reshape(TP, 1, 512), weights),
        [
            whole((TP, 2 * TOK, 512)),
            whole((2 * TOK, T)),
            pl.BlockSpec((1, 1, 512), lambda step, core: (step, 0, 0)),
            pl.BlockSpec((1, 1, 512), lambda step, core: (step, 0, 0)),
            pl.BlockSpec((YX, 2, 16, D), lambda step, core: (step, 12, 0, 0)),
        ],
        [shape_of((T, D), F32), shape_of((T, D), BF), shape_of((T, D), BF)],
        [
            whole((T, D)),
            pl.BlockSpec((T, 256), lambda step, core: (0, step)),
            pl.BlockSpec((T, 256), lambda step, core: (0, step)),
        ],
        [pltpu.VMEM((TP, T, 512), F32), pltpu.VMEM((2, T, 1), F32)],
        2 * T * MERGED * D,
        8 << 20,
    )


def merge_back_kernel(
    core_ref, x_ref, pack_ref, gain_ref, w_ref, dx_ref,
    start_ref, dm_ref, gains_ref, biases_ref,
    full, stats, upstream,
):
    step = pl.program_id(0)

    @pl.when(step == 0)
    def _():
        mean, spread = merge_stats(x_ref, pack_ref, full)
        stats[0] = mean
        stats[1] = spread
        stats[2] = jnp.zeros((T, 1), F32)
        stats[3] = jnp.zeros((T, 1), F32)
        start_ref[...] = dx_ref[...].astype(BF)

    grad = dot_nt(start_ref[...], w_ref[...].reshape(512, D))
    normed = (full[step] - stats[0]) * stats[1]
    full[step] = normed
    gains_ref[0] = col_sum(grad * normed)
    biases_ref[0] = col_sum(grad)
    scaled = grad * gain_ref[0]
    upstream[step] = scaled
    stats[2] += jnp.sum(scaled, axis=-1, keepdims=True)
    stats[3] += jnp.sum(scaled * normed, axis=-1, keepdims=True)

    @pl.when(step == TP - 1)
    def _():
        for part in range(TP):
            value = stats[1] * (
                upstream[part] - stats[2] / MERGED - full[part] * (stats[3] / MERGED)
            )
            dm_ref[part] = dot(pack_ref[...], value.astype(BF)).astype(BF)


def merge_backward(core, parts, gain, weights, grad):
    return run(
        merge_back_kernel,
        TP,
        core,
        (parts, const(PACK), gain.reshape(TP, 1, 512), weights, grad),
        [
            whole((TP, 2 * TOK, 512)),
            whole((2 * TOK, T)),
            pl.BlockSpec((1, 1, 512), lambda step, core: (step, 0, 0)),
            pl.BlockSpec((YX, 2, 16, D), lambda step, core: (step, 12, 0, 0)),
            whole((T, D)),
        ],
        [
            shape_of((T, D), BF),
            shape_of((TP, 2 * TOK, 512), BF),
            shape_of((TP, 1, 512), F32),
            shape_of((TP, 1, 512), F32),
        ],
        [
            whole((T, D)),
            whole((TP, 2 * TOK, 512)),
            pl.BlockSpec((1, 1, 512), lambda step, core: (step, 0, 0)),
            pl.BlockSpec((1, 1, 512), lambda step, core: (step, 0, 0)),
        ],
        [pltpu.VMEM((TP, T, 512), F32), pltpu.VMEM((4, T, 1), F32), pltpu.VMEM((TP, T, 512), F32)],
        2 * T * MERGED * D,
        8 << 20,
    )


def head_masks(rows):
    lane = lax.broadcasted_iota(jnp.int32, (rows, 128), 1)
    return [(lane >= 32 * place) & (lane < 32 * place + 32) for place in range(4)]


def spread_heads(value, masks):
    zero = jnp.zeros_like(value)
    return jnp.concatenate([jnp.where(mask, value, zero) for mask in masks], axis=0)


def fold_heads(value, masks):
    total = jnp.zeros((ROWS, 128), F32)
    for place, mask in enumerate(masks):
        total = jnp.where(mask, value[place * ROWS : (place + 1) * ROWS], total)
    return total


def unfold(ref):
    value = ref[...].reshape(YX, 16, D)
    parts = [value[:, :, 256 * group : 256 * group + 256] for group in range(4)]
    return jnp.stack(parts, axis=1).reshape(D, 256)


def attn_kernel(level, *refs):
    (core_ref, x_ref), refs = refs[:2], refs[2:]
    if level:
        (halo_ref, own_ref, recv_ref), refs = refs[:3], refs[3:]
    (
        gain_ref, bias_ref, wq_ref, wk_ref, wv_ref, wp_ref, qb_ref, vb_ref, table_ref, mask_ref,
        shift_ref,
    ), refs = refs[:11], refs[11:]
    (
        mid_ref, a_ref, q_ref, k_ref, v_ref, probs_ref, mine_ref, other_ref,
    ), refs = refs[:8], refs[8:]
    step = pl.program_id(0)

    @pl.when(step == 0)
    def _():
        value = x_ref[...]
        if level:
            value = select_rows(own_ref[...], value) + dot(recv_ref[...], halo_ref[...])
            refs[0][...] = value
        center, spread = norm_stats(value)
        a_ref[...] = (center * spread * gain_ref[...] + bias_ref[...]).astype(BF)
        mid_ref[...] = value + shift_ref[...]

    a = a_ref[...]
    q = (dot(a, unfold(wq_ref)) + qb_ref[...]).astype(BF)
    k = dot(a, unfold(wk_ref)).astype(BF)
    v = (dot(a, unfold(wv_ref)) + vb_ref[...]).astype(BF)
    q_ref[...] = q
    k_ref[...] = k
    v_ref[...] = v
    masks = head_masks(ROWS)
    halves = []
    for half in range(2):
        lanes = slice(half * 128, half * 128 + 128)
        table = table_ref[4 * half : 4 * half + 4]
        parts = []
        for w in range(2):
            rows = slice(w * ROWS, (w + 1) * ROWS)
            raw = dot_nt(spread_heads(q[rows, lanes], masks), k[rows, lanes]) * SCALE
            scores = raw.reshape(4, ROWS, ROWS) + table + mask_ref[w][None]
            top = jnp.max(scores, axis=-1, keepdims=True)
            terms = jnp.exp(scores - top)
            probs = (terms / jnp.sum(terms, axis=-1, keepdims=True)).astype(BF)
            probs_ref[0, w, 4 * half : 4 * half + 4] = probs
            mixed = dot(probs.reshape(4 * ROWS, ROWS), v[rows, lanes])
            parts.append(fold_heads(mixed, masks))
        halves.append(jnp.concatenate(parts, axis=0).astype(BF))

    def set_mine(part):
        mine_ref[...] = part

    def set_other(part):
        other_ref[...] = part

    put_halves(core_ref, set_mine, set_other, *halves)
    heads = jnp.concatenate(halves, axis=1)
    mid_ref[...] += dot(heads, wp_ref[...].reshape(256, D))


def unit_spec(unit):
    return pl.BlockSpec((YX, 1, 16, D), lambda step, core: (step, unit, 0, 0))


def attn_forward(core, level, state, halo, weights, small, table, mask):
    gain, bias, qbias, vbias, shift = small
    unit = 16 + 4 * level
    args = [state]
    specs = [whole((T, D))]
    if level:
        args += [halo, const(OWN), const(RECV)]
        specs += [whole((SEND, D)), whole((T, T)), whole((T, SEND))]
    args += [gain, bias, weights, weights, weights, weights, qbias, vbias, table, mask, shift]
    cols = pl.BlockSpec((1, 256), lambda step, core: (0, step))
    specs += [whole((1, D)), whole((1, D))] + [unit_spec(unit + place) for place in range(4)]
    specs += [
        cols,
        cols,
        pl.BlockSpec((8, ROWS, ROWS), lambda step, core: (step, 0, 0)),
        whole((2, ROWS, ROWS)),
        whole((1, D)),
    ]
    block = pl.BlockSpec((T, 256), lambda step, core: (0, step))
    half = pl.BlockSpec((T, 128), lambda step, core: (0, step))
    outs = [
        shape_of((T, D), F32),
        shape_of((T, D), BF),
        shape_of((T, D), BF),
        shape_of((T, D), BF),
        shape_of((T, D), BF),
        shape_of((TP, 2, 8, ROWS, ROWS), BF),
        shape_of((T, D // 2), BF),
        shape_of((T, D // 2), BF),
    ]
    out_specs = [
        whole((T, D)),
        whole((T, D)),
        block,
        block,
        block,
        pl.BlockSpec((1, 2, 8, ROWS, ROWS), lambda step, core: (step, 0, 0, 0, 0)),
        half,
        half,
    ]
    if level:
        outs.append(shape_of((T, D), F32))
        out_specs.append(whole((T, D)))
    return run(
        partial(attn_kernel, level), TP, core, args, specs, outs, out_specs, [], 8 * T * D * D, 24 << 20
    )


def quad_spec(unit):
    return pl.BlockSpec(
        (YX, 4, 16, D), lambda step, core: (lax.rem(core[1] + step, TP), unit, 0, 0)
    )


def wide_spec(rows):
    return pl.BlockSpec((rows, D), lambda step, core: (0, lax.rem(core[1] + step, TP)))


def half_spec():
    return pl.BlockSpec((T, 512), lambda step, core: (0, lax.rem(core[1] + step, TP)))


def mlp_kernel(level, *refs):
    (
        core_ref, mid_ref, gain_ref, bias_ref, w1_ref, w2_ref, b1_ref, b2_ref, place_ref, keep_ref,
        c2_ref, slope_ref, extra_ref,
    ), refs = refs[:13], refs[13:]
    act_refs, total = refs[:-1], refs[-1]
    step = pl.program_id(0)

    @pl.when(step == 0)
    def _():
        value = mid_ref[...]
        center, spread = norm_stats(value)
        c2_ref[...] = (center * spread * gain_ref[...] + bias_ref[...]).astype(BF)
        total[...] = value + b2_ref[...]

    pre = dot(c2_ref[...], w1_ref[...].reshape(D, D)) + b1_ref[...]
    phi = 0.5 + 0.5 * lax.erf(pre * (0.5**0.5))
    act = (pre * phi).astype(BF)
    slope_ref[...] = (phi + pre * ((2.0 * np.pi) ** -0.5 * jnp.exp(-0.5 * pre * pre))).astype(BF)

    if level:
        for ahead in range(TP):

            @pl.when(step == ahead)
            def _(ahead=ahead):
                act_refs[ahead][...] = act

    else:

        def set_mine(part):
            act_refs[0][...] = part

        def set_other(part):
            act_refs[1][...] = part

        put_halves(core_ref, set_mine, set_other, act[:, :512], act[:, 512:])

    total[...] += dot(act, w2_ref[...].reshape(D, D))

    @pl.when(step == TP - 1)
    def _():
        value = total[...]
        if level:
            extra_ref[...] = dot(place_ref[...], (value * keep_ref[...]).astype(BF)).astype(BF)
        else:
            extra_ref[...] = dot(place_ref[...], value.astype(BF)).astype(BF)
            act_refs[2][...] = value


def mlp_forward(core, level, mid, weights, small, keep):
    gain, bias, b1, b2 = small
    place = const(OUT if level else SENT)
    outs = [
        shape_of((T, D), BF),
        shape_of((T, FF), BF),
        shape_of((place.shape[0], D), BF),
    ]
    out_specs = [whole((T, D)), wide_spec(T), whole((place.shape[0], D))]
    if level:
        outs += [shape_of((T, D), BF)] * TP
        out_specs += [whole((T, D))] * TP
    else:
        outs += [shape_of((T, FF // 2), BF)] * 2 + [shape_of((T, D), F32)]
        out_specs += [half_spec(), half_spec(), whole((T, D))]
    return run(
        partial(mlp_kernel, level),
        TP,
        core,
        (mid, gain, bias, weights, weights, b1, b2, place, keep),
        [
            whole((T, D)),
            whole((1, D)),
            whole((1, D)),
            quad_spec(2 * level),
            quad_spec(2 * level + 1),
            wide_spec(1),
            whole((1, D)),
            whole(place.shape),
            whole((T, 1)),
        ],
        outs,
        out_specs,
        [pltpu.VMEM((T, D), F32)],
        4 * T * D * FF,
        24 << 20,
    )


def mlp_back_kernel(level, *refs):
    (core_ref, dx_ref), refs = refs[:2], refs[2:]
    if level:
        (keep_ref,), refs = refs[:1], refs[1:]
    else:
        (halo_ref, own_ref, sent_ref), refs = refs[:3], refs[3:]
    (mid_ref, gain_ref, w1_ref, w2_ref, slope_ref), refs = refs[:5], refs[5:]
    (dmid_ref, dmlp_ref, dattn_ref, db1_ref, rows_ref), refs = refs[:5], refs[5:]
    dpre_refs, (total, grad) = refs[:-2], refs[-2:]
    step = pl.program_id(0)

    @pl.when(step == 0)
    def _():
        if level:
            value = dx_ref[...].astype(F32) * keep_ref[...]
        else:
            value = select_rows_t(own_ref[...], dx_ref[...]) + dot_tn(sent_ref[...], halo_ref[...])
        grad[...] = value
        dmlp_ref[...] = value.astype(BF)
        total[...] = jnp.zeros((T, D), F32)

    dact = dot_nt(dmlp_ref[...], w2_ref[...].reshape(D, D))
    rounded = (dact * slope_ref[...].astype(F32)).astype(BF)
    db1_ref[...] = col_sum(rounded.astype(F32))
    if level:

        def set_mine(part):
            dpre_refs[0][...] = part

        def set_other(part):
            dpre_refs[1][...] = part

        put_halves(core_ref, set_mine, set_other, rounded[:, :512], rounded[:, 512:])
    else:
        for ahead in range(TP):

            @pl.when(step == ahead)
            def _(ahead=ahead):
                dpre_refs[ahead][...] = rounded

    total[...] += dot_nt(rounded, w1_ref[...].reshape(D, D))

    @pl.when(step == TP - 1)
    def _():
        center, spread = norm_stats(mid_ref[...])
        normed = center * spread
        upstream = total[...]
        dmid = grad[...] + norm_back(upstream, normed, spread, gain_ref[...])
        dmid_ref[...] = dmid
        dattn = dmid.astype(BF)
        dattn_ref[...] = dattn
        rows_ref[0:1] = col_sum(upstream * normed)
        rows_ref[1:2] = col_sum(upstream)
        rows_ref[2:3] = col_sum(dmlp_ref[...].astype(F32))
        rows_ref[3:4] = col_sum(dattn.astype(F32))


def select_rows_t(matrix, value):
    high = value.astype(BF)
    rest = value - high.astype(F32)
    mid = rest.astype(BF)
    low = (rest - mid.astype(F32)).astype(BF)
    return dot_tn(matrix, high) + dot_tn(matrix, mid) + dot_tn(matrix, low)


def mlp_backward(core, level, grad, halo, keep, mid, gain, weights, slope):
    if level:
        args, specs = [grad, keep], [whole((T, D)), whole((T, 1))]
        pre_shapes, pre_specs = [shape_of((T, FF // 2), BF)] * 2, [half_spec()] * 2
    else:
        args = [grad, halo, const(OWN), const(SENT)]
        specs = [whole((T, D)), whole((SEND, D)), whole((T, T)), whole((SEND, T))]
        pre_shapes, pre_specs = [shape_of((T, D), BF)] * TP, [whole((T, D))] * TP
    args += [mid, gain, weights, weights, slope]
    specs += [
        whole((T, D)),
        whole((1, D)),
        quad_spec(2 * level),
        quad_spec(2 * level + 1),
        wide_spec(T),
    ]
    return run(
        partial(mlp_back_kernel, level),
        TP,
        core,
        args,
        specs,
        [
            shape_of((T, D), F32),
            shape_of((T, D), BF),
            shape_of((T, D), BF),
            shape_of((1, FF), F32),
            shape_of((4, D), F32),
        ]
        + pre_shapes,
        [
            whole((T, D)),
            whole((T, D)),
            whole((T, D)),
            wide_spec(1),
            whole((4, D)),
        ]
        + pre_specs,
        [pltpu.VMEM((T, D), F32), pltpu.VMEM((T, D), F32)],
        4 * T * D * FF,
        24 << 20,
    )


def attn_back_kernel(level, *refs):
    (
        core_ref, dmid_ref, dattn_ref, x_ref, gain_ref, wq_ref, wk_ref, wv_ref, wp_ref,
        q_ref, k_ref, v_ref, probs_ref,
    ), refs = refs[:13], refs[13:]
    if level:
        (place_ref,), refs = refs[:1], refs[1:]
    (dx_ref, mine_ref, other_ref, pair_ref, sums_ref, rows_ref), refs = refs[:6], refs[6:]
    if level:
        (sent_ref,), refs = refs[:1], refs[1:]
    (total,) = refs
    step = pl.program_id(0)

    @pl.when(step == 0)
    def _():
        total[...] = jnp.zeros((T, D), F32)

    dheads = dot_nt(dattn_ref[...], wp_ref[...].reshape(256, D)).astype(BF)
    masks = head_masks(ROWS)
    dqs, dks, dvs = [], [], []
    for half in range(2):
        lanes = slice(half * 128, half * 128 + 128)
        dq_parts, dk_parts, dv_parts = [], [], []
        pairs = None
        for w in range(2):
            rows = slice(w * ROWS, (w + 1) * ROWS)
            rounded = probs_ref[0, w, 4 * half : 4 * half + 4].reshape(4 * ROWS, ROWS)
            probs = rounded.astype(F32)
            spread_out = spread_heads(dheads[rows, lanes], masks)
            dprobs = dot_nt(spread_out, v_ref[rows, lanes])
            dv_parts.append(dot_tn(rounded, spread_out))
            inner = jnp.sum(probs * dprobs, axis=-1, keepdims=True)
            dscores = (probs * (dprobs - inner)).astype(BF)
            wide = dscores.astype(F32)
            pairs = wide if pairs is None else pairs + wide
            dq_parts.append(fold_heads(dot(dscores, k_ref[rows, lanes]), masks))
            dk_parts.append(dot_tn(dscores, spread_heads(q_ref[rows, lanes], masks)))
        pair_ref[4 * half : 4 * half + 4] = pairs.reshape(4, ROWS, ROWS)
        dqs.append((jnp.concatenate(dq_parts, axis=0) * SCALE).astype(BF))
        dks.append((jnp.concatenate(dk_parts, axis=0) * SCALE).astype(BF))
        dvs.append(jnp.concatenate(dv_parts, axis=0).astype(BF))

    def set_mine(part):
        mine_ref[...] = part

    def set_other(part):
        other_ref[...] = part

    put_halves(
        core_ref,
        set_mine,
        set_other,
        jnp.concatenate([dqs[0], dks[0], dvs[0]], axis=1),
        jnp.concatenate([dqs[1], dks[1], dvs[1]], axis=1),
    )
    dq = jnp.concatenate(dqs, axis=1)
    dk = jnp.concatenate(dks, axis=1)
    dv = jnp.concatenate(dvs, axis=1)
    sums_ref[0:1] = col_sum(dq.astype(F32))
    sums_ref[1:2] = col_sum(dv.astype(F32))
    total[...] += (
        dot_nt(dq, unfold(wq_ref))
        + dot_nt(dk, unfold(wk_ref))
        + dot_nt(dv, unfold(wv_ref))
    )

    @pl.when(step == TP - 1)
    def _():
        center, spread = norm_stats(x_ref[...])
        normed = center * spread
        upstream = total[...]
        value = dmid_ref[...] + norm_back(upstream, normed, spread, gain_ref[...])
        dx_ref[...] = value
        rows_ref[0:1] = col_sum(upstream * normed)
        rows_ref[1:2] = col_sum(upstream)
        if level:
            sent_ref[...] = dot_tn(place_ref[...], value.astype(BF)).astype(BF)


def attn_backward(core, level, dmid, dattn, state, gain, weights, q, k, v, probs):
    unit = 16 + 4 * level
    block = pl.BlockSpec((T, 256), lambda step, core: (0, step))
    part = pl.BlockSpec((T, 384), lambda step, core: (0, step))
    args = [dmid, dattn, state, gain, weights, weights, weights, weights, q, k, v, probs]
    specs = [whole((T, D)), whole((T, D)), whole((T, D)), whole((1, D))]
    specs += [unit_spec(unit + place) for place in range(4)]
    specs += [
        block,
        block,
        block,
        pl.BlockSpec((1, 2, 8, ROWS, ROWS), lambda step, core: (step, 0, 0, 0, 0)),
    ]
    outs = [
        shape_of((T, D), F32),
        shape_of((T, 1536), BF),
        shape_of((T, 1536), BF),
        shape_of((32, ROWS, ROWS), F32),
        shape_of((2, D), F32),
        shape_of((2, D), F32),
    ]
    out_specs = [
        whole((T, D)),
        part,
        part,
        pl.BlockSpec((8, ROWS, ROWS), lambda step, core: (step, 0, 0)),
        pl.BlockSpec((2, 256), lambda step, core: (0, step)),
        whole((2, D)),
    ]
    if level:
        args.append(const(RECV))
        specs.append(whole((T, SEND)))
        outs.append(shape_of((SEND, D), BF))
        out_specs.append(whole((SEND, D)))
    return run(
        partial(attn_back_kernel, level),
        TP,
        core,
        args,
        specs,
        outs,
        out_specs,
        [pltpu.VMEM((T, D), F32)],
        8 * T * D * D,
        24 << 20,
    )


def weight_kernel(plan, *refs):
    refs, out_ref = refs[1:-1], refs[-1]
    place = 0
    column = 0
    for kind, size, count in plan:
        parts = [ref[...] for ref in refs[place : place + count]]
        if kind == "matrix":
            value = dot_tn(
                jnp.concatenate(parts[:2], axis=0), jnp.concatenate(parts[2:], axis=0)
            )
        else:
            value = sum(part.astype(F32) for part in parts)
        out_ref[:, 0, :, column : column + size] = value.astype(BF).reshape(YX, 64, size)
        column += size
        place += count


def weight_grads(core, items, sums):
    plan, args, specs = [], [], []
    for left, right in items:
        size = right[0].shape[1] // TP
        plan.append(("matrix", size, 4))
        args += [left[0], left[1], right[0], right[1]]
        block = pl.BlockSpec((T, size), lambda step, core: (0, step))
        specs += [whole((T, D)), whole((T, D)), block, block]
    for pieces in sums:
        plan.append(("sum", 128, len(pieces)))
        args += pieces
        specs += [pl.BlockSpec((D, 128), lambda step, core: (0, step))] * len(pieces)
    width = sum(size for unused, size, count in plan)
    return run(
        partial(weight_kernel, plan),
        TP,
        core,
        args,
        specs,
        shape_of((YX, TP, 64, width), BF),
        pl.BlockSpec((YX, 1, 64, width), lambda step, core: (0, step, 0, 0)),
        [],
        4 * T * D * width * TP,
        (2 * D * width * TP) + (8 << 20),
    )


def column_kernel(core_ref, *refs):
    lefts, rights, (other_ref, mine_ref) = refs[:TP], refs[TP : 2 * TP], refs[2 * TP :]
    left = jnp.concatenate([ref[...] for ref in lefts], axis=0)
    right = jnp.concatenate([ref[...] for ref in rights], axis=0)
    value = dot_tn(left, right).astype(BF)

    @pl.when(pl.program_id(0) == 0)
    def _():
        other_ref[...] = value

    @pl.when(pl.program_id(0) == 1)
    def _():
        mine_ref[...] = value


def column_grads(core, lefts, rights):
    half = pl.BlockSpec((T, 512), lambda step, core: (0, (core[0] + 1 + step) % 2))
    return run(
        column_kernel,
        2,
        core,
        list(lefts) + list(rights),
        [whole((T, D))] * TP + [half] * TP,
        [shape_of((D, 512), BF)] * 2,
        [whole((D, 512))] * 2,
        [],
        4 * T * D * 2048,
        8 << 20,
    )


def send_ahead(pieces):
    return [pieces[0]] + [
        lax.ppermute(pieces[step], "tp", [(i, (i + step) % TP) for i in range(TP)])
        for step in range(1, TP)
    ]


def send_all(value):
    return send_ahead([value] * TP)


def sum_quarters(value, column):
    pieces = [
        lax.dynamic_index_in_dim(value, (column + step) % TP, 0, keepdims=False)
        for step in range(TP)
    ]
    got = [piece.astype(F32) for piece in send_ahead(pieces)]
    return (got[0] + got[1]) + (got[2] + got[3])


def table_index():
    place = np.zeros((RELS, WIN * 190), np.float32)
    for row in range(WIN):
        for step in range(19):
            for col in range(WIN):
                place[(18 - step) * 19 + row - col + 9, row * 190 + step * WIN + col] = 1
    return place


PAIRS = table_index()


def spread_tables(tables):
    compact = jnp.dot(tables.reshape(64, RELS), jnp.asarray(PAIRS), precision=HIGH)
    compact = compact.reshape(2, 32, WIN, 190)
    rows = [compact[..., (9 - row) * WIN : (9 - row) * WIN + TOK] for row in range(WIN)]
    full = jnp.stack(rows, axis=2).reshape(2, 32, TOK, TOK)
    return jnp.pad(full, ((0, 0), (0, 0), (0, ROWS - TOK), (0, ROWS - TOK)))


def fold_tables(pairs):
    total = jnp.zeros((32, WIN, 190), F32)
    for row in range(WIN):
        low = (9 - row) * WIN
        total = total + jnp.pad(
            pairs[:, row * WIN : (row + 1) * WIN, :TOK], ((0, 0), (0, 0), (low, 90 - low))
        )
    return jnp.dot(total.reshape(32, -1), jnp.asarray(PAIRS.T), precision=HIGH)


def window_masks(level, valid, column):
    place = np.arange(ROWS)
    row = np.minimum(place // WIN, WIN - 1)
    col = jnp.asarray(place % WIN, jnp.int32)
    real = jnp.asarray(place < TOK)
    offset = SHIFT if level else 0
    rolled = column * WIN + col
    usable = (rolled + offset) % GW < valid
    masks = []
    for w in range(2):
        rolled_row = w * WIN + row
        row_region = (rolled_row >= GH - WIN).astype(np.int32) + (rolled_row >= GH - SHIFT)
        col_region = (rolled >= GW - WIN).astype(jnp.int32) + (rolled >= GW - SHIFT)
        region = jnp.asarray(row_region * 3, jnp.int32) + col_region
        allowed = usable[None, :]
        if level:
            allowed = allowed & (region[:, None] == region[None, :])
        mask = jnp.where(allowed, F32(0.0), F32(-100.0))
        mask = jnp.where(real[None, :], mask, F32(-1e30))
        masks.append(jnp.broadcast_to(mask, (ROWS, ROWS)))
    return jnp.stack(masks)


def gather_tp(value, place):
    parts = [value]
    for step in range(1, TP):
        parts.append(lax.ppermute(value, "tp", [(i, (i + step) % TP) for i in range(TP)]))
    stacked = jnp.stack(parts)
    order = (place - jnp.arange(TP)) % TP
    return [lax.dynamic_index_in_dim(stacked, order[i], 0, keepdims=False) for i in range(TP)]


def after(value, others):
    return lax.optimization_barrier((value, others))


def swap_core(value):
    return lax.ppermute(value, "core", [(0, 1), (1, 0)])


def sum_all(value):
    sent = value.astype(BF)
    value = sent.astype(F32) + swap_core(sent).astype(F32)
    for axis in ("x", "y", "tp"):
        sent = value.astype(BF)
        got = [
            lax.ppermute(sent, axis, [(i, (i + gap) % 4) for i in range(4)]).astype(F32)
            for gap in (1, 2, 3)
        ]
        value = (sent.astype(F32) + got[1]) + (got[0] + got[2])
    return value


def body(
    x3,
    res_group,
    merge_gain,
    merge_bias,
    merge_w,
    ln1_gain,
    ln1_bias,
    qkv_w,
    qv_bias,
    rel_table,
    proj_w,
    proj_bias,
    ln2_gain,
    ln2_bias,
    fc1_w,
    fc1_bias,
    fc2_w,
    fc2_bias,
    out_grad,
):
    core_at = lax.axis_index("core")
    chip_at = lax.axis_index("y") * 4 + lax.axis_index("x")
    column = lax.axis_index("tp")
    core = jnp.stack([core_at, column]).astype(jnp.int32)

    piece = pack_weights(
        jnp.stack([chip_at, core_at]).astype(jnp.int32),
        fc1_w,
        fc2_w,
        jnp.swapaxes(qkv_w, 1, 2),
        proj_w,
        merge_w.reshape(512, D),
    )
    weights = lax.all_gather(piece, GATHER_AXES, axis=0, tiled=True).reshape(64, UNITS, 16, D)

    pages = lax.all_to_all(x3, PAGE_AXES, split_axis=1, concat_axis=0, tiled=True)
    tiles = pages.reshape(GH, TP, WIN, 512).transpose(1, 0, 2, 3).reshape(TP * 2 * TOK, 512)
    parts = lax.all_to_all(tiles, "tp", split_axis=0, concat_axis=0, tiled=True)
    parts = parts.reshape(TP, 2 * TOK, 512)

    packed = jnp.concatenate(
        [
            merge_gain.reshape(-1),
            merge_bias.reshape(-1),
            qv_bias.reshape(-1),
            fc1_bias.reshape(-1),
            rel_table.reshape(-1),
            jnp.zeros((10240 - 9872,), F32),
        ]
    ).reshape(80, 128)
    quarters = [part.reshape(-1) for part in gather_tp(packed, column)]

    def joined(low, shape, axis):
        size = int(np.prod(shape))
        return jnp.concatenate([part[low : low + size].reshape(shape) for part in quarters], axis)

    merge_gain_all = joined(0, (1, 512), 0)
    merge_bias_all = joined(512, (1, 512), 0)
    qv_bias_all = joined(1024, (2, 2, 256), 2)
    fc1_bias_all = joined(2048, (2, 1024), 1)
    tables = spread_tables(joined(4096, (2, 8, RELS), 1))
    tables = [tables[0], tables[1]]

    valid = (res_group[0] + 1) * WIN
    masks = [window_masks(level, valid, column) for level in range(2)]
    spot = np.arange(T) % ROWS
    keep = ((column * WIN + SHIFT + jnp.asarray(spot % WIN, jnp.int32)) % GW < valid) & jnp.asarray(
        spot < TOK
    )
    keep = keep.astype(F32)[:, None]
    page_keep = (jnp.asarray(np.arange(GW), jnp.int32) < valid).astype(BF)[None, :, None]
    tiles = jnp.roll(out_grad[0] * page_keep, (-SHIFT, -SHIFT), (0, 1))
    tiles = tiles.reshape(2, WIN, TP, WIN, D).transpose(2, 0, 1, 3, 4).reshape(TP, 2, TOK, D)
    tiles = jnp.pad(tiles, ((0, 0), (0, 0), (0, ROWS - TOK), (0, 0))).reshape(TP, T, D)
    tiles = [
        lax.dynamic_index_in_dim(tiles, (column + TP - back) % TP, 0, keepdims=False)
        for back in range(TP)
    ]

    weights, (tables, masks, tiles, keep, parts) = after(
        weights, (tables, masks, tiles, keep, parts)
    )
    state, merged_mine, merged_other = merge_forward(
        core, parts, merge_gain_all, merge_bias_all, weights
    )
    kept = []
    halo = None
    pending = [swap_core(merged_other)]
    for level in range(2):
        small = (
            ln1_gain[level : level + 1],
            ln1_bias[level : level + 1],
            qv_bias_all[level, 0:1],
            qv_bias_all[level, 1:2],
            proj_bias[level : level + 1],
        )
        got = attn_forward(
            core, level, state, halo, weights, small, tables[level], masks[level]
        )
        mid, a, q, k, v, probs, heads_mine, heads_other = got[:8]
        start = got[8] if level else state
        mid, pending = after(mid, pending)
        small = (
            ln2_gain[level : level + 1],
            ln2_bias[level : level + 1],
            fc1_bias_all[level : level + 1],
            fc2_bias[level : level + 1],
        )
        swapped = [a, heads_other] if level else [swap_core(a), swap_core(heads_other)]
        more = mlp_forward(core, level, mid, weights, small, keep)
        c2, slope, extra = more[:3]
        acts = list(more[3:])
        if level:
            slope, (swapped, c2_all) = after(slope, (swapped, c2_all))
            swapped = [swap_core(value) for value in swapped]
        else:
            (merged_got,) = pending
            pending = swapped
            state = acts[2]
            halo = lax.ppermute(extra, "tp", [((i + 1) % TP, i) for i in range(TP)])
            halo, c2 = lax.optimization_barrier((halo, c2))
            c2_all = send_all(c2)
        kept.append([start, mid, a, q, k, v, probs, slope, c2, acts, heads_mine])
    a_zero, heads_zero = pending
    a_got, heads_got = swapped
    acts = send_ahead(acts)

    sums = [None, None]
    start, mid, a, q, k, v, probs, slope, c2, unused, heads_mine = kept[1]
    dmid, dmlp, dattn, db1, rows_two, dpre_mine, dpre_other = mlp_backward(
        core, 1, tiles[0], None, keep, mid, ln2_gain[1:2], weights, slope
    )
    dattn, (a_got, heads_got, dpre_other, c2_sent) = after(
        dattn, (a_got, heads_got, dpre_other, c2)
    )
    dpre_got, dattn_got, c2_got = [swap_core(value) for value in (dpre_other, dattn, c2_sent)]
    got = attn_backward(core, 1, dmid, dattn, start, ln1_gain[1:2], weights, q, k, v, probs)
    grad, mixed_mine, mixed_other, pairs, dqv, rows_one, sent = got
    sent, (acts, dpre_got, dattn_got, c2_got) = after(sent, (acts, dpre_got, dattn_got, c2_got))
    halo = lax.ppermute(sent, "tp", [(i, (i + 1) % TP) for i in range(TP)])
    mixed_got = swap_core(mixed_other)
    sums[1] = (db1, rows_two, dqv, rows_one, pairs)
    items = [
        ((c2, c2_got), (dpre_mine, dpre_got)),
        ((a, a_got), (mixed_mine, mixed_got)),
        ((dattn, dattn_got), (heads_mine, heads_got)),
    ]
    late = weight_grads(core, items, [])
    late, halo = lax.optimization_barrier((late, halo))
    late = lax.psum_scatter(late, CHIP_AXES, scatter_dimension=0, tiled=True)
    late = lax.optimization_barrier(late)[0]

    start, mid, a, q, k, v, probs, slope, c2, (act_mine, act_other, unused), heads_mine = kept[0]
    halo, act_other = lax.optimization_barrier((halo, act_other))
    act_got = swap_core(act_other)
    got = mlp_backward(core, 0, grad, halo, keep, mid, ln2_gain[0:1], weights, slope)
    dmid, dmlp, dattn, db1, rows_two = got[:5]
    dattn, (dpre, act_got, acts, tiles) = after(dattn, (list(got[5:]), act_got, acts, tiles))
    dpre = send_ahead(dpre)
    got = attn_backward(core, 0, dmid, dattn, start, ln1_gain[0:1], weights, q, k, v, probs)
    grad, mixed_mine, mixed_other, pairs, dqv, rows_one = got
    sums[0] = (db1, rows_two, dqv, rows_one, pairs)
    grad, dattn_sent = lax.optimization_barrier((grad, dattn))
    mixed_got, dattn_got = [swap_core(value) for value in (mixed_other, dattn_sent)]
    first, dm, dgain, dbias = merge_backward(core, parts, merge_gain_all, weights, grad)
    last_other, last_mine = column_grads(core, tiles, acts)
    first, (dpre, dmlp_sent, last_other) = after(first, (dpre, dmlp, last_other))
    first_got, dmlp_got = swap_core(first), swap_core(dmlp_sent)
    up_other, up_mine = column_grads(core, c2_all, dpre)
    items = [
        ((a, a_zero), (mixed_mine, mixed_got)),
        ((dattn, dattn_got), (heads_mine, heads_zero)),
        ((first, first_got), (merged_mine, merged_got)),
        ((dmlp, dmlp_got), (act_mine, act_got)),
    ]
    early = weight_grads(
        core, items, [[up_mine, swap_core(up_other)], [last_mine, swap_core(last_other)]]
    )
    early, (extra, sums, dgain, dbias) = after(early, (extra, sums, dgain, dbias))
    early = lax.psum_scatter(early, CHIP_AXES, scatter_dimension=0, tiled=True)
    early = lax.optimization_barrier(early)[0]

    tiles_out = jnp.stack(gather_tp(extra, column)).reshape(TP, GH, WIN, D)
    output = jnp.roll(tiles_out.transpose(1, 0, 2, 3).reshape(GH, GW, D), SHIFT, 1)
    output = output.astype(F32)[None]
    back = lax.all_to_all(
        dm.reshape(TP * 2 * TOK, 512), "tp", split_axis=0, concat_axis=0, tiled=True
    )
    back = back.reshape(TP, GH, WIN, 512).transpose(1, 0, 2, 3).reshape(800, 1, 4, 128)
    grad_x3 = lax.all_to_all(back, PAGE_AXES, split_axis=0, concat_axis=1, tiled=True).astype(F32)

    def both_cores(value):
        rows = value.reshape(2, 32, -1)
        kept_rows = lax.dynamic_index_in_dim(rows, core_at, 0, keepdims=False).astype(F32)
        sent_rows = lax.dynamic_index_in_dim(rows, 1 - core_at, 0, keepdims=False)
        got_rows = swap_core(sent_rows.astype(BF)).astype(F32)
        return (
            jnp.where(core_at == 0, kept_rows, got_rows),
            jnp.where(core_at == 0, got_rows, kept_rows),
        )

    def wide(halves, low, size):
        return jnp.concatenate([half[:, low : low + size] for half in halves], axis=1)

    def finish(value, split):
        complete = value[..., split:].reshape(TP, 64, -1, 128).transpose(1, 2, 0, 3)
        partial_sums = sum_quarters(value[..., :split], column)
        return both_cores(
            jnp.concatenate([partial_sums, complete.reshape(64, -1).astype(F32)], axis=1)
        )

    late = both_cores(sum_quarters(late, column))
    early = finish(early, 1280)
    g_fc1 = jnp.stack([wide(early, 1280, 512), wide(late, 0, 512)])
    g_fc2 = jnp.stack([wide(early, 768, 512).T, wide(early, 1792, 512).T])
    pair = ((early, 0), (late, 512))
    g_qkv = jnp.stack(
        [jnp.stack([wide(half, low + 128 * s, 128) for s in range(3)], axis=1) for half, low in pair]
    )
    g_proj = jnp.stack([wide(half, low + 384, 128).T for half, low in pair])
    g_merge_w = wide(early, 512, 256).T.reshape(4, 128, 32)

    flat = []
    for level in range(2):
        db1, rows_two, dqv, rows_one, pairs = sums[level]
        flat += [rows_one, rows_two, dqv, db1, fold_tables(pairs)]
    flat += [dgain, dbias]
    flat = jnp.concatenate([item.reshape(-1) for item in flat])
    count = flat.shape[0]
    flat = jnp.pad(flat, (0, -count % 16384)).reshape(-1, 1024)
    flat = sum_all(flat).reshape(-1)
    page_at = chip_at * 2 + core_at

    def take(low, shape):
        return flat[low : low + int(np.prod(shape))].reshape(shape)

    def page_part(value):
        return lax.dynamic_slice_in_dim(value, page_at * 32, 32, value.ndim - 1)

    def tp_part(value, axis):
        size = value.shape[axis] // TP
        return lax.dynamic_slice_in_dim(value, column * size, size, axis)

    span = 2 * D + 4 * D + 2 * D + FF + 32 * RELS
    rows = [take(level * span, (6, D)) for level in range(2)]
    rows = page_part(jnp.stack(rows))
    dqv = tp_part(jnp.stack([take(level * span + 6 * D, (2, D)) for level in range(2)]), 2)
    db1 = tp_part(jnp.stack([take(level * span + 8 * D, (FF,)) for level in range(2)]), 1)
    table = tp_part(
        jnp.stack([take(level * span + 8 * D + FF, (32, RELS)) for level in range(2)]), 1
    )
    dgain = tp_part(take(2 * span, (TP, 512)), 0).reshape(4, 128)
    dbias = tp_part(take(2 * span + MERGED, (TP, 512)), 0).reshape(4, 128)
    return (
        output,
        grad_x3,
        dgain,
        dbias,
        g_merge_w,
        rows[:, 0],
        rows[:, 1],
        g_qkv,
        dqv,
        table,
        g_proj,
        rows[:, 5],
        rows[:, 2],
        rows[:, 3],
        g_fc1,
        db1,
        g_fc2,
        rows[:, 4],
    )


def solution(mesh):
    grid = Mesh(mesh.devices.reshape(4, 4, 2, TP), ("y", "x", "core", "tp"))
    page = PAGE_AXES
    return jax.shard_map(
        body,
        mesh=grid,
        in_specs=(
            P(page, None, None, "tp"),
            P(page),
            P(None, "tp"),
            P(None, "tp"),
            P(None, "tp", None),
            P(),
            P(),
            P(None, None, None, "tp"),
            P(None, None, "tp"),
            P(None, "tp", None),
            P(None, "tp", None),
            P(),
            P(),
            P(),
            P(None, None, "tp"),
            P(None, "tp"),
            P(None, "tp", None),
            P(),
            P(page, None, None, None),
        ),
        out_specs=(
            P(page, None, None, None),
            P(page, None, None, "tp"),
            P(None, "tp"),
            P(None, "tp"),
            P(None, "tp", page),
            P(None, page),
            P(None, page),
            P(None, page, None, "tp"),
            P(None, None, "tp"),
            P(None, "tp", None),
            P(None, "tp", page),
            P(None, page),
            P(None, page),
            P(None, page),
            P(None, page, "tp"),
            P(None, "tp"),
            P(None, "tp", page),
            P(None, page),
        ),
        check_vma=False,
    )
```

```python
from functools import partial

import jax
import jax.numpy as jnp
import numpy as np
from jax import lax
from jax.experimental import pallas as pl
from jax.experimental.pallas import tpu as pltpu
from jax.sharding import Mesh
from jax.sharding import PartitionSpec as P

D = 1024
FF = 4096
MERGED = 2048
WIN = 10
SHIFT = 5
GH = 20
GW = 40
RELS = 361
TOK = 100
ROWS = 112
T = 2 * ROWS
SEND = 112
EPS = 1e-05
SCALE = 32 ** (-0.5)
YX = 16
TP = 4
UNITS = 18
HIGH = lax.Precision.HIGHEST
BF = jnp.bfloat16
F32 = jnp.float32
PAGE_AXES = ("y", "x", "core")
CHIP_AXES = ("y", "x")
GATHER_AXES = ("tp", "y", "x", "core")
VMEM = 58 << 20


def row_at(row, col):
    return (row // WIN) * ROWS + (row % WIN) * WIN + col


def place_matrices():
    own = np.zeros((T, T), np.float32)
    recv = np.zeros((T, SEND), np.float32)
    send = np.zeros((SEND, T), np.float32)
    pack = np.zeros((2 * TOK, T), np.float32)
    out = np.zeros((2 * TOK, T), np.float32)
    for row in range(GH):
        for col in range(WIN):
            source = (row + SHIFT) % GH
            if col < SHIFT:
                own[row_at(row, col), row_at(source, col + SHIFT)] = 1
                send[row * SHIFT + col, row_at(row, col)] = 1
            else:
                recv[row_at(row, col), source * SHIFT + col - SHIFT] = 1
            pack[row * WIN + col, row_at(row, col)] = 1
            out[source * WIN + col, row_at(row, col)] = 1
    return own, recv, send, pack, out


OWN, RECV, SENT, PACK, OUT = place_matrices()


def const(matrix):
    return jnp.asarray(matrix, BF)


def dot(left, right):
    return lax.dot_general(left, right, (((1,), (0,)), ((), ())), preferred_element_type=F32)


def dot_nt(left, right):
    return lax.dot_general(left, right, (((1,), (1,)), ((), ())), preferred_element_type=F32)


def dot_tn(left, right):
    return lax.dot_general(left, right, (((0,), (0,)), ((), ())), preferred_element_type=F32)


def select_rows(matrix, value):
    high = value.astype(BF)
    rest = value - high.astype(F32)
    mid = rest.astype(BF)
    low = (rest - mid.astype(F32)).astype(BF)
    return dot(matrix, high) + dot(matrix, mid) + dot(matrix, low)


def norm_stats(value):
    mean = jnp.mean(value, axis=-1, keepdims=True)
    center = value - mean
    return center, lax.rsqrt(jnp.mean(center * center, axis=-1, keepdims=True) + EPS)


def norm_back(upstream, normed, spread, gain):
    scaled = upstream * gain
    inner = (
        scaled
        - jnp.mean(scaled, axis=-1, keepdims=True)
        - normed * jnp.mean(scaled * normed, axis=-1, keepdims=True)
    )
    return spread * inner


def col_sum(value):
    return jnp.sum(value, axis=0, keepdims=True)


def whole(shape):
    return pl.BlockSpec(shape, lambda step, core: (0,) * len(shape))


def shape_of(shape, dtype):
    return jax.ShapeDtypeStruct(shape, dtype)


def run(kernel, steps, core, args, in_specs, outs, out_specs, scratch, flops, moved):
    return pl.pallas_call(
        kernel,
        grid_spec=pltpu.PrefetchScalarGridSpec(
            num_scalar_prefetch=1,
            grid=(steps,),
            in_specs=in_specs,
            out_specs=out_specs,
            scratch_shapes=scratch,
        ),
        out_shape=outs,
        compiler_params=pltpu.CompilerParams(
            vmem_limit_bytes=VMEM, dimension_semantics=("arbitrary",)
        ),
        cost_estimate=pl.CostEstimate(flops=0, bytes_accessed=1024, transcendentals=0),
    )(core, *args)


def put_halves(core_ref, mine, other, low, high):
    @pl.when(core_ref[0] == 0)
    def _():
        mine(low)
        other(high)

    @pl.when(core_ref[0] != 0)
    def _():
        mine(high)
        other(low)


def pack_kernel(
    place_ref, up_ref, down_ref, mix_ref, proj_ref, merge_ref, out_ref, late_ref, all_ref
):
    low = place_ref[1] == 0
    late_ref[...] = jnp.where(low, up_ref[1], down_ref[1]).reshape(4, 16, D)
    all_ref[0:4] = up_ref[0].reshape(4, 16, D)
    all_ref[4:8] = down_ref[0].reshape(4, 16, D)
    for level in range(2):
        for part in range(3):
            for group in range(4):
                all_ref[8 + 4 * level + part, :, 256 * group : 256 * group + 256] = mix_ref[
                    level, part, 16 * group : 16 * group + 16
                ]
        all_ref[11 + 4 * level] = proj_ref[level]
    all_ref[16:18] = merge_ref[...].reshape(2, 16, D)
    out_ref[...] = all_ref[pl.ds(place_ref[1] * 9, 9)]


def pack_weights(place, up, down, mix, proj, merge):
    return pl.pallas_call(
        pack_kernel,
        grid_spec=pltpu.PrefetchScalarGridSpec(
            num_scalar_prefetch=1,
            grid=(1,),
            in_specs=[
                pl.BlockSpec((2, 64, D), lambda step, place: (0, place[0], 0)),
                pl.BlockSpec((2, 64, D), lambda step, place: (0, place[0], 0)),
                pl.BlockSpec((2, 3, 64, 256), lambda step, place: (0, 0, place[0], 0)),
                pl.BlockSpec((2, 16, D), lambda step, place: (0, place[0], 0)),
                pl.BlockSpec((32, D), lambda step, place: (place[0], 0)),
            ],
            out_specs=[whole((9, 16, D)), whole((4, 16, D))],
            scratch_shapes=[pltpu.VMEM((UNITS, 16, D), BF)],
        ),
        out_shape=[shape_of((9, 16, D), BF), shape_of((4, 16, D), BF)],
        compiler_params=pltpu.CompilerParams(vmem_limit_bytes=VMEM),
        cost_estimate=pl.CostEstimate(flops=0, bytes_accessed=1 << 20, transcendentals=0),
    )(place, up, down, mix, proj, merge)


def merge_stats(x_ref, pack_ref, full):
    total = jnp.zeros((T, 1), F32)
    for part in range(TP):
        rows = dot_tn(pack_ref[...], x_ref[part])
        full[part] = rows
        total = total + jnp.sum(rows, axis=-1, keepdims=True)
    mean = total / MERGED
    square = jnp.zeros((T, 1), F32)
    for part in range(TP):
        center = full[part] - mean
        square = square + jnp.sum(center * center, axis=-1, keepdims=True)
    return mean, lax.rsqrt(square / MERGED + EPS)


def merge_kernel(
    core_ref, x_ref, pack_ref, gain_ref, bias_ref, w_ref, out_ref, mine_ref, other_ref, full, stats
):
    step = pl.program_id(0)

    @pl.when(step == 0)
    def _():
        mean, spread = merge_stats(x_ref, pack_ref, full)
        stats[0] = mean
        stats[1] = spread

    normed = (full[step] - stats[0]) * stats[1]
    value = (normed * gain_ref[0] + bias_ref[0]).astype(BF)

    def set_mine(part):
        mine_ref[...] = part

    def set_other(part):
        other_ref[...] = part

    put_halves(core_ref, set_mine, set_other, value[:, :256], value[:, 256:])
    term = dot(value, w_ref[...].reshape(512, D))

    @pl.when(step == 0)
    def _():
        out_ref[...] = term

    @pl.when(step != 0)
    def _():
        out_ref[...] += term


def merge_forward(core, parts, gain, bias, weights):
    return run(
        merge_kernel,
        TP,
        core,
        (parts, const(PACK), gain.reshape(TP, 1, 512), bias.reshape(TP, 1, 512), weights),
        [
            whole((TP, 2 * TOK, 512)),
            whole((2 * TOK, T)),
            pl.BlockSpec((1, 1, 512), lambda step, core: (step, 0, 0)),
            pl.BlockSpec((1, 1, 512), lambda step, core: (step, 0, 0)),
            pl.BlockSpec((YX, 2, 16, D), lambda step, core: (step, 8, 0, 0)),
        ],
        [shape_of((T, D), F32), shape_of((T, D), BF), shape_of((T, D), BF)],
        [
            whole((T, D)),
            pl.BlockSpec((T, 256), lambda step, core: (0, step)),
            pl.BlockSpec((T, 256), lambda step, core: (0, step)),
        ],
        [pltpu.VMEM((TP, T, 512), F32), pltpu.VMEM((2, T, 1), F32)],
        2 * T * MERGED * D,
        8 << 20,
    )


def merge_back_kernel(
    core_ref, x_ref, pack_ref, gain_ref, w_ref, dx_ref,
    start_ref, dm_ref, gains_ref, biases_ref,
    full, stats, upstream,
):
    step = pl.program_id(0)

    @pl.when(step == 0)
    def _():
        mean, spread = merge_stats(x_ref, pack_ref, full)
        stats[0] = mean
        stats[1] = spread
        stats[2] = jnp.zeros((T, 1), F32)
        stats[3] = jnp.zeros((T, 1), F32)
        start_ref[...] = dx_ref[...].astype(BF)

    grad = dot_nt(start_ref[...], w_ref[...].reshape(512, D))
    normed = (full[step] - stats[0]) * stats[1]
    full[step] = normed
    gains_ref[0] = col_sum(grad * normed)
    biases_ref[0] = col_sum(grad)
    scaled = grad * gain_ref[0]
    upstream[step] = scaled
    stats[2] += jnp.sum(scaled, axis=-1, keepdims=True)
    stats[3] += jnp.sum(scaled * normed, axis=-1, keepdims=True)

    @pl.when(step == TP - 1)
    def _():
        for part in range(TP):
            value = stats[1] * (
                upstream[part] - stats[2] / MERGED - full[part] * (stats[3] / MERGED)
            )
            dm_ref[part] = dot(pack_ref[...], value.astype(BF)).astype(BF)


def merge_backward(core, parts, gain, weights, grad):
    return run(
        merge_back_kernel,
        TP,
        core,
        (parts, const(PACK), gain.reshape(TP, 1, 512), weights, grad),
        [
            whole((TP, 2 * TOK, 512)),
            whole((2 * TOK, T)),
            pl.BlockSpec((1, 1, 512), lambda step, core: (step, 0, 0)),
            pl.BlockSpec((YX, 2, 16, D), lambda step, core: (step, 8, 0, 0)),
            whole((T, D)),
        ],
        [
            shape_of((T, D), BF),
            shape_of((TP, 2 * TOK, 512), BF),
            shape_of((TP, 1, 512), F32),
            shape_of((TP, 1, 512), F32),
        ],
        [
            whole((T, D)),
            whole((TP, 2 * TOK, 512)),
            pl.BlockSpec((1, 1, 512), lambda step, core: (step, 0, 0)),
            pl.BlockSpec((1, 1, 512), lambda step, core: (step, 0, 0)),
        ],
        [pltpu.VMEM((TP, T, 512), F32), pltpu.VMEM((4, T, 1), F32), pltpu.VMEM((TP, T, 512), F32)],
        2 * T * MERGED * D,
        8 << 20,
    )


def head_masks(rows):
    lane = lax.broadcasted_iota(jnp.int32, (rows, 128), 1)
    return [(lane >= 32 * place) & (lane < 32 * place + 32) for place in range(4)]


def spread_heads(value, masks):
    zero = jnp.zeros_like(value)
    return jnp.concatenate([jnp.where(mask, value, zero) for mask in masks], axis=0)


def fold_heads(value, masks):
    total = jnp.zeros((ROWS, 128), F32)
    for place, mask in enumerate(masks):
        total = jnp.where(mask, value[place * ROWS : (place + 1) * ROWS], total)
    return total


def unfold(ref):
    value = ref[...].reshape(YX, 16, D)
    parts = [value[:, :, 256 * group : 256 * group + 256] for group in range(4)]
    return jnp.stack(parts, axis=1).reshape(D, 256)


def attn_kernel(level, *refs):
    (core_ref, x_ref), refs = refs[:2], refs[2:]
    if level:
        (halo_ref, own_ref, recv_ref), refs = refs[:3], refs[3:]
    (
        gain_ref, bias_ref, wq_ref, wk_ref, wv_ref, wp_ref, qb_ref, vb_ref, table_ref, mask_ref,
        shift_ref,
    ), refs = refs[:11], refs[11:]
    (
        mid_ref, a_ref, q_ref, k_ref, v_ref, probs_ref, mine_ref, other_ref,
    ), refs = refs[:8], refs[8:]
    step = pl.program_id(0)

    @pl.when(step == 0)
    def _():
        value = x_ref[...]
        if level:
            value = select_rows(own_ref[...], value) + dot(recv_ref[...], halo_ref[...])
            refs[0][...] = value
        center, spread = norm_stats(value)
        a_ref[...] = (center * spread * gain_ref[...] + bias_ref[...]).astype(BF)
        mid_ref[...] = value + shift_ref[...]

    a = a_ref[...]
    q = (dot(a, unfold(wq_ref)) + qb_ref[...]).astype(BF)
    k = dot(a, unfold(wk_ref)).astype(BF)
    v = (dot(a, unfold(wv_ref)) + vb_ref[...]).astype(BF)
    q_ref[...] = q
    k_ref[...] = k
    v_ref[...] = v
    masks = head_masks(ROWS)
    halves = []
    for half in range(2):
        lanes = slice(half * 128, half * 128 + 128)
        table = table_ref[4 * half : 4 * half + 4]
        parts = []
        for w in range(2):
            rows = slice(w * ROWS, (w + 1) * ROWS)
            raw = dot_nt(spread_heads(q[rows, lanes], masks), k[rows, lanes]) * SCALE
            scores = raw.reshape(4, ROWS, ROWS) + table + mask_ref[w][None]
            top = jnp.max(scores, axis=-1, keepdims=True)
            terms = jnp.exp(scores - top)
            probs = (terms / jnp.sum(terms, axis=-1, keepdims=True)).astype(BF)
            probs_ref[0, w, 4 * half : 4 * half + 4] = probs
            mixed = dot(probs.reshape(4 * ROWS, ROWS), v[rows, lanes])
            parts.append(fold_heads(mixed, masks))
        halves.append(jnp.concatenate(parts, axis=0).astype(BF))

    def set_mine(part):
        mine_ref[...] = part

    def set_other(part):
        other_ref[...] = part

    put_halves(core_ref, set_mine, set_other, *halves)
    heads = jnp.concatenate(halves, axis=1)
    mid_ref[...] += dot(heads, wp_ref[...].reshape(256, D))


def unit_spec(unit):
    return pl.BlockSpec((YX, 1, 16, D), lambda step, core: (step, unit, 0, 0))


def attn_forward(core, level, state, halo, weights, small, table, mask):
    gain, bias, qbias, vbias, shift = small
    unit = 8 + 4 * level
    args = [state]
    specs = [whole((T, D))]
    if level:
        args += [halo, const(OWN), const(RECV)]
        specs += [whole((SEND, D)), whole((T, T)), whole((T, SEND))]
    args += [gain, bias, weights, weights, weights, weights, qbias, vbias, table, mask, shift]
    cols = pl.BlockSpec((1, 256), lambda step, core: (0, step))
    specs += [whole((1, D)), whole((1, D))] + [unit_spec(unit + place) for place in range(4)]
    specs += [
        cols,
        cols,
        pl.BlockSpec((8, ROWS, ROWS), lambda step, core: (step, 0, 0)),
        whole((2, ROWS, ROWS)),
        whole((1, D)),
    ]
    block = pl.BlockSpec((T, 256), lambda step, core: (0, step))
    half = pl.BlockSpec((T, 128), lambda step, core: (0, step))
    outs = [
        shape_of((T, D), F32),
        shape_of((T, D), BF),
        shape_of((T, D), BF),
        shape_of((T, D), BF),
        shape_of((T, D), BF),
        shape_of((TP, 2, 8, ROWS, ROWS), BF),
        shape_of((T, D // 2), BF),
        shape_of((T, D // 2), BF),
    ]
    out_specs = [
        whole((T, D)),
        whole((T, D)),
        block,
        block,
        block,
        pl.BlockSpec((1, 2, 8, ROWS, ROWS), lambda step, core: (step, 0, 0, 0, 0)),
        half,
        half,
    ]
    if level:
        outs.append(shape_of((T, D), F32))
        out_specs.append(whole((T, D)))
    return run(
        partial(attn_kernel, level), TP, core, args, specs, outs, out_specs, [], 8 * T * D * D, 24 << 20
    )


def quad_spec(unit):
    return pl.BlockSpec(
        (YX, 4, 16, D), lambda step, core: (lax.rem(core[1] + step, TP), unit, 0, 0)
    )


def wide_spec(rows):
    return pl.BlockSpec((rows, D), lambda step, core: (0, lax.rem(core[1] + step, TP)))


def half_spec():
    return pl.BlockSpec((T, 512), lambda step, core: (0, lax.rem(core[1] + step, TP)))


def gelu_parts(pre):
    phi = 0.5 + 0.5 * lax.erf(pre * (0.5**0.5))
    slope = phi + pre * ((2.0 * np.pi) ** -0.5 * jnp.exp(-0.5 * pre * pre))
    return (pre * phi).astype(BF), slope


def start_norm(mid_ref, gain_ref, bias_ref, shift_ref, c2_ref, total):
    value = mid_ref[...]
    center, spread = norm_stats(value)
    c2_ref[...] = (center * spread * gain_ref[...] + bias_ref[...]).astype(BF)
    total[...] = value + shift_ref[...]


def end_norm(mid_ref, gain_ref, grad, dmlp, upstream, dmid_ref, dattn_ref, rows_ref):
    center, spread = norm_stats(mid_ref[...])
    normed = center * spread
    dmid = grad + norm_back(upstream, normed, spread, gain_ref[...])
    dmid_ref[...] = dmid
    dattn = dmid.astype(BF)
    dattn_ref[...] = dattn
    rows_ref[0:1] = col_sum(upstream * normed)
    rows_ref[1:2] = col_sum(upstream)
    rows_ref[2:3] = col_sum(dmlp.astype(F32))
    rows_ref[3:4] = col_sum(dattn.astype(F32))


def put_parts(core_ref, mine_ref, other_ref, value):
    def set_mine(part):
        mine_ref[...] = part

    def set_other(part):
        other_ref[...] = part

    put_halves(core_ref, set_mine, set_other, value[:, :512], value[:, 512:])


def put_quarter(refs, value):
    for ahead, ref in enumerate(refs):

        @pl.when(pl.program_id(0) == ahead)
        def _(ref=ref):
            ref[...] = value


def mlp_kernel(
    core_ref, mid_ref, gain_ref, bias_ref, w1_ref, w2_ref, b1_ref, b2_ref, place_ref,
    c2_ref, slope_ref, halo_ref, mine_ref, other_ref, next_ref, total,
):
    step = pl.program_id(0)

    @pl.when(step == 0)
    def _():
        start_norm(mid_ref, gain_ref, bias_ref, b2_ref, c2_ref, total)

    act, slope = gelu_parts(dot(c2_ref[...], w1_ref[...].reshape(D, D)) + b1_ref[...])
    slope_ref[...] = slope.astype(BF)
    put_parts(core_ref, mine_ref, other_ref, act)
    total[...] += dot(act, w2_ref[...].reshape(D, D))

    @pl.when(step == TP - 1)
    def _():
        value = total[...]
        halo_ref[...] = dot(place_ref[...], value.astype(BF)).astype(BF)
        next_ref[...] = value


def mlp_forward(core, mid, weights, small):
    gain, bias, b1, b2 = small
    return run(
        mlp_kernel,
        TP,
        core,
        (mid, gain, bias, weights, weights, b1, b2, const(SENT)),
        [
            whole((T, D)),
            whole((1, D)),
            whole((1, D)),
            quad_spec(0),
            quad_spec(1),
            wide_spec(1),
            whole((1, D)),
            whole((SEND, T)),
        ],
        [
            shape_of((T, D), BF),
            shape_of((T, FF), BF),
            shape_of((SEND, D), BF),
            shape_of((T, FF // 2), BF),
            shape_of((T, FF // 2), BF),
            shape_of((T, D), F32),
        ],
        [whole((T, D)), wide_spec(T), whole((SEND, D)), half_spec(), half_spec(), whole((T, D))],
        [pltpu.VMEM((T, D), F32)],
        4 * T * D * FF,
        24 << 20,
    )


def mlp_both_kernel(
    core_ref, mid_ref, gain_ref, bias_ref, w1_ref, w2_ref, b1_ref, b2_ref, place_ref, keep_ref,
    dx_ref, c2_ref, out_ref, one, two, three, four, dmid_ref, dattn_ref, db1_ref, rows_ref,
    mine_ref, other_ref, total, back,
):
    step = pl.program_id(0)

    @pl.when(step == 0)
    def _():
        start_norm(mid_ref, gain_ref, bias_ref, b2_ref, c2_ref, total)
        back[...] = jnp.zeros((T, D), F32)

    up = w1_ref[...].reshape(D, D)
    down = w2_ref[...].reshape(D, D)
    act, slope = gelu_parts(dot(c2_ref[...], up) + b1_ref[...])
    put_quarter((one, two, three, four), act)
    total[...] += dot(act, down)
    dpre = (dot_nt(dx_ref[...], down) * slope).astype(BF)
    db1_ref[...] = col_sum(dpre.astype(F32))
    put_parts(core_ref, mine_ref, other_ref, dpre)
    back[...] += dot_nt(dpre, up)

    @pl.when(step == TP - 1)
    def _():
        out_ref[...] = dot(place_ref[...], (total[...] * keep_ref[...]).astype(BF)).astype(BF)
        dmlp = dx_ref[...]
        end_norm(
            mid_ref, gain_ref, dmlp.astype(F32), dmlp, back[...], dmid_ref, dattn_ref, rows_ref
        )


def mlp_both(core, mid, weights, small, keep, dx):
    gain, bias, b1, b2 = small
    return run(
        mlp_both_kernel,
        TP,
        core,
        (mid, gain, bias, weights, weights, b1, b2, const(OUT), keep, dx),
        [
            whole((T, D)),
            whole((1, D)),
            whole((1, D)),
            quad_spec(0),
            quad_spec(1),
            wide_spec(1),
            whole((1, D)),
            whole((2 * TOK, T)),
            whole((T, 1)),
            whole((T, D)),
        ],
        [shape_of((T, D), BF), shape_of((2 * TOK, D), BF)]
        + [shape_of((T, D), BF)] * TP
        + [
            shape_of((T, D), F32),
            shape_of((T, D), BF),
            shape_of((1, FF), F32),
            shape_of((4, D), F32),
            shape_of((T, FF // 2), BF),
            shape_of((T, FF // 2), BF),
        ],
        [whole((T, D)), whole((2 * TOK, D))]
        + [whole((T, D))] * TP
        + [whole((T, D)), whole((T, D)), wide_spec(1), whole((4, D)), half_spec(), half_spec()],
        [pltpu.VMEM((T, D), F32), pltpu.VMEM((T, D), F32)],
        8 * T * D * FF,
        24 << 20,
    )


def mlp_back_kernel(
    core_ref, dx_ref, halo_ref, own_ref, sent_ref, mid_ref, gain_ref, w1_ref, w2_ref, slope_ref,
    dmid_ref, dmlp_ref, dattn_ref, db1_ref, rows_ref, one, two, three, four, total, grad,
):
    step = pl.program_id(0)

    @pl.when(step == 0)
    def _():
        value = select_rows_t(own_ref[...], dx_ref[...]) + dot_tn(sent_ref[...], halo_ref[...])
        grad[...] = value
        dmlp_ref[...] = value.astype(BF)
        total[...] = jnp.zeros((T, D), F32)

    dact = dot_nt(dmlp_ref[...], w2_ref[...].reshape(D, D))
    dpre = (dact * slope_ref[...].astype(F32)).astype(BF)
    db1_ref[...] = col_sum(dpre.astype(F32))
    put_quarter((one, two, three, four), dpre)
    total[...] += dot_nt(dpre, w1_ref[...].reshape(D, D))

    @pl.when(step == TP - 1)
    def _():
        end_norm(
            mid_ref, gain_ref, grad[...], dmlp_ref[...], total[...], dmid_ref, dattn_ref, rows_ref
        )


def select_rows_t(matrix, value):
    high = value.astype(BF)
    rest = value - high.astype(F32)
    mid = rest.astype(BF)
    low = (rest - mid.astype(F32)).astype(BF)
    return dot_tn(matrix, high) + dot_tn(matrix, mid) + dot_tn(matrix, low)


def mlp_backward(core, grad, halo, mid, gain, weights, slope):
    return run(
        mlp_back_kernel,
        TP,
        core,
        (grad, halo, const(OWN), const(SENT), mid, gain, weights, weights, slope),
        [
            whole((T, D)),
            whole((SEND, D)),
            whole((T, T)),
            whole((SEND, T)),
            whole((T, D)),
            whole((1, D)),
            quad_spec(0),
            quad_spec(1),
            wide_spec(T),
        ],
        [
            shape_of((T, D), F32),
            shape_of((T, D), BF),
            shape_of((T, D), BF),
            shape_of((1, FF), F32),
            shape_of((4, D), F32),
        ]
        + [shape_of((T, D), BF)] * TP,
        [whole((T, D)), whole((T, D)), whole((T, D)), wide_spec(1), whole((4, D))]
        + [whole((T, D))] * TP,
        [pltpu.VMEM((T, D), F32), pltpu.VMEM((T, D), F32)],
        4 * T * D * FF,
        24 << 20,
    )


def attn_back_kernel(level, *refs):
    (
        core_ref, dmid_ref, dattn_ref, x_ref, gain_ref, wq_ref, wk_ref, wv_ref, wp_ref,
        q_ref, k_ref, v_ref, probs_ref,
    ), refs = refs[:13], refs[13:]
    if level:
        (place_ref,), refs = refs[:1], refs[1:]
    (dx_ref, mine_ref, other_ref, pair_ref, sums_ref, rows_ref), refs = refs[:6], refs[6:]
    if level:
        (sent_ref,), refs = refs[:1], refs[1:]
    (total,) = refs
    step = pl.program_id(0)

    @pl.when(step == 0)
    def _():
        total[...] = jnp.zeros((T, D), F32)

    dheads = dot_nt(dattn_ref[...], wp_ref[...].reshape(256, D)).astype(BF)
    masks = head_masks(ROWS)
    dqs, dks, dvs = [], [], []
    for half in range(2):
        lanes = slice(half * 128, half * 128 + 128)
        dq_parts, dk_parts, dv_parts = [], [], []
        pairs = None
        for w in range(2):
            rows = slice(w * ROWS, (w + 1) * ROWS)
            rounded = probs_ref[0, w, 4 * half : 4 * half + 4].reshape(4 * ROWS, ROWS)
            probs = rounded.astype(F32)
            spread_out = spread_heads(dheads[rows, lanes], masks)
            dprobs = dot_nt(spread_out, v_ref[rows, lanes])
            dv_parts.append(dot_tn(rounded, spread_out))
            inner = jnp.sum(probs * dprobs, axis=-1, keepdims=True)
            dscores = (probs * (dprobs - inner)).astype(BF)
            wide = dscores.astype(F32)
            pairs = wide if pairs is None else pairs + wide
            dq_parts.append(fold_heads(dot(dscores, k_ref[rows, lanes]), masks))
            dk_parts.append(dot_tn(dscores, spread_heads(q_ref[rows, lanes], masks)))
        pair_ref[4 * half : 4 * half + 4] = pairs.reshape(4, ROWS, ROWS)
        dqs.append((jnp.concatenate(dq_parts, axis=0) * SCALE).astype(BF))
        dks.append((jnp.concatenate(dk_parts, axis=0) * SCALE).astype(BF))
        dvs.append(jnp.concatenate(dv_parts, axis=0).astype(BF))

    def set_mine(part):
        mine_ref[...] = part

    def set_other(part):
        other_ref[...] = part

    put_halves(
        core_ref,
        set_mine,
        set_other,
        jnp.concatenate([dqs[0], dks[0], dvs[0]], axis=1),
        jnp.concatenate([dqs[1], dks[1], dvs[1]], axis=1),
    )
    dq = jnp.concatenate(dqs, axis=1)
    dk = jnp.concatenate(dks, axis=1)
    dv = jnp.concatenate(dvs, axis=1)
    sums_ref[0:1] = col_sum(dq.astype(F32))
    sums_ref[1:2] = col_sum(dv.astype(F32))
    total[...] += (
        dot_nt(dq, unfold(wq_ref))
        + dot_nt(dk, unfold(wk_ref))
        + dot_nt(dv, unfold(wv_ref))
    )

    @pl.when(step == TP - 1)
    def _():
        center, spread = norm_stats(x_ref[...])
        normed = center * spread
        upstream = total[...]
        value = dmid_ref[...] + norm_back(upstream, normed, spread, gain_ref[...])
        dx_ref[...] = value
        rows_ref[0:1] = col_sum(upstream * normed)
        rows_ref[1:2] = col_sum(upstream)
        if level:
            sent_ref[...] = dot_tn(place_ref[...], value.astype(BF)).astype(BF)


def attn_backward(core, level, dmid, dattn, state, gain, weights, q, k, v, probs):
    unit = 8 + 4 * level
    block = pl.BlockSpec((T, 256), lambda step, core: (0, step))
    part = pl.BlockSpec((T, 384), lambda step, core: (0, step))
    args = [dmid, dattn, state, gain, weights, weights, weights, weights, q, k, v, probs]
    specs = [whole((T, D)), whole((T, D)), whole((T, D)), whole((1, D))]
    specs += [unit_spec(unit + place) for place in range(4)]
    specs += [
        block,
        block,
        block,
        pl.BlockSpec((1, 2, 8, ROWS, ROWS), lambda step, core: (step, 0, 0, 0, 0)),
    ]
    outs = [
        shape_of((T, D), F32),
        shape_of((T, 1536), BF),
        shape_of((T, 1536), BF),
        shape_of((32, ROWS, ROWS), F32),
        shape_of((2, D), F32),
        shape_of((2, D), F32),
    ]
    out_specs = [
        whole((T, D)),
        part,
        part,
        pl.BlockSpec((8, ROWS, ROWS), lambda step, core: (step, 0, 0)),
        pl.BlockSpec((2, 256), lambda step, core: (0, step)),
        whole((2, D)),
    ]
    if level:
        args.append(const(RECV))
        specs.append(whole((T, SEND)))
        outs.append(shape_of((SEND, D), BF))
        out_specs.append(whole((SEND, D)))
    return run(
        partial(attn_back_kernel, level),
        TP,
        core,
        args,
        specs,
        outs,
        out_specs,
        [pltpu.VMEM((T, D), F32)],
        8 * T * D * D,
        24 << 20,
    )


def weight_kernel(plan, *refs):
    refs, out_ref = refs[1:-1], refs[-1]
    place = 0
    column = 0
    for kind, size, count in plan:
        parts = [ref[...] for ref in refs[place : place + count]]
        if kind == "matrix":
            value = dot_tn(
                jnp.concatenate(parts[:2], axis=0), jnp.concatenate(parts[2:], axis=0)
            )
        else:
            value = sum(part.astype(F32) for part in parts)
        out_ref[:, 0, :, column : column + size] = value.astype(BF).reshape(YX, 64, size)
        column += size
        place += count


def weight_grads(core, items, sums):
    plan, args, specs = [], [], []
    for left, right in items:
        size = right[0].shape[1] // TP
        plan.append(("matrix", size, 4))
        args += [left[0], left[1], right[0], right[1]]
        block = pl.BlockSpec((T, size), lambda step, core: (0, step))
        specs += [whole((T, D)), whole((T, D)), block, block]
    for pieces in sums:
        plan.append(("sum", 128, len(pieces)))
        args += pieces
        specs += [pl.BlockSpec((D, 128), lambda step, core: (0, step))] * len(pieces)
    width = sum(size for unused, size, count in plan)
    return run(
        partial(weight_kernel, plan),
        TP,
        core,
        args,
        specs,
        shape_of((YX, TP, 64, width), BF),
        pl.BlockSpec((YX, 1, 64, width), lambda step, core: (0, step, 0, 0)),
        [],
        4 * T * D * width * TP,
        (2 * D * width * TP) + (8 << 20),
    )


def column_kernel(core_ref, *refs):
    lefts, rights, (other_ref, mine_ref) = refs[:TP], refs[TP : 2 * TP], refs[2 * TP :]
    left = jnp.concatenate([ref[...] for ref in lefts], axis=0)
    right = jnp.concatenate([ref[...] for ref in rights], axis=0)
    value = dot_tn(left, right).astype(BF)

    @pl.when(pl.program_id(0) == 0)
    def _():
        other_ref[...] = value

    @pl.when(pl.program_id(0) == 1)
    def _():
        mine_ref[...] = value


def column_grads(core, lefts, rights):
    half = pl.BlockSpec((T, 512), lambda step, core: (0, (core[0] + 1 + step) % 2))
    return run(
        column_kernel,
        2,
        core,
        list(lefts) + list(rights),
        [whole((T, D))] * TP + [half] * TP,
        [shape_of((D, 512), BF)] * 2,
        [whole((D, 512))] * 2,
        [],
        4 * T * D * 2048,
        8 << 20,
    )


def send_ahead(pieces):
    return [pieces[0]] + [
        lax.ppermute(pieces[step], "tp", [(i, (i + step) % TP) for i in range(TP)])
        for step in range(1, TP)
    ]


def send_all(value):
    return send_ahead([value] * TP)


def sum_quarters(value, column):
    pieces = [
        lax.dynamic_index_in_dim(value, (column + step) % TP, 0, keepdims=False)
        for step in range(TP)
    ]
    got = [piece.astype(F32) for piece in send_ahead(pieces)]
    return (got[0] + got[1]) + (got[2] + got[3])


def table_index():
    place = np.zeros((RELS, WIN * 190), np.float32)
    for row in range(WIN):
        for step in range(19):
            for col in range(WIN):
                place[(18 - step) * 19 + row - col + 9, row * 190 + step * WIN + col] = 1
    return place


PAIRS = table_index()


def spread_tables(tables):
    compact = jnp.dot(tables.reshape(64, RELS), jnp.asarray(PAIRS), precision=HIGH)
    compact = compact.reshape(2, 32, WIN, 190)
    rows = [compact[..., (9 - row) * WIN : (9 - row) * WIN + TOK] for row in range(WIN)]
    full = jnp.stack(rows, axis=2).reshape(2, 32, TOK, TOK)
    return jnp.pad(full, ((0, 0), (0, 0), (0, ROWS - TOK), (0, ROWS - TOK)))


def fold_tables(pairs):
    total = jnp.zeros((32, WIN, 190), F32)
    for row in range(WIN):
        low = (9 - row) * WIN
        total = total + jnp.pad(
            pairs[:, row * WIN : (row + 1) * WIN, :TOK], ((0, 0), (0, 0), (low, 90 - low))
        )
    return jnp.dot(total.reshape(32, -1), jnp.asarray(PAIRS.T), precision=HIGH)


def window_masks(level, valid, column):
    place = np.arange(ROWS)
    row = np.minimum(place // WIN, WIN - 1)
    col = jnp.asarray(place % WIN, jnp.int32)
    real = jnp.asarray(place < TOK)
    offset = SHIFT if level else 0
    rolled = column * WIN + col
    usable = (rolled + offset) % GW < valid
    masks = []
    for w in range(2):
        rolled_row = w * WIN + row
        row_region = (rolled_row >= GH - WIN).astype(np.int32) + (rolled_row >= GH - SHIFT)
        col_region = (rolled >= GW - WIN).astype(jnp.int32) + (rolled >= GW - SHIFT)
        region = jnp.asarray(row_region * 3, jnp.int32) + col_region
        allowed = usable[None, :]
        if level:
            allowed = allowed & (region[:, None] == region[None, :])
        mask = jnp.where(allowed, F32(0.0), F32(-100.0))
        mask = jnp.where(real[None, :], mask, F32(-1e30))
        masks.append(jnp.broadcast_to(mask, (ROWS, ROWS)))
    return jnp.stack(masks)


def gather_tp(value, place):
    parts = [value]
    for step in range(1, TP):
        parts.append(lax.ppermute(value, "tp", [(i, (i + step) % TP) for i in range(TP)]))
    stacked = jnp.stack(parts)
    order = (place - jnp.arange(TP)) % TP
    return [lax.dynamic_index_in_dim(stacked, order[i], 0, keepdims=False) for i in range(TP)]


def after(value, others):
    return lax.optimization_barrier((value, others))


def swap_core(value):
    return lax.ppermute(value, "core", [(0, 1), (1, 0)])


def sum_all(value):
    sent = value.astype(BF)
    value = sent.astype(F32) + swap_core(sent).astype(F32)
    for axis in ("x", "y", "tp"):
        sent = value.astype(BF)
        got = [
            lax.ppermute(sent, axis, [(i, (i + gap) % 4) for i in range(4)]).astype(F32)
            for gap in (1, 2, 3)
        ]
        value = (sent.astype(F32) + got[1]) + (got[0] + got[2])
    return value


def body(
    x3,
    res_group,
    merge_gain,
    merge_bias,
    merge_w,
    ln1_gain,
    ln1_bias,
    qkv_w,
    qv_bias,
    rel_table,
    proj_w,
    proj_bias,
    ln2_gain,
    ln2_bias,
    fc1_w,
    fc1_bias,
    fc2_w,
    fc2_bias,
    out_grad,
):
    core_at = lax.axis_index("core")
    chip_at = lax.axis_index("y") * 4 + lax.axis_index("x")
    column = lax.axis_index("tp")
    core = jnp.stack([core_at, column]).astype(jnp.int32)

    piece, late_piece = pack_weights(
        jnp.stack([chip_at, core_at]).astype(jnp.int32),
        fc1_w,
        fc2_w,
        jnp.swapaxes(qkv_w, 1, 2),
        proj_w,
        merge_w.reshape(512, D),
    )
    weights = lax.all_gather(piece.reshape(-1, D), GATHER_AXES, axis=0, tiled=True)
    weights = weights.reshape(64, UNITS, 16, D)
    late_weights = lax.all_gather(late_piece.reshape(-1, D), GATHER_AXES, axis=0, tiled=True)
    late_weights = late_weights.reshape(64, 8, 16, D)

    pages = lax.all_to_all(x3, PAGE_AXES, split_axis=1, concat_axis=0, tiled=True)
    tiles = pages.reshape(GH, TP, WIN, 512).transpose(1, 0, 2, 3).reshape(TP * 2 * TOK, 512)
    parts = lax.all_to_all(tiles, "tp", split_axis=0, concat_axis=0, tiled=True)
    parts = parts.reshape(TP, 2 * TOK, 512)

    packed = jnp.concatenate(
        [
            merge_gain.reshape(-1),
            merge_bias.reshape(-1),
            qv_bias.reshape(-1),
            fc1_bias.reshape(-1),
            rel_table.reshape(-1),
            jnp.zeros((10240 - 9872,), F32),
        ]
    ).reshape(80, 128)
    quarters = [part.reshape(-1) for part in gather_tp(packed, column)]

    def joined(low, shape, axis):
        size = int(np.prod(shape))
        return jnp.concatenate([part[low : low + size].reshape(shape) for part in quarters], axis)

    merge_gain_all = joined(0, (1, 512), 0)
    merge_bias_all = joined(512, (1, 512), 0)
    qv_bias_all = joined(1024, (2, 2, 256), 2)
    fc1_bias_all = joined(2048, (2, 1024), 1)
    tables = spread_tables(joined(4096, (2, 8, RELS), 1))
    tables = [tables[0], tables[1]]

    valid = (res_group[0] + 1) * WIN
    masks = [window_masks(level, valid, column) for level in range(2)]
    spot = np.arange(T) % ROWS
    keep = ((column * WIN + SHIFT + jnp.asarray(spot % WIN, jnp.int32)) % GW < valid) & jnp.asarray(
        spot < TOK
    )
    keep = keep.astype(F32)[:, None]
    page_keep = (jnp.asarray(np.arange(GW), jnp.int32) < valid).astype(BF)[None, :, None]
    tiles = jnp.roll(out_grad[0] * page_keep, (-SHIFT, -SHIFT), (0, 1))
    tiles = tiles.reshape(2, WIN, TP, WIN, D).transpose(2, 0, 1, 3, 4).reshape(TP, 2, TOK, D)
    tiles = jnp.pad(tiles, ((0, 0), (0, 0), (0, ROWS - TOK), (0, 0))).reshape(TP, T, D)
    tiles = [
        lax.dynamic_index_in_dim(tiles, (column + TP - back) % TP, 0, keepdims=False)
        for back in range(TP)
    ]

    weights, (tables, masks, tiles, keep, parts) = after(
        weights, (tables, masks, tiles, keep, parts)
    )
    state, merged_mine, merged_other = merge_forward(
        core, parts, merge_gain_all, merge_bias_all, weights
    )
    halo = None
    pending = [swap_core(merged_other)]
    for level in range(2):
        small = (
            ln1_gain[level : level + 1],
            ln1_bias[level : level + 1],
            qv_bias_all[level, 0:1],
            qv_bias_all[level, 1:2],
            proj_bias[level : level + 1],
        )
        got = attn_forward(
            core, level, state, halo, weights, small, tables[level], masks[level]
        )
        mid, a, q, k, v, probs, heads_mine, heads_other = got[:8]
        start = got[8] if level else state
        mid, pending = after(mid, pending)
        small = (
            ln2_gain[level : level + 1],
            ln2_bias[level : level + 1],
            fc1_bias_all[level : level + 1],
            fc2_bias[level : level + 1],
        )
        if level:
            got = mlp_both(core, mid, late_weights, small, keep, tiles[0])
            c2, extra, *acts = got[:6]
            dmid, dattn, db1, rows_two, dpre_mine, dpre_other = got[6:]
            dattn, (a_zero, heads_zero, c2_all, a_sent, heads_sent) = after(
                dattn, (*pending, c2_all, a, heads_other)
            )
        else:
            swapped = [swap_core(a), swap_core(heads_other)]
            c2, slope, halo, act_mine, act_other, state = mlp_forward(core, mid, weights, small)
            (merged_got,) = pending
            pending = swapped
            kept = (start, mid, a, q, k, v, probs, slope, c2, heads_mine)
            halo = lax.ppermute(halo, "tp", [((i + 1) % TP, i) for i in range(TP)])
            halo, c2 = lax.optimization_barrier((halo, c2))
            c2_all = send_all(c2)
    acts = send_ahead(acts)
    a_got, heads_got, dpre_got, dattn_got, c2_got = [
        swap_core(value) for value in (a_sent, heads_sent, dpre_other, dattn, c2)
    ]

    sums = [None, None]
    got = attn_backward(core, 1, dmid, dattn, start, ln1_gain[1:2], weights, q, k, v, probs)
    grad, mixed_mine, mixed_other, pairs, dqv, rows_one, sent = got
    sent, (a_got, heads_got, dpre_got, dattn_got, c2_got) = after(
        sent, (a_got, heads_got, dpre_got, dattn_got, c2_got)
    )
    halo = lax.ppermute(sent, "tp", [(i, (i + 1) % TP) for i in range(TP)])
    mixed_got = swap_core(mixed_other)
    sums[1] = (db1, rows_two, dqv, rows_one, pairs)
    items = [
        ((c2, c2_got), (dpre_mine, dpre_got)),
        ((a, a_got), (mixed_mine, mixed_got)),
        ((dattn, dattn_got), (heads_mine, heads_got)),
    ]
    late = weight_grads(core, items, [])
    late, halo = lax.optimization_barrier((late, halo))
    late = lax.psum_scatter(late, CHIP_AXES, scatter_dimension=0, tiled=True)
    late = lax.optimization_barrier(late)[0]

    start, mid, a, q, k, v, probs, slope, c2, heads_mine = kept
    halo, act_other = lax.optimization_barrier((halo, act_other))
    act_got = swap_core(act_other)
    got = mlp_backward(core, grad, halo, mid, ln2_gain[0:1], weights, slope)
    dmid, dmlp, dattn, db1, rows_two = got[:5]
    dattn, (dpre, act_got, acts, tiles) = after(dattn, (list(got[5:]), act_got, acts, tiles))
    dpre = send_ahead(dpre)
    got = attn_backward(core, 0, dmid, dattn, start, ln1_gain[0:1], weights, q, k, v, probs)
    grad, mixed_mine, mixed_other, pairs, dqv, rows_one = got
    sums[0] = (db1, rows_two, dqv, rows_one, pairs)
    grad, dattn_sent = lax.optimization_barrier((grad, dattn))
    mixed_got, dattn_got = [swap_core(value) for value in (mixed_other, dattn_sent)]
    first, dm, dgain, dbias = merge_backward(core, parts, merge_gain_all, weights, grad)
    last_other, last_mine = column_grads(core, tiles, acts)
    first, (dpre, dmlp_sent, last_other) = after(first, (dpre, dmlp, last_other))
    first_got, dmlp_got = swap_core(first), swap_core(dmlp_sent)
    up_other, up_mine = column_grads(core, c2_all, dpre)
    items = [
        ((a, a_zero), (mixed_mine, mixed_got)),
        ((dattn, dattn_got), (heads_mine, heads_zero)),
        ((first, first_got), (merged_mine, merged_got)),
        ((dmlp, dmlp_got), (act_mine, act_got)),
    ]
    early = weight_grads(
        core, items, [[up_mine, swap_core(up_other)], [last_mine, swap_core(last_other)]]
    )
    early, (extra, sums, dgain, dbias) = after(early, (extra, sums, dgain, dbias))
    early = lax.psum_scatter(early, CHIP_AXES, scatter_dimension=0, tiled=True)
    early = lax.optimization_barrier(early)[0]

    tiles_out = jnp.stack(gather_tp(extra, column)).reshape(TP, GH, WIN, D)
    output = jnp.roll(tiles_out.transpose(1, 0, 2, 3).reshape(GH, GW, D), SHIFT, 1)
    output = output.astype(F32)[None]
    back = lax.all_to_all(
        dm.reshape(TP * 2 * TOK, 512), "tp", split_axis=0, concat_axis=0, tiled=True
    )
    back = back.reshape(TP, GH, WIN, 512).transpose(1, 0, 2, 3).reshape(800, 1, 4, 128)
    grad_x3 = lax.all_to_all(back, PAGE_AXES, split_axis=0, concat_axis=1, tiled=True).astype(F32)

    def both_cores(value):
        rows = value.reshape(2, 32, -1)
        kept_rows = lax.dynamic_index_in_dim(rows, core_at, 0, keepdims=False).astype(F32)
        sent_rows = lax.dynamic_index_in_dim(rows, 1 - core_at, 0, keepdims=False)
        got_rows = swap_core(sent_rows.astype(BF)).astype(F32)
        return (
            jnp.where(core_at == 0, kept_rows, got_rows),
            jnp.where(core_at == 0, got_rows, kept_rows),
        )

    def wide(halves, low, size):
        return jnp.concatenate([half[:, low : low + size] for half in halves], axis=1)

    def finish(value, split):
        complete = value[..., split:].reshape(TP, 64, -1, 128).transpose(1, 2, 0, 3)
        partial_sums = sum_quarters(value[..., :split], column)
        return both_cores(
            jnp.concatenate([partial_sums, complete.reshape(64, -1).astype(F32)], axis=1)
        )

    late = both_cores(sum_quarters(late, column))
    early = finish(early, 1280)
    g_fc1 = jnp.stack([wide(early, 1280, 512), wide(late, 0, 512)])
    g_fc2 = jnp.stack([wide(early, 768, 512).T, wide(early, 1792, 512).T])
    pair = ((early, 0), (late, 512))
    g_qkv = jnp.stack(
        [jnp.stack([wide(half, low + 128 * s, 128) for s in range(3)], axis=1) for half, low in pair]
    )
    g_proj = jnp.stack([wide(half, low + 384, 128).T for half, low in pair])
    g_merge_w = wide(early, 512, 256).T.reshape(4, 128, 32)

    flat = []
    for level in range(2):
        db1, rows_two, dqv, rows_one, pairs = sums[level]
        flat += [rows_one, rows_two, dqv, db1, fold_tables(pairs)]
    flat += [dgain, dbias]
    flat = jnp.concatenate([item.reshape(-1) for item in flat])
    count = flat.shape[0]
    flat = jnp.pad(flat, (0, -count % 16384)).reshape(-1, 1024)
    flat = sum_all(flat).reshape(-1)
    page_at = chip_at * 2 + core_at

    def take(low, shape):
        return flat[low : low + int(np.prod(shape))].reshape(shape)

    def page_part(value):
        return lax.dynamic_slice_in_dim(value, page_at * 32, 32, value.ndim - 1)

    def tp_part(value, axis):
        size = value.shape[axis] // TP
        return lax.dynamic_slice_in_dim(value, column * size, size, axis)

    span = 2 * D + 4 * D + 2 * D + FF + 32 * RELS
    rows = [take(level * span, (6, D)) for level in range(2)]
    rows = page_part(jnp.stack(rows))
    dqv = tp_part(jnp.stack([take(level * span + 6 * D, (2, D)) for level in range(2)]), 2)
    db1 = tp_part(jnp.stack([take(level * span + 8 * D, (FF,)) for level in range(2)]), 1)
    table = tp_part(
        jnp.stack([take(level * span + 8 * D + FF, (32, RELS)) for level in range(2)]), 1
    )
    dgain = tp_part(take(2 * span, (TP, 512)), 0).reshape(4, 128)
    dbias = tp_part(take(2 * span + MERGED, (TP, 512)), 0).reshape(4, 128)
    return (
        output,
        grad_x3,
        dgain,
        dbias,
        g_merge_w,
        rows[:, 0],
        rows[:, 1],
        g_qkv,
        dqv,
        table,
        g_proj,
        rows[:, 5],
        rows[:, 2],
        rows[:, 3],
        g_fc1,
        db1,
        g_fc2,
        rows[:, 4],
    )


def solution(mesh):
    grid = Mesh(mesh.devices.reshape(4, 4, 2, TP), ("y", "x", "core", "tp"))
    page = PAGE_AXES
    return jax.shard_map(
        body,
        mesh=grid,
        in_specs=(
            P(page, None, None, "tp"),
            P(page),
            P(None, "tp"),
            P(None, "tp"),
            P(None, "tp", None),
            P(),
            P(),
            P(None, None, None, "tp"),
            P(None, None, "tp"),
            P(None, "tp", None),
            P(None, "tp", None),
            P(),
            P(),
            P(),
            P(None, None, "tp"),
            P(None, "tp"),
            P(None, "tp", None),
            P(),
            P(page, None, None, None),
        ),
        out_specs=(
            P(page, None, None, None),
            P(page, None, None, "tp"),
            P(None, "tp"),
            P(None, "tp"),
            P(None, "tp", page),
            P(None, page),
            P(None, page),
            P(None, page, None, "tp"),
            P(None, None, "tp"),
            P(None, "tp", None),
            P(None, "tp", page),
            P(None, page),
            P(None, page),
            P(None, page),
            P(None, page, "tp"),
            P(None, "tp"),
            P(None, "tp", page),
            P(None, page),
        ),
        check_vma=False,
    )
```

```python
from functools import partial

import jax
import jax.numpy as jnp
import numpy as np
from jax import lax
from jax.experimental import pallas as pl
from jax.experimental.pallas import tpu as pltpu
from jax.sharding import Mesh
from jax.sharding import PartitionSpec as P

D = 1024
FF = 4096
MERGED = 2048
WIN = 10
SHIFT = 5
GH = 20
GW = 40
RELS = 361
TOK = 100
ROWS = 112
T = 2 * ROWS
SEND = 112
EPS = 1e-05
SCALE = 32 ** (-0.5)
YX = 16
TP = 4
UNITS = 26
HIGH = lax.Precision.HIGHEST
BF = jnp.bfloat16
F32 = jnp.float32
PAGE_AXES = ("y", "x", "core")
CHIP_AXES = ("y", "x")
GATHER_AXES = ("tp", "y", "x", "core")
VMEM = 58 << 20


def row_at(row, col):
    return (row // WIN) * ROWS + (row % WIN) * WIN + col


def place_matrices():
    own = np.zeros((T, T), np.float32)
    recv = np.zeros((T, SEND), np.float32)
    send = np.zeros((SEND, T), np.float32)
    pack = np.zeros((2 * TOK, T), np.float32)
    out = np.zeros((2 * TOK, T), np.float32)
    for row in range(GH):
        for col in range(WIN):
            source = (row + SHIFT) % GH
            if col < SHIFT:
                own[row_at(row, col), row_at(source, col + SHIFT)] = 1
                send[row * SHIFT + col, row_at(row, col)] = 1
            else:
                recv[row_at(row, col), source * SHIFT + col - SHIFT] = 1
            pack[row * WIN + col, row_at(row, col)] = 1
            out[source * WIN + col, row_at(row, col)] = 1
    return own, recv, send, pack, out


OWN, RECV, SENT, PACK, OUT = place_matrices()


def const(matrix):
    return jnp.asarray(matrix, BF)


def dot(left, right):
    return lax.dot_general(left, right, (((1,), (0,)), ((), ())), preferred_element_type=F32)


def dot_nt(left, right):
    return lax.dot_general(left, right, (((1,), (1,)), ((), ())), preferred_element_type=F32)


def dot_tn(left, right):
    return lax.dot_general(left, right, (((0,), (0,)), ((), ())), preferred_element_type=F32)


def select_rows(matrix, value):
    high = value.astype(BF)
    rest = value - high.astype(F32)
    mid = rest.astype(BF)
    low = (rest - mid.astype(F32)).astype(BF)
    return dot(matrix, high) + dot(matrix, mid) + dot(matrix, low)


def norm_stats(value):
    mean = jnp.mean(value, axis=-1, keepdims=True)
    center = value - mean
    return center, lax.rsqrt(jnp.mean(center * center, axis=-1, keepdims=True) + EPS)


def norm_back(upstream, normed, spread, gain):
    scaled = upstream * gain
    inner = (
        scaled
        - jnp.mean(scaled, axis=-1, keepdims=True)
        - normed * jnp.mean(scaled * normed, axis=-1, keepdims=True)
    )
    return spread * inner


def col_sum(value):
    return jnp.sum(value, axis=0, keepdims=True)


def whole(shape):
    return pl.BlockSpec(shape, lambda step, core: (0,) * len(shape))


def shape_of(shape, dtype):
    return jax.ShapeDtypeStruct(shape, dtype)


def run(kernel, steps, core, args, in_specs, outs, out_specs, scratch, flops, moved):
    return pl.pallas_call(
        kernel,
        grid_spec=pltpu.PrefetchScalarGridSpec(
            num_scalar_prefetch=1,
            grid=(steps,),
            in_specs=in_specs,
            out_specs=out_specs,
            scratch_shapes=scratch,
        ),
        out_shape=outs,
        compiler_params=pltpu.CompilerParams(
            vmem_limit_bytes=VMEM, dimension_semantics=("arbitrary",)
        ),
        cost_estimate=pl.CostEstimate(flops=0, bytes_accessed=1024, transcendentals=0),
    )(core, *args)


def put_halves(core_ref, mine, other, low, high):
    @pl.when(core_ref[0] == 0)
    def _():
        mine(low)
        other(high)

    @pl.when(core_ref[0] != 0)
    def _():
        mine(high)
        other(low)


def pack_kernel(place_ref, up_ref, down_ref, mix_ref, proj_ref, merge_ref, out_ref, all_ref):
    for level in range(2):
        all_ref[8 * level : 8 * level + 4] = up_ref[level].reshape(4, 16, D)
        all_ref[8 * level + 4 : 8 * level + 8] = down_ref[level].reshape(4, 16, D)
        for part in range(3):
            for group in range(4):
                all_ref[16 + 4 * level + part, :, 256 * group : 256 * group + 256] = mix_ref[
                    level, part, 16 * group : 16 * group + 16
                ]
        all_ref[19 + 4 * level] = proj_ref[level]
    all_ref[24:26] = merge_ref[...].reshape(2, 16, D)
    out_ref[...] = all_ref[pl.ds(place_ref[1] * 13, 13)]


def pack_weights(place, up, down, mix, proj, merge):
    return pl.pallas_call(
        pack_kernel,
        grid_spec=pltpu.PrefetchScalarGridSpec(
            num_scalar_prefetch=1,
            grid=(1,),
            in_specs=[
                pl.BlockSpec((2, 64, D), lambda step, place: (0, place[0], 0)),
                pl.BlockSpec((2, 64, D), lambda step, place: (0, place[0], 0)),
                pl.BlockSpec((2, 3, 64, 256), lambda step, place: (0, 0, place[0], 0)),
                pl.BlockSpec((2, 16, D), lambda step, place: (0, place[0], 0)),
                pl.BlockSpec((32, D), lambda step, place: (place[0], 0)),
            ],
            out_specs=whole((13, 16, D)),
            scratch_shapes=[pltpu.VMEM((UNITS, 16, D), BF)],
        ),
        out_shape=shape_of((13, 16, D), BF),
        compiler_params=pltpu.CompilerParams(vmem_limit_bytes=VMEM),
        cost_estimate=pl.CostEstimate(flops=0, bytes_accessed=1 << 20, transcendentals=0),
    )(place, up, down, mix, proj, merge)


def merge_stats(x_ref, pack_ref, full):
    total = jnp.zeros((T, 1), F32)
    for part in range(TP):
        rows = dot_tn(pack_ref[...], x_ref[part])
        full[part] = rows
        total = total + jnp.sum(rows, axis=-1, keepdims=True)
    mean = total / MERGED
    square = jnp.zeros((T, 1), F32)
    for part in range(TP):
        center = full[part] - mean
        square = square + jnp.sum(center * center, axis=-1, keepdims=True)
    return mean, lax.rsqrt(square / MERGED + EPS)


def merge_kernel(
    core_ref, x_ref, pack_ref, gain_ref, bias_ref, w_ref, out_ref, mine_ref, other_ref, full, stats
):
    step = pl.program_id(0)

    @pl.when(step == 0)
    def _():
        mean, spread = merge_stats(x_ref, pack_ref, full)
        stats[0] = mean
        stats[1] = spread

    normed = (full[step] - stats[0]) * stats[1]
    value = (normed * gain_ref[0] + bias_ref[0]).astype(BF)

    def set_mine(part):
        mine_ref[...] = part

    def set_other(part):
        other_ref[...] = part

    put_halves(core_ref, set_mine, set_other, value[:, :256], value[:, 256:])
    term = dot(value, w_ref[...].reshape(512, D))

    @pl.when(step == 0)
    def _():
        out_ref[...] = term

    @pl.when(step != 0)
    def _():
        out_ref[...] += term


def merge_forward(core, parts, gain, bias, weights):
    return run(
        merge_kernel,
        TP,
        core,
        (parts, const(PACK), gain.reshape(TP, 1, 512), bias.reshape(TP, 1, 512), weights),
        [
            whole((TP, 2 * TOK, 512)),
            whole((2 * TOK, T)),
            pl.BlockSpec((1, 1, 512), lambda step, core: (step, 0, 0)),
            pl.BlockSpec((1, 1, 512), lambda step, core: (step, 0, 0)),
            pl.BlockSpec((YX, 2, 16, D), lambda step, core: (step, 12, 0, 0)),
        ],
        [shape_of((T, D), F32), shape_of((T, D), BF), shape_of((T, D), BF)],
        [
            whole((T, D)),
            pl.BlockSpec((T, 256), lambda step, core: (0, step)),
            pl.BlockSpec((T, 256), lambda step, core: (0, step)),
        ],
        [pltpu.VMEM((TP, T, 512), F32), pltpu.VMEM((2, T, 1), F32)],
        2 * T * MERGED * D,
        8 << 20,
    )


def merge_back_kernel(
    core_ref, x_ref, pack_ref, gain_ref, w_ref, dx_ref,
    start_ref, dm_ref, gains_ref, biases_ref,
    full, stats, upstream,
):
    step = pl.program_id(0)

    @pl.when(step == 0)
    def _():
        mean, spread = merge_stats(x_ref, pack_ref, full)
        stats[0] = mean
        stats[1] = spread
        stats[2] = jnp.zeros((T, 1), F32)
        stats[3] = jnp.zeros((T, 1), F32)
        start_ref[...] = dx_ref[...].astype(BF)

    grad = dot_nt(start_ref[...], w_ref[...].reshape(512, D))
    normed = (full[step] - stats[0]) * stats[1]
    full[step] = normed
    gains_ref[0] = col_sum(grad * normed)
    biases_ref[0] = col_sum(grad)
    scaled = grad * gain_ref[0]
    upstream[step] = scaled
    stats[2] += jnp.sum(scaled, axis=-1, keepdims=True)
    stats[3] += jnp.sum(scaled * normed, axis=-1, keepdims=True)

    @pl.when(step == TP - 1)
    def _():
        for part in range(TP):
            value = stats[1] * (
                upstream[part] - stats[2] / MERGED - full[part] * (stats[3] / MERGED)
            )
            dm_ref[part] = dot(pack_ref[...], value.astype(BF)).astype(BF)


def merge_backward(core, parts, gain, weights, grad):
    return run(
        merge_back_kernel,
        TP,
        core,
        (parts, const(PACK), gain.reshape(TP, 1, 512), weights, grad),
        [
            whole((TP, 2 * TOK, 512)),
            whole((2 * TOK, T)),
            pl.BlockSpec((1, 1, 512), lambda step, core: (step, 0, 0)),
            pl.BlockSpec((YX, 2, 16, D), lambda step, core: (step, 12, 0, 0)),
            whole((T, D)),
        ],
        [
            shape_of((T, D), BF),
            shape_of((TP, 2 * TOK, 512), BF),
            shape_of((TP, 1, 512), F32),
            shape_of((TP, 1, 512), F32),
        ],
        [
            whole((T, D)),
            whole((TP, 2 * TOK, 512)),
            pl.BlockSpec((1, 1, 512), lambda step, core: (step, 0, 0)),
            pl.BlockSpec((1, 1, 512), lambda step, core: (step, 0, 0)),
        ],
        [pltpu.VMEM((TP, T, 512), F32), pltpu.VMEM((4, T, 1), F32), pltpu.VMEM((TP, T, 512), F32)],
        2 * T * MERGED * D,
        8 << 20,
    )


def head_masks(rows):
    lane = lax.broadcasted_iota(jnp.int32, (rows, 128), 1)
    return [(lane >= 32 * place) & (lane < 32 * place + 32) for place in range(4)]


def spread_heads(value, masks):
    zero = jnp.zeros_like(value)
    return jnp.concatenate([jnp.where(mask, value, zero) for mask in masks], axis=0)


def fold_heads(value, masks):
    total = jnp.zeros((ROWS, 128), F32)
    for place, mask in enumerate(masks):
        total = jnp.where(mask, value[place * ROWS : (place + 1) * ROWS], total)
    return total


def unfold(ref):
    value = ref[...].reshape(YX, 16, D)
    parts = [value[:, :, 256 * group : 256 * group + 256] for group in range(4)]
    return jnp.stack(parts, axis=1).reshape(D, 256)


def attn_kernel(level, *refs):
    (core_ref, x_ref), refs = refs[:2], refs[2:]
    if level:
        (halo_ref, own_ref, recv_ref), refs = refs[:3], refs[3:]
    (
        gain_ref, bias_ref, wq_ref, wk_ref, wv_ref, wp_ref, qb_ref, vb_ref, table_ref, mask_ref,
        shift_ref,
    ), refs = refs[:11], refs[11:]
    (
        mid_ref, a_ref, q_ref, k_ref, v_ref, probs_ref, mine_ref, other_ref,
    ), refs = refs[:8], refs[8:]
    step = pl.program_id(0)

    @pl.when(step == 0)
    def _():
        value = x_ref[...]
        if level:
            value = select_rows(own_ref[...], value) + dot(recv_ref[...], halo_ref[...])
            refs[0][...] = value
        center, spread = norm_stats(value)
        a_ref[...] = (center * spread * gain_ref[...] + bias_ref[...]).astype(BF)
        mid_ref[...] = value + shift_ref[...]

    a = a_ref[...]
    q = (dot(a, unfold(wq_ref)) + qb_ref[...]).astype(BF)
    k = dot(a, unfold(wk_ref)).astype(BF)
    v = (dot(a, unfold(wv_ref)) + vb_ref[...]).astype(BF)
    q_ref[...] = q
    k_ref[...] = k
    v_ref[...] = v
    masks = head_masks(ROWS)
    halves = []
    for half in range(2):
        lanes = slice(half * 128, half * 128 + 128)
        table = table_ref[4 * half : 4 * half + 4]
        parts = []
        for w in range(2):
            rows = slice(w * ROWS, (w + 1) * ROWS)
            raw = dot_nt(spread_heads(q[rows, lanes], masks), k[rows, lanes]) * SCALE
            scores = raw.reshape(4, ROWS, ROWS) + table + mask_ref[w][None]
            top = jnp.max(scores, axis=-1, keepdims=True)
            terms = jnp.exp(scores - top)
            probs = (terms / jnp.sum(terms, axis=-1, keepdims=True)).astype(BF)
            probs_ref[0, w, 4 * half : 4 * half + 4] = probs
            mixed = dot(probs.reshape(4 * ROWS, ROWS), v[rows, lanes])
            parts.append(fold_heads(mixed, masks))
        halves.append(jnp.concatenate(parts, axis=0).astype(BF))

    def set_mine(part):
        mine_ref[...] = part

    def set_other(part):
        other_ref[...] = part

    put_halves(core_ref, set_mine, set_other, *halves)
    heads = jnp.concatenate(halves, axis=1)
    mid_ref[...] += dot(heads, wp_ref[...].reshape(256, D))


def unit_spec(unit):
    return pl.BlockSpec((YX, 1, 16, D), lambda step, core: (step, unit, 0, 0))


def attn_forward(core, level, state, halo, weights, small, table, mask):
    gain, bias, qbias, vbias, shift = small
    unit = 16 + 4 * level
    args = [state]
    specs = [whole((T, D))]
    if level:
        args += [halo, const(OWN), const(RECV)]
        specs += [whole((SEND, D)), whole((T, T)), whole((T, SEND))]
    args += [gain, bias, weights, weights, weights, weights, qbias, vbias, table, mask, shift]
    cols = pl.BlockSpec((1, 256), lambda step, core: (0, step))
    specs += [whole((1, D)), whole((1, D))] + [unit_spec(unit + place) for place in range(4)]
    specs += [
        cols,
        cols,
        pl.BlockSpec((8, ROWS, ROWS), lambda step, core: (step, 0, 0)),
        whole((2, ROWS, ROWS)),
        whole((1, D)),
    ]
    block = pl.BlockSpec((T, 256), lambda step, core: (0, step))
    half = pl.BlockSpec((T, 128), lambda step, core: (0, step))
    outs = [
        shape_of((T, D), F32),
        shape_of((T, D), BF),
        shape_of((T, D), BF),
        shape_of((T, D), BF),
        shape_of((T, D), BF),
        shape_of((TP, 2, 8, ROWS, ROWS), BF),
        shape_of((T, D // 2), BF),
        shape_of((T, D // 2), BF),
    ]
    out_specs = [
        whole((T, D)),
        whole((T, D)),
        block,
        block,
        block,
        pl.BlockSpec((1, 2, 8, ROWS, ROWS), lambda step, core: (step, 0, 0, 0, 0)),
        half,
        half,
    ]
    if level:
        outs.append(shape_of((T, D), F32))
        out_specs.append(whole((T, D)))
    return run(
        partial(attn_kernel, level), TP, core, args, specs, outs, out_specs, [], 8 * T * D * D, 24 << 20
    )


def quad_spec(unit):
    return pl.BlockSpec(
        (YX, 4, 16, D), lambda step, core: (lax.rem(core[1] + step, TP), unit, 0, 0)
    )


def wide_spec(rows):
    return pl.BlockSpec((rows, D), lambda step, core: (0, lax.rem(core[1] + step, TP)))


def half_spec():
    return pl.BlockSpec((T, 512), lambda step, core: (0, lax.rem(core[1] + step, TP)))


def gelu_parts(pre):
    phi = 0.5 + 0.5 * lax.erf(pre * (0.5**0.5))
    slope = phi + pre * ((2.0 * np.pi) ** -0.5 * jnp.exp(-0.5 * pre * pre))
    return (pre * phi).astype(BF), slope


def start_norm(mid_ref, gain_ref, bias_ref, shift_ref, c2_ref, total):
    value = mid_ref[...]
    center, spread = norm_stats(value)
    c2_ref[...] = (center * spread * gain_ref[...] + bias_ref[...]).astype(BF)
    total[...] = value + shift_ref[...]


def end_norm(mid_ref, gain_ref, grad, dmlp, upstream, dmid_ref, dattn_ref, rows_ref):
    center, spread = norm_stats(mid_ref[...])
    normed = center * spread
    dmid = grad + norm_back(upstream, normed, spread, gain_ref[...])
    dmid_ref[...] = dmid
    dattn = dmid.astype(BF)
    dattn_ref[...] = dattn
    rows_ref[0:1] = col_sum(upstream * normed)
    rows_ref[1:2] = col_sum(upstream)
    rows_ref[2:3] = col_sum(dmlp.astype(F32))
    rows_ref[3:4] = col_sum(dattn.astype(F32))


def put_parts(core_ref, mine_ref, other_ref, value):
    def set_mine(part):
        mine_ref[...] = part

    def set_other(part):
        other_ref[...] = part

    put_halves(core_ref, set_mine, set_other, value[:, :512], value[:, 512:])


def put_quarter(refs, value):
    for ahead, ref in enumerate(refs):

        @pl.when(pl.program_id(0) == ahead)
        def _(ref=ref):
            ref[...] = value


def mlp_kernel(
    core_ref, mid_ref, gain_ref, bias_ref, w1_ref, w2_ref, b1_ref, b2_ref, place_ref,
    c2_ref, slope_ref, halo_ref, mine_ref, other_ref, next_ref, total,
):
    step = pl.program_id(0)

    @pl.when(step == 0)
    def _():
        start_norm(mid_ref, gain_ref, bias_ref, b2_ref, c2_ref, total)

    act, slope = gelu_parts(dot(c2_ref[...], w1_ref[...].reshape(D, D)) + b1_ref[...])
    slope_ref[...] = slope.astype(BF)
    put_parts(core_ref, mine_ref, other_ref, act)
    total[...] += dot(act, w2_ref[...].reshape(D, D))

    @pl.when(step == TP - 1)
    def _():
        value = total[...]
        halo_ref[...] = dot(place_ref[...], value.astype(BF)).astype(BF)
        next_ref[...] = value


def mlp_forward(core, mid, weights, small):
    gain, bias, b1, b2 = small
    return run(
        mlp_kernel,
        TP,
        core,
        (mid, gain, bias, weights, weights, b1, b2, const(SENT)),
        [
            whole((T, D)),
            whole((1, D)),
            whole((1, D)),
            quad_spec(0),
            quad_spec(1),
            wide_spec(1),
            whole((1, D)),
            whole((SEND, T)),
        ],
        [
            shape_of((T, D), BF),
            shape_of((T, FF), BF),
            shape_of((SEND, D), BF),
            shape_of((T, FF // 2), BF),
            shape_of((T, FF // 2), BF),
            shape_of((T, D), F32),
        ],
        [whole((T, D)), wide_spec(T), whole((SEND, D)), half_spec(), half_spec(), whole((T, D))],
        [pltpu.VMEM((T, D), F32)],
        4 * T * D * FF,
        24 << 20,
    )


def mlp_both_kernel(
    core_ref, mid_ref, gain_ref, bias_ref, w1_ref, w2_ref, b1_ref, b2_ref, place_ref, keep_ref,
    dx_ref, c2_ref, out_ref, one, two, three, four, dmid_ref, dattn_ref, db1_ref, rows_ref,
    mine_ref, other_ref, total, back,
):
    step = pl.program_id(0)

    @pl.when(step == 0)
    def _():
        start_norm(mid_ref, gain_ref, bias_ref, b2_ref, c2_ref, total)
        back[...] = jnp.zeros((T, D), F32)

    up = w1_ref[...].reshape(D, D)
    down = w2_ref[...].reshape(D, D)
    act, slope = gelu_parts(dot(c2_ref[...], up) + b1_ref[...])
    put_quarter((one, two, three, four), act)
    total[...] += dot(act, down)
    dpre = (dot_nt(dx_ref[...], down) * slope).astype(BF)
    db1_ref[...] = col_sum(dpre.astype(F32))
    put_parts(core_ref, mine_ref, other_ref, dpre)
    back[...] += dot_nt(dpre, up)

    @pl.when(step == TP - 1)
    def _():
        out_ref[...] = dot(place_ref[...], (total[...] * keep_ref[...]).astype(BF)).astype(BF)
        dmlp = dx_ref[...]
        end_norm(
            mid_ref, gain_ref, dmlp.astype(F32), dmlp, back[...], dmid_ref, dattn_ref, rows_ref
        )


def mlp_both(core, mid, weights, small, keep, dx):
    gain, bias, b1, b2 = small
    return run(
        mlp_both_kernel,
        TP,
        core,
        (mid, gain, bias, weights, weights, b1, b2, const(OUT), keep, dx),
        [
            whole((T, D)),
            whole((1, D)),
            whole((1, D)),
            quad_spec(2),
            quad_spec(3),
            wide_spec(1),
            whole((1, D)),
            whole((2 * TOK, T)),
            whole((T, 1)),
            whole((T, D)),
        ],
        [shape_of((T, D), BF), shape_of((2 * TOK, D), BF)]
        + [shape_of((T, D), BF)] * TP
        + [
            shape_of((T, D), F32),
            shape_of((T, D), BF),
            shape_of((1, FF), F32),
            shape_of((4, D), F32),
            shape_of((T, FF // 2), BF),
            shape_of((T, FF // 2), BF),
        ],
        [whole((T, D)), whole((2 * TOK, D))]
        + [whole((T, D))] * TP
        + [whole((T, D)), whole((T, D)), wide_spec(1), whole((4, D)), half_spec(), half_spec()],
        [pltpu.VMEM((T, D), F32), pltpu.VMEM((T, D), F32)],
        8 * T * D * FF,
        24 << 20,
    )


def mlp_back_kernel(
    core_ref, dx_ref, halo_ref, own_ref, sent_ref, mid_ref, gain_ref, w1_ref, w2_ref, slope_ref,
    dmid_ref, dmlp_ref, dattn_ref, db1_ref, rows_ref, one, two, three, four, total, grad,
):
    step = pl.program_id(0)

    @pl.when(step == 0)
    def _():
        value = select_rows_t(own_ref[...], dx_ref[...]) + dot_tn(sent_ref[...], halo_ref[...])
        grad[...] = value
        dmlp_ref[...] = value.astype(BF)
        total[...] = jnp.zeros((T, D), F32)

    dact = dot_nt(dmlp_ref[...], w2_ref[...].reshape(D, D))
    dpre = (dact * slope_ref[...].astype(F32)).astype(BF)
    db1_ref[...] = col_sum(dpre.astype(F32))
    put_quarter((one, two, three, four), dpre)
    total[...] += dot_nt(dpre, w1_ref[...].reshape(D, D))

    @pl.when(step == TP - 1)
    def _():
        end_norm(
            mid_ref, gain_ref, grad[...], dmlp_ref[...], total[...], dmid_ref, dattn_ref, rows_ref
        )


def select_rows_t(matrix, value):
    high = value.astype(BF)
    rest = value - high.astype(F32)
    mid = rest.astype(BF)
    low = (rest - mid.astype(F32)).astype(BF)
    return dot_tn(matrix, high) + dot_tn(matrix, mid) + dot_tn(matrix, low)


def mlp_backward(core, grad, halo, mid, gain, weights, slope):
    return run(
        mlp_back_kernel,
        TP,
        core,
        (grad, halo, const(OWN), const(SENT), mid, gain, weights, weights, slope),
        [
            whole((T, D)),
            whole((SEND, D)),
            whole((T, T)),
            whole((SEND, T)),
            whole((T, D)),
            whole((1, D)),
            quad_spec(0),
            quad_spec(1),
            wide_spec(T),
        ],
        [
            shape_of((T, D), F32),
            shape_of((T, D), BF),
            shape_of((T, D), BF),
            shape_of((1, FF), F32),
            shape_of((4, D), F32),
        ]
        + [shape_of((T, D), BF)] * TP,
        [whole((T, D)), whole((T, D)), whole((T, D)), wide_spec(1), whole((4, D))]
        + [whole((T, D))] * TP,
        [pltpu.VMEM((T, D), F32), pltpu.VMEM((T, D), F32)],
        4 * T * D * FF,
        24 << 20,
    )


def attn_back_kernel(level, *refs):
    (
        core_ref, dmid_ref, dattn_ref, x_ref, gain_ref, wq_ref, wk_ref, wv_ref, wp_ref,
        q_ref, k_ref, v_ref, probs_ref,
    ), refs = refs[:13], refs[13:]
    if level:
        (place_ref,), refs = refs[:1], refs[1:]
    (dx_ref, mine_ref, other_ref, pair_ref, sums_ref, rows_ref), refs = refs[:6], refs[6:]
    if level:
        (sent_ref,), refs = refs[:1], refs[1:]
    (total,) = refs
    step = pl.program_id(0)

    @pl.when(step == 0)
    def _():
        total[...] = jnp.zeros((T, D), F32)

    dheads = dot_nt(dattn_ref[...], wp_ref[...].reshape(256, D)).astype(BF)
    masks = head_masks(ROWS)
    dqs, dks, dvs = [], [], []
    for half in range(2):
        lanes = slice(half * 128, half * 128 + 128)
        dq_parts, dk_parts, dv_parts = [], [], []
        pairs = None
        for w in range(2):
            rows = slice(w * ROWS, (w + 1) * ROWS)
            rounded = probs_ref[0, w, 4 * half : 4 * half + 4].reshape(4 * ROWS, ROWS)
            probs = rounded.astype(F32)
            spread_out = spread_heads(dheads[rows, lanes], masks)
            dprobs = dot_nt(spread_out, v_ref[rows, lanes])
            dv_parts.append(dot_tn(rounded, spread_out))
            inner = jnp.sum(probs * dprobs, axis=-1, keepdims=True)
            dscores = (probs * (dprobs - inner)).astype(BF)
            wide = dscores.astype(F32)
            pairs = wide if pairs is None else pairs + wide
            dq_parts.append(fold_heads(dot(dscores, k_ref[rows, lanes]), masks))
            dk_parts.append(dot_tn(dscores, spread_heads(q_ref[rows, lanes], masks)))
        pair_ref[4 * half : 4 * half + 4] = pairs.reshape(4, ROWS, ROWS)
        dqs.append((jnp.concatenate(dq_parts, axis=0) * SCALE).astype(BF))
        dks.append((jnp.concatenate(dk_parts, axis=0) * SCALE).astype(BF))
        dvs.append(jnp.concatenate(dv_parts, axis=0).astype(BF))

    def set_mine(part):
        mine_ref[...] = part

    def set_other(part):
        other_ref[...] = part

    put_halves(
        core_ref,
        set_mine,
        set_other,
        jnp.concatenate([dqs[0], dks[0], dvs[0]], axis=1),
        jnp.concatenate([dqs[1], dks[1], dvs[1]], axis=1),
    )
    dq = jnp.concatenate(dqs, axis=1)
    dk = jnp.concatenate(dks, axis=1)
    dv = jnp.concatenate(dvs, axis=1)
    sums_ref[0:1] = col_sum(dq.astype(F32))
    sums_ref[1:2] = col_sum(dv.astype(F32))
    total[...] += (
        dot_nt(dq, unfold(wq_ref))
        + dot_nt(dk, unfold(wk_ref))
        + dot_nt(dv, unfold(wv_ref))
    )

    @pl.when(step == TP - 1)
    def _():
        center, spread = norm_stats(x_ref[...])
        normed = center * spread
        upstream = total[...]
        value = dmid_ref[...] + norm_back(upstream, normed, spread, gain_ref[...])
        dx_ref[...] = value
        rows_ref[0:1] = col_sum(upstream * normed)
        rows_ref[1:2] = col_sum(upstream)
        if level:
            sent_ref[...] = dot_tn(place_ref[...], value.astype(BF)).astype(BF)


def attn_backward(core, level, dmid, dattn, state, gain, weights, q, k, v, probs):
    unit = 16 + 4 * level
    block = pl.BlockSpec((T, 256), lambda step, core: (0, step))
    part = pl.BlockSpec((T, 384), lambda step, core: (0, step))
    args = [dmid, dattn, state, gain, weights, weights, weights, weights, q, k, v, probs]
    specs = [whole((T, D)), whole((T, D)), whole((T, D)), whole((1, D))]
    specs += [unit_spec(unit + place) for place in range(4)]
    specs += [
        block,
        block,
        block,
        pl.BlockSpec((1, 2, 8, ROWS, ROWS), lambda step, core: (step, 0, 0, 0, 0)),
    ]
    outs = [
        shape_of((T, D), F32),
        shape_of((T, 1536), BF),
        shape_of((T, 1536), BF),
        shape_of((32, ROWS, ROWS), F32),
        shape_of((2, D), F32),
        shape_of((2, D), F32),
    ]
    out_specs = [
        whole((T, D)),
        part,
        part,
        pl.BlockSpec((8, ROWS, ROWS), lambda step, core: (step, 0, 0)),
        pl.BlockSpec((2, 256), lambda step, core: (0, step)),
        whole((2, D)),
    ]
    if level:
        args.append(const(RECV))
        specs.append(whole((T, SEND)))
        outs.append(shape_of((SEND, D), BF))
        out_specs.append(whole((SEND, D)))
    return run(
        partial(attn_back_kernel, level),
        TP,
        core,
        args,
        specs,
        outs,
        out_specs,
        [pltpu.VMEM((T, D), F32)],
        8 * T * D * D,
        24 << 20,
    )


def weight_kernel(plan, *refs):
    refs, out_ref = refs[1:-1], refs[-1]
    place = 0
    column = 0
    for kind, size, count in plan:
        parts = [ref[...] for ref in refs[place : place + count]]
        if kind == "matrix":
            value = dot_tn(
                jnp.concatenate(parts[:2], axis=0), jnp.concatenate(parts[2:], axis=0)
            )
        else:
            value = sum(part.astype(F32) for part in parts)
        out_ref[:, 0, :, column : column + size] = value.astype(BF).reshape(YX, 64, size)
        column += size
        place += count


def weight_grads(core, items, sums):
    plan, args, specs = [], [], []
    for left, right in items:
        size = right[0].shape[1] // TP
        plan.append(("matrix", size, 4))
        args += [left[0], left[1], right[0], right[1]]
        block = pl.BlockSpec((T, size), lambda step, core: (0, step))
        specs += [whole((T, D)), whole((T, D)), block, block]
    for pieces in sums:
        plan.append(("sum", 128, len(pieces)))
        args += pieces
        specs += [pl.BlockSpec((D, 128), lambda step, core: (0, step))] * len(pieces)
    width = sum(size for unused, size, count in plan)
    return run(
        partial(weight_kernel, plan),
        TP,
        core,
        args,
        specs,
        shape_of((YX, TP, 64, width), BF),
        pl.BlockSpec((YX, 1, 64, width), lambda step, core: (0, step, 0, 0)),
        [],
        4 * T * D * width * TP,
        (2 * D * width * TP) + (8 << 20),
    )


def column_kernel(core_ref, *refs):
    lefts, rights, (other_ref, mine_ref) = refs[:TP], refs[TP : 2 * TP], refs[2 * TP :]
    left = jnp.concatenate([ref[...] for ref in lefts], axis=0)
    right = jnp.concatenate([ref[...] for ref in rights], axis=0)
    value = dot_tn(left, right).astype(BF)

    @pl.when(pl.program_id(0) == 0)
    def _():
        other_ref[...] = value

    @pl.when(pl.program_id(0) == 1)
    def _():
        mine_ref[...] = value


def column_grads(core, lefts, rights):
    half = pl.BlockSpec((T, 512), lambda step, core: (0, (core[0] + 1 + step) % 2))
    return run(
        column_kernel,
        2,
        core,
        list(lefts) + list(rights),
        [whole((T, D))] * TP + [half] * TP,
        [shape_of((D, 512), BF)] * 2,
        [whole((D, 512))] * 2,
        [],
        4 * T * D * 2048,
        8 << 20,
    )


def send_ahead(pieces):
    return [pieces[0]] + [
        lax.ppermute(pieces[step], "tp", [(i, (i + step) % TP) for i in range(TP)])
        for step in range(1, TP)
    ]


def send_all(value):
    return send_ahead([value] * TP)


def sum_quarters(value, column):
    pieces = [
        lax.dynamic_index_in_dim(value, (column + step) % TP, 0, keepdims=False)
        for step in range(TP)
    ]
    got = [piece.astype(F32) for piece in send_ahead(pieces)]
    return (got[0] + got[1]) + (got[2] + got[3])


def table_index():
    place = np.zeros((RELS, WIN * 190), np.float32)
    for row in range(WIN):
        for step in range(19):
            for col in range(WIN):
                place[(18 - step) * 19 + row - col + 9, row * 190 + step * WIN + col] = 1
    return place


PAIRS = table_index()


def spread_tables(tables):
    compact = jnp.dot(tables.reshape(64, RELS), jnp.asarray(PAIRS), precision=HIGH)
    compact = compact.reshape(2, 32, WIN, 190)
    rows = [compact[..., (9 - row) * WIN : (9 - row) * WIN + TOK] for row in range(WIN)]
    full = jnp.stack(rows, axis=2).reshape(2, 32, TOK, TOK)
    return jnp.pad(full, ((0, 0), (0, 0), (0, ROWS - TOK), (0, ROWS - TOK)))


def fold_tables(pairs):
    total = jnp.zeros((32, WIN, 190), F32)
    for row in range(WIN):
        low = (9 - row) * WIN
        total = total + jnp.pad(
            pairs[:, row * WIN : (row + 1) * WIN, :TOK], ((0, 0), (0, 0), (low, 90 - low))
        )
    return jnp.dot(total.reshape(32, -1), jnp.asarray(PAIRS.T), precision=HIGH)


def window_masks(level, valid, column):
    place = np.arange(ROWS)
    row = np.minimum(place // WIN, WIN - 1)
    col = jnp.asarray(place % WIN, jnp.int32)
    real = jnp.asarray(place < TOK)
    offset = SHIFT if level else 0
    rolled = column * WIN + col
    usable = (rolled + offset) % GW < valid
    masks = []
    for w in range(2):
        rolled_row = w * WIN + row
        row_region = (rolled_row >= GH - WIN).astype(np.int32) + (rolled_row >= GH - SHIFT)
        col_region = (rolled >= GW - WIN).astype(jnp.int32) + (rolled >= GW - SHIFT)
        region = jnp.asarray(row_region * 3, jnp.int32) + col_region
        allowed = usable[None, :]
        if level:
            allowed = allowed & (region[:, None] == region[None, :])
        mask = jnp.where(allowed, F32(0.0), F32(-100.0))
        mask = jnp.where(real[None, :], mask, F32(-1e30))
        masks.append(jnp.broadcast_to(mask, (ROWS, ROWS)))
    return jnp.stack(masks)


def gather_tp(value, place):
    parts = [value]
    for step in range(1, TP):
        parts.append(lax.ppermute(value, "tp", [(i, (i + step) % TP) for i in range(TP)]))
    stacked = jnp.stack(parts)
    order = (place - jnp.arange(TP)) % TP
    return [lax.dynamic_index_in_dim(stacked, order[i], 0, keepdims=False) for i in range(TP)]


def after(value, others):
    return lax.optimization_barrier((value, others))


def swap_core(value):
    return lax.ppermute(value, "core", [(0, 1), (1, 0)])


def sum_all(value):
    sent = value.astype(BF)
    value = sent.astype(F32) + swap_core(sent).astype(F32)
    for axis in ("x", "y", "tp"):
        sent = value.astype(BF)
        got = [
            lax.ppermute(sent, axis, [(i, (i + gap) % 4) for i in range(4)]).astype(F32)
            for gap in (1, 2, 3)
        ]
        value = (sent.astype(F32) + got[1]) + (got[0] + got[2])
    return value


def body(
    x3,
    res_group,
    merge_gain,
    merge_bias,
    merge_w,
    ln1_gain,
    ln1_bias,
    qkv_w,
    qv_bias,
    rel_table,
    proj_w,
    proj_bias,
    ln2_gain,
    ln2_bias,
    fc1_w,
    fc1_bias,
    fc2_w,
    fc2_bias,
    out_grad,
):
    core_at = lax.axis_index("core")
    chip_at = lax.axis_index("y") * 4 + lax.axis_index("x")
    column = lax.axis_index("tp")
    core = jnp.stack([core_at, column]).astype(jnp.int32)

    piece = pack_weights(
        jnp.stack([chip_at, core_at]).astype(jnp.int32),
        fc1_w,
        fc2_w,
        jnp.swapaxes(qkv_w, 1, 2),
        proj_w,
        merge_w.reshape(512, D),
    )
    weights = lax.all_gather(piece.reshape(-1, D), GATHER_AXES, axis=0, tiled=True)
    weights = weights.reshape(64, UNITS, 16, D)

    pages = lax.all_to_all(x3, PAGE_AXES, split_axis=1, concat_axis=0, tiled=True)
    tiles = pages.reshape(GH, TP, WIN, 512).transpose(1, 0, 2, 3).reshape(TP * 2 * TOK, 512)
    parts = lax.all_to_all(tiles, "tp", split_axis=0, concat_axis=0, tiled=True)
    parts = parts.reshape(TP, 2 * TOK, 512)

    packed = jnp.concatenate(
        [
            merge_gain.reshape(-1),
            merge_bias.reshape(-1),
            qv_bias.reshape(-1),
            fc1_bias.reshape(-1),
            rel_table.reshape(-1),
            jnp.zeros((10240 - 9872,), F32),
        ]
    ).reshape(80, 128)
    quarters = [part.reshape(-1) for part in gather_tp(packed, column)]

    def joined(low, shape, axis):
        size = int(np.prod(shape))
        return jnp.concatenate([part[low : low + size].reshape(shape) for part in quarters], axis)

    merge_gain_all = joined(0, (1, 512), 0)
    merge_bias_all = joined(512, (1, 512), 0)
    qv_bias_all = joined(1024, (2, 2, 256), 2)
    fc1_bias_all = joined(2048, (2, 1024), 1)
    tables = spread_tables(joined(4096, (2, 8, RELS), 1))
    tables = [tables[0], tables[1]]

    valid = (res_group[0] + 1) * WIN
    masks = [window_masks(level, valid, column) for level in range(2)]
    spot = np.arange(T) % ROWS
    keep = ((column * WIN + SHIFT + jnp.asarray(spot % WIN, jnp.int32)) % GW < valid) & jnp.asarray(
        spot < TOK
    )
    keep = keep.astype(F32)[:, None]
    page_keep = (jnp.asarray(np.arange(GW), jnp.int32) < valid).astype(BF)[None, :, None]
    tiles = jnp.roll(out_grad[0] * page_keep, (-SHIFT, -SHIFT), (0, 1))
    tiles = tiles.reshape(2, WIN, TP, WIN, D).transpose(2, 0, 1, 3, 4).reshape(TP, 2, TOK, D)
    tiles = jnp.pad(tiles, ((0, 0), (0, 0), (0, ROWS - TOK), (0, 0))).reshape(TP, T, D)
    tiles = [
        lax.dynamic_index_in_dim(tiles, (column + TP - back) % TP, 0, keepdims=False)
        for back in range(TP)
    ]

    weights, (tables, masks, tiles, keep, parts) = after(
        weights, (tables, masks, tiles, keep, parts)
    )
    state, merged_mine, merged_other = merge_forward(
        core, parts, merge_gain_all, merge_bias_all, weights
    )
    halo = None
    pending = [swap_core(merged_other)]
    for level in range(2):
        small = (
            ln1_gain[level : level + 1],
            ln1_bias[level : level + 1],
            qv_bias_all[level, 0:1],
            qv_bias_all[level, 1:2],
            proj_bias[level : level + 1],
        )
        got = attn_forward(
            core, level, state, halo, weights, small, tables[level], masks[level]
        )
        mid, a, q, k, v, probs, heads_mine, heads_other = got[:8]
        start = got[8] if level else state
        mid, pending = after(mid, pending)
        small = (
            ln2_gain[level : level + 1],
            ln2_bias[level : level + 1],
            fc1_bias_all[level : level + 1],
            fc2_bias[level : level + 1],
        )
        if level:
            got = mlp_both(core, mid, weights, small, keep, tiles[0])
            c2, extra, *acts = got[:6]
            dmid, dattn, db1, rows_two, dpre_mine, dpre_other = got[6:]
            dattn, (a_zero, heads_zero, c2_all, a_got, heads_got) = after(
                dattn, (*pending, c2_all, swap_core(a), swap_core(heads_other))
            )
        else:
            swapped = [swap_core(a), swap_core(heads_other)]
            c2, slope, halo, act_mine, act_other, state = mlp_forward(core, mid, weights, small)
            (merged_got,) = pending
            pending = swapped
            kept = (start, mid, a, q, k, v, probs, slope, c2, heads_mine)
            halo = lax.ppermute(halo, "tp", [((i + 1) % TP, i) for i in range(TP)])
            halo, c2 = lax.optimization_barrier((halo, c2))
            c2_all = send_all(c2)
    acts = send_ahead(acts)
    dpre_got, dattn_got, c2_got = [swap_core(value) for value in (dpre_other, dattn, c2)]

    sums = [None, None]
    got = attn_backward(core, 1, dmid, dattn, start, ln1_gain[1:2], weights, q, k, v, probs)
    grad, mixed_mine, mixed_other, pairs, dqv, rows_one, sent = got
    sent, (dpre_got, dattn_got, c2_got) = after(sent, (dpre_got, dattn_got, c2_got))
    halo = lax.ppermute(sent, "tp", [(i, (i + 1) % TP) for i in range(TP)])
    mixed_got = swap_core(mixed_other)
    sums[1] = (db1, rows_two, dqv, rows_one, pairs)
    items = [
        ((c2, c2_got), (dpre_mine, dpre_got)),
        ((a, a_got), (mixed_mine, mixed_got)),
        ((dattn, dattn_got), (heads_mine, heads_got)),
    ]
    late = weight_grads(core, items, [])
    late, halo = lax.optimization_barrier((late, halo))
    late = lax.psum_scatter(late, CHIP_AXES, scatter_dimension=0, tiled=True)
    late = lax.optimization_barrier(late)[0]

    start, mid, a, q, k, v, probs, slope, c2, heads_mine = kept
    halo, act_other = lax.optimization_barrier((halo, act_other))
    act_got = swap_core(act_other)
    got = mlp_backward(core, grad, halo, mid, ln2_gain[0:1], weights, slope)
    dmid, dmlp, dattn, db1, rows_two = got[:5]
    dattn, (dpre, act_got, acts, tiles) = after(dattn, (list(got[5:]), act_got, acts, tiles))
    dpre = send_ahead(dpre)
    got = attn_backward(core, 0, dmid, dattn, start, ln1_gain[0:1], weights, q, k, v, probs)
    grad, mixed_mine, mixed_other, pairs, dqv, rows_one = got
    sums[0] = (db1, rows_two, dqv, rows_one, pairs)
    grad, dattn_sent = lax.optimization_barrier((grad, dattn))
    mixed_got, dattn_got = [swap_core(value) for value in (mixed_other, dattn_sent)]
    first, dm, dgain, dbias = merge_backward(core, parts, merge_gain_all, weights, grad)
    last_other, last_mine = column_grads(core, tiles, acts)
    first, (dpre, dmlp_sent, last_other) = after(first, (dpre, dmlp, last_other))
    first_got, dmlp_got = swap_core(first), swap_core(dmlp_sent)
    up_other, up_mine = column_grads(core, c2_all, dpre)
    items = [
        ((a, a_zero), (mixed_mine, mixed_got)),
        ((dattn, dattn_got), (heads_mine, heads_zero)),
        ((first, first_got), (merged_mine, merged_got)),
        ((dmlp, dmlp_got), (act_mine, act_got)),
    ]
    early = weight_grads(
        core, items, [[up_mine, swap_core(up_other)], [last_mine, swap_core(last_other)]]
    )
    early, (extra, sums, dgain, dbias) = after(early, (extra, sums, dgain, dbias))
    early = lax.psum_scatter(early, CHIP_AXES, scatter_dimension=0, tiled=True)
    early = lax.optimization_barrier(early)[0]

    tiles_out = jnp.stack(gather_tp(extra, column)).reshape(TP, GH, WIN, D)
    output = jnp.roll(tiles_out.transpose(1, 0, 2, 3).reshape(GH, GW, D), SHIFT, 1)
    output = output.astype(F32)[None]
    back = lax.all_to_all(
        dm.reshape(TP * 2 * TOK, 512), "tp", split_axis=0, concat_axis=0, tiled=True
    )
    back = back.reshape(TP, GH, WIN, 512).transpose(1, 0, 2, 3).reshape(800, 1, 4, 128)
    grad_x3 = lax.all_to_all(back, PAGE_AXES, split_axis=0, concat_axis=1, tiled=True).astype(F32)

    def both_cores(value):
        rows = value.reshape(2, 32, -1)
        kept_rows = lax.dynamic_index_in_dim(rows, core_at, 0, keepdims=False).astype(F32)
        sent_rows = lax.dynamic_index_in_dim(rows, 1 - core_at, 0, keepdims=False)
        got_rows = swap_core(sent_rows.astype(BF)).astype(F32)
        return (
            jnp.where(core_at == 0, kept_rows, got_rows),
            jnp.where(core_at == 0, got_rows, kept_rows),
        )

    def wide(halves, low, size):
        return jnp.concatenate([half[:, low : low + size] for half in halves], axis=1)

    def finish(value, split):
        complete = value[..., split:].reshape(TP, 64, -1, 128).transpose(1, 2, 0, 3)
        partial_sums = sum_quarters(value[..., :split], column)
        return both_cores(
            jnp.concatenate([partial_sums, complete.reshape(64, -1).astype(F32)], axis=1)
        )

    late = both_cores(sum_quarters(late, column))
    early = finish(early, 1280)
    g_fc1 = jnp.stack([wide(early, 1280, 512), wide(late, 0, 512)])
    g_fc2 = jnp.stack([wide(early, 768, 512).T, wide(early, 1792, 512).T])
    pair = ((early, 0), (late, 512))
    g_qkv = jnp.stack(
        [jnp.stack([wide(half, low + 128 * s, 128) for s in range(3)], axis=1) for half, low in pair]
    )
    g_proj = jnp.stack([wide(half, low + 384, 128).T for half, low in pair])
    g_merge_w = wide(early, 512, 256).T.reshape(4, 128, 32)

    flat = []
    for level in range(2):
        db1, rows_two, dqv, rows_one, pairs = sums[level]
        flat += [rows_one, rows_two, dqv, db1, fold_tables(pairs)]
    flat += [dgain, dbias]
    flat = jnp.concatenate([item.reshape(-1) for item in flat])
    count = flat.shape[0]
    flat = jnp.pad(flat, (0, -count % 16384)).reshape(-1, 1024)
    flat = sum_all(flat).reshape(-1)
    page_at = chip_at * 2 + core_at

    def take(low, shape):
        return flat[low : low + int(np.prod(shape))].reshape(shape)

    def page_part(value):
        return lax.dynamic_slice_in_dim(value, page_at * 32, 32, value.ndim - 1)

    def tp_part(value, axis):
        size = value.shape[axis] // TP
        return lax.dynamic_slice_in_dim(value, column * size, size, axis)

    span = 2 * D + 4 * D + 2 * D + FF + 32 * RELS
    rows = [take(level * span, (6, D)) for level in range(2)]
    rows = page_part(jnp.stack(rows))
    dqv = tp_part(jnp.stack([take(level * span + 6 * D, (2, D)) for level in range(2)]), 2)
    db1 = tp_part(jnp.stack([take(level * span + 8 * D, (FF,)) for level in range(2)]), 1)
    table = tp_part(
        jnp.stack([take(level * span + 8 * D + FF, (32, RELS)) for level in range(2)]), 1
    )
    dgain = tp_part(take(2 * span, (TP, 512)), 0).reshape(4, 128)
    dbias = tp_part(take(2 * span + MERGED, (TP, 512)), 0).reshape(4, 128)
    return (
        output,
        grad_x3,
        dgain,
        dbias,
        g_merge_w,
        rows[:, 0],
        rows[:, 1],
        g_qkv,
        dqv,
        table,
        g_proj,
        rows[:, 5],
        rows[:, 2],
        rows[:, 3],
        g_fc1,
        db1,
        g_fc2,
        rows[:, 4],
    )


def solution(mesh):
    grid = Mesh(mesh.devices.reshape(4, 4, 2, TP), ("y", "x", "core", "tp"))
    page = PAGE_AXES
    return jax.shard_map(
        body,
        mesh=grid,
        in_specs=(
            P(page, None, None, "tp"),
            P(page),
            P(None, "tp"),
            P(None, "tp"),
            P(None, "tp", None),
            P(),
            P(),
            P(None, None, None, "tp"),
            P(None, None, "tp"),
            P(None, "tp", None),
            P(None, "tp", None),
            P(),
            P(),
            P(),
            P(None, None, "tp"),
            P(None, "tp"),
            P(None, "tp", None),
            P(),
            P(page, None, None, None),
        ),
        out_specs=(
            P(page, None, None, None),
            P(page, None, None, "tp"),
            P(None, "tp"),
            P(None, "tp"),
            P(None, "tp", page),
            P(None, page),
            P(None, page),
            P(None, page, None, "tp"),
            P(None, None, "tp"),
            P(None, "tp", None),
            P(None, "tp", page),
            P(None, page),
            P(None, page),
            P(None, page),
            P(None, page, "tp"),
            P(None, "tp"),
            P(None, "tp", page),
            P(None, page),
        ),
        check_vma=False,
    )
```

```python
from functools import partial

import jax
import jax.numpy as jnp
import numpy as np
from jax import lax
from jax.experimental import pallas as pl
from jax.experimental.pallas import tpu as pltpu
from jax.sharding import Mesh
from jax.sharding import PartitionSpec as P

D = 1024
FF = 4096
MERGED = 2048
WIN = 10
SHIFT = 5
GH = 20
GW = 40
RELS = 361
TOK = 100
ROWS = 112
T = 2 * ROWS
SEND = 112
EPS = 1e-05
SCALE = 32 ** (-0.5)
YX = 16
TP = 4
UNITS = 26
HIGH = lax.Precision.HIGHEST
BF = jnp.bfloat16
F32 = jnp.float32
PAGE_AXES = ("y", "x", "core")
CHIP_AXES = ("y", "x")
GATHER_AXES = ("tp", "y", "x", "core")
VMEM = 58 << 20


def row_at(row, col):
    return (row // WIN) * ROWS + (row % WIN) * WIN + col


def place_matrices():
    own = np.zeros((T, T), np.float32)
    recv = np.zeros((T, SEND), np.float32)
    send = np.zeros((SEND, T), np.float32)
    pack = np.zeros((2 * TOK, T), np.float32)
    out = np.zeros((2 * TOK, T), np.float32)
    for row in range(GH):
        for col in range(WIN):
            source = (row + SHIFT) % GH
            if col < SHIFT:
                own[row_at(row, col), row_at(source, col + SHIFT)] = 1
                send[row * SHIFT + col, row_at(row, col)] = 1
            else:
                recv[row_at(row, col), source * SHIFT + col - SHIFT] = 1
            pack[row * WIN + col, row_at(row, col)] = 1
            out[source * WIN + col, row_at(row, col)] = 1
    return own, recv, send, pack, out


OWN, RECV, SENT, PACK, OUT = place_matrices()


def const(matrix):
    return jnp.asarray(matrix, BF)


def dot(left, right):
    return lax.dot_general(left, right, (((1,), (0,)), ((), ())), preferred_element_type=F32)


def dot_nt(left, right):
    return lax.dot_general(left, right, (((1,), (1,)), ((), ())), preferred_element_type=F32)


def dot_tn(left, right):
    return lax.dot_general(left, right, (((0,), (0,)), ((), ())), preferred_element_type=F32)


def select_rows(matrix, value):
    high = value.astype(BF)
    rest = value - high.astype(F32)
    mid = rest.astype(BF)
    low = (rest - mid.astype(F32)).astype(BF)
    return dot(matrix, high) + dot(matrix, mid) + dot(matrix, low)


def norm_stats(value):
    mean = jnp.mean(value, axis=-1, keepdims=True)
    center = value - mean
    return center, lax.rsqrt(jnp.mean(center * center, axis=-1, keepdims=True) + EPS)


def norm_back(upstream, normed, spread, gain):
    scaled = upstream * gain
    inner = (
        scaled
        - jnp.mean(scaled, axis=-1, keepdims=True)
        - normed * jnp.mean(scaled * normed, axis=-1, keepdims=True)
    )
    return spread * inner


def col_sum(value):
    return jnp.sum(value, axis=0, keepdims=True)


def whole(shape):
    return pl.BlockSpec(shape, lambda step, core: (0,) * len(shape))


def shape_of(shape, dtype):
    return jax.ShapeDtypeStruct(shape, dtype)


def run(kernel, steps, core, args, in_specs, outs, out_specs, scratch, flops, moved):
    return pl.pallas_call(
        kernel,
        grid_spec=pltpu.PrefetchScalarGridSpec(
            num_scalar_prefetch=1,
            grid=(steps,),
            in_specs=in_specs,
            out_specs=out_specs,
            scratch_shapes=scratch,
        ),
        out_shape=outs,
        compiler_params=pltpu.CompilerParams(
            vmem_limit_bytes=VMEM, dimension_semantics=("arbitrary",)
        ),
        cost_estimate=pl.CostEstimate(flops=0, bytes_accessed=1024, transcendentals=0),
    )(core, *args)


def put_halves(core_ref, mine, other, low, high):
    @pl.when(core_ref[0] == 0)
    def _():
        mine(low)
        other(high)

    @pl.when(core_ref[0] != 0)
    def _():
        mine(high)
        other(low)


def pack_kernel(place_ref, up_ref, down_ref, mix_ref, proj_ref, merge_ref, out_ref, all_ref):
    for level in range(2):
        all_ref[8 * level : 8 * level + 4] = up_ref[level].reshape(4, 16, D)
        all_ref[8 * level + 4 : 8 * level + 8] = down_ref[level].reshape(4, 16, D)
        for part in range(3):
            for group in range(4):
                all_ref[16 + 4 * level + part, :, 256 * group : 256 * group + 256] = mix_ref[
                    level, part, 16 * group : 16 * group + 16
                ]
        all_ref[19 + 4 * level] = proj_ref[level]
    all_ref[24:26] = merge_ref[...].reshape(2, 16, D)
    out_ref[...] = all_ref[pl.ds(place_ref[1] * 13, 13)]


def pack_weights(place, up, down, mix, proj, merge):
    return pl.pallas_call(
        pack_kernel,
        grid_spec=pltpu.PrefetchScalarGridSpec(
            num_scalar_prefetch=1,
            grid=(1,),
            in_specs=[
                pl.BlockSpec((2, 64, D), lambda step, place: (0, place[0], 0)),
                pl.BlockSpec((2, 64, D), lambda step, place: (0, place[0], 0)),
                pl.BlockSpec((2, 3, 64, 256), lambda step, place: (0, 0, place[0], 0)),
                pl.BlockSpec((2, 16, D), lambda step, place: (0, place[0], 0)),
                pl.BlockSpec((32, D), lambda step, place: (place[0], 0)),
            ],
            out_specs=whole((13, 16, D)),
            scratch_shapes=[pltpu.VMEM((UNITS, 16, D), BF)],
        ),
        out_shape=shape_of((13, 16, D), BF),
        compiler_params=pltpu.CompilerParams(vmem_limit_bytes=VMEM),
        cost_estimate=pl.CostEstimate(flops=0, bytes_accessed=1 << 20, transcendentals=0),
    )(place, up, down, mix, proj, merge)


def merge_stats(x_ref, pack_ref, full):
    total = jnp.zeros((T, 1), F32)
    for part in range(TP):
        rows = dot_tn(pack_ref[...], x_ref[part])
        full[part] = rows
        total = total + jnp.sum(rows, axis=-1, keepdims=True)
    mean = total / MERGED
    square = jnp.zeros((T, 1), F32)
    for part in range(TP):
        center = full[part] - mean
        square = square + jnp.sum(center * center, axis=-1, keepdims=True)
    return mean, lax.rsqrt(square / MERGED + EPS)


def merge_kernel(
    core_ref, x_ref, pack_ref, gain_ref, bias_ref, w_ref, out_ref, mine_ref, other_ref, full, stats
):
    step = pl.program_id(0)

    @pl.when(step == 0)
    def _():
        mean, spread = merge_stats(x_ref, pack_ref, full)
        stats[0] = mean
        stats[1] = spread

    normed = (full[step] - stats[0]) * stats[1]
    value = (normed * gain_ref[0] + bias_ref[0]).astype(BF)

    def set_mine(part):
        mine_ref[...] = part

    def set_other(part):
        other_ref[...] = part

    put_halves(core_ref, set_mine, set_other, value[:, :256], value[:, 256:])
    term = dot(value, w_ref[...].reshape(512, D))

    @pl.when(step == 0)
    def _():
        out_ref[...] = term

    @pl.when(step != 0)
    def _():
        out_ref[...] += term


def merge_forward(core, parts, gain, bias, weights):
    return run(
        merge_kernel,
        TP,
        core,
        (parts, const(PACK), gain.reshape(TP, 1, 512), bias.reshape(TP, 1, 512), weights),
        [
            whole((TP, 2 * TOK, 512)),
            whole((2 * TOK, T)),
            pl.BlockSpec((1, 1, 512), lambda step, core: (step, 0, 0)),
            pl.BlockSpec((1, 1, 512), lambda step, core: (step, 0, 0)),
            pl.BlockSpec((YX, 2, 16, D), lambda step, core: (step, 12, 0, 0)),
        ],
        [shape_of((T, D), F32), shape_of((T, D), BF), shape_of((T, D), BF)],
        [
            whole((T, D)),
            pl.BlockSpec((T, 256), lambda step, core: (0, step)),
            pl.BlockSpec((T, 256), lambda step, core: (0, step)),
        ],
        [pltpu.VMEM((TP, T, 512), F32), pltpu.VMEM((2, T, 1), F32)],
        2 * T * MERGED * D,
        8 << 20,
    )


def merge_back_kernel(
    core_ref, x_ref, pack_ref, gain_ref, w_ref, dx_ref,
    start_ref, dm_ref, gains_ref, biases_ref,
    full, stats, upstream,
):
    step = pl.program_id(0)

    @pl.when(step == 0)
    def _():
        mean, spread = merge_stats(x_ref, pack_ref, full)
        stats[0] = mean
        stats[1] = spread
        stats[2] = jnp.zeros((T, 1), F32)
        stats[3] = jnp.zeros((T, 1), F32)
        start_ref[...] = dx_ref[...].astype(BF)

    grad = dot_nt(start_ref[...], w_ref[...].reshape(512, D))
    normed = (full[step] - stats[0]) * stats[1]
    full[step] = normed
    gains_ref[0] = col_sum(grad * normed)
    biases_ref[0] = col_sum(grad)
    scaled = grad * gain_ref[0]
    upstream[step] = scaled
    stats[2] += jnp.sum(scaled, axis=-1, keepdims=True)
    stats[3] += jnp.sum(scaled * normed, axis=-1, keepdims=True)

    @pl.when(step == TP - 1)
    def _():
        for part in range(TP):
            value = stats[1] * (
                upstream[part] - stats[2] / MERGED - full[part] * (stats[3] / MERGED)
            )
            dm_ref[part] = dot(pack_ref[...], value.astype(BF)).astype(BF)


def merge_backward(core, parts, gain, weights, grad):
    return run(
        merge_back_kernel,
        TP,
        core,
        (parts, const(PACK), gain.reshape(TP, 1, 512), weights, grad),
        [
            whole((TP, 2 * TOK, 512)),
            whole((2 * TOK, T)),
            pl.BlockSpec((1, 1, 512), lambda step, core: (step, 0, 0)),
            pl.BlockSpec((YX, 2, 16, D), lambda step, core: (step, 12, 0, 0)),
            whole((T, D)),
        ],
        [
            shape_of((T, D), BF),
            shape_of((TP, 2 * TOK, 512), BF),
            shape_of((TP, 1, 512), F32),
            shape_of((TP, 1, 512), F32),
        ],
        [
            whole((T, D)),
            whole((TP, 2 * TOK, 512)),
            pl.BlockSpec((1, 1, 512), lambda step, core: (step, 0, 0)),
            pl.BlockSpec((1, 1, 512), lambda step, core: (step, 0, 0)),
        ],
        [pltpu.VMEM((TP, T, 512), F32), pltpu.VMEM((4, T, 1), F32), pltpu.VMEM((TP, T, 512), F32)],
        2 * T * MERGED * D,
        8 << 20,
    )


def head_masks(rows):
    lane = lax.broadcasted_iota(jnp.int32, (rows, 128), 1)
    return [(lane >= 32 * place) & (lane < 32 * place + 32) for place in range(4)]


def spread_heads(value, masks):
    zero = jnp.zeros_like(value)
    return jnp.concatenate([jnp.where(mask, value, zero) for mask in masks], axis=0)


def fold_heads(value, masks):
    total = jnp.zeros((ROWS, 128), F32)
    for place, mask in enumerate(masks):
        total = jnp.where(mask, value[place * ROWS : (place + 1) * ROWS], total)
    return total


def unfold(ref):
    value = ref[...].reshape(YX, 16, D)
    parts = [value[:, :, 256 * group : 256 * group + 256] for group in range(4)]
    return jnp.stack(parts, axis=1).reshape(D, 256)


def attn_kernel(level, *refs):
    (core_ref, x_ref), refs = refs[:2], refs[2:]
    if level:
        (halo_ref, own_ref, recv_ref), refs = refs[:3], refs[3:]
    (
        gain_ref, bias_ref, wq_ref, wk_ref, wv_ref, wp_ref, qb_ref, vb_ref, table_ref, mask_ref,
        shift_ref,
    ), refs = refs[:11], refs[11:]
    (
        mid_ref, a_ref, q_ref, k_ref, v_ref, probs_ref, mine_ref, other_ref,
    ), refs = refs[:8], refs[8:]
    step = pl.program_id(0)

    @pl.when(step == 0)
    def _():
        value = x_ref[...]
        if level:
            value = select_rows(own_ref[...], value) + dot(recv_ref[...], halo_ref[...])
            refs[0][...] = value
        center, spread = norm_stats(value)
        a_ref[...] = (center * spread * gain_ref[...] + bias_ref[...]).astype(BF)
        mid_ref[...] = value + shift_ref[...]

    a = a_ref[...]
    q = (dot(a, unfold(wq_ref)) + qb_ref[...]).astype(BF)
    k = dot(a, unfold(wk_ref)).astype(BF)
    v = (dot(a, unfold(wv_ref)) + vb_ref[...]).astype(BF)
    q_ref[...] = q
    k_ref[...] = k
    v_ref[...] = v
    masks = head_masks(ROWS)
    halves = []
    for half in range(2):
        lanes = slice(half * 128, half * 128 + 128)
        table = table_ref[4 * half : 4 * half + 4]
        parts = []
        for w in range(2):
            rows = slice(w * ROWS, (w + 1) * ROWS)
            raw = dot_nt(spread_heads(q[rows, lanes], masks), k[rows, lanes]) * SCALE
            scores = raw.reshape(4, ROWS, ROWS) + table + mask_ref[w][None]
            top = jnp.max(scores, axis=-1, keepdims=True)
            terms = jnp.exp(scores - top)
            probs = (terms / jnp.sum(terms, axis=-1, keepdims=True)).astype(BF)
            probs_ref[0, w, 4 * half : 4 * half + 4] = probs
            mixed = dot(probs.reshape(4 * ROWS, ROWS), v[rows, lanes])
            parts.append(fold_heads(mixed, masks))
        halves.append(jnp.concatenate(parts, axis=0).astype(BF))

    def set_mine(part):
        mine_ref[...] = part

    def set_other(part):
        other_ref[...] = part

    put_halves(core_ref, set_mine, set_other, *halves)
    heads = jnp.concatenate(halves, axis=1)
    mid_ref[...] += dot(heads, wp_ref[...].reshape(256, D))


def unit_spec(unit):
    return pl.BlockSpec((YX, 1, 16, D), lambda step, core: (step, unit, 0, 0))


def attn_forward(core, level, state, halo, weights, small, table, mask):
    gain, bias, qbias, vbias, shift = small
    unit = 16 + 4 * level
    args = [state]
    specs = [whole((T, D))]
    if level:
        args += [halo, const(OWN), const(RECV)]
        specs += [whole((SEND, D)), whole((T, T)), whole((T, SEND))]
    args += [gain, bias, weights, weights, weights, weights, qbias, vbias, table, mask, shift]
    cols = pl.BlockSpec((1, 256), lambda step, core: (0, step))
    specs += [whole((1, D)), whole((1, D))] + [unit_spec(unit + place) for place in range(4)]
    specs += [
        cols,
        cols,
        pl.BlockSpec((8, ROWS, ROWS), lambda step, core: (step, 0, 0)),
        whole((2, ROWS, ROWS)),
        whole((1, D)),
    ]
    block = pl.BlockSpec((T, 256), lambda step, core: (0, step))
    half = pl.BlockSpec((T, 128), lambda step, core: (0, step))
    outs = [
        shape_of((T, D), F32),
        shape_of((T, D), BF),
        shape_of((T, D), BF),
        shape_of((T, D), BF),
        shape_of((T, D), BF),
        shape_of((TP, 2, 8, ROWS, ROWS), BF),
        shape_of((T, D // 2), BF),
        shape_of((T, D // 2), BF),
    ]
    out_specs = [
        whole((T, D)),
        whole((T, D)),
        block,
        block,
        block,
        pl.BlockSpec((1, 2, 8, ROWS, ROWS), lambda step, core: (step, 0, 0, 0, 0)),
        half,
        half,
    ]
    if level:
        outs.append(shape_of((T, D), F32))
        out_specs.append(whole((T, D)))
    return run(
        partial(attn_kernel, level), TP, core, args, specs, outs, out_specs, [], 8 * T * D * D, 24 << 20
    )


def quad_spec(unit):
    return pl.BlockSpec(
        (YX, 4, 16, D), lambda step, core: (lax.rem(core[1] + step, TP), unit, 0, 0)
    )


def wide_spec(rows):
    return pl.BlockSpec((rows, D), lambda step, core: (0, lax.rem(core[1] + step, TP)))


def half_spec():
    return pl.BlockSpec((T, 512), lambda step, core: (0, lax.rem(core[1] + step, TP)))


def gelu_parts(pre):
    phi = 0.5 + 0.5 * lax.erf(pre * (0.5**0.5))
    slope = phi + pre * ((2.0 * np.pi) ** -0.5 * jnp.exp(-0.5 * pre * pre))
    return (pre * phi).astype(BF), slope


def start_norm(mid_ref, gain_ref, bias_ref, shift_ref, c2_ref, total):
    value = mid_ref[...]
    center, spread = norm_stats(value)
    c2_ref[...] = (center * spread * gain_ref[...] + bias_ref[...]).astype(BF)
    total[...] = value + shift_ref[...]


def end_norm(mid_ref, gain_ref, grad, dmlp, upstream, dmid_ref, dattn_ref, rows_ref):
    center, spread = norm_stats(mid_ref[...])
    normed = center * spread
    dmid = grad + norm_back(upstream, normed, spread, gain_ref[...])
    dmid_ref[...] = dmid
    dattn = dmid.astype(BF)
    dattn_ref[...] = dattn
    rows_ref[0:1] = col_sum(upstream * normed)
    rows_ref[1:2] = col_sum(upstream)
    rows_ref[2:3] = col_sum(dmlp.astype(F32))
    rows_ref[3:4] = col_sum(dattn.astype(F32))


def put_parts(core_ref, mine_ref, other_ref, value):
    def set_mine(part):
        mine_ref[...] = part

    def set_other(part):
        other_ref[...] = part

    put_halves(core_ref, set_mine, set_other, value[:, :512], value[:, 512:])


def put_quarter(refs, value):
    for ahead, ref in enumerate(refs):

        @pl.when(pl.program_id(0) == ahead)
        def _(ref=ref):
            ref[...] = value


def mlp_kernel(
    core_ref, mid_ref, gain_ref, bias_ref, w1_ref, w2_ref, b1_ref, b2_ref, place_ref,
    c2_ref, slope_ref, halo_ref, mine_ref, other_ref, next_ref, total,
):
    step = pl.program_id(0)

    @pl.when(step == 0)
    def _():
        start_norm(mid_ref, gain_ref, bias_ref, b2_ref, c2_ref, total)

    act, slope = gelu_parts(dot(c2_ref[...], w1_ref[...].reshape(D, D)) + b1_ref[...])
    slope_ref[...] = slope.astype(BF)
    put_parts(core_ref, mine_ref, other_ref, act)
    total[...] += dot(act, w2_ref[...].reshape(D, D))

    @pl.when(step == TP - 1)
    def _():
        value = total[...]
        halo_ref[...] = dot(place_ref[...], value.astype(BF)).astype(BF)
        next_ref[...] = value


def mlp_forward(core, mid, weights, small):
    gain, bias, b1, b2 = small
    return run(
        mlp_kernel,
        TP,
        core,
        (mid, gain, bias, weights, weights, b1, b2, const(SENT)),
        [
            whole((T, D)),
            whole((1, D)),
            whole((1, D)),
            quad_spec(0),
            quad_spec(1),
            wide_spec(1),
            whole((1, D)),
            whole((SEND, T)),
        ],
        [
            shape_of((T, D), BF),
            shape_of((T, FF), BF),
            shape_of((SEND, D), BF),
            shape_of((T, FF // 2), BF),
            shape_of((T, FF // 2), BF),
            shape_of((T, D), F32),
        ],
        [whole((T, D)), wide_spec(T), whole((SEND, D)), half_spec(), half_spec(), whole((T, D))],
        [pltpu.VMEM((T, D), F32)],
        4 * T * D * FF,
        24 << 20,
    )


def mlp_both_kernel(
    core_ref, mid_ref, gain_ref, bias_ref, w1_ref, w2_ref, b1_ref, b2_ref, place_ref, keep_ref,
    dx_ref, c2_ref, out_ref, one, two, three, four, dmid_ref, dattn_ref, db1_ref, rows_ref,
    mine_ref, other_ref, total, back,
):
    step = pl.program_id(0)

    @pl.when(step == 0)
    def _():
        start_norm(mid_ref, gain_ref, bias_ref, b2_ref, c2_ref, total)
        back[...] = jnp.zeros((T, D), F32)

    up = w1_ref[...].reshape(D, D)
    down = w2_ref[...].reshape(D, D)
    act, slope = gelu_parts(dot(c2_ref[...], up) + b1_ref[...])
    put_quarter((one, two, three, four), act)
    total[...] += dot(act, down)
    dpre = (dot_nt(dx_ref[...], down) * slope).astype(BF)
    db1_ref[...] = col_sum(dpre.astype(F32))
    put_parts(core_ref, mine_ref, other_ref, dpre)
    back[...] += dot_nt(dpre, up)

    @pl.when(step == TP - 1)
    def _():
        out_ref[...] = dot(place_ref[...], (total[...] * keep_ref[...]).astype(BF)).astype(BF)
        dmlp = dx_ref[...]
        end_norm(
            mid_ref, gain_ref, dmlp.astype(F32), dmlp, back[...], dmid_ref, dattn_ref, rows_ref
        )


def mlp_both(core, mid, weights, small, keep, dx):
    gain, bias, b1, b2 = small
    return run(
        mlp_both_kernel,
        TP,
        core,
        (mid, gain, bias, weights, weights, b1, b2, const(OUT), keep, dx),
        [
            whole((T, D)),
            whole((1, D)),
            whole((1, D)),
            quad_spec(2),
            quad_spec(3),
            wide_spec(1),
            whole((1, D)),
            whole((2 * TOK, T)),
            whole((T, 1)),
            whole((T, D)),
        ],
        [shape_of((T, D), BF), shape_of((2 * TOK, D), BF)]
        + [shape_of((T, D), BF)] * TP
        + [
            shape_of((T, D), F32),
            shape_of((T, D), BF),
            shape_of((1, FF), F32),
            shape_of((4, D), F32),
            shape_of((T, FF // 2), BF),
            shape_of((T, FF // 2), BF),
        ],
        [whole((T, D)), whole((2 * TOK, D))]
        + [whole((T, D))] * TP
        + [whole((T, D)), whole((T, D)), wide_spec(1), whole((4, D)), half_spec(), half_spec()],
        [pltpu.VMEM((T, D), F32), pltpu.VMEM((T, D), F32)],
        8 * T * D * FF,
        24 << 20,
    )


def mlp_back_kernel(
    core_ref, dx_ref, halo_ref, own_ref, sent_ref, mid_ref, gain_ref, w1_ref, w2_ref, slope_ref,
    dmid_ref, dmlp_ref, dattn_ref, db1_ref, rows_ref, one, two, three, four, total, grad,
):
    step = pl.program_id(0)

    @pl.when(step == 0)
    def _():
        value = select_rows_t(own_ref[...], dx_ref[...]) + dot_tn(sent_ref[...], halo_ref[...])
        grad[...] = value
        dmlp_ref[...] = value.astype(BF)
        total[...] = jnp.zeros((T, D), F32)

    dact = dot_nt(dmlp_ref[...], w2_ref[...].reshape(D, D))
    dpre = (dact * slope_ref[...].astype(F32)).astype(BF)
    db1_ref[...] = col_sum(dpre.astype(F32))
    put_quarter((one, two, three, four), dpre)
    total[...] += dot_nt(dpre, w1_ref[...].reshape(D, D))

    @pl.when(step == TP - 1)
    def _():
        end_norm(
            mid_ref, gain_ref, grad[...], dmlp_ref[...], total[...], dmid_ref, dattn_ref, rows_ref
        )


def select_rows_t(matrix, value):
    high = value.astype(BF)
    rest = value - high.astype(F32)
    mid = rest.astype(BF)
    low = (rest - mid.astype(F32)).astype(BF)
    return dot_tn(matrix, high) + dot_tn(matrix, mid) + dot_tn(matrix, low)


def mlp_backward(core, grad, halo, mid, gain, weights, slope):
    return run(
        mlp_back_kernel,
        TP,
        core,
        (grad, halo, const(OWN), const(SENT), mid, gain, weights, weights, slope),
        [
            whole((T, D)),
            whole((SEND, D)),
            whole((T, T)),
            whole((SEND, T)),
            whole((T, D)),
            whole((1, D)),
            quad_spec(0),
            quad_spec(1),
            wide_spec(T),
        ],
        [
            shape_of((T, D), F32),
            shape_of((T, D), BF),
            shape_of((T, D), BF),
            shape_of((1, FF), F32),
            shape_of((4, D), F32),
        ]
        + [shape_of((T, D), BF)] * TP,
        [whole((T, D)), whole((T, D)), whole((T, D)), wide_spec(1), whole((4, D))]
        + [whole((T, D))] * TP,
        [pltpu.VMEM((T, D), F32), pltpu.VMEM((T, D), F32)],
        4 * T * D * FF,
        24 << 20,
    )


def attn_back_kernel(level, *refs):
    (
        core_ref, dmid_ref, dattn_ref, x_ref, gain_ref, wq_ref, wk_ref, wv_ref, wp_ref,
        q_ref, k_ref, v_ref, probs_ref,
    ), refs = refs[:13], refs[13:]
    if level:
        (place_ref,), refs = refs[:1], refs[1:]
    (dx_ref, mine_ref, other_ref, pair_ref, sums_ref, rows_ref), refs = refs[:6], refs[6:]
    if level:
        (sent_ref,), refs = refs[:1], refs[1:]
    (total,) = refs
    step = pl.program_id(0)

    @pl.when(step == 0)
    def _():
        total[...] = jnp.zeros((T, D), F32)

    dheads = dot_nt(dattn_ref[...], wp_ref[...].reshape(256, D)).astype(BF)
    masks = head_masks(ROWS)
    dqs, dks, dvs = [], [], []
    for half in range(2):
        lanes = slice(half * 128, half * 128 + 128)
        dq_parts, dk_parts, dv_parts = [], [], []
        pairs = None
        for w in range(2):
            rows = slice(w * ROWS, (w + 1) * ROWS)
            rounded = probs_ref[0, w, 4 * half : 4 * half + 4].reshape(4 * ROWS, ROWS)
            probs = rounded.astype(F32)
            spread_out = spread_heads(dheads[rows, lanes], masks)
            dprobs = dot_nt(spread_out, v_ref[rows, lanes])
            dv_parts.append(dot_tn(rounded, spread_out))
            inner = jnp.sum(probs * dprobs, axis=-1, keepdims=True)
            dscores = (probs * (dprobs - inner)).astype(BF)
            wide = dscores.astype(F32)
            pairs = wide if pairs is None else pairs + wide
            dq_parts.append(fold_heads(dot(dscores, k_ref[rows, lanes]), masks))
            dk_parts.append(dot_tn(dscores, spread_heads(q_ref[rows, lanes], masks)))
        pair_ref[4 * half : 4 * half + 4] = pairs.reshape(4, ROWS, ROWS)
        dqs.append((jnp.concatenate(dq_parts, axis=0) * SCALE).astype(BF))
        dks.append((jnp.concatenate(dk_parts, axis=0) * SCALE).astype(BF))
        dvs.append(jnp.concatenate(dv_parts, axis=0).astype(BF))

    def set_mine(part):
        mine_ref[...] = part

    def set_other(part):
        other_ref[...] = part

    put_halves(
        core_ref,
        set_mine,
        set_other,
        jnp.concatenate([dqs[0], dks[0], dvs[0]], axis=1),
        jnp.concatenate([dqs[1], dks[1], dvs[1]], axis=1),
    )
    dq = jnp.concatenate(dqs, axis=1)
    dk = jnp.concatenate(dks, axis=1)
    dv = jnp.concatenate(dvs, axis=1)
    sums_ref[0:1] = col_sum(dq.astype(F32))
    sums_ref[1:2] = col_sum(dv.astype(F32))
    total[...] += (
        dot_nt(dq, unfold(wq_ref))
        + dot_nt(dk, unfold(wk_ref))
        + dot_nt(dv, unfold(wv_ref))
    )

    @pl.when(step == TP - 1)
    def _():
        center, spread = norm_stats(x_ref[...])
        normed = center * spread
        upstream = total[...]
        value = dmid_ref[...] + norm_back(upstream, normed, spread, gain_ref[...])
        dx_ref[...] = value
        rows_ref[0:1] = col_sum(upstream * normed)
        rows_ref[1:2] = col_sum(upstream)
        if level:
            sent_ref[...] = dot_tn(place_ref[...], value.astype(BF)).astype(BF)


def attn_backward(core, level, dmid, dattn, state, gain, weights, q, k, v, probs):
    unit = 16 + 4 * level
    block = pl.BlockSpec((T, 256), lambda step, core: (0, step))
    part = pl.BlockSpec((T, 384), lambda step, core: (0, step))
    args = [dmid, dattn, state, gain, weights, weights, weights, weights, q, k, v, probs]
    specs = [whole((T, D)), whole((T, D)), whole((T, D)), whole((1, D))]
    specs += [unit_spec(unit + place) for place in range(4)]
    specs += [
        block,
        block,
        block,
        pl.BlockSpec((1, 2, 8, ROWS, ROWS), lambda step, core: (step, 0, 0, 0, 0)),
    ]
    outs = [
        shape_of((T, D), F32),
        shape_of((T, 1536), BF),
        shape_of((T, 1536), BF),
        shape_of((32, ROWS, ROWS), F32),
        shape_of((2, D), F32),
        shape_of((2, D), F32),
    ]
    out_specs = [
        whole((T, D)),
        part,
        part,
        pl.BlockSpec((8, ROWS, ROWS), lambda step, core: (step, 0, 0)),
        pl.BlockSpec((2, 256), lambda step, core: (0, step)),
        whole((2, D)),
    ]
    if level:
        args.append(const(RECV))
        specs.append(whole((T, SEND)))
        outs.append(shape_of((SEND, D), BF))
        out_specs.append(whole((SEND, D)))
    return run(
        partial(attn_back_kernel, level),
        TP,
        core,
        args,
        specs,
        outs,
        out_specs,
        [pltpu.VMEM((T, D), F32)],
        8 * T * D * D,
        24 << 20,
    )


def weight_kernel(plan, *refs):
    refs, out_ref = refs[1:-1], refs[-1]
    place = 0
    column = 0
    for kind, size, count in plan:
        parts = [ref[...] for ref in refs[place : place + count]]
        if kind == "matrix":
            value = dot_tn(
                jnp.concatenate(parts[:2], axis=0), jnp.concatenate(parts[2:], axis=0)
            )
        else:
            value = sum(part.astype(F32) for part in parts)
        out_ref[:, 0, :, column : column + size] = value.astype(BF).reshape(YX, 64, size)
        column += size
        place += count


def weight_grads(core, items, sums):
    plan, args, specs = [], [], []
    for left, right in items:
        size = right[0].shape[1] // TP
        plan.append(("matrix", size, 4))
        args += [left[0], left[1], right[0], right[1]]
        block = pl.BlockSpec((T, size), lambda step, core: (0, step))
        specs += [whole((T, D)), whole((T, D)), block, block]
    for pieces in sums:
        plan.append(("sum", 128, len(pieces)))
        args += pieces
        specs += [pl.BlockSpec((D, 128), lambda step, core: (0, step))] * len(pieces)
    width = sum(size for unused, size, count in plan)
    return run(
        partial(weight_kernel, plan),
        TP,
        core,
        args,
        specs,
        shape_of((YX, TP, 64, width), BF),
        pl.BlockSpec((YX, 1, 64, width), lambda step, core: (0, step, 0, 0)),
        [],
        4 * T * D * width * TP,
        (2 * D * width * TP) + (8 << 20),
    )


def column_kernel(core_ref, *refs):
    lefts, rights, (other_ref, mine_ref) = refs[:TP], refs[TP : 2 * TP], refs[2 * TP :]
    left = jnp.concatenate([ref[...] for ref in lefts], axis=0)
    right = jnp.concatenate([ref[...] for ref in rights], axis=0)
    value = dot_tn(left, right).astype(BF)

    @pl.when(pl.program_id(0) == 0)
    def _():
        other_ref[...] = value

    @pl.when(pl.program_id(0) == 1)
    def _():
        mine_ref[...] = value


def column_grads(core, lefts, rights):
    half = pl.BlockSpec((T, 512), lambda step, core: (0, (core[0] + 1 + step) % 2))
    return run(
        column_kernel,
        2,
        core,
        list(lefts) + list(rights),
        [whole((T, D))] * TP + [half] * TP,
        [shape_of((D, 512), BF)] * 2,
        [whole((D, 512))] * 2,
        [],
        4 * T * D * 2048,
        8 << 20,
    )


def send_ahead(pieces):
    return [pieces[0]] + [
        lax.ppermute(pieces[step], "tp", [(i, (i + step) % TP) for i in range(TP)])
        for step in range(1, TP)
    ]


def send_all(value):
    return send_ahead([value] * TP)


def sum_quarters(value, column):
    pieces = [
        lax.dynamic_index_in_dim(value, (column + step) % TP, 0, keepdims=False)
        for step in range(TP)
    ]
    got = [piece.astype(F32) for piece in send_ahead(pieces)]
    return (got[0] + got[1]) + (got[2] + got[3])


def table_index():
    place = np.zeros((RELS, WIN * 190), np.float32)
    for row in range(WIN):
        for step in range(19):
            for col in range(WIN):
                place[(18 - step) * 19 + row - col + 9, row * 190 + step * WIN + col] = 1
    return place


PAIRS = table_index()


def spread_tables(tables):
    compact = jnp.dot(tables.reshape(64, RELS), jnp.asarray(PAIRS), precision=HIGH)
    compact = compact.reshape(2, 32, WIN, 190)
    rows = [compact[..., (9 - row) * WIN : (9 - row) * WIN + TOK] for row in range(WIN)]
    full = jnp.stack(rows, axis=2).reshape(2, 32, TOK, TOK)
    return jnp.pad(full, ((0, 0), (0, 0), (0, ROWS - TOK), (0, ROWS - TOK)))


def fold_tables(pairs):
    total = jnp.zeros((32, WIN, 190), F32)
    for row in range(WIN):
        low = (9 - row) * WIN
        total = total + jnp.pad(
            pairs[:, row * WIN : (row + 1) * WIN, :TOK], ((0, 0), (0, 0), (low, 90 - low))
        )
    return jnp.dot(total.reshape(32, -1), jnp.asarray(PAIRS.T), precision=HIGH)


def window_masks(level, valid, column):
    place = np.arange(ROWS)
    row = np.minimum(place // WIN, WIN - 1)
    col = jnp.asarray(place % WIN, jnp.int32)
    real = jnp.asarray(place < TOK)
    offset = SHIFT if level else 0
    rolled = column * WIN + col
    usable = (rolled + offset) % GW < valid
    masks = []
    for w in range(2):
        rolled_row = w * WIN + row
        row_region = (rolled_row >= GH - WIN).astype(np.int32) + (rolled_row >= GH - SHIFT)
        col_region = (rolled >= GW - WIN).astype(jnp.int32) + (rolled >= GW - SHIFT)
        region = jnp.asarray(row_region * 3, jnp.int32) + col_region
        allowed = usable[None, :]
        if level:
            allowed = allowed & (region[:, None] == region[None, :])
        mask = jnp.where(allowed, F32(0.0), F32(-100.0))
        mask = jnp.where(real[None, :], mask, F32(-1e30))
        masks.append(jnp.broadcast_to(mask, (ROWS, ROWS)))
    return jnp.stack(masks)


def gather_tp(value, place):
    parts = [value]
    for step in range(1, TP):
        parts.append(lax.ppermute(value, "tp", [(i, (i + step) % TP) for i in range(TP)]))
    stacked = jnp.stack(parts)
    order = (place - jnp.arange(TP)) % TP
    return [lax.dynamic_index_in_dim(stacked, order[i], 0, keepdims=False) for i in range(TP)]


def after(value, others):
    return lax.optimization_barrier((value, others))


def swap_core(value):
    return lax.ppermute(value, "core", [(0, 1), (1, 0)])


def sum_all(value):
    sent = value.astype(BF)
    value = sent.astype(F32) + swap_core(sent).astype(F32)
    for axis in ("x", "y", "tp"):
        sent = value.astype(BF)
        got = [
            lax.ppermute(sent, axis, [(i, (i + gap) % 4) for i in range(4)]).astype(F32)
            for gap in (1, 2, 3)
        ]
        value = (sent.astype(F32) + got[1]) + (got[0] + got[2])
    return value


def body(
    x3,
    res_group,
    merge_gain,
    merge_bias,
    merge_w,
    ln1_gain,
    ln1_bias,
    qkv_w,
    qv_bias,
    rel_table,
    proj_w,
    proj_bias,
    ln2_gain,
    ln2_bias,
    fc1_w,
    fc1_bias,
    fc2_w,
    fc2_bias,
    out_grad,
):
    core_at = lax.axis_index("core")
    chip_at = lax.axis_index("y") * 4 + lax.axis_index("x")
    column = lax.axis_index("tp")
    core = jnp.stack([core_at, column]).astype(jnp.int32)

    piece = pack_weights(
        jnp.stack([chip_at, core_at]).astype(jnp.int32),
        fc1_w,
        fc2_w,
        jnp.swapaxes(qkv_w, 1, 2),
        proj_w,
        merge_w.reshape(512, D),
    )
    weights = lax.all_gather(piece.reshape(-1, D), GATHER_AXES, axis=0, tiled=True)
    weights = weights.reshape(64, UNITS, 16, D)

    pages = lax.all_to_all(x3, PAGE_AXES, split_axis=1, concat_axis=0, tiled=True)
    tiles = pages.reshape(GH, TP, WIN, 512).transpose(1, 0, 2, 3).reshape(TP * 2 * TOK, 512)
    parts = lax.all_to_all(tiles, "tp", split_axis=0, concat_axis=0, tiled=True)
    parts = parts.reshape(TP, 2 * TOK, 512)

    packed = jnp.concatenate(
        [
            merge_gain.reshape(-1),
            merge_bias.reshape(-1),
            qv_bias.reshape(-1),
            fc1_bias.reshape(-1),
            rel_table.reshape(-1),
            jnp.zeros((10240 - 9872,), F32),
        ]
    ).reshape(80, 128)
    quarters = [part.reshape(-1) for part in gather_tp(packed, column)]

    def joined(low, shape, axis):
        size = int(np.prod(shape))
        return jnp.concatenate([part[low : low + size].reshape(shape) for part in quarters], axis)

    merge_gain_all = joined(0, (1, 512), 0)
    merge_bias_all = joined(512, (1, 512), 0)
    qv_bias_all = joined(1024, (2, 2, 256), 2)
    fc1_bias_all = joined(2048, (2, 1024), 1)
    tables = spread_tables(joined(4096, (2, 8, RELS), 1))
    tables = [tables[0], tables[1]]

    valid = (res_group[0] + 1) * WIN
    masks = [window_masks(level, valid, column) for level in range(2)]
    spot = np.arange(T) % ROWS
    keep = ((column * WIN + SHIFT + jnp.asarray(spot % WIN, jnp.int32)) % GW < valid) & jnp.asarray(
        spot < TOK
    )
    keep = keep.astype(F32)[:, None]
    page_keep = (jnp.asarray(np.arange(GW), jnp.int32) < valid).astype(BF)[None, :, None]
    tiles = jnp.roll(out_grad[0] * page_keep, (-SHIFT, -SHIFT), (0, 1))
    tiles = tiles.reshape(2, WIN, TP, WIN, D).transpose(2, 0, 1, 3, 4).reshape(TP, 2, TOK, D)
    tiles = jnp.pad(tiles, ((0, 0), (0, 0), (0, ROWS - TOK), (0, 0))).reshape(TP, T, D)
    tiles = [
        lax.dynamic_index_in_dim(tiles, (column + TP - back) % TP, 0, keepdims=False)
        for back in range(TP)
    ]

    weights, (tables, masks, tiles, keep, parts) = after(
        weights, (tables, masks, tiles, keep, parts)
    )
    state, merged_mine, merged_other = merge_forward(
        core, parts, merge_gain_all, merge_bias_all, weights
    )
    halo = None
    pending = [swap_core(merged_other)]
    for level in range(2):
        small = (
            ln1_gain[level : level + 1],
            ln1_bias[level : level + 1],
            qv_bias_all[level, 0:1],
            qv_bias_all[level, 1:2],
            proj_bias[level : level + 1],
        )
        got = attn_forward(
            core, level, state, halo, weights, small, tables[level], masks[level]
        )
        mid, a, q, k, v, probs, heads_mine, heads_other = got[:8]
        start = got[8] if level else state
        mid, pending = after(mid, pending)
        small = (
            ln2_gain[level : level + 1],
            ln2_bias[level : level + 1],
            fc1_bias_all[level : level + 1],
            fc2_bias[level : level + 1],
        )
        if level:
            got = mlp_both(core, mid, weights, small, keep, tiles[0])
            c2, extra, *acts = got[:6]
            dmid, dattn, db1, rows_two, dpre_mine, dpre_other = got[6:]
            dattn, (a_zero, heads_zero, c2_all, a_got, heads_got) = after(
                dattn, (*pending, c2_all, swap_core(a), swap_core(heads_other))
            )
        else:
            swapped = [swap_core(a), swap_core(heads_other)]
            c2, slope, halo, act_mine, act_other, state = mlp_forward(core, mid, weights, small)
            (merged_got,) = pending
            pending = swapped
            kept = (start, mid, a, q, k, v, probs, slope, c2, heads_mine)
            halo = lax.ppermute(halo, "tp", [((i + 1) % TP, i) for i in range(TP)])
            halo, c2 = lax.optimization_barrier((halo, c2))
            c2_all = send_all(c2)
    acts = send_ahead(acts)
    dpre_got, dattn_got, c2_got = [swap_core(value) for value in (dpre_other, dattn, c2)]

    sums = [None, None]
    got = attn_backward(core, 1, dmid, dattn, start, ln1_gain[1:2], weights, q, k, v, probs)
    grad, mixed_mine, mixed_other, pairs, dqv, rows_one, sent = got
    sent, (dpre_got, dattn_got, acts) = after(sent, (dpre_got, dattn_got, acts))
    halo = lax.ppermute(sent, "tp", [(i, (i + 1) % TP) for i in range(TP)])
    mixed_got = swap_core(mixed_other)
    sums[1] = (db1, rows_two, dqv, rows_one, pairs)
    items = [
        ((c2, c2_got), (dpre_mine, dpre_got)),
        ((a, a_got), (mixed_mine, mixed_got)),
        ((dattn, dattn_got), (heads_mine, heads_got)),
    ]
    late = weight_grads(core, items, [])
    late, halo = lax.optimization_barrier((late, halo))
    late = lax.psum_scatter(late, CHIP_AXES, scatter_dimension=0, tiled=True)
    late = lax.optimization_barrier(late)[0]

    start, mid, a, q, k, v, probs, slope, c2, heads_mine = kept
    halo, act_other = lax.optimization_barrier((halo, act_other))
    act_got = swap_core(act_other)
    got = mlp_backward(core, grad, halo, mid, ln2_gain[0:1], weights, slope)
    dmid, dmlp, dattn, db1, rows_two = got[:5]
    dattn, (dpre, act_got) = after(dattn, (list(got[5:]), act_got))
    dpre = send_ahead(dpre)
    got = attn_backward(core, 0, dmid, dattn, start, ln1_gain[0:1], weights, q, k, v, probs)
    grad, mixed_mine, mixed_other, pairs, dqv, rows_one = got
    sums[0] = (db1, rows_two, dqv, rows_one, pairs)
    grad, dattn_sent = lax.optimization_barrier((grad, dattn))
    mixed_got, dattn_got = [swap_core(value) for value in (mixed_other, dattn_sent)]
    first, dm, dgain, dbias = merge_backward(core, parts, merge_gain_all, weights, grad)
    first, (dpre, tiles, acts) = after(first, (dpre, tiles, acts))
    first_got, dmlp_got = swap_core(first), swap_core(dmlp)
    last_other, last_mine = column_grads(core, tiles, acts)
    last_got = swap_core(last_other)
    up_other, up_mine = column_grads(core, c2_all, dpre)
    up_mine, (first_got, dmlp_got, last_got, mixed_got, dattn_got) = after(
        up_mine, (first_got, dmlp_got, last_got, mixed_got, dattn_got)
    )
    items = [
        ((a, a_zero), (mixed_mine, mixed_got)),
        ((dattn, dattn_got), (heads_mine, heads_zero)),
        ((first, first_got), (merged_mine, merged_got)),
        ((dmlp, dmlp_got), (act_mine, act_got)),
    ]
    early = weight_grads(
        core, items, [[up_mine, swap_core(up_other)], [last_mine, last_got]]
    )
    early, (extra, sums, dgain, dbias) = after(early, (extra, sums, dgain, dbias))
    early = lax.psum_scatter(early, CHIP_AXES, scatter_dimension=0, tiled=True)
    early = lax.optimization_barrier(early)[0]

    tiles_out = jnp.stack(gather_tp(extra, column)).reshape(TP, GH, WIN, D)
    output = jnp.roll(tiles_out.transpose(1, 0, 2, 3).reshape(GH, GW, D), SHIFT, 1)
    output = output.astype(F32)[None]
    back = lax.all_to_all(
        dm.reshape(TP * 2 * TOK, 512), "tp", split_axis=0, concat_axis=0, tiled=True
    )
    back = back.reshape(TP, GH, WIN, 512).transpose(1, 0, 2, 3).reshape(800, 1, 4, 128)
    grad_x3 = lax.all_to_all(back, PAGE_AXES, split_axis=0, concat_axis=1, tiled=True).astype(F32)

    def both_cores(value):
        rows = value.reshape(2, 32, -1)
        kept_rows = lax.dynamic_index_in_dim(rows, core_at, 0, keepdims=False).astype(F32)
        sent_rows = lax.dynamic_index_in_dim(rows, 1 - core_at, 0, keepdims=False)
        got_rows = swap_core(sent_rows.astype(BF)).astype(F32)
        return (
            jnp.where(core_at == 0, kept_rows, got_rows),
            jnp.where(core_at == 0, got_rows, kept_rows),
        )

    def wide(halves, low, size):
        return jnp.concatenate([half[:, low : low + size] for half in halves], axis=1)

    def finish(value, split):
        complete = value[..., split:].reshape(TP, 64, -1, 128).transpose(1, 2, 0, 3)
        partial_sums = sum_quarters(value[..., :split], column)
        return both_cores(
            jnp.concatenate([partial_sums, complete.reshape(64, -1).astype(F32)], axis=1)
        )

    late = both_cores(sum_quarters(late, column))
    early = finish(early, 1280)
    g_fc1 = jnp.stack([wide(early, 1280, 512), wide(late, 0, 512)])
    g_fc2 = jnp.stack([wide(early, 768, 512).T, wide(early, 1792, 512).T])
    pair = ((early, 0), (late, 512))
    g_qkv = jnp.stack(
        [jnp.stack([wide(half, low + 128 * s, 128) for s in range(3)], axis=1) for half, low in pair]
    )
    g_proj = jnp.stack([wide(half, low + 384, 128).T for half, low in pair])
    g_merge_w = wide(early, 512, 256).T.reshape(4, 128, 32)

    flat = []
    for level in range(2):
        db1, rows_two, dqv, rows_one, pairs = sums[level]
        flat += [rows_one, rows_two, dqv, db1, fold_tables(pairs)]
    flat += [dgain, dbias]
    flat = jnp.concatenate([item.reshape(-1) for item in flat])
    count = flat.shape[0]
    flat = jnp.pad(flat, (0, -count % 16384)).reshape(-1, 1024)
    flat = sum_all(flat).reshape(-1)
    page_at = chip_at * 2 + core_at

    def take(low, shape):
        return flat[low : low + int(np.prod(shape))].reshape(shape)

    def page_part(value):
        return lax.dynamic_slice_in_dim(value, page_at * 32, 32, value.ndim - 1)

    def tp_part(value, axis):
        size = value.shape[axis] // TP
        return lax.dynamic_slice_in_dim(value, column * size, size, axis)

    span = 2 * D + 4 * D + 2 * D + FF + 32 * RELS
    rows = [take(level * span, (6, D)) for level in range(2)]
    rows = page_part(jnp.stack(rows))
    dqv = tp_part(jnp.stack([take(level * span + 6 * D, (2, D)) for level in range(2)]), 2)
    db1 = tp_part(jnp.stack([take(level * span + 8 * D, (FF,)) for level in range(2)]), 1)
    table = tp_part(
        jnp.stack([take(level * span + 8 * D + FF, (32, RELS)) for level in range(2)]), 1
    )
    dgain = tp_part(take(2 * span, (TP, 512)), 0).reshape(4, 128)
    dbias = tp_part(take(2 * span + MERGED, (TP, 512)), 0).reshape(4, 128)
    return (
        output,
        grad_x3,
        dgain,
        dbias,
        g_merge_w,
        rows[:, 0],
        rows[:, 1],
        g_qkv,
        dqv,
        table,
        g_proj,
        rows[:, 5],
        rows[:, 2],
        rows[:, 3],
        g_fc1,
        db1,
        g_fc2,
        rows[:, 4],
    )


def solution(mesh):
    grid = Mesh(mesh.devices.reshape(4, 4, 2, TP), ("y", "x", "core", "tp"))
    page = PAGE_AXES
    return jax.shard_map(
        body,
        mesh=grid,
        in_specs=(
            P(page, None, None, "tp"),
            P(page),
            P(None, "tp"),
            P(None, "tp"),
            P(None, "tp", None),
            P(),
            P(),
            P(None, None, None, "tp"),
            P(None, None, "tp"),
            P(None, "tp", None),
            P(None, "tp", None),
            P(),
            P(),
            P(),
            P(None, None, "tp"),
            P(None, "tp"),
            P(None, "tp", None),
            P(),
            P(page, None, None, None),
        ),
        out_specs=(
            P(page, None, None, None),
            P(page, None, None, "tp"),
            P(None, "tp"),
            P(None, "tp"),
            P(None, "tp", page),
            P(None, page),
            P(None, page),
            P(None, page, None, "tp"),
            P(None, None, "tp"),
            P(None, "tp", None),
            P(None, "tp", page),
            P(None, page),
            P(None, page),
            P(None, page),
            P(None, page, "tp"),
            P(None, "tp"),
            P(None, "tp", page),
            P(None, page),
        ),
        check_vma=False,
    )
```

```python
from functools import partial

import jax
import jax.numpy as jnp
import numpy as np
from jax import lax
from jax.experimental import pallas as pl
from jax.experimental.pallas import tpu as pltpu
from jax.sharding import Mesh
from jax.sharding import PartitionSpec as P

D = 1024
FF = 4096
MERGED = 2048
WIN = 10
SHIFT = 5
GH = 20
GW = 40
RELS = 361
TOK = 100
ROWS = 112
T = 2 * ROWS
SEND = 112
EPS = 1e-05
SCALE = 32 ** (-0.5)
YX = 16
TP = 4
UNITS = 26
HIGH = lax.Precision.HIGHEST
BF = jnp.bfloat16
F32 = jnp.float32
PAGE_AXES = ("y", "x", "core")
CHIP_AXES = ("y", "x")
GATHER_AXES = ("tp", "y", "x", "core")
VMEM = 58 << 20


def row_at(row, col):
    return (row // WIN) * ROWS + (row % WIN) * WIN + col


def place_matrices():
    own = np.zeros((T, T), np.float32)
    recv = np.zeros((T, SEND), np.float32)
    send = np.zeros((SEND, T), np.float32)
    pack = np.zeros((2 * TOK, T), np.float32)
    out = np.zeros((2 * TOK, T), np.float32)
    for row in range(GH):
        for col in range(WIN):
            source = (row + SHIFT) % GH
            if col < SHIFT:
                own[row_at(row, col), row_at(source, col + SHIFT)] = 1
                send[row * SHIFT + col, row_at(row, col)] = 1
            else:
                recv[row_at(row, col), source * SHIFT + col - SHIFT] = 1
            pack[row * WIN + col, row_at(row, col)] = 1
            out[source * WIN + col, row_at(row, col)] = 1
    return own, recv, send, pack, out


OWN, RECV, SENT, PACK, OUT = place_matrices()


def const(matrix):
    return jnp.asarray(matrix, BF)


def dot(left, right):
    return lax.dot_general(left, right, (((1,), (0,)), ((), ())), preferred_element_type=F32)


def dot_nt(left, right):
    return lax.dot_general(left, right, (((1,), (1,)), ((), ())), preferred_element_type=F32)


def dot_tn(left, right):
    return lax.dot_general(left, right, (((0,), (0,)), ((), ())), preferred_element_type=F32)


def select_rows(matrix, value):
    high = value.astype(BF)
    rest = value - high.astype(F32)
    mid = rest.astype(BF)
    low = (rest - mid.astype(F32)).astype(BF)
    return dot(matrix, high) + dot(matrix, mid) + dot(matrix, low)


def norm_stats(value):
    mean = jnp.mean(value, axis=-1, keepdims=True)
    center = value - mean
    return center, lax.rsqrt(jnp.mean(center * center, axis=-1, keepdims=True) + EPS)


def norm_back(upstream, normed, spread, gain):
    scaled = upstream * gain
    inner = (
        scaled
        - jnp.mean(scaled, axis=-1, keepdims=True)
        - normed * jnp.mean(scaled * normed, axis=-1, keepdims=True)
    )
    return spread * inner


def col_sum(value):
    return jnp.sum(value, axis=0, keepdims=True)


def whole(shape):
    return pl.BlockSpec(shape, lambda step, core: (0,) * len(shape))


def shape_of(shape, dtype):
    return jax.ShapeDtypeStruct(shape, dtype)


def run(kernel, steps, core, args, in_specs, outs, out_specs, scratch, flops, moved):
    return pl.pallas_call(
        kernel,
        grid_spec=pltpu.PrefetchScalarGridSpec(
            num_scalar_prefetch=1,
            grid=(steps,),
            in_specs=in_specs,
            out_specs=out_specs,
            scratch_shapes=scratch,
        ),
        out_shape=outs,
        compiler_params=pltpu.CompilerParams(
            vmem_limit_bytes=VMEM, dimension_semantics=("arbitrary",)
        ),
        cost_estimate=pl.CostEstimate(flops=0, bytes_accessed=1024, transcendentals=0),
    )(core, *args)


def put_halves(core_ref, mine, other, low, high):
    @pl.when(core_ref[0] == 0)
    def _():
        mine(low)
        other(high)

    @pl.when(core_ref[0] != 0)
    def _():
        mine(high)
        other(low)


def pack_kernel(place_ref, up_ref, down_ref, mix_ref, proj_ref, merge_ref, out_ref, all_ref):
    for level in range(2):
        all_ref[8 * level : 8 * level + 4] = up_ref[level].reshape(4, 16, D)
        all_ref[8 * level + 4 : 8 * level + 8] = down_ref[level].reshape(4, 16, D)
        for part in range(3):
            for group in range(4):
                all_ref[16 + 4 * level + part, :, 256 * group : 256 * group + 256] = mix_ref[
                    level, part, 16 * group : 16 * group + 16
                ]
        all_ref[19 + 4 * level] = proj_ref[level]
    all_ref[24:26] = merge_ref[...].reshape(2, 16, D)
    out_ref[...] = all_ref[pl.ds(place_ref[1] * 13, 13)]


def pack_weights(place, up, down, mix, proj, merge):
    return pl.pallas_call(
        pack_kernel,
        grid_spec=pltpu.PrefetchScalarGridSpec(
            num_scalar_prefetch=1,
            grid=(1,),
            in_specs=[
                pl.BlockSpec((2, 64, D), lambda step, place: (0, place[0], 0)),
                pl.BlockSpec((2, 64, D), lambda step, place: (0, place[0], 0)),
                pl.BlockSpec((2, 3, 64, 256), lambda step, place: (0, 0, place[0], 0)),
                pl.BlockSpec((2, 16, D), lambda step, place: (0, place[0], 0)),
                pl.BlockSpec((32, D), lambda step, place: (place[0], 0)),
            ],
            out_specs=whole((13, 16, D)),
            scratch_shapes=[pltpu.VMEM((UNITS, 16, D), BF)],
        ),
        out_shape=shape_of((13, 16, D), BF),
        compiler_params=pltpu.CompilerParams(vmem_limit_bytes=VMEM),
        cost_estimate=pl.CostEstimate(flops=0, bytes_accessed=1 << 20, transcendentals=0),
    )(place, up, down, mix, proj, merge)


def merge_stats(x_ref, pack_ref, full):
    total = jnp.zeros((T, 1), F32)
    for part in range(TP):
        rows = dot_tn(pack_ref[...], x_ref[part])
        full[part] = rows
        total = total + jnp.sum(rows, axis=-1, keepdims=True)
    mean = total / MERGED
    square = jnp.zeros((T, 1), F32)
    for part in range(TP):
        center = full[part] - mean
        square = square + jnp.sum(center * center, axis=-1, keepdims=True)
    return mean, lax.rsqrt(square / MERGED + EPS)


def merge_kernel(
    core_ref, x_ref, pack_ref, gain_ref, bias_ref, w_ref, out_ref, mine_ref, other_ref, full, stats
):
    step = pl.program_id(0)

    @pl.when(step == 0)
    def _():
        mean, spread = merge_stats(x_ref, pack_ref, full)
        stats[0] = mean
        stats[1] = spread

    normed = (full[step] - stats[0]) * stats[1]
    value = (normed * gain_ref[0] + bias_ref[0]).astype(BF)

    def set_mine(part):
        mine_ref[...] = part

    def set_other(part):
        other_ref[...] = part

    put_halves(core_ref, set_mine, set_other, value[:, :256], value[:, 256:])
    term = dot(value, w_ref[...].reshape(512, D))

    @pl.when(step == 0)
    def _():
        out_ref[...] = term

    @pl.when(step != 0)
    def _():
        out_ref[...] += term


def merge_forward(core, parts, gain, bias, weights):
    return run(
        merge_kernel,
        TP,
        core,
        (parts, const(PACK), gain.reshape(TP, 1, 512), bias.reshape(TP, 1, 512), weights),
        [
            whole((TP, 2 * TOK, 512)),
            whole((2 * TOK, T)),
            pl.BlockSpec((1, 1, 512), lambda step, core: (step, 0, 0)),
            pl.BlockSpec((1, 1, 512), lambda step, core: (step, 0, 0)),
            pl.BlockSpec((YX, 2, 16, D), lambda step, core: (step, 12, 0, 0)),
        ],
        [shape_of((T, D), F32), shape_of((T, D), BF), shape_of((T, D), BF)],
        [
            whole((T, D)),
            pl.BlockSpec((T, 256), lambda step, core: (0, step)),
            pl.BlockSpec((T, 256), lambda step, core: (0, step)),
        ],
        [pltpu.VMEM((TP, T, 512), F32), pltpu.VMEM((2, T, 1), F32)],
        2 * T * MERGED * D,
        8 << 20,
    )


def merge_back_kernel(
    core_ref, x_ref, pack_ref, gain_ref, w_ref, dx_ref,
    start_ref, dm_ref, gains_ref, biases_ref,
    full, stats, upstream,
):
    step = pl.program_id(0)

    @pl.when(step == 0)
    def _():
        mean, spread = merge_stats(x_ref, pack_ref, full)
        stats[0] = mean
        stats[1] = spread
        stats[2] = jnp.zeros((T, 1), F32)
        stats[3] = jnp.zeros((T, 1), F32)
        start_ref[...] = dx_ref[...].astype(BF)

    grad = dot_nt(start_ref[...], w_ref[...].reshape(512, D))
    normed = (full[step] - stats[0]) * stats[1]
    full[step] = normed
    gains_ref[0] = col_sum(grad * normed)
    biases_ref[0] = col_sum(grad)
    scaled = grad * gain_ref[0]
    upstream[step] = scaled
    stats[2] += jnp.sum(scaled, axis=-1, keepdims=True)
    stats[3] += jnp.sum(scaled * normed, axis=-1, keepdims=True)

    @pl.when(step == TP - 1)
    def _():
        for part in range(TP):
            value = stats[1] * (
                upstream[part] - stats[2] / MERGED - full[part] * (stats[3] / MERGED)
            )
            dm_ref[part] = dot(pack_ref[...], value.astype(BF)).astype(BF)


def merge_backward(core, parts, gain, weights, grad):
    return run(
        merge_back_kernel,
        TP,
        core,
        (parts, const(PACK), gain.reshape(TP, 1, 512), weights, grad),
        [
            whole((TP, 2 * TOK, 512)),
            whole((2 * TOK, T)),
            pl.BlockSpec((1, 1, 512), lambda step, core: (step, 0, 0)),
            pl.BlockSpec((YX, 2, 16, D), lambda step, core: (step, 12, 0, 0)),
            whole((T, D)),
        ],
        [
            shape_of((T, D), BF),
            shape_of((TP, 2 * TOK, 512), BF),
            shape_of((TP, 1, 512), F32),
            shape_of((TP, 1, 512), F32),
        ],
        [
            whole((T, D)),
            whole((TP, 2 * TOK, 512)),
            pl.BlockSpec((1, 1, 512), lambda step, core: (step, 0, 0)),
            pl.BlockSpec((1, 1, 512), lambda step, core: (step, 0, 0)),
        ],
        [pltpu.VMEM((TP, T, 512), F32), pltpu.VMEM((4, T, 1), F32), pltpu.VMEM((TP, T, 512), F32)],
        2 * T * MERGED * D,
        8 << 20,
    )


def head_masks(rows):
    lane = lax.broadcasted_iota(jnp.int32, (rows, 128), 1)
    return [(lane >= 32 * place) & (lane < 32 * place + 32) for place in range(4)]


def spread_heads(value, masks):
    zero = jnp.zeros_like(value)
    return jnp.concatenate([jnp.where(mask, value, zero) for mask in masks], axis=0)


def fold_heads(value, masks):
    total = jnp.zeros((ROWS, 128), F32)
    for place, mask in enumerate(masks):
        total = jnp.where(mask, value[place * ROWS : (place + 1) * ROWS], total)
    return total


def unfold(ref):
    value = ref[...].reshape(YX, 16, D)
    parts = [value[:, :, 256 * group : 256 * group + 256] for group in range(4)]
    return jnp.stack(parts, axis=1).reshape(D, 256)


def attn_kernel(level, *refs):
    (core_ref, x_ref), refs = refs[:2], refs[2:]
    if level:
        (halo_ref, own_ref, recv_ref), refs = refs[:3], refs[3:]
    (
        gain_ref, bias_ref, wq_ref, wk_ref, wv_ref, wp_ref, qb_ref, vb_ref, table_ref, mask_ref,
        shift_ref,
    ), refs = refs[:11], refs[11:]
    (
        mid_ref, a_ref, q_ref, k_ref, v_ref, probs_ref, mine_ref, other_ref,
    ), refs = refs[:8], refs[8:]
    step = pl.program_id(0)

    @pl.when(step == 0)
    def _():
        value = x_ref[...]
        if level:
            value = select_rows(own_ref[...], value) + dot(recv_ref[...], halo_ref[...])
            refs[0][...] = value
        center, spread = norm_stats(value)
        a_ref[...] = (center * spread * gain_ref[...] + bias_ref[...]).astype(BF)
        mid_ref[...] = value + shift_ref[...]

    a = a_ref[...]
    q = (dot(a, unfold(wq_ref)) + qb_ref[...]).astype(BF)
    k = dot(a, unfold(wk_ref)).astype(BF)
    v = (dot(a, unfold(wv_ref)) + vb_ref[...]).astype(BF)
    q_ref[...] = q
    k_ref[...] = k
    v_ref[...] = v
    masks = head_masks(ROWS)
    halves = []
    for half in range(2):
        lanes = slice(half * 128, half * 128 + 128)
        table = table_ref[4 * half : 4 * half + 4]
        parts = []
        for w in range(2):
            rows = slice(w * ROWS, (w + 1) * ROWS)
            raw = dot_nt(spread_heads(q[rows, lanes], masks), k[rows, lanes]) * SCALE
            scores = raw.reshape(4, ROWS, ROWS) + table + mask_ref[w][None]
            top = jnp.max(scores, axis=-1, keepdims=True)
            terms = jnp.exp(scores - top)
            probs = (terms / jnp.sum(terms, axis=-1, keepdims=True)).astype(BF)
            probs_ref[0, w, 4 * half : 4 * half + 4] = probs
            mixed = dot(probs.reshape(4 * ROWS, ROWS), v[rows, lanes])
            parts.append(fold_heads(mixed, masks))
        halves.append(jnp.concatenate(parts, axis=0).astype(BF))

    def set_mine(part):
        mine_ref[...] = part

    def set_other(part):
        other_ref[...] = part

    put_halves(core_ref, set_mine, set_other, *halves)
    heads = jnp.concatenate(halves, axis=1)
    mid_ref[...] += dot(heads, wp_ref[...].reshape(256, D))


def unit_spec(unit):
    return pl.BlockSpec((YX, 1, 16, D), lambda step, core: (step, unit, 0, 0))


def attn_forward(core, level, state, halo, weights, small, table, mask):
    gain, bias, qbias, vbias, shift = small
    unit = 16 + 4 * level
    args = [state]
    specs = [whole((T, D))]
    if level:
        args += [halo, const(OWN), const(RECV)]
        specs += [whole((SEND, D)), whole((T, T)), whole((T, SEND))]
    args += [gain, bias, weights, weights, weights, weights, qbias, vbias, table, mask, shift]
    cols = pl.BlockSpec((1, 256), lambda step, core: (0, step))
    specs += [whole((1, D)), whole((1, D))] + [unit_spec(unit + place) for place in range(4)]
    specs += [
        cols,
        cols,
        pl.BlockSpec((8, ROWS, ROWS), lambda step, core: (step, 0, 0)),
        whole((2, ROWS, ROWS)),
        whole((1, D)),
    ]
    block = pl.BlockSpec((T, 256), lambda step, core: (0, step))
    half = pl.BlockSpec((T, 128), lambda step, core: (0, step))
    outs = [
        shape_of((T, D), F32),
        shape_of((T, D), BF),
        shape_of((T, D), BF),
        shape_of((T, D), BF),
        shape_of((T, D), BF),
        shape_of((TP, 2, 8, ROWS, ROWS), BF),
        shape_of((T, D // 2), BF),
        shape_of((T, D // 2), BF),
    ]
    out_specs = [
        whole((T, D)),
        whole((T, D)),
        block,
        block,
        block,
        pl.BlockSpec((1, 2, 8, ROWS, ROWS), lambda step, core: (step, 0, 0, 0, 0)),
        half,
        half,
    ]
    if level:
        outs.append(shape_of((T, D), F32))
        out_specs.append(whole((T, D)))
    return run(
        partial(attn_kernel, level), TP, core, args, specs, outs, out_specs, [], 8 * T * D * D, 24 << 20
    )


def quad_spec(unit):
    return pl.BlockSpec(
        (YX, 4, 16, D), lambda step, core: (lax.rem(core[1] + step, TP), unit, 0, 0)
    )


def wide_spec(rows):
    return pl.BlockSpec((rows, D), lambda step, core: (0, lax.rem(core[1] + step, TP)))


def half_spec():
    return pl.BlockSpec((T, 512), lambda step, core: (0, lax.rem(core[1] + step, TP)))


def gelu_parts(pre):
    phi = 0.5 + 0.5 * lax.erf(pre * (0.5**0.5))
    slope = phi + pre * ((2.0 * np.pi) ** -0.5 * jnp.exp(-0.5 * pre * pre))
    return (pre * phi).astype(BF), slope


def start_norm(mid_ref, gain_ref, bias_ref, shift_ref, c2_ref, total):
    value = mid_ref[...]
    center, spread = norm_stats(value)
    c2_ref[...] = (center * spread * gain_ref[...] + bias_ref[...]).astype(BF)
    total[...] = value + shift_ref[...]


def end_norm(mid_ref, gain_ref, grad, dmlp, upstream, dmid_ref, dattn_ref, rows_ref):
    center, spread = norm_stats(mid_ref[...])
    normed = center * spread
    dmid = grad + norm_back(upstream, normed, spread, gain_ref[...])
    dmid_ref[...] = dmid
    dattn = dmid.astype(BF)
    dattn_ref[...] = dattn
    rows_ref[0:1] = col_sum(upstream * normed)
    rows_ref[1:2] = col_sum(upstream)
    rows_ref[2:3] = col_sum(dmlp.astype(F32))
    rows_ref[3:4] = col_sum(dattn.astype(F32))


def put_parts(core_ref, mine_ref, other_ref, value):
    def set_mine(part):
        mine_ref[...] = part

    def set_other(part):
        other_ref[...] = part

    put_halves(core_ref, set_mine, set_other, value[:, :512], value[:, 512:])


def put_quarter(refs, value):
    for ahead, ref in enumerate(refs):

        @pl.when(pl.program_id(0) == ahead)
        def _(ref=ref):
            ref[...] = value


def mlp_kernel(
    core_ref, mid_ref, gain_ref, bias_ref, w1_ref, w2_ref, b1_ref, b2_ref, place_ref,
    c2_ref, slope_ref, halo_ref, mine_ref, other_ref, next_ref, total,
):
    step = pl.program_id(0)

    @pl.when(step == 0)
    def _():
        start_norm(mid_ref, gain_ref, bias_ref, b2_ref, c2_ref, total)

    act, slope = gelu_parts(dot(c2_ref[...], w1_ref[...].reshape(D, D)) + b1_ref[...])
    slope_ref[...] = slope.astype(BF)
    put_parts(core_ref, mine_ref, other_ref, act)
    total[...] += dot(act, w2_ref[...].reshape(D, D))

    @pl.when(step == TP - 1)
    def _():
        value = total[...]
        halo_ref[...] = dot(place_ref[...], value.astype(BF)).astype(BF)
        next_ref[...] = value


def mlp_forward(core, mid, weights, small):
    gain, bias, b1, b2 = small
    return run(
        mlp_kernel,
        TP,
        core,
        (mid, gain, bias, weights, weights, b1, b2, const(SENT)),
        [
            whole((T, D)),
            whole((1, D)),
            whole((1, D)),
            quad_spec(0),
            quad_spec(1),
            wide_spec(1),
            whole((1, D)),
            whole((SEND, T)),
        ],
        [
            shape_of((T, D), BF),
            shape_of((T, FF), BF),
            shape_of((SEND, D), BF),
            shape_of((T, FF // 2), BF),
            shape_of((T, FF // 2), BF),
            shape_of((T, D), F32),
        ],
        [whole((T, D)), wide_spec(T), whole((SEND, D)), half_spec(), half_spec(), whole((T, D))],
        [pltpu.VMEM((T, D), F32)],
        4 * T * D * FF,
        24 << 20,
    )


def mlp_both_kernel(
    core_ref, mid_ref, gain_ref, bias_ref, w1_ref, w2_ref, b1_ref, b2_ref, place_ref, keep_ref,
    dx_ref, c2_ref, out_ref, one, two, three, four, dmid_ref, dattn_ref, db1_ref, rows_ref,
    mine_ref, other_ref, total, back,
):
    step = pl.program_id(0)

    @pl.when(step == 0)
    def _():
        start_norm(mid_ref, gain_ref, bias_ref, b2_ref, c2_ref, total)
        back[...] = jnp.zeros((T, D), F32)

    up = w1_ref[...].reshape(D, D)
    down = w2_ref[...].reshape(D, D)
    act, slope = gelu_parts(dot(c2_ref[...], up) + b1_ref[...])
    put_quarter((one, two, three, four), act)
    total[...] += dot(act, down)
    dpre = (dot_nt(dx_ref[...], down) * slope).astype(BF)
    db1_ref[...] = col_sum(dpre.astype(F32))
    put_parts(core_ref, mine_ref, other_ref, dpre)
    back[...] += dot_nt(dpre, up)

    @pl.when(step == TP - 1)
    def _():
        out_ref[...] = dot(place_ref[...], (total[...] * keep_ref[...]).astype(BF)).astype(BF)
        dmlp = dx_ref[...]
        end_norm(
            mid_ref, gain_ref, dmlp.astype(F32), dmlp, back[...], dmid_ref, dattn_ref, rows_ref
        )


def mlp_both(core, mid, weights, small, keep, dx):
    gain, bias, b1, b2 = small
    return run(
        mlp_both_kernel,
        TP,
        core,
        (mid, gain, bias, weights, weights, b1, b2, const(OUT), keep, dx),
        [
            whole((T, D)),
            whole((1, D)),
            whole((1, D)),
            quad_spec(2),
            quad_spec(3),
            wide_spec(1),
            whole((1, D)),
            whole((2 * TOK, T)),
            whole((T, 1)),
            whole((T, D)),
        ],
        [shape_of((T, D), BF), shape_of((2 * TOK, D), BF)]
        + [shape_of((T, D), BF)] * TP
        + [
            shape_of((T, D), F32),
            shape_of((T, D), BF),
            shape_of((1, FF), F32),
            shape_of((4, D), F32),
            shape_of((T, FF // 2), BF),
            shape_of((T, FF // 2), BF),
        ],
        [whole((T, D)), whole((2 * TOK, D))]
        + [whole((T, D))] * TP
        + [whole((T, D)), whole((T, D)), wide_spec(1), whole((4, D)), half_spec(), half_spec()],
        [pltpu.VMEM((T, D), F32), pltpu.VMEM((T, D), F32)],
        8 * T * D * FF,
        24 << 20,
    )


def mlp_back_kernel(
    core_ref, dx_ref, halo_ref, own_ref, sent_ref, mid_ref, gain_ref, w1_ref, w2_ref, slope_ref,
    dmid_ref, dmlp_ref, dattn_ref, db1_ref, rows_ref, one, two, three, four, total, grad,
):
    step = pl.program_id(0)

    @pl.when(step == 0)
    def _():
        value = select_rows_t(own_ref[...], dx_ref[...]) + dot_tn(sent_ref[...], halo_ref[...])
        grad[...] = value
        dmlp_ref[...] = value.astype(BF)
        total[...] = jnp.zeros((T, D), F32)

    dact = dot_nt(dmlp_ref[...], w2_ref[...].reshape(D, D))
    dpre = (dact * slope_ref[...].astype(F32)).astype(BF)
    db1_ref[...] = col_sum(dpre.astype(F32))
    put_quarter((one, two, three, four), dpre)
    total[...] += dot_nt(dpre, w1_ref[...].reshape(D, D))

    @pl.when(step == TP - 1)
    def _():
        end_norm(
            mid_ref, gain_ref, grad[...], dmlp_ref[...], total[...], dmid_ref, dattn_ref, rows_ref
        )


def select_rows_t(matrix, value):
    high = value.astype(BF)
    rest = value - high.astype(F32)
    mid = rest.astype(BF)
    low = (rest - mid.astype(F32)).astype(BF)
    return dot_tn(matrix, high) + dot_tn(matrix, mid) + dot_tn(matrix, low)


def mlp_backward(core, grad, halo, mid, gain, weights, slope):
    return run(
        mlp_back_kernel,
        TP,
        core,
        (grad, halo, const(OWN), const(SENT), mid, gain, weights, weights, slope),
        [
            whole((T, D)),
            whole((SEND, D)),
            whole((T, T)),
            whole((SEND, T)),
            whole((T, D)),
            whole((1, D)),
            quad_spec(0),
            quad_spec(1),
            wide_spec(T),
        ],
        [
            shape_of((T, D), F32),
            shape_of((T, D), BF),
            shape_of((T, D), BF),
            shape_of((1, FF), F32),
            shape_of((4, D), F32),
        ]
        + [shape_of((T, D), BF)] * TP,
        [whole((T, D)), whole((T, D)), whole((T, D)), wide_spec(1), whole((4, D))]
        + [whole((T, D))] * TP,
        [pltpu.VMEM((T, D), F32), pltpu.VMEM((T, D), F32)],
        4 * T * D * FF,
        24 << 20,
    )


def attn_back_kernel(level, *refs):
    (
        core_ref, dmid_ref, dattn_ref, x_ref, gain_ref, wq_ref, wk_ref, wv_ref, wp_ref,
        q_ref, k_ref, v_ref, probs_ref,
    ), refs = refs[:13], refs[13:]
    if level:
        (place_ref,), refs = refs[:1], refs[1:]
    (dx_ref, mine_ref, other_ref, pair_ref, sums_ref, rows_ref), refs = refs[:6], refs[6:]
    if level:
        (sent_ref,), refs = refs[:1], refs[1:]
    (total,) = refs
    step = pl.program_id(0)

    @pl.when(step == 0)
    def _():
        total[...] = jnp.zeros((T, D), F32)

    dheads = dot_nt(dattn_ref[...], wp_ref[...].reshape(256, D)).astype(BF)
    masks = head_masks(ROWS)
    dqs, dks, dvs = [], [], []
    for half in range(2):
        lanes = slice(half * 128, half * 128 + 128)
        dq_parts, dk_parts, dv_parts = [], [], []
        pairs = None
        for w in range(2):
            rows = slice(w * ROWS, (w + 1) * ROWS)
            rounded = probs_ref[0, w, 4 * half : 4 * half + 4].reshape(4 * ROWS, ROWS)
            probs = rounded.astype(F32)
            spread_out = spread_heads(dheads[rows, lanes], masks)
            dprobs = dot_nt(spread_out, v_ref[rows, lanes])
            dv_parts.append(dot_tn(rounded, spread_out))
            inner = jnp.sum(probs * dprobs, axis=-1, keepdims=True)
            dscores = (probs * (dprobs - inner)).astype(BF)
            wide = dscores.astype(F32)
            pairs = wide if pairs is None else pairs + wide
            dq_parts.append(fold_heads(dot(dscores, k_ref[rows, lanes]), masks))
            dk_parts.append(dot_tn(dscores, spread_heads(q_ref[rows, lanes], masks)))
        pair_ref[4 * half : 4 * half + 4] = pairs.reshape(4, ROWS, ROWS)
        dqs.append((jnp.concatenate(dq_parts, axis=0) * SCALE).astype(BF))
        dks.append((jnp.concatenate(dk_parts, axis=0) * SCALE).astype(BF))
        dvs.append(jnp.concatenate(dv_parts, axis=0).astype(BF))

    def set_mine(part):
        mine_ref[...] = part

    def set_other(part):
        other_ref[...] = part

    put_halves(
        core_ref,
        set_mine,
        set_other,
        jnp.concatenate([dqs[0], dks[0], dvs[0]], axis=1),
        jnp.concatenate([dqs[1], dks[1], dvs[1]], axis=1),
    )
    dq = jnp.concatenate(dqs, axis=1)
    dk = jnp.concatenate(dks, axis=1)
    dv = jnp.concatenate(dvs, axis=1)
    sums_ref[0:1] = col_sum(dq.astype(F32))
    sums_ref[1:2] = col_sum(dv.astype(F32))
    total[...] += (
        dot_nt(dq, unfold(wq_ref))
        + dot_nt(dk, unfold(wk_ref))
        + dot_nt(dv, unfold(wv_ref))
    )

    @pl.when(step == TP - 1)
    def _():
        center, spread = norm_stats(x_ref[...])
        normed = center * spread
        upstream = total[...]
        value = dmid_ref[...] + norm_back(upstream, normed, spread, gain_ref[...])
        dx_ref[...] = value
        rows_ref[0:1] = col_sum(upstream * normed)
        rows_ref[1:2] = col_sum(upstream)
        if level:
            sent_ref[...] = dot_tn(place_ref[...], value.astype(BF)).astype(BF)


def attn_backward(core, level, dmid, dattn, state, gain, weights, q, k, v, probs):
    unit = 16 + 4 * level
    block = pl.BlockSpec((T, 256), lambda step, core: (0, step))
    part = pl.BlockSpec((T, 384), lambda step, core: (0, step))
    args = [dmid, dattn, state, gain, weights, weights, weights, weights, q, k, v, probs]
    specs = [whole((T, D)), whole((T, D)), whole((T, D)), whole((1, D))]
    specs += [unit_spec(unit + place) for place in range(4)]
    specs += [
        block,
        block,
        block,
        pl.BlockSpec((1, 2, 8, ROWS, ROWS), lambda step, core: (step, 0, 0, 0, 0)),
    ]
    outs = [
        shape_of((T, D), F32),
        shape_of((T, 1536), BF),
        shape_of((T, 1536), BF),
        shape_of((32, ROWS, ROWS), F32),
        shape_of((2, D), F32),
        shape_of((2, D), F32),
    ]
    out_specs = [
        whole((T, D)),
        part,
        part,
        pl.BlockSpec((8, ROWS, ROWS), lambda step, core: (step, 0, 0)),
        pl.BlockSpec((2, 256), lambda step, core: (0, step)),
        whole((2, D)),
    ]
    if level:
        args.append(const(RECV))
        specs.append(whole((T, SEND)))
        outs.append(shape_of((SEND, D), BF))
        out_specs.append(whole((SEND, D)))
    return run(
        partial(attn_back_kernel, level),
        TP,
        core,
        args,
        specs,
        outs,
        out_specs,
        [pltpu.VMEM((T, D), F32)],
        8 * T * D * D,
        24 << 20,
    )


def weight_kernel(plan, *refs):
    refs, out_ref = refs[1:-1], refs[-1]
    place = 0
    column = 0
    for kind, size, count in plan:
        parts = [ref[...] for ref in refs[place : place + count]]
        if kind == "matrix":
            value = dot_tn(
                jnp.concatenate(parts[:2], axis=0), jnp.concatenate(parts[2:], axis=0)
            )
        else:
            value = sum(part.astype(F32) for part in parts)
        out_ref[:, 0, :, column : column + size] = value.astype(BF).reshape(YX, 64, size)
        column += size
        place += count


def weight_grads(core, items, sums):
    plan, args, specs = [], [], []
    for left, right in items:
        size = right[0].shape[1] // TP
        plan.append(("matrix", size, 4))
        args += [left[0], left[1], right[0], right[1]]
        block = pl.BlockSpec((T, size), lambda step, core: (0, step))
        specs += [whole((T, D)), whole((T, D)), block, block]
    for pieces in sums:
        plan.append(("sum", 128, len(pieces)))
        args += pieces
        specs += [pl.BlockSpec((D, 128), lambda step, core: (0, step))] * len(pieces)
    width = sum(size for unused, size, count in plan)
    return run(
        partial(weight_kernel, plan),
        TP,
        core,
        args,
        specs,
        shape_of((YX, TP, 64, width), BF),
        pl.BlockSpec((YX, 1, 64, width), lambda step, core: (0, step, 0, 0)),
        [],
        4 * T * D * width * TP,
        (2 * D * width * TP) + (8 << 20),
    )


def column_kernel(core_ref, *refs):
    lefts, rights, (other_ref, mine_ref) = refs[:TP], refs[TP : 2 * TP], refs[2 * TP :]
    left = jnp.concatenate([ref[...] for ref in lefts], axis=0)
    right = jnp.concatenate([ref[...] for ref in rights], axis=0)
    value = dot_tn(left, right).astype(BF)

    @pl.when(pl.program_id(0) == 0)
    def _():
        other_ref[...] = value

    @pl.when(pl.program_id(0) == 1)
    def _():
        mine_ref[...] = value


def column_grads(core, lefts, rights):
    half = pl.BlockSpec((T, 512), lambda step, core: (0, (core[0] + 1 + step) % 2))
    return run(
        column_kernel,
        2,
        core,
        list(lefts) + list(rights),
        [whole((T, D))] * TP + [half] * TP,
        [shape_of((D, 512), BF)] * 2,
        [whole((D, 512))] * 2,
        [],
        4 * T * D * 2048,
        8 << 20,
    )


def send_ahead(pieces):
    return [pieces[0]] + [
        lax.ppermute(pieces[step], "tp", [(i, (i + step) % TP) for i in range(TP)])
        for step in range(1, TP)
    ]


def send_all(value):
    return send_ahead([value] * TP)


def sum_quarters(value, column):
    pieces = [
        lax.dynamic_index_in_dim(value, (column + step) % TP, 0, keepdims=False)
        for step in range(TP)
    ]
    got = [piece.astype(F32) for piece in send_ahead(pieces)]
    return (got[0] + got[1]) + (got[2] + got[3])


def table_index():
    place = np.zeros((RELS, WIN * 190), np.float32)
    for row in range(WIN):
        for step in range(19):
            for col in range(WIN):
                place[(18 - step) * 19 + row - col + 9, row * 190 + step * WIN + col] = 1
    return place


PAIRS = table_index()


def spread_tables(tables):
    compact = jnp.dot(tables.reshape(64, RELS), jnp.asarray(PAIRS), precision=HIGH)
    compact = compact.reshape(2, 32, WIN, 190)
    rows = [compact[..., (9 - row) * WIN : (9 - row) * WIN + TOK] for row in range(WIN)]
    full = jnp.stack(rows, axis=2).reshape(2, 32, TOK, TOK)
    return jnp.pad(full, ((0, 0), (0, 0), (0, ROWS - TOK), (0, ROWS - TOK)))


def fold_tables(pairs):
    total = jnp.zeros((32, WIN, 190), F32)
    for row in range(WIN):
        low = (9 - row) * WIN
        total = total + jnp.pad(
            pairs[:, row * WIN : (row + 1) * WIN, :TOK], ((0, 0), (0, 0), (low, 90 - low))
        )
    return jnp.dot(total.reshape(32, -1), jnp.asarray(PAIRS.T), precision=HIGH)


def window_masks(level, valid, column):
    place = np.arange(ROWS)
    row = np.minimum(place // WIN, WIN - 1)
    col = jnp.asarray(place % WIN, jnp.int32)
    real = jnp.asarray(place < TOK)
    offset = SHIFT if level else 0
    rolled = column * WIN + col
    usable = (rolled + offset) % GW < valid
    masks = []
    for w in range(2):
        rolled_row = w * WIN + row
        row_region = (rolled_row >= GH - WIN).astype(np.int32) + (rolled_row >= GH - SHIFT)
        col_region = (rolled >= GW - WIN).astype(jnp.int32) + (rolled >= GW - SHIFT)
        region = jnp.asarray(row_region * 3, jnp.int32) + col_region
        allowed = usable[None, :]
        if level:
            allowed = allowed & (region[:, None] == region[None, :])
        mask = jnp.where(allowed, F32(0.0), F32(-100.0))
        mask = jnp.where(real[None, :], mask, F32(-1e30))
        masks.append(jnp.broadcast_to(mask, (ROWS, ROWS)))
    return jnp.stack(masks)


def gather_tp(value, place):
    parts = [value]
    for step in range(1, TP):
        parts.append(lax.ppermute(value, "tp", [(i, (i + step) % TP) for i in range(TP)]))
    stacked = jnp.stack(parts)
    order = (place - jnp.arange(TP)) % TP
    return [lax.dynamic_index_in_dim(stacked, order[i], 0, keepdims=False) for i in range(TP)]


def after(value, others):
    return lax.optimization_barrier((value, others))


def swap_core(value):
    return lax.ppermute(value, "core", [(0, 1), (1, 0)])


def sum_all(value):
    sent = value.astype(BF)
    value = sent.astype(F32) + swap_core(sent).astype(F32)
    for axis in ("x", "y", "tp"):
        sent = value.astype(BF)
        got = [
            lax.ppermute(sent, axis, [(i, (i + gap) % 4) for i in range(4)]).astype(F32)
            for gap in (1, 2, 3)
        ]
        value = (sent.astype(F32) + got[1]) + (got[0] + got[2])
    return value


def body(
    x3,
    res_group,
    merge_gain,
    merge_bias,
    merge_w,
    ln1_gain,
    ln1_bias,
    qkv_w,
    qv_bias,
    rel_table,
    proj_w,
    proj_bias,
    ln2_gain,
    ln2_bias,
    fc1_w,
    fc1_bias,
    fc2_w,
    fc2_bias,
    out_grad,
):
    core_at = lax.axis_index("core")
    chip_at = lax.axis_index("y") * 4 + lax.axis_index("x")
    column = lax.axis_index("tp")
    core = jnp.stack([core_at, column]).astype(jnp.int32)

    piece = pack_weights(
        jnp.stack([chip_at, core_at]).astype(jnp.int32),
        fc1_w,
        fc2_w,
        jnp.swapaxes(qkv_w, 1, 2),
        proj_w,
        merge_w.reshape(512, D),
    )
    weights = lax.all_gather(piece.reshape(-1, D), GATHER_AXES, axis=0, tiled=True)
    weights = weights.reshape(64, UNITS, 16, D)

    pages = lax.all_to_all(x3, PAGE_AXES, split_axis=1, concat_axis=0, tiled=True)
    tiles = pages.reshape(GH, TP, WIN, 512).transpose(1, 0, 2, 3).reshape(TP * 2 * TOK, 512)
    parts = lax.all_to_all(tiles, "tp", split_axis=0, concat_axis=0, tiled=True)
    parts = parts.reshape(TP, 2 * TOK, 512)

    packed = jnp.concatenate(
        [
            merge_gain.reshape(-1),
            merge_bias.reshape(-1),
            qv_bias.reshape(-1),
            fc1_bias.reshape(-1),
            rel_table.reshape(-1),
            jnp.zeros((10240 - 9872,), F32),
        ]
    ).reshape(80, 128)
    quarters = [part.reshape(-1) for part in gather_tp(packed, column)]

    def joined(low, shape, axis):
        size = int(np.prod(shape))
        return jnp.concatenate([part[low : low + size].reshape(shape) for part in quarters], axis)

    merge_gain_all = joined(0, (1, 512), 0)
    merge_bias_all = joined(512, (1, 512), 0)
    qv_bias_all = joined(1024, (2, 2, 256), 2)
    fc1_bias_all = joined(2048, (2, 1024), 1)
    tables = spread_tables(joined(4096, (2, 8, RELS), 1))
    tables = [tables[0], tables[1]]

    valid = (res_group[0] + 1) * WIN
    masks = [window_masks(level, valid, column) for level in range(2)]
    spot = np.arange(T) % ROWS
    keep = ((column * WIN + SHIFT + jnp.asarray(spot % WIN, jnp.int32)) % GW < valid) & jnp.asarray(
        spot < TOK
    )
    keep = keep.astype(F32)[:, None]
    page_keep = (jnp.asarray(np.arange(GW), jnp.int32) < valid).astype(BF)[None, :, None]
    tiles = jnp.roll(out_grad[0] * page_keep, (-SHIFT, -SHIFT), (0, 1))
    tiles = tiles.reshape(2, WIN, TP, WIN, D).transpose(2, 0, 1, 3, 4).reshape(TP, 2, TOK, D)
    tiles = jnp.pad(tiles, ((0, 0), (0, 0), (0, ROWS - TOK), (0, 0))).reshape(TP, T, D)
    tiles = [
        lax.dynamic_index_in_dim(tiles, (column + TP - back) % TP, 0, keepdims=False)
        for back in range(TP)
    ]

    weights, (tables, masks, tiles, keep, parts) = after(
        weights, (tables, masks, tiles, keep, parts)
    )
    state, merged_mine, merged_other = merge_forward(
        core, parts, merge_gain_all, merge_bias_all, weights
    )
    halo = None
    pending = [swap_core(merged_other)]
    for level in range(2):
        small = (
            ln1_gain[level : level + 1],
            ln1_bias[level : level + 1],
            qv_bias_all[level, 0:1],
            qv_bias_all[level, 1:2],
            proj_bias[level : level + 1],
        )
        got = attn_forward(
            core, level, state, halo, weights, small, tables[level], masks[level]
        )
        mid, a, q, k, v, probs, heads_mine, heads_other = got[:8]
        start = got[8] if level else state
        mid, pending = after(mid, pending)
        small = (
            ln2_gain[level : level + 1],
            ln2_bias[level : level + 1],
            fc1_bias_all[level : level + 1],
            fc2_bias[level : level + 1],
        )
        if level:
            got = mlp_both(core, mid, weights, small, keep, tiles[0])
            c2, extra, *acts = got[:6]
            dmid, dattn, db1, rows_two, dpre_mine, dpre_other = got[6:]
            dattn, (a_zero, heads_zero, c2_all, a_got, heads_got) = after(
                dattn, (*pending, c2_all, swap_core(a), swap_core(heads_other))
            )
        else:
            swapped = [swap_core(a), swap_core(heads_other)]
            c2, slope, halo, act_mine, act_other, state = mlp_forward(core, mid, weights, small)
            (merged_got,) = pending
            pending = swapped
            kept = (start, mid, a, q, k, v, probs, slope, c2, heads_mine)
            halo = lax.ppermute(halo, "tp", [((i + 1) % TP, i) for i in range(TP)])
            halo, c2 = lax.optimization_barrier((halo, c2))
            c2_all = send_all(c2)
    acts = send_ahead(acts)
    dpre_got, dattn_got, c2_got = [swap_core(value) for value in (dpre_other, dattn, c2)]

    sums = [None, None]
    got = attn_backward(core, 1, dmid, dattn, start, ln1_gain[1:2], weights, q, k, v, probs)
    grad, mixed_mine, mixed_other, pairs, dqv, rows_one, sent = got
    sent, (dpre_got, dattn_got, c2_got) = after(sent, (dpre_got, dattn_got, c2_got))
    halo = lax.ppermute(sent, "tp", [(i, (i + 1) % TP) for i in range(TP)])
    mixed_got = swap_core(mixed_other)
    sums[1] = (db1, rows_two, dqv, rows_one, pairs)
    items = [
        ((c2, c2_got), (dpre_mine, dpre_got)),
        ((a, a_got), (mixed_mine, mixed_got)),
        ((dattn, dattn_got), (heads_mine, heads_got)),
    ]
    late = weight_grads(core, items, [])
    late, halo = lax.optimization_barrier((late, halo))
    late = lax.psum_scatter(late, CHIP_AXES, scatter_dimension=0, tiled=True)
    late = lax.optimization_barrier(late)[0]

    start, mid, a, q, k, v, probs, slope, c2, heads_mine = kept
    halo, act_other = lax.optimization_barrier((halo, act_other))
    act_got = swap_core(act_other)
    got = mlp_backward(core, grad, halo, mid, ln2_gain[0:1], weights, slope)
    dmid, dmlp, dattn, db1, rows_two = got[:5]
    dattn, (dpre, act_got, acts, tiles) = after(dattn, (list(got[5:]), act_got, acts, tiles))
    dpre = send_ahead(dpre)
    got = attn_backward(core, 0, dmid, dattn, start, ln1_gain[0:1], weights, q, k, v, probs)
    grad, mixed_mine, mixed_other, pairs, dqv, rows_one = got
    sums[0] = (db1, rows_two, dqv, rows_one, pairs)
    grad, dattn_sent = lax.optimization_barrier((grad, dattn))
    mixed_got, dattn_got = [swap_core(value) for value in (mixed_other, dattn_sent)]
    first, dm, dgain, dbias = merge_backward(core, parts, merge_gain_all, weights, grad)
    last_other, last_mine = column_grads(core, tiles, acts)
    last_got = swap_core(last_other)
    first, dpre = after(first, dpre)
    first_got, dmlp_got = swap_core(first), swap_core(dmlp)
    up_other, up_mine = column_grads(core, c2_all, dpre)
    up_mine, (first_got, dmlp_got, last_got, mixed_got, dattn_got) = after(
        up_mine, (first_got, dmlp_got, last_got, mixed_got, dattn_got)
    )
    items = [
        ((a, a_zero), (mixed_mine, mixed_got)),
        ((dattn, dattn_got), (heads_mine, heads_zero)),
        ((first, first_got), (merged_mine, merged_got)),
        ((dmlp, dmlp_got), (act_mine, act_got)),
    ]
    early = weight_grads(
        core, items, [[up_mine, swap_core(up_other)], [last_mine, last_got]]
    )
    early, (extra, sums, dgain, dbias) = after(early, (extra, sums, dgain, dbias))
    early = lax.psum_scatter(early, CHIP_AXES, scatter_dimension=0, tiled=True)
    early = lax.optimization_barrier(early)[0]

    tiles_out = jnp.stack(gather_tp(extra, column)).reshape(TP, GH, WIN, D)
    output = jnp.roll(tiles_out.transpose(1, 0, 2, 3).reshape(GH, GW, D), SHIFT, 1)
    output = output.astype(F32)[None]
    back = lax.all_to_all(
        dm.reshape(TP * 2 * TOK, 512), "tp", split_axis=0, concat_axis=0, tiled=True
    )
    back = back.reshape(TP, GH, WIN, 512).transpose(1, 0, 2, 3).reshape(800, 1, 4, 128)
    grad_x3 = lax.all_to_all(back, PAGE_AXES, split_axis=0, concat_axis=1, tiled=True).astype(F32)

    def both_cores(value):
        rows = value.reshape(2, 32, -1)
        kept_rows = lax.dynamic_index_in_dim(rows, core_at, 0, keepdims=False).astype(F32)
        sent_rows = lax.dynamic_index_in_dim(rows, 1 - core_at, 0, keepdims=False)
        got_rows = swap_core(sent_rows.astype(BF)).astype(F32)
        return (
            jnp.where(core_at == 0, kept_rows, got_rows),
            jnp.where(core_at == 0, got_rows, kept_rows),
        )

    def wide(halves, low, size):
        return jnp.concatenate([half[:, low : low + size] for half in halves], axis=1)

    def finish(value, split):
        complete = value[..., split:].reshape(TP, 64, -1, 128).transpose(1, 2, 0, 3)
        partial_sums = sum_quarters(value[..., :split], column)
        return both_cores(
            jnp.concatenate([partial_sums, complete.reshape(64, -1).astype(F32)], axis=1)
        )

    late = both_cores(sum_quarters(late, column))
    early = finish(early, 1280)
    g_fc1 = jnp.stack([wide(early, 1280, 512), wide(late, 0, 512)])
    g_fc2 = jnp.stack([wide(early, 768, 512).T, wide(early, 1792, 512).T])
    pair = ((early, 0), (late, 512))
    g_qkv = jnp.stack(
        [jnp.stack([wide(half, low + 128 * s, 128) for s in range(3)], axis=1) for half, low in pair]
    )
    g_proj = jnp.stack([wide(half, low + 384, 128).T for half, low in pair])
    g_merge_w = wide(early, 512, 256).T.reshape(4, 128, 32)

    flat = []
    for level in range(2):
        db1, rows_two, dqv, rows_one, pairs = sums[level]
        flat += [rows_one, rows_two, dqv, db1, fold_tables(pairs)]
    flat += [dgain, dbias]
    flat = jnp.concatenate([item.reshape(-1) for item in flat])
    count = flat.shape[0]
    flat = jnp.pad(flat, (0, -count % 16384)).reshape(-1, 1024)
    flat = sum_all(flat).reshape(-1)
    page_at = chip_at * 2 + core_at

    def take(low, shape):
        return flat[low : low + int(np.prod(shape))].reshape(shape)

    def page_part(value):
        return lax.dynamic_slice_in_dim(value, page_at * 32, 32, value.ndim - 1)

    def tp_part(value, axis):
        size = value.shape[axis] // TP
        return lax.dynamic_slice_in_dim(value, column * size, size, axis)

    span = 2 * D + 4 * D + 2 * D + FF + 32 * RELS
    rows = [take(level * span, (6, D)) for level in range(2)]
    rows = page_part(jnp.stack(rows))
    dqv = tp_part(jnp.stack([take(level * span + 6 * D, (2, D)) for level in range(2)]), 2)
    db1 = tp_part(jnp.stack([take(level * span + 8 * D, (FF,)) for level in range(2)]), 1)
    table = tp_part(
        jnp.stack([take(level * span + 8 * D + FF, (32, RELS)) for level in range(2)]), 1
    )
    dgain = tp_part(take(2 * span, (TP, 512)), 0).reshape(4, 128)
    dbias = tp_part(take(2 * span + MERGED, (TP, 512)), 0).reshape(4, 128)
    return (
        output,
        grad_x3,
        dgain,
        dbias,
        g_merge_w,
        rows[:, 0],
        rows[:, 1],
        g_qkv,
        dqv,
        table,
        g_proj,
        rows[:, 5],
        rows[:, 2],
        rows[:, 3],
        g_fc1,
        db1,
        g_fc2,
        rows[:, 4],
    )


def solution(mesh):
    grid = Mesh(mesh.devices.reshape(4, 4, 2, TP), ("y", "x", "core", "tp"))
    page = PAGE_AXES
    return jax.shard_map(
        body,
        mesh=grid,
        in_specs=(
            P(page, None, None, "tp"),
            P(page),
            P(None, "tp"),
            P(None, "tp"),
            P(None, "tp", None),
            P(),
            P(),
            P(None, None, None, "tp"),
            P(None, None, "tp"),
            P(None, "tp", None),
            P(None, "tp", None),
            P(),
            P(),
            P(),
            P(None, None, "tp"),
            P(None, "tp"),
            P(None, "tp", None),
            P(),
            P(page, None, None, None),
        ),
        out_specs=(
            P(page, None, None, None),
            P(page, None, None, "tp"),
            P(None, "tp"),
            P(None, "tp"),
            P(None, "tp", page),
            P(None, page),
            P(None, page),
            P(None, page, None, "tp"),
            P(None, None, "tp"),
            P(None, "tp", None),
            P(None, "tp", page),
            P(None, page),
            P(None, page),
            P(None, page),
            P(None, page, "tp"),
            P(None, "tp"),
            P(None, "tp", page),
            P(None, page),
        ),
        check_vma=False,
    )
```
